32 devices in a mesh: seq: 16 (over z, y, x), tp: 2 (over core).
Axes of the slice: x: 2, y: 2, z: 4, core: 2. Of those that a mesh axis runs over, the one named last changes fastest.
Arguments:
- block_input: bfloat16 [2, 4096, 2048], P(None, 'seq'), may hold values from -6 to 6
- lengths: int32 [2], replicated, may hold values from 1024 to 4096, as said below
- attn_gain: float32 [2048], P('seq'), may hold values from 0.5 to 1.5
- query_weight: float32 [2048, 2048], P('seq', 'tp'), may hold values from -0.125 to 0.125
- key_weight: float32 [2048, 2048], P('seq', 'tp'), may hold values from -0.125 to 0.125
- value_weight: float32 [2048, 2048], P('seq', 'tp'), may hold values from -0.125 to 0.125
- outgate_weight: float32 [2048, 2048], P('seq', 'tp'), may hold values from -0.125 to 0.125
- beta_weight: float32 [2048, 16], P('seq', 'tp'), may hold values from -0.125 to 0.125
- conv_kernel: float32 [16, 3, 4, 128], P('tp', None, None, 'seq'), may hold values from -3 to 3
- head_gain: float32 [128], P('seq'), may hold values from 0.5 to 1.5
- output_weight: float32 [2048, 2048], P('tp', 'seq'), may hold values from -0.125 to 0.125
- mlp_gain: float32 [2048], P('seq'), may hold values from 0.5 to 1.5
- swish_weight: float32 [2048, 5632], P('seq', 'tp'), may hold values from -0.125 to 0.125
- upward_weight: float32 [2048, 5632], P('seq', 'tp'), may hold values from -0.125 to 0.125
- downward_weight: float32 [5632, 2048], P('tp', 'seq'), may hold values from -0.078125 to 0.078125
- out_grad: bfloat16 [2, 4096, 2048], P(None, 'seq'), may hold values from -6 to 6
Outputs:
- block_output: bfloat16 [2, 4096, 2048], P(None, 'seq')
- input_grad: bfloat16 [2, 4096, 2048], P(None, 'seq')
- attn_gain_grad: float32 [2048], P('seq')
- query_grad: float32 [2048, 2048], P('seq', 'tp')
- key_grad: float32 [2048, 2048], P('seq', 'tp')
- value_grad: float32 [2048, 2048], P('seq', 'tp')
- outgate_grad: float32 [2048, 2048], P('seq', 'tp')
- beta_grad: float32 [2048, 16], P('seq', 'tp')
- conv_grad: float32 [16, 3, 4, 128], P('tp', None, None, 'seq')
- head_gain_grad: float32 [128], P('seq')
- output_grad: float32 [2048, 2048], P('tp', 'seq')
- mlp_gain_grad: float32 [2048], P('seq')
- swish_grad: float32 [2048, 5632], P('seq', 'tp')
- upward_grad: float32 [2048, 5632], P('seq', 'tp')
- downward_grad: float32 [5632, 2048], P('tp', 'seq')
The draws below stay inside these ranges and needn't reach their ends.
Inputs may be any that keep to these rules, and one draw needn't show every extreme that they name: `lengths`: one of the two sequences, chosen by the seed, has 4096 live positions; the other has 1024 or more.
All inputs are finite; a program needn't handle non-finite values.
Results may differ from the reference program's by a relative error of at most 0.02.
The reference program's roundings to bfloat16 on the way count: a program that leaves them out, or rounds other values in their place, can miss the bound.
Values may be sent and summed in bfloat16 or wider, within the bound.
A program may use at most 640 MiB of HBM per device.

```python
import jax
import jax.numpy as jnp
from jax import lax

D = 2048
H = 16
DH = 128
FF = 5632
BLOCK = 64
CONV = 4
SEQS = 2
L = 4096


def draw_lengths(key, part):
    key = jax.random.fold_in(key, 7)
    first_key, second_key = jax.random.split(key)
    longest = jax.random.randint(first_key, (), 0, SEQS)
    others = jax.random.randint(second_key, (SEQS,), L // 4, L + 1)
    return jnp.where(jnp.arange(SEQS) == longest, L, others).astype(jnp.int32)


def level_of(stream_key, shape, cuts, smallest, top_value):
    level, own = 1.0, jax.random.fold_in(stream_key, 6)
    for position, shards_of in cuts:
        heights = jnp.exp(jax.random.uniform(jax.random.fold_in(own, position), (shards_of,), jnp.float32, smallest / len(cuts), top_value / len(cuts)))
        level = level * jnp.repeat(heights, shape[position] // shards_of).reshape([-1 if axis == position else 1 for axis in range(len(shape))])
    return level


def bell_draw(own_key, shape, spread, limit, shards=(), held_as=jnp.bfloat16):
    values = spread * jax.random.normal(own_key, shape, jnp.float32)
    if shards:
        values = values * level_of(own_key, shape, shards, -0.22, 0.18)
    return jnp.clip(values, -limit, limit).astype(held_as)


def setup_inputs(seed: int = 0) -> dict:
    streams_of = jax.random.split(jax.random.key(seed), 17)
    return {
        "block_input": bell_draw(streams_of[0], (SEQS, L, D), 1.0, 6.0, ((1, 16),)),
        "lengths": draw_lengths(jax.random.fold_in(streams_of[16], 71), 0),
        "attn_gain": jnp.clip(1.0 + 0.1 * jax.random.normal(streams_of[2], (D,), jnp.float32), 0.5, 1.5),
        "query_weight": bell_draw(streams_of[3], (D, D), D ** -0.5, 0.125, ((0, 16), (1, 2)), jnp.float32),
        "key_weight": bell_draw(streams_of[4], (D, D), D ** -0.5, 0.125, ((0, 16), (1, 2)), jnp.float32),
        "value_weight": bell_draw(streams_of[5], (D, D), D ** -0.5, 0.125, ((0, 16), (1, 2)), jnp.float32),
        "outgate_weight": bell_draw(streams_of[6], (D, D), D ** -0.5, 0.125, ((0, 16), (1, 2)), jnp.float32),
        "beta_weight": bell_draw(streams_of[7], (D, H), D ** -0.5, 0.125, ((0, 16), (1, 2)), jnp.float32),
        "conv_kernel": bell_draw(streams_of[8], (H, 3, CONV, DH), CONV ** -0.5, 3.0, ((0, 2), (3, 16)), jnp.float32),
        "head_gain": jnp.clip(1.0 + 0.1 * jax.random.normal(streams_of[9], (DH,), jnp.float32), 0.5, 1.5),
        "output_weight": bell_draw(streams_of[10], (D, D), D ** -0.5, 0.125, ((0, 2), (1, 16)), jnp.float32),
        "mlp_gain": jnp.clip(1.0 + 0.1 * jax.random.normal(streams_of[11], (D,), jnp.float32), 0.5, 1.5),
        "swish_weight": bell_draw(streams_of[12], (D, FF), D ** -0.5, 0.125, ((0, 16), (1, 2)), jnp.float32),
        "upward_weight": bell_draw(streams_of[13], (D, FF), D ** -0.5, 0.125, ((0, 16), (1, 2)), jnp.float32),
        "downward_weight": bell_draw(streams_of[14], (FF, D), FF ** -0.5, 0.078125, ((0, 2), (1, 16)), jnp.float32),
        "out_grad": bell_draw(streams_of[15], (SEQS, L, D), 1.0, 6.0, ((1, 16),)),
    }


PRECISE = lax.Precision.HIGHEST
epsilon = 1e-06

@jax.custom_vjp
def low(v):
    return lax.optimization_barrier(v.astype(jnp.bfloat16)).astype(jnp.float32)

@jax.custom_vjp
def low_back(v):
    return v

def low_keep(v):
    return (low(v), None)

def low_pass(kept, grad):
    return (grad,)

def back_keep(v):
    return (v, None)

def back_low(kept, grad):
    return (low(grad),)
low.defvjp(low_keep, low_pass)
low_back.defvjp(back_keep, back_low)

def matmul(left, right):
    return jnp.dot(left.astype(jnp.float32), right.astype(jnp.float32), precision=PRECISE, preferred_element_type=jnp.float32)

def product(form, left, right):
    return jnp.einsum(form, left, right, precision=PRECISE)

def rms_scale(value):
    return lax.rsqrt(lax.optimization_barrier(jnp.mean(value * value, axis=-1, keepdims=True)) + epsilon)

def block_step(state, pieces):
    queries, keys, values, betas = pieces
    width = keys.shape[-2]
    head_size = keys.shape[-1]
    gram = product('...id,...jd->...ij', keys, keys)
    strict = jnp.tril(jnp.ones((width, width), jnp.float32), -1)
    system = jnp.eye(width, dtype=jnp.float32) + betas[..., :, None] * gram * strict
    right_side = jnp.concatenate([betas[..., None] * keys, betas[..., None] * values], axis=-1)
    solved = lax.linalg.triangular_solve(system, right_side, left_side=True, lower=True, unit_diagonal=True)
    wy_keys = solved[..., :head_size]
    wy_values = solved[..., head_size:]
    fresh = wy_values - product('...cd,...de->...ce', wy_keys, state)
    causal = jnp.tril(jnp.ones((width, width), jnp.float32))
    scores = product('...id,...jd->...ij', queries, keys) * causal
    output = product('...cd,...de->...ce', queries, state) + product('...ij,...je->...ie', scores, fresh)
    return (state + product('...cd,...ce->...de', keys, fresh), output)

def delta_rule(queries, keys, values, betas):
    count = L // BLOCK

    def to_blocks(array):
        return array.reshape(SEQS, count, BLOCK, H, DH).transpose(1, 0, 3, 2, 4)
    beta_blocks = betas.reshape(SEQS, count, BLOCK, H).transpose(1, 0, 3, 2)
    start = jnp.zeros((SEQS, H, DH, DH), jnp.float32)
    final, outputs = lax.scan(jax.checkpoint(block_step), start, (to_blocks(queries), to_blocks(keys), to_blocks(values), beta_blocks))
    return outputs.transpose(1, 0, 3, 2, 4).reshape(SEQS, L, H, DH)

def causal_conv(raw, taps):
    padded = jnp.pad(raw, ((0, 0), (CONV - 1, 0), (0, 0)))
    total = jnp.zeros_like(raw)
    for offset in range(CONV):
        total = total + taps[offset] * padded[:, offset:offset + L]
    return total

def reference(block_input, lengths, attn_gain, query_weight, key_weight, value_weight, outgate_weight, beta_weight, conv_kernel, head_gain, output_weight, mlp_gain, swish_weight, upward_weight, downward_weight, out_grad):
    live = (jnp.arange(L)[None, :] < lengths[:, None]).astype(jnp.float32)

    def forward(source, attn_gain, query_weight, key_weight, value_weight, outgate_weight, beta_weight, conv_kernel, head_gain, output_weight, mlp_gain, swish_weight, upward_weight, downward_weight):
        attn_gain, query_weight, key_weight, value_weight = (low(attn_gain), low(query_weight), low(key_weight), low(value_weight))
        outgate_weight, beta_weight, conv_kernel, head_gain = (low(outgate_weight), low(beta_weight), low(conv_kernel), low(head_gain))
        output_weight, mlp_gain, swish_weight = (low(output_weight), low(mlp_gain), low(swish_weight))
        upward_weight, downward_weight = (low(upward_weight), low(downward_weight))
        normed = low(source * rms_scale(source) * attn_gain)
        taps = conv_kernel.transpose(1, 2, 0, 3).reshape(3, CONV, D)
        acts = []
        for index, weight in enumerate((query_weight, key_weight, value_weight)):
            raw = low_back(low(matmul(normed, weight)))
            acts.append(jax.nn.silu(causal_conv(raw, taps[index])).reshape(SEQS, L, H, DH))
        gate_raw = low_back(low(matmul(normed, outgate_weight))).reshape(SEQS, L, H, DH)
        beta_logit = low_back(matmul(normed, beta_weight))
        betas = jax.nn.sigmoid(beta_logit) * live[:, :, None]
        queries = low(acts[0] * lax.rsqrt(lax.optimization_barrier(jnp.sum(acts[0] * acts[0], axis=-1, keepdims=True)) + epsilon) * DH ** (-0.5))
        keys = low(acts[1] * lax.rsqrt(lax.optimization_barrier(jnp.sum(acts[1] * acts[1], axis=-1, keepdims=True)) + epsilon))
        values = low(acts[2])
        mixed = delta_rule(queries, keys, values, betas)
        head_out = mixed * rms_scale(mixed) * head_gain
        gated = low(head_out * jax.nn.silu(gate_raw)).reshape(SEQS, L, D)
        middle = source + low_back(matmul(gated, output_weight))
        normed_two = low(middle * rms_scale(middle) * mlp_gain)
        gate_act = low_back(matmul(normed_two, swish_weight))
        up_act = low_back(matmul(normed_two, upward_weight))
        hidden = low(jax.nn.silu(gate_act) * up_act)
        return middle + matmul(hidden, downward_weight)
    result, back = jax.vjp(forward, block_input.astype(jnp.float32), attn_gain, query_weight, key_weight, value_weight, outgate_weight, beta_weight, conv_kernel, head_gain, output_weight, mlp_gain, swish_weight, upward_weight, downward_weight)
    grads = back(out_grad.astype(jnp.float32))
    return (result.astype(jnp.bfloat16), grads[0].astype(jnp.bfloat16), grads[1], grads[2], grads[3], grads[4], grads[5], grads[6], grads[7], grads[8], grads[9], grads[10], grads[11], grads[12], grads[13])
```

```python
import jax
import jax.numpy as jnp
from jax import lax
from jax.sharding import PartitionSpec as P

BLOCK = 64
CONV = 4
MATES = 4
SMALL = 8


PRECISE = lax.Precision.HIGHEST
epsilon = 1e-06
low = jnp.bfloat16
wide = jnp.float32


def other_core(value):
    return lax.ppermute(value, "tp", [(0, 1), (1, 0)])


def to_mate(value, flip):
    count = lax.axis_size("seq")
    return lax.ppermute(value, "seq", [(source, source ^ flip) for source in range(count)])


def along(value, step, lines_kept=None):
    count = lax.axis_size("seq")
    lines = count // MATES
    pairs = []
    for source in range(count):
        line = source // MATES
        if 0 <= line + step < lines and (lines_kept is None or line in lines_kept):
            pairs.append((source, source + step * MATES))
    return lax.ppermute(value, "seq", pairs)


def mate_of():
    return lax.axis_index("seq") % MATES


def line_of():
    return lax.axis_index("seq") // MATES


def line_groups():
    lines = lax.axis_size("seq") // MATES
    return [[mate + MATES * line for line in range(lines)] for mate in range(MATES)]


def pick(blocks, index):
    return lax.dynamic_index_in_dim(blocks, index, 0, False)


def in_order(by_flip):
    mate = mate_of()
    out = jnp.zeros((MATES,) + by_flip[0].shape, by_flip[0].dtype)
    for flip, piece in enumerate(by_flip):
        out = lax.dynamic_update_index_in_dim(out, piece, mate ^ flip, 0)
    return out


def swap_blocks(blocks):
    mate = mate_of()
    pieces = [pick(blocks, mate)]
    for flip in range(1, MATES):
        pieces.append(to_mate(pick(blocks, mate ^ flip), flip))
    return in_order(pieces)


def gather_mates(value):
    half = value.shape[-1] // 2
    from_x = to_mate(value, 1)
    from_y = to_mate(value, 2)
    far = jnp.concatenate(
        [to_mate(from_x[..., :half], 2), to_mate(from_y[..., half:], 1)], axis=-1
    )
    return [value, from_x, from_y, far]


def scatter_mates(blocks):
    half = blocks[0].shape[-1] // 2
    far_y = to_mate(blocks[3][..., :half], 2)
    far_x = to_mate(blocks[3][..., half:], 1)
    for_x = jnp.concatenate(
        [(blocks[1][..., :half].astype(wide) + far_y.astype(wide)).astype(low), blocks[1][..., half:]], axis=-1
    )
    for_y = jnp.concatenate(
        [blocks[2][..., :half], (blocks[2][..., half:].astype(wide) + far_x.astype(wide)).astype(low)], axis=-1
    )
    return blocks[0].astype(wide) + to_mate(for_x, 1).astype(wide) + to_mate(for_y, 2).astype(wide)


def gather_lines(block):
    lines = lax.axis_size("seq") // MATES
    if lines > 4:
        return lax.all_gather(block, "seq", axis_index_groups=line_groups())
    line = line_of()
    ups, downs = [block], [block]
    for _ in range(1, lines):
        ups.append(along(ups[-1], 1))
        downs.append(along(downs[-1], -1))
    out = jnp.zeros((lines,) + block.shape, block.dtype)
    out = lax.dynamic_update_index_in_dim(out, block, line, 0)
    for step in range(1, lines):
        out = lax.dynamic_update_index_in_dim(
            out, ups[step] + downs[lines - step], (line - step) % lines, 0
        )
    return out


def scatter_lines(blocks):
    lines = lax.axis_size("seq") // MATES
    if lines > 4:
        return lax.psum_scatter(
            blocks, "seq", scatter_dimension=0, axis_index_groups=line_groups()
        ).astype(wide)
    line = line_of()
    from_below = from_above = None
    for step in range(1, lines):
        up = pick(blocks, (line + lines - step) % lines)
        down = pick(blocks, (line + step) % lines)
        if step > 1:
            up = (up.astype(wide) + from_below.astype(wide)).astype(low)
            down = (down.astype(wide) + from_above.astype(wide)).astype(low)
        from_below = along(up, 1, range(step))
        from_above = along(down, -1, range(lines - step, lines))
    total = pick(blocks, line).astype(wide)
    if lines > 1:
        total = total + from_below.astype(wide) + from_above.astype(wide)
    return total


def hop_states(matrix, offset, step):
    lines = lax.axis_size("seq") // MATES
    state = along(offset, step)
    for _ in range(lines - 2):
        state = along(product("...ij,...jk->...ik", matrix, state) + offset, step)
    return state


def product(form, left, right):
    return jnp.einsum(form, left, right, precision=PRECISE)


def matmul(form, left, right):
    return jnp.einsum(form, left, right, preferred_element_type=wide)


def silu_slope(value):
    squash = jax.nn.sigmoid(value)
    return squash * (1.0 + value * (1.0 - squash))


def rms_scale(value):
    return lax.rsqrt(jnp.mean(value * value, axis=-1, keepdims=True) + epsilon)


def norm_back(grad_normed, source, inverse, scale):
    scaled = grad_normed * scale
    gain_grad = jnp.sum(grad_normed * source * inverse, axis=0)
    source_grad = inverse * (
        scaled - source * inverse * inverse * jnp.mean(scaled * source, axis=-1, keepdims=True)
    )
    return (source_grad, gain_grad)


def unit_back(grad_unit, source, inverse, factor):
    return (
        factor
        * inverse
        * (
            grad_unit
            - source * inverse * inverse * jnp.sum(grad_unit * source, axis=-1, keepdims=True)
        )
    )


def wy_form(keys, values, betas):
    width = keys.shape[-2]
    head_size = keys.shape[-1]
    gram = product("...id,...jd->...ij", keys, keys)
    strict = jnp.tril(jnp.ones((width, width), jnp.float32), -1)
    system = jnp.eye(width, dtype=jnp.float32) + betas[..., :, None] * gram * strict
    right_side = jnp.concatenate([betas[..., None] * keys, betas[..., None] * values], axis=-1)
    solved = lax.linalg.triangular_solve(
        system, right_side, left_side=True, lower=True, unit_diagonal=True
    )
    return (solved[..., :head_size], solved[..., head_size:])


def delta_maps(keys, wy_keys, wy_values):
    head_size = keys.shape[-1]
    identity = jnp.broadcast_to(
        jnp.eye(head_size, dtype=jnp.float32), keys.shape[:2] + (head_size, head_size)
    )

    def advance(carry, pieces):
        matrix, offset = carry
        key_block, wkey_block, wvalue_block = pieces
        step_map = identity - product("...cd,...ce->...de", key_block, wkey_block)
        new_matrix = product("...ij,...jk->...ik", step_map, matrix)
        new_offset = product("...ij,...jk->...ik", step_map, offset) + product(
            "...cd,...ce->...de", key_block, wvalue_block
        )
        return ((new_matrix, new_offset), None)

    moved = tuple((jnp.moveaxis(array, 2, 0) for array in (keys, wy_keys, wy_values)))
    result, _ = lax.scan(advance, (identity, jnp.zeros_like(identity)), moved)
    return result


def delta_rule(queries, keys, wy_keys, wy_values, start):
    width = queries.shape[-2]
    causal = jnp.tril(jnp.ones((width, width), jnp.float32))

    def advance(state, pieces):
        query_block, key_block, wkey_block, wvalue_block = pieces
        fresh = wvalue_block - product("...cd,...de->...ce", wkey_block, state)
        scores = product("...id,...jd->...ij", query_block, key_block) * causal
        output = product("...cd,...de->...ce", query_block, state) + product(
            "...ij,...je->...ie", scores, fresh
        )
        return (state + product("...cd,...ce->...de", key_block, fresh), output)

    moved = tuple((jnp.moveaxis(array, 2, 0) for array in (queries, keys, wy_keys, wy_values)))
    final, outputs = lax.scan(advance, start, moved)
    return (jnp.moveaxis(outputs, 0, 2), final)


def cut_columns(weight):
    depth, columns = weight.shape
    return weight.reshape(depth, MATES, columns // MATES).transpose(1, 0, 2)


def join_columns(blocks):
    return blocks.transpose(1, 0, 2).reshape(blocks.shape[1], -1)


def gather_weights(blocks):
    return gather_lines(swap_blocks(blocks))


def scatter_grads(blocks):
    return swap_blocks(scatter_lines(blocks.astype(low)).astype(low)).astype(wide)


def on_device(
    block_input,
    lengths,
    attn_gain,
    query_weight,
    key_weight,
    value_weight,
    outgate_weight,
    beta_weight,
    conv_kernel,
    head_gain,
    output_weight,
    mlp_gain,
    swish_weight,
    upward_weight,
    downward_weight,
    out_grad,
):
    count = lax.axis_size("seq")
    lines = count // MATES
    core = lax.axis_index("tp")
    seq_count, tokens, model_width = block_input.shape
    depth = attn_gain.shape[0]
    gain_part = head_gain.shape[0]
    head_size = gain_part * count
    heads = beta_weight.shape[1] // MATES
    width = heads * head_size
    units = swish_weight.shape[1] // MATES

    small = jnp.concatenate(
        [
            beta_weight.astype(low).reshape(depth, MATES, heads).transpose(1, 0, 2).reshape(MATES, -1),
            conv_kernel.astype(low).reshape(MATES, -1),
            jnp.broadcast_to(
                jnp.concatenate([attn_gain, mlp_gain, head_gain]).astype(low)[None],
                (MATES, 2 * depth + gain_part),
            ),
        ],
        axis=1,
    )
    small_size = small.shape[1]
    small = jnp.pad(small, ((0, 0), (0, SMALL * 3 * width - small_size))).reshape(
        MATES, SMALL, 3 * width
    )
    streams_cut = jnp.concatenate(
        [cut_columns(w.astype(low)) for w in (query_weight, key_weight, value_weight)], axis=2
    )
    first = gather_weights(jnp.concatenate([streams_cut, small], axis=1))
    streams_full = first[:, :, :depth].reshape(model_width, 3 * width)
    small = first[:, :, depth:].reshape(count, SMALL * 3 * width)[:, :small_size]
    gates_cut = jnp.concatenate(
        [cut_columns(w.astype(low)) for w in (outgate_weight, output_weight.T)], axis=2
    )
    gates_full = gather_weights(gates_cut).reshape(model_width, 2 * width)
    outgate_full, output_full = gates_full[:, :width], gates_full[:, width:]
    ups_cut = jnp.concatenate(
        [cut_columns(w.astype(low)) for w in (swish_weight, upward_weight)], axis=2
    )
    ups_full = gather_weights(ups_cut).reshape(model_width, 2 * units)
    downward_full = gather_weights(cut_columns(downward_weight.astype(low).T)).reshape(
        model_width, units
    )
    sizes = (depth * heads, heads * 3 * CONV * gain_part, depth, depth, gain_part)
    starts = [sum(sizes[:index]) for index in range(len(sizes) + 1)]
    beta_small, conv_small, attn_small, mlp_small, head_small = (
        small[:, starts[index] : starts[index + 1]] for index in range(len(sizes))
    )
    beta_full = beta_small.reshape(model_width, heads)
    taps = (
        conv_small.reshape(count, heads, 3, CONV, gain_part)
        .transpose(2, 3, 1, 0, 4)
        .reshape(3, CONV, width)
        .astype(wide)
    )
    attn_scale = attn_small.reshape(model_width).astype(wide)
    mlp_scale = mlp_small.reshape(model_width).astype(wide)
    head_scale = head_small.reshape(head_size).astype(wide)

    span = MATES * tokens
    rows = seq_count * span

    def ordered_rows(mine):
        gathered = in_order(gather_mates(mine)).reshape(span, model_width)
        return jnp.concatenate([gathered, other_core(gathered)], axis=0)

    def loose_rows(mine):
        gathered = jnp.concatenate(gather_mates(mine), axis=0)
        return jnp.concatenate([gathered, other_core(gathered)], axis=0)

    def sum_cores(partial):
        own = partial[:span]
        return (own.astype(wide) + other_core(partial[span:]).astype(wide)).astype(low)

    def sum_ordered(partial):
        blocks = sum_cores(partial).reshape(MATES, tokens, model_width)
        return scatter_mates([pick(blocks, mate_of() ^ flip) for flip in range(MATES)])

    def sum_loose(partial):
        blocks = sum_cores(partial).reshape(MATES, tokens, model_width)
        return scatter_mates([blocks[flip] for flip in range(MATES)])

    mine_low = pick(block_input, core)
    mine_input = mine_low.astype(wide)
    first_inverse = rms_scale(mine_input)
    grad_mine = pick(out_grad, core)
    grad_rows = loose_rows(grad_mine)
    input_rows = ordered_rows(mine_low).astype(wide)
    flat_normed = (input_rows * rms_scale(input_rows) * attn_scale).astype(low)

    lengths_here = jnp.stack([pick(lengths, core), pick(lengths, 1 - core)])
    positions = line_of() * span + jnp.arange(span, dtype=jnp.int32)
    validity = (positions[None, :] < lengths_here[:, None]).astype(wide)

    block_count = span // BLOCK

    def to_blocks(array):
        return array.reshape(seq_count, block_count, BLOCK, heads, head_size).transpose(
            0, 3, 1, 2, 4
        )

    def from_blocks(array):
        return array.transpose(0, 2, 3, 1, 4).reshape(seq_count, span, heads, head_size)

    raw_streams = (
        matmul("rd,dc->rc", flat_normed, streams_full).astype(low).reshape(seq_count, span, 3, width)
    ).transpose(2, 0, 1, 3)
    gate_values = matmul("rd,dc->rc", flat_normed, outgate_full).astype(low)
    beta_logits = matmul("rd,dh->rh", flat_normed, beta_full).reshape(seq_count, span, heads)
    tails = along(raw_streams[:, :, span - (CONV - 1) :], 1)
    extended = jnp.concatenate([tails, raw_streams], axis=2).astype(wide)
    pre_act = sum(
        (
            taps[:, offset][:, None, None, :] * extended[:, :, offset : offset + span]
            for offset in range(CONV)
        )
    )
    activated = jax.nn.silu(pre_act)
    query_raw = activated[0].reshape(seq_count, span, heads, head_size)
    key_raw = activated[1].reshape(seq_count, span, heads, head_size)
    query_inverse = lax.rsqrt(jnp.sum(query_raw * query_raw, axis=-1, keepdims=True) + epsilon)
    key_inverse = lax.rsqrt(jnp.sum(key_raw * key_raw, axis=-1, keepdims=True) + epsilon)
    queries = (query_raw * query_inverse * head_size ** (-0.5)).astype(low).astype(wide)
    keys = (key_raw * key_inverse).astype(low).astype(wide)
    values = activated[2].astype(low).astype(wide).reshape(seq_count, span, heads, head_size)
    beta_squash = jax.nn.sigmoid(beta_logits)
    beta_gate = beta_squash * validity[:, :, None]
    query_blocks = to_blocks(queries)
    key_blocks = to_blocks(keys)
    value_blocks = to_blocks(values)
    beta_blocks = beta_gate.reshape(seq_count, block_count, BLOCK, heads).transpose(0, 3, 1, 2)
    (wy_keys, wy_values), wy_back = jax.vjp(wy_form, key_blocks, value_blocks, beta_blocks)
    map_matrix, map_offset = delta_maps(key_blocks, wy_keys, wy_values)
    entering = hop_states(map_matrix, map_offset, 1)
    (mixed_blocks, leaving), rule_back = jax.vjp(
        delta_rule, query_blocks, key_blocks, wy_keys, wy_values, entering
    )
    mixed = from_blocks(mixed_blocks)
    mix_inverse = rms_scale(mixed)
    head_normed = mixed * mix_inverse * head_scale
    gate_wide = gate_values.astype(wide).reshape(seq_count, span, heads, head_size)
    silu_gate = jax.nn.silu(gate_wide)
    gated = (head_normed * silu_gate).astype(low).reshape(rows, width)
    attn_out = sum_ordered(matmul("rc,dc->rd", gated, output_full).astype(low))
    middle = mine_input + attn_out
    second_inverse = rms_scale(middle)
    mlp_normed = loose_rows((middle * second_inverse * mlp_scale).astype(low))
    acts = matmul("rd,df->rf", mlp_normed, ups_full)
    gate_act, up_act = acts[:, :units], acts[:, units:]
    silu_act = jax.nn.silu(gate_act)
    hidden = (silu_act * up_act).astype(low)
    mlp_out = sum_loose(matmul("rf,df->rd", hidden, downward_full).astype(low))
    output_mine = (middle + mlp_out).astype(low)

    hidden_grad = matmul("rd,df->rf", grad_rows, downward_full)
    downward_grad = matmul("rd,rf->df", grad_rows, hidden)
    acts_grad = jnp.concatenate(
        [
            (hidden_grad * up_act * silu_slope(gate_act)).astype(low),
            (hidden_grad * silu_act).astype(low),
        ],
        axis=1,
    )
    ups_grad = matmul("rd,rf->df", mlp_normed, acts_grad)
    normed_two_grad = sum_loose(matmul("rf,df->rd", acts_grad, ups_full).astype(low))
    middle_part, mlp_gain_grad = norm_back(normed_two_grad, middle, second_inverse, mlp_scale)
    middle_grad = grad_mine.astype(wide) + middle_part
    attn_grad_rows = ordered_rows(middle_grad.astype(low))
    output_grad = matmul("rd,rc->dc", attn_grad_rows, gated)
    gated_grad = matmul("rd,dc->rc", attn_grad_rows, output_full).reshape(
        seq_count, span, heads, head_size
    )
    outgate_act_grad = (
        (gated_grad * head_normed * silu_slope(gate_wide)).astype(low).reshape(rows, width)
    )
    mixed_flat_grad, head_gain_part = norm_back(
        (gated_grad * silu_gate).reshape(-1, head_size),
        mixed.reshape(-1, head_size),
        mix_inverse.reshape(-1, 1),
        head_scale,
    )
    mixed_grad = mixed_flat_grad.reshape(seq_count, span, heads, head_size)
    query_bgrad, key_bgrad, wkey_grad, wvalue_grad, local_state = rule_back(
        (to_blocks(mixed_grad), jnp.zeros_like(leaving))
    )
    leaving_grad = hop_states(jnp.swapaxes(map_matrix, -1, -2), local_state, -1)
    later_back = rule_back((jnp.zeros_like(mixed_blocks), leaving_grad))
    key_bgrad = key_bgrad + later_back[1]
    wkey_grad = wkey_grad + later_back[2]
    wvalue_grad = wvalue_grad + later_back[3]
    key_cgrad, value_bgrad, beta_bgrad = wy_back((wkey_grad, wvalue_grad))
    query_grad_unit = from_blocks(query_bgrad)
    key_grad_unit = from_blocks(key_bgrad + key_cgrad)
    value_grad_act = from_blocks(value_bgrad)
    beta_token_grad = beta_bgrad.transpose(0, 2, 3, 1).reshape(seq_count, span, heads)
    beta_logit_grad = (
        (beta_token_grad * validity[:, :, None] * beta_squash * (1.0 - beta_squash))
        .astype(low)
        .reshape(rows, heads)
    )
    act_grads = jnp.stack(
        [
            unit_back(query_grad_unit, query_raw, query_inverse, head_size ** (-0.5)).reshape(
                seq_count, span, width
            ),
            unit_back(key_grad_unit, key_raw, key_inverse, 1.0).reshape(seq_count, span, width),
            value_grad_act.reshape(seq_count, span, width),
        ]
    )
    pre_grad = act_grads * silu_slope(pre_act)
    padded_grad = jnp.pad(pre_grad, ((0, 0), (0, 0), (CONV - 1, CONV - 1), (0, 0)))
    reach = span + CONV - 1
    extended_grad = sum(
        (
            taps[:, offset][:, None, None, :]
            * padded_grad[:, :, CONV - 1 - offset : CONV - 1 - offset + reach]
            for offset in range(CONV)
        )
    )
    taps_grad = jnp.stack(
        [
            jnp.sum(pre_grad * extended[:, :, offset : offset + span], axis=(1, 2))
            for offset in range(CONV)
        ],
        axis=1,
    )
    returned = along(extended_grad[:, :, : CONV - 1].astype(low), -1).astype(wide)
    raw_grad = extended_grad[:, :, CONV - 1 :].at[:, :, span - (CONV - 1) :].add(returned)
    raw_grad_low = raw_grad.astype(low).transpose(1, 2, 0, 3).reshape(rows, 3 * width)
    streams_grad = matmul("rd,rc->dc", flat_normed, raw_grad_low)
    outgate_grad = matmul("rd,rc->dc", flat_normed, outgate_act_grad)
    beta_grad = matmul("rd,rh->dh", flat_normed, beta_logit_grad)
    normed_part = (
        matmul("rc,dc->rd", outgate_act_grad, outgate_full)
        + matmul("rh,dh->rd", beta_logit_grad, beta_full)
        + matmul("rc,dc->rd", raw_grad_low, streams_full)
    )
    normed_grad = sum_ordered(normed_part.astype(low))
    input_part, attn_gain_grad = norm_back(normed_grad, mine_input, first_inverse, attn_scale)
    input_grad_mine = (middle_grad + input_part).astype(low)

    def both_sequences(mine):
        other = other_core(mine)
        return jnp.stack([jnp.where(core == 0, mine, other), jnp.where(core == 0, other, mine)])

    def cut_rows(grad):
        return grad.reshape(lines, MATES, depth, grad.shape[1])

    downward_sum = join_columns(scatter_grads(cut_rows(downward_grad))).T
    ups_sum = scatter_grads(cut_rows(ups_grad))
    gates_sum = scatter_grads(cut_rows(jnp.concatenate([outgate_grad, output_grad], axis=1)))
    conv_grad = (
        taps_grad.reshape(3, CONV, heads, count, gain_part)
        .transpose(3, 2, 0, 1, 4)
        .reshape(count, -1)
    )
    small_grad = jnp.concatenate(
        [
            beta_grad.reshape(count, depth * heads),
            conv_grad,
            attn_gain_grad.reshape(count, depth),
            mlp_gain_grad.reshape(count, depth),
            head_gain_part.reshape(count, gain_part),
        ],
        axis=1,
    ).astype(low)
    small_grad = jnp.pad(small_grad, ((0, 0), (0, SMALL * 3 * width - small_size)))
    first_sum = scatter_grads(
        jnp.concatenate(
            [
                cut_rows(streams_grad.astype(low)),
                small_grad.reshape(lines, MATES, SMALL, 3 * width),
            ],
            axis=2,
        )
    )
    streams_sum = first_sum[:, :depth]
    small_sum = first_sum[:, depth:].reshape(MATES, SMALL * 3 * width)
    beta_sum, conv_sum, attn_sum, mlp_sum, head_sum = (
        small_sum[:, starts[index] : starts[index + 1]] for index in range(len(sizes))
    )
    gains_sum = jnp.sum(jnp.concatenate([attn_sum, mlp_sum, head_sum], axis=1), axis=0)
    gains_sum = gains_sum + other_core(gains_sum)
    return (
        both_sequences(output_mine),
        both_sequences(input_grad_mine),
        gains_sum[:depth],
        join_columns(streams_sum[:, :, :width]),
        join_columns(streams_sum[:, :, width : 2 * width]),
        join_columns(streams_sum[:, :, 2 * width :]),
        join_columns(gates_sum[:, :, :width]),
        join_columns(beta_sum.reshape(MATES, depth, heads)),
        conv_sum.reshape(MATES * heads, 3, CONV, gain_part),
        gains_sum[2 * depth :],
        join_columns(gates_sum[:, :, width:]).T,
        gains_sum[depth : 2 * depth],
        join_columns(ups_sum[:, :, :units]),
        join_columns(ups_sum[:, :, units:]),
        downward_sum,
    )


def solution(mesh):
    return jax.shard_map(
        on_device,
        mesh=mesh,
        in_specs=(
            P(None, "seq", None),
            P(),
            P("seq"),
            P("seq", "tp"),
            P("seq", "tp"),
            P("seq", "tp"),
            P("seq", "tp"),
            P("seq", "tp"),
            P("tp", None, None, "seq"),
            P("seq"),
            P("tp", "seq"),
            P("seq"),
            P("seq", "tp"),
            P("seq", "tp"),
            P("tp", "seq"),
            P(None, "seq", None),
        ),
        out_specs=(
            P(None, "seq", None),
            P(None, "seq", None),
            P("seq"),
            P("seq", "tp"),
            P("seq", "tp"),
            P("seq", "tp"),
            P("seq", "tp"),
            P("seq", "tp"),
            P("tp", None, None, "seq"),
            P("seq"),
            P("tp", "seq"),
            P("seq"),
            P("seq", "tp"),
            P("seq", "tp"),
            P("tp", "seq"),
        ),
        check_vma=False,
    )
```

```python
import jax
import jax.numpy as jnp
from jax import lax
from jax.experimental import pallas as pl
from jax.experimental.pallas import tpu as pltpu
from jax.sharding import PartitionSpec as P

CONV = 4
MATES = 4
SMALL = 8


PRECISE = lax.Precision.HIGHEST
epsilon = 1e-06
low = jnp.bfloat16
wide = jnp.float32


def other_core(value):
    return lax.ppermute(value, "tp", [(0, 1), (1, 0)])


def to_mate(value, flip):
    count = lax.axis_size("seq")
    return lax.ppermute(value, "seq", [(source, source ^ flip) for source in range(count)])


def along(value, step, lines_kept=None):
    count = lax.axis_size("seq")
    lines = count // MATES
    pairs = []
    for source in range(count):
        line = source // MATES
        if 0 <= line + step < lines and (lines_kept is None or line in lines_kept):
            pairs.append((source, source + step * MATES))
    return lax.ppermute(value, "seq", pairs)


def mate_of():
    return lax.axis_index("seq") % MATES


def line_of():
    return lax.axis_index("seq") // MATES


def line_groups():
    lines = lax.axis_size("seq") // MATES
    return [[mate + MATES * line for line in range(lines)] for mate in range(MATES)]


def pick(blocks, index):
    return lax.dynamic_index_in_dim(blocks, index, 0, False)


def in_order(by_flip):
    mate = mate_of()
    out = jnp.zeros((MATES,) + by_flip[0].shape, by_flip[0].dtype)
    for flip, piece in enumerate(by_flip):
        out = lax.dynamic_update_index_in_dim(out, piece, mate ^ flip, 0)
    return out


def swap_blocks(blocks):
    mate = mate_of()
    pieces = [pick(blocks, mate)]
    for flip in range(1, MATES):
        pieces.append(to_mate(pick(blocks, mate ^ flip), flip))
    return in_order(pieces)


def gather_mates(value):
    half = value.shape[-1] // 2
    from_x = to_mate(value, 1)
    from_y = to_mate(value, 2)
    far = jnp.concatenate(
        [to_mate(from_x[..., :half], 2), to_mate(from_y[..., half:], 1)], axis=-1
    )
    return [value, from_x, from_y, far]


def scatter_mates(blocks):
    half = blocks[0].shape[-1] // 2
    far_y = to_mate(blocks[3][..., :half], 2)
    far_x = to_mate(blocks[3][..., half:], 1)
    for_x = jnp.concatenate(
        [(blocks[1][..., :half].astype(wide) + far_y.astype(wide)).astype(low), blocks[1][..., half:]], axis=-1
    )
    for_y = jnp.concatenate(
        [blocks[2][..., :half], (blocks[2][..., half:].astype(wide) + far_x.astype(wide)).astype(low)], axis=-1
    )
    return blocks[0].astype(wide) + to_mate(for_x, 1).astype(wide) + to_mate(for_y, 2).astype(wide)


def gather_lines(block):
    lines = lax.axis_size("seq") // MATES
    if lines > 4:
        return lax.all_gather(block, "seq", axis_index_groups=line_groups())
    line = line_of()
    ups, downs = [block], [block]
    for _ in range(1, lines):
        ups.append(along(ups[-1], 1))
        downs.append(along(downs[-1], -1))
    out = jnp.zeros((lines,) + block.shape, block.dtype)
    out = lax.dynamic_update_index_in_dim(out, block, line, 0)
    for step in range(1, lines):
        out = lax.dynamic_update_index_in_dim(
            out, ups[step] + downs[lines - step], (line - step) % lines, 0
        )
    return out


def scatter_lines(blocks):
    lines = lax.axis_size("seq") // MATES
    if lines > 4:
        return lax.psum_scatter(
            blocks, "seq", scatter_dimension=0, axis_index_groups=line_groups()
        ).astype(wide)
    line = line_of()
    from_below = from_above = None
    for step in range(1, lines):
        up = pick(blocks, (line + lines - step) % lines)
        down = pick(blocks, (line + step) % lines)
        if step > 1:
            up = (up.astype(wide) + from_below.astype(wide)).astype(low)
            down = (down.astype(wide) + from_above.astype(wide)).astype(low)
        from_below = along(up, 1, range(step))
        from_above = along(down, -1, range(lines - step, lines))
    total = pick(blocks, line).astype(wide)
    if lines > 1:
        total = total + from_below.astype(wide) + from_above.astype(wide)
    return total


def hop_states(matrix, offset, step):
    lines = lax.axis_size("seq") // MATES
    state = along(offset, step)
    for _ in range(lines - 2):
        state = along(product("...ij,...jk->...ik", matrix, state) + offset, step)
    return state


def hop_states_back(matrix, offset):
    lines = lax.axis_size("seq") // MATES
    state = along(offset, -1)
    for _ in range(lines - 2):
        state = along(product("...ij,...jk->...ik", state, matrix) + offset, -1)
    return state


def product(form, left, right):
    return jnp.einsum(form, left, right, precision=PRECISE)


def matmul(form, left, right):
    return jnp.einsum(form, left, right, preferred_element_type=wide)


def silu_slope(value):
    squash = jax.nn.sigmoid(value)
    return squash * (1.0 + value * (1.0 - squash))


def rms_scale(value):
    return lax.rsqrt(jnp.mean(value * value, axis=-1, keepdims=True) + epsilon)


def norm_back(grad_normed, source, inverse, scale):
    scaled = grad_normed * scale
    gain_grad = jnp.sum(grad_normed * source * inverse, axis=0)
    source_grad = inverse * (
        scaled - source * inverse * inverse * jnp.mean(scaled * source, axis=-1, keepdims=True)
    )
    return (source_grad, gain_grad)


CHUNK = 128
TOGETHER = 4
VMEM_BYTES = 52 * 1024 * 1024
NN = (((1,), (0,)), ((), ()))
NT = (((1,), (1,)), ((), ()))


def dot(left, right, dims):
    return lax.dot_general(left, right, dims, preferred_element_type=wide)


def pair(value):
    high = value.astype(low)
    return high, (value - high.astype(wide)).astype(low)


def side(left, right):
    return jnp.concatenate([left, right], axis=1)


def over(top, bottom):
    return jnp.concatenate([top, bottom], axis=0)


def nn(left, right):
    width = right[0].shape[1]
    both = side(*right)
    out = dot(side(*left), over(both, both), NN)
    return out[:, :width] + out[:, width:]


def nt(left, right):
    width = right[0].shape[0]
    out = dot(side(*left), over(side(right[0], right[0]), side(right[1], right[1])), NT)
    return out[:, :width] + out[:, width:]


def nn_wide(left, right):
    return dot(side(*left), over(right[0], right[0]), NN) + dot(left[0], right[1], NN)


def nn_low(left, right):
    return dot(side(*left), over(right, right), NN)


def low_nn(left, right):
    return dot(side(left, left), over(*right), NN)


def low_nt(left, right):
    return dot(side(left, left), side(*right), NT)


def grid_of_rows():
    rows = lax.broadcasted_iota(jnp.int32, (CHUNK, CHUNK), 0)
    columns = lax.broadcasted_iota(jnp.int32, (CHUNK, CHUNK), 1)
    return rows, columns


def inverse_of(strict):
    rows, columns = grid_of_rows()
    one = jnp.where(rows == columns, 1.0, 0.0).astype(wide)

    def joining(shift):
        upper = columns >> shift
        return ((rows >> shift) == upper + 1) & ((upper & 1) == 0)

    solved = [one - jnp.where(joining(0), s, 0.0) for s in strict]
    shift = 1
    while (1 << shift) < CHUNK:
        mask = joining(shift)
        pairs = [pair(d) for d in solved]
        crossed = [nn(pair(jnp.where(mask, s, 0.0)), p) for s, p in zip(strict, pairs)]
        solved = [d - nn(p, pair(c)) for d, p, c in zip(solved, pairs, crossed)]
        shift += 1
    return solved


def convolved(block, taps, stream):
    columns = block[:, stream * CHUNK : (stream + 1) * CHUNK]
    total = None
    for offset in range(CONV):
        first = 16 - (CONV - 1) + offset
        term = taps[stream * CONV + offset][None, :] * columns[first : first + CHUNK]
        total = term if total is None else total + term
    return total


def silu_parts(value):
    squash = jax.nn.sigmoid(value)
    return value * squash, squash * (1.0 + value * (1.0 - squash))


def live_rows(limit, start):
    rows = lax.broadcasted_iota(jnp.int32, (CHUNK, CHUNK), 0)
    return jnp.where(rows + start < limit, 1.0, 0.0).astype(wide)


def write_extended(ext, tail_ref, raw_ref):
    ext[:16] = tail_ref[0].astype(wide)
    ext[16:] = raw_ref[...].astype(wide)


def prepare_kernel(
    limit_ref, raw_ref, tail_ref, taps_ref, logit_ref,
    qkv_ref, solved_ref, wu_ref, map_ref, prefix_ref, local_ref, ends_ref,
    ext, offsets, maps,
):
    seq, head = pl.program_id(0), pl.program_id(1)
    heads = pl.num_programs(1)
    chain = seq * heads + head
    chains, chunks = prefix_ref.shape[0], prefix_ref.shape[1]
    write_extended(ext, tail_ref, raw_ref)
    taps = taps_ref[0]
    limit = limit_ref[seq]
    rows, columns = grid_of_rows()
    identity = jnp.where(rows == columns, 1.0, 0.0).astype(wide)
    head_size = CHUNK

    def group(index, carry):
        first = index * TOGETHER
        parts = []
        for step in range(TOGETHER):
            start = pl.multiple_of((first + step) * CHUNK, CHUNK)
            block = ext[pl.ds(start, CHUNK + 16)]
            query = jax.nn.silu(convolved(block, taps, 0))
            key = jax.nn.silu(convolved(block, taps, 1))
            value = jax.nn.silu(convolved(block, taps, 2)).astype(low)
            query = query * lax.rsqrt(jnp.sum(query * query, axis=1, keepdims=True) + epsilon)
            query = (query * head_size ** (-0.5)).astype(low)
            key = key * lax.rsqrt(jnp.sum(key * key, axis=1, keepdims=True) + epsilon)
            key = key.astype(low)
            beta = jax.nn.sigmoid(logit_ref[pl.ds(start, CHUNK)]) * live_rows(limit, start)
            qkv_ref[pl.ds(start, CHUNK)] = jnp.concatenate([query, key, value], axis=1)
            parts.append((key, value, beta))
        strict = [
            jnp.where(rows > columns, beta * dot(key, key, NT), 0.0) for key, _, beta in parts
        ]
        solved = inverse_of(strict)
        for step in range(TOGETHER):
            key, value, beta = parts[step]
            solved_ref[0, first + step] = solved[step]
            weighted = pair(solved[step] * beta.T)
            both = nn_low(weighted, side(key, value))
            wu_ref[0, first + step] = both
            moved = low_nn(key.T, pair(both))
            step_map = identity - moved[:, :head_size]
            map_ref[0, first + step] = step_map
            maps[chain, first + step] = step_map
            offsets[chain, first + step] = moved[:, head_size:]
        return carry

    lax.fori_loop(0, chunks // TOGETHER, group, 0)

    @pl.when(chain == chains - 1)
    def _():
        start = side(identity, jnp.zeros_like(identity))

        def advance(chunk, states):
            out = []
            for index in range(chains):
                state = states[index]
                prefix_ref[index, chunk] = state[:, :head_size]
                local_ref[index, chunk] = state[:, head_size:]
                moved = nn_wide(pair(maps[index, chunk]), pair(state))
                out.append(
                    side(moved[:, :head_size], moved[:, head_size:] + offsets[index, chunk])
                )
            return tuple(out)

        ends = lax.fori_loop(0, chunks, advance, (start,) * chains)
        for index in range(chains):
            ends_ref[index] = ends[index]


def mix_kernel(
    qkv_ref, wu_ref, prefix_ref, local_ref, enter_ref, gate_ref, scale_ref,
    state_ref, fresh_ref, mixed_ref, gated_ref,
):
    chunks = prefix_ref.shape[1]
    head_size = CHUNK
    rows, columns = grid_of_rows()
    enter = pair(enter_ref[0])
    scale = scale_ref[...]

    def group(index, carry):
        for step in range(TOGETHER):
            chunk = index * TOGETHER + step
            start = pl.multiple_of(chunk * CHUNK, CHUNK)
            here = pl.ds(start, CHUNK)
            state = nn(pair(prefix_ref[0, chunk]), enter) + local_ref[0, chunk]
            state_ref[0, chunk] = state
            states = pair(state)
            both = wu_ref[0, chunk]
            fresh = both[:, head_size:] - nn(pair(both[:, :head_size]), states)
            fresh_ref[0, chunk] = fresh
            query, key = qkv_ref[here, :head_size], qkv_ref[here, head_size : 2 * head_size]
            scores = jnp.where(rows >= columns, dot(query, key, NT), 0.0)
            mixed = low_nn(query, states) + nn(pair(scores), pair(fresh))
            mixed_ref[here] = mixed
            inverse = lax.rsqrt(jnp.mean(mixed * mixed, axis=1, keepdims=True) + epsilon)
            normed = mixed * inverse * scale
            gated_ref[here] = (normed * jax.nn.silu(gate_ref[here].astype(wide))).astype(low)
        return carry

    lax.fori_loop(0, chunks // TOGETHER, group, 0)


def turn_kernel(
    grad_ref, mixed_ref, gate_ref, scale_ref, qkv_ref, wu_ref, map_ref,
    out_ref, fresh_ref, gate_grad_ref, gain_ref, source_ref, end_ref,
    maps, sources,
):
    seq, head = pl.program_id(0), pl.program_id(1)
    heads = pl.num_programs(1)
    chain = seq * heads + head
    chains, chunks = maps.shape[0], maps.shape[1]
    head_size = CHUNK
    rows, columns = grid_of_rows()
    scale = scale_ref[...]

    def group(index, gain):
        for step in range(TOGETHER):
            chunk = index * TOGETHER + step
            start = pl.multiple_of(chunk * CHUNK, CHUNK)
            here = pl.ds(start, CHUNK)
            grad, mixed = grad_ref[here], mixed_ref[here]
            silu_gate, slope = silu_parts(gate_ref[here].astype(wide))
            inverse = lax.rsqrt(jnp.mean(mixed * mixed, axis=1, keepdims=True) + epsilon)
            unit = mixed * inverse
            gate_grad_ref[here] = (grad * unit * scale * slope).astype(low)
            passed = grad * silu_gate
            gain = gain + jnp.sum(passed * unit, axis=0, keepdims=True)
            scaled = passed * scale
            mixed_grad = inverse * (
                scaled - unit * inverse * jnp.mean(scaled * mixed, axis=1, keepdims=True)
            )
            out_ref[0, chunk] = mixed_grad
            query, key = qkv_ref[here, :head_size], qkv_ref[here, head_size : 2 * head_size]
            scores = jnp.where(rows >= columns, dot(query, key, NT), 0.0)
            turned = jnp.where(rows <= columns, dot(key, query, NT), 0.0)
            grads = pair(mixed_grad)
            fresh_ref[0, chunk] = nn(pair(turned), grads)
            reading = query.astype(wide) - nn(pair(scores), pair(wu_ref[0, chunk, :, :head_size]))
            source = nn(pair(mixed_grad.T), pair(reading))
            source_ref[0, chunk] = source
            sources[chain, chunk] = source
            maps[chain, chunk] = map_ref[0, chunk]
        return gain

    gain = lax.fori_loop(0, chunks // TOGETHER, group, jnp.zeros((1, head_size), wide))
    gain_ref[0] = jnp.broadcast_to(gain, (8, head_size))

    @pl.when(chain == chains - 1)
    def _():
        def advance(step, states):
            chunk = chunks - 1 - step
            return tuple(
                nn(pair(states[index]), pair(maps[index, chunk])) + sources[index, chunk]
                for index in range(chains)
            )

        ends = lax.fori_loop(
            0, chunks, advance, (jnp.zeros((head_size, head_size), wide),) * chains
        )
        for index in range(chains):
            end_ref[index] = ends[index]


def unwind_kernel(
    limit_ref, raw_ref, tail_ref, taps_ref, logit_ref, qkv_ref, solved_ref, wu_ref, state_ref,
    fresh_in_ref, out_ref, fresh_grad_ref, maps_ref, sources_ref, leave_ref,
    raw_grad_ref, edge_ref, halo_ref, taps_grad_ref, logit_grad_ref,
    ext, pre_grads, leaving,
):
    seq, head = pl.program_id(0), pl.program_id(1)
    heads = pl.num_programs(1)
    chain = seq * heads + head
    chains, chunks = maps_ref.shape[0], maps_ref.shape[1]
    head_size = CHUNK
    span = chunks * CHUNK
    rows, columns = grid_of_rows()
    write_extended(ext, tail_ref, raw_ref)
    taps = taps_ref[0]
    limit = limit_ref[seq]

    @pl.when(chain == 0)
    def _():
        def advance(step, states):
            chunk = chunks - 1 - step
            out = []
            for index in range(chains):
                leaving[index, chunk] = states[index]
                out.append(
                    nn(pair(states[index]), pair(maps_ref[index, chunk]))
                    + sources_ref[index, chunk]
                )
            return tuple(out)

        lax.fori_loop(0, chunks, advance, tuple(leave_ref[index] for index in range(chains)))

    pre_grads[:16] = jnp.zeros((16, 3 * head_size), wide)
    pre_grads[span + 16 :] = jnp.zeros((16, 3 * head_size), wide)

    def one(chunk):
        start = pl.multiple_of(chunk * CHUNK, CHUNK)
        here = pl.ds(start, CHUNK)
        query = qkv_ref[here, :head_size]
        key = qkv_ref[here, head_size : 2 * head_size]
        value = qkv_ref[here, 2 * head_size :]
        live = live_rows(limit, start)
        squash = jax.nn.sigmoid(logit_ref[here])
        beta = squash * live
        grads = pair(out_ref[0, chunk])
        fresh = pair(fresh_in_ref[0, chunk])
        state = pair(state_ref[0, chunk])
        leave = pair(leaving[chain, chunk])
        both = wu_ref[0, chunk]
        fresh_grad = fresh_grad_ref[0, chunk] + low_nt(key, leave)
        fresh_grads = pair(fresh_grad)
        score_grad = jnp.where(rows >= columns, nt(grads, fresh), 0.0)
        turned_grad = jnp.where(rows <= columns, nt(fresh, grads), 0.0)
        query_grad = nt(grads, state) + nn_low(pair(score_grad), key)
        key_grad = nn_low(pair(turned_grad), query) + nn(fresh, leave)
        wkey_grad = -nt(fresh_grads, state)
        right_grad = nn_wide(pair(solved_ref[0, chunk].T), pair(side(wkey_grad, fresh_grad)))
        right = pair(right_grad)
        twos = pair(both)
        found = dot(right[0], over(*twos), NT)
        system_grad = found[:, :CHUNK] + found[:, CHUNK:] + dot(right[1], twos[0], NT)
        system_grad = jnp.where(rows > columns, -system_grad, 0.0)
        gram = dot(key, key, NT)
        gram_grad = beta * system_grad
        key_grad = key_grad + nn_low(pair(gram_grad + gram_grad.T), key)
        key_right, value_right = right_grad[:, :head_size], right_grad[:, head_size:]
        key_grad = key_grad + beta * key_right
        value_grad = beta * value_right
        beta_grad = jnp.sum(
            key_right * key.astype(wide) + value_right * value.astype(wide) + system_grad * gram,
            axis=1,
            keepdims=True,
        )
        logit_grad_ref[here] = (beta_grad * (live * squash * (1.0 - squash))).astype(low)

        block = ext[pl.ds(start, CHUNK + 16)]
        grads_pre = []
        for stream, grad in enumerate((query_grad, key_grad, value_grad)):
            act, slope = silu_parts(convolved(block, taps, stream))
            if stream < 2:
                inverse = lax.rsqrt(jnp.sum(act * act, axis=1, keepdims=True) + epsilon)
                inner = jnp.sum(act * grad, axis=1, keepdims=True)
                grad = inverse * (grad - act * (inverse * inverse * inner))
                if stream == 0:
                    grad = grad * head_size ** (-0.5)
            grads_pre.append(grad * slope)
        pre_grads[pl.ds(start + 16, CHUNK)] = jnp.concatenate(grads_pre, axis=1)

    def group(index, carry):
        for step in range(2):
            one(index * 2 + step)
        return carry

    lax.fori_loop(0, chunks // 2, group, 0)

    def back(block, offset_of_first):
        streams = []
        for stream in range(3):
            part = block[:, stream * head_size : (stream + 1) * head_size]
            total = None
            for offset in range(CONV):
                first = offset_of_first + CONV - 1 - offset
                term = taps[stream * CONV + offset][None, :] * part[first : first + CHUNK]
                total = term if total is None else total + term
            streams.append(total)
        return jnp.concatenate(streams, axis=1)

    def finish(chunk, totals):
        start = pl.multiple_of(chunk * CHUNK, CHUNK)
        block = pre_grads[pl.ds(start + 16, CHUNK + 16)]
        grad = back(block, 0)
        raw_grad_ref[pl.ds(start, CHUNK)] = grad.astype(low)
        edge_ref[0] = grad[CHUNK - 16 :]
        before = ext[pl.ds(start, CHUNK + 16)]
        pre = block[:CHUNK]
        out = []
        for offset in range(CONV):
            first = 16 - (CONV - 1) + offset
            term = jnp.sum(pre * before[first : first + CHUNK], axis=0, keepdims=True)
            out.append(totals[offset] + term)
        return tuple(out)

    zero = jnp.zeros((1, 3 * head_size), wide)
    totals = lax.fori_loop(0, chunks, finish, (zero,) * CONV)
    for offset in range(CONV):
        taps_grad_ref[0, offset : offset + 1] = totals[offset]
    halo = back(pre_grads[: CHUNK + 32], 0)
    halo_ref[0] = halo[:16]


def kernel_call(body, grid, ins, outs, scratch):
    return pl.pallas_call(
        body,
        grid=grid,
        in_specs=[spec for _, spec in ins],
        out_specs=[spec for _, _, spec in outs],
        out_shape=[jax.ShapeDtypeStruct(shape, dtype) for shape, dtype, _ in outs],
        scratch_shapes=scratch,
        compiler_params=pltpu.CompilerParams(
            vmem_limit_bytes=VMEM_BYTES, dimension_semantics=("arbitrary",) * len(grid)
        ),
    )(*[array for array, _ in ins])


def delta_specs(heads, span):
    head_size = CHUNK
    chunks = span // CHUNK

    def chain(s, h):
        return s * heads + h

    return {
        "scalar": pl.BlockSpec(memory_space=pltpu.SMEM),
        "three": pl.BlockSpec((span, 3 * head_size), lambda s, h: (s, h)),
        "edge": pl.BlockSpec((1, 16, 3 * head_size), lambda s, h: (s, 0, h)),
        "taps": pl.BlockSpec((1, 3 * CONV, head_size), lambda s, h: (h, 0, 0)),
        "one": pl.BlockSpec((span, head_size), lambda s, h: (s, h)),
        "square": pl.BlockSpec((1, chunks, CHUNK, head_size), lambda s, h: (chain(s, h), 0, 0, 0)),
        "double": pl.BlockSpec(
            (1, chunks, CHUNK, 2 * head_size), lambda s, h: (chain(s, h), 0, 0, 0)
        ),
        "state": pl.BlockSpec((1, head_size, head_size), lambda s, h: (chain(s, h), 0, 0)),
        "scale": pl.BlockSpec((1, head_size), lambda s, h: (0, 0)),
        "gain": pl.BlockSpec((1, 8, head_size), lambda s, h: (chain(s, h), 0, 0)),
        "tapped": pl.BlockSpec((1, 8, 3 * head_size), lambda s, h: (chain(s, h), 0, 0)),
        "all_squares": lambda chains: pl.BlockSpec(
            (chains, chunks, CHUNK, head_size), lambda s, h: (0, 0, 0, 0)
        ),
        "all_states": lambda chains, columns: pl.BlockSpec(
            (chains, head_size, columns), lambda s, h: (0, 0, 0)
        ),
    }


def delta_prepare(limit, raw, tails, taps, logits, seqs, heads, span):
    specs = delta_specs(heads, span)
    chains, chunks, size = seqs * heads, span // CHUNK, CHUNK
    squares = (chains, chunks, CHUNK, size)
    return kernel_call(
        prepare_kernel,
        (seqs, heads),
        [
            (limit, specs["scalar"]),
            (raw, specs["three"]),
            (tails, specs["edge"]),
            (taps, specs["taps"]),
            (logits, specs["one"]),
        ],
        [
            (raw.shape, low, specs["three"]),
            (squares, wide, specs["square"]),
            ((chains, chunks, CHUNK, 2 * size), wide, specs["double"]),
            (squares, wide, specs["square"]),
            (squares, wide, specs["all_squares"](chains)),
            (squares, wide, specs["all_squares"](chains)),
            ((chains, size, 2 * size), wide, specs["all_states"](chains, 2 * size)),
        ],
        [
            pltpu.VMEM((span + 16, 3 * size), wide),
            pltpu.VMEM(squares, wide),
            pltpu.VMEM(squares, wide),
        ],
    )


def delta_mix(qkv, wu, prefix, local, enter, gate, scale, seqs, heads, span):
    specs = delta_specs(heads, span)
    chains, chunks, size = seqs * heads, span // CHUNK, CHUNK
    squares = (chains, chunks, CHUNK, size)
    return kernel_call(
        mix_kernel,
        (seqs, heads),
        [
            (qkv, specs["three"]),
            (wu, specs["double"]),
            (prefix, specs["square"]),
            (local, specs["square"]),
            (enter, specs["state"]),
            (gate, specs["one"]),
            (scale, specs["scale"]),
        ],
        [
            (squares, wide, specs["square"]),
            (squares, wide, specs["square"]),
            (gate.shape, wide, specs["one"]),
            (gate.shape, low, specs["one"]),
        ],
        [],
    )


def delta_turn(grad, mixed, gate, scale, qkv, wu, maps, seqs, heads, span):
    specs = delta_specs(heads, span)
    chains, chunks, size = seqs * heads, span // CHUNK, CHUNK
    squares = (chains, chunks, CHUNK, size)
    return kernel_call(
        turn_kernel,
        (seqs, heads),
        [
            (grad, specs["one"]),
            (mixed, specs["one"]),
            (gate, specs["one"]),
            (scale, specs["scale"]),
            (qkv, specs["three"]),
            (wu, specs["double"]),
            (maps, specs["square"]),
        ],
        [
            (squares, wide, specs["square"]),
            (squares, wide, specs["square"]),
            (gate.shape, low, specs["one"]),
            ((chains, 8, size), wide, specs["gain"]),
            (squares, wide, specs["square"]),
            ((chains, size, size), wide, specs["all_states"](chains, size)),
        ],
        [pltpu.VMEM(squares, wide), pltpu.VMEM(squares, wide)],
    )


def delta_unwind(
    limit, raw, tails, taps, logits, qkv, solved, wu, state, fresh, out, fresh_grad, maps,
    sources, leave, seqs, heads, span,
):
    specs = delta_specs(heads, span)
    chains, chunks, size = seqs * heads, span // CHUNK, CHUNK
    squares = (chains, chunks, CHUNK, size)
    edges = (seqs, 16, 3 * heads * size)
    return kernel_call(
        unwind_kernel,
        (seqs, heads),
        [
            (limit, specs["scalar"]),
            (raw, specs["three"]),
            (tails, specs["edge"]),
            (taps, specs["taps"]),
            (logits, specs["one"]),
            (qkv, specs["three"]),
            (solved, specs["square"]),
            (wu, specs["double"]),
            (state, specs["square"]),
            (fresh, specs["square"]),
            (out, specs["square"]),
            (fresh_grad, specs["square"]),
            (maps, specs["all_squares"](chains)),
            (sources, specs["all_squares"](chains)),
            (leave, specs["all_states"](chains, size)),
        ],
        [
            (raw.shape, low, specs["three"]),
            (edges, wide, specs["edge"]),
            (edges, wide, specs["edge"]),
            ((chains, 8, 3 * size), wide, specs["tapped"]),
            (logits.shape, low, specs["one"]),
        ],
        [
            pltpu.VMEM((span + 16, 3 * size), wide),
            pltpu.VMEM((span + 32, 3 * size), wide),
            pltpu.VMEM(squares, wide),
        ],
    )


def cut_columns(weight):
    depth, columns = weight.shape
    return weight.reshape(depth, MATES, columns // MATES).transpose(1, 0, 2)


def join_columns(blocks):
    return blocks.transpose(1, 0, 2).reshape(blocks.shape[1], -1)


def gather_weights(blocks):
    return gather_lines(swap_blocks(blocks))


def scatter_grads(blocks):
    return swap_blocks(scatter_lines(blocks.astype(low)).astype(low)).astype(wide)


def on_device(
    block_input,
    lengths,
    attn_gain,
    query_weight,
    key_weight,
    value_weight,
    outgate_weight,
    beta_weight,
    conv_kernel,
    head_gain,
    output_weight,
    mlp_gain,
    swish_weight,
    upward_weight,
    downward_weight,
    out_grad,
):
    count = lax.axis_size("seq")
    lines = count // MATES
    core = lax.axis_index("tp")
    seq_count, tokens, model_width = block_input.shape
    depth = attn_gain.shape[0]
    gain_part = head_gain.shape[0]
    head_size = gain_part * count
    heads = beta_weight.shape[1] // MATES
    width = heads * head_size
    units = swish_weight.shape[1] // MATES

    small = jnp.concatenate(
        [
            beta_weight.astype(low).reshape(depth, MATES, heads).transpose(1, 0, 2).reshape(MATES, -1),
            conv_kernel.astype(low).reshape(MATES, -1),
            jnp.broadcast_to(
                jnp.concatenate([attn_gain, mlp_gain, head_gain]).astype(low)[None],
                (MATES, 2 * depth + gain_part),
            ),
        ],
        axis=1,
    )
    small_size = small.shape[1]
    small = jnp.pad(small, ((0, 0), (0, SMALL * 3 * width - small_size))).reshape(
        MATES, SMALL, 3 * width
    )
    streams_cut = jnp.stack(
        [
            w.astype(low).reshape(depth, MATES, heads, head_size)
            for w in (query_weight, key_weight, value_weight)
        ],
        axis=3,
    )
    streams_cut = streams_cut.transpose(1, 0, 2, 3, 4).reshape(MATES, depth, 3 * width)
    first = gather_weights(jnp.concatenate([streams_cut, small], axis=1))
    streams_full = first[:, :, :depth].reshape(model_width, 3 * width)
    small = first[:, :, depth:].reshape(count, SMALL * 3 * width)[:, :small_size]
    gates_cut = jnp.concatenate(
        [cut_columns(w.astype(low)) for w in (outgate_weight, output_weight.T)], axis=2
    )
    gates_full = gather_weights(gates_cut).reshape(model_width, 2 * width)
    outgate_full, output_full = gates_full[:, :width], gates_full[:, width:]
    ups_cut = jnp.concatenate(
        [cut_columns(w.astype(low)) for w in (swish_weight, upward_weight)], axis=2
    )
    ups_full = gather_weights(ups_cut).reshape(model_width, 2 * units)
    downward_full = gather_weights(cut_columns(downward_weight.astype(low).T)).reshape(
        model_width, units
    )
    sizes = (depth * heads, heads * 3 * CONV * gain_part, depth, depth, gain_part)
    starts = [sum(sizes[:index]) for index in range(len(sizes) + 1)]
    beta_small, conv_small, attn_small, mlp_small, head_small = (
        small[:, starts[index] : starts[index + 1]] for index in range(len(sizes))
    )
    beta_full = beta_small.reshape(model_width, heads)
    taps = (
        conv_small.reshape(count, heads, 3, CONV, gain_part)
        .transpose(1, 2, 3, 0, 4)
        .reshape(heads, 3 * CONV, head_size)
        .astype(wide)
    )
    attn_scale = attn_small.reshape(model_width).astype(wide)
    mlp_scale = mlp_small.reshape(model_width).astype(wide)
    head_scale = head_small.reshape(head_size).astype(wide)

    span = MATES * tokens
    rows = seq_count * span

    def ordered_rows(mine):
        gathered = in_order(gather_mates(mine)).reshape(span, model_width)
        return jnp.concatenate([gathered, other_core(gathered)], axis=0)

    def loose_rows(mine):
        gathered = jnp.concatenate(gather_mates(mine), axis=0)
        return jnp.concatenate([gathered, other_core(gathered)], axis=0)

    def sum_cores(partial):
        own = partial[:span]
        return (own.astype(wide) + other_core(partial[span:]).astype(wide)).astype(low)

    def sum_ordered(partial):
        blocks = sum_cores(partial).reshape(MATES, tokens, model_width)
        return scatter_mates([pick(blocks, mate_of() ^ flip) for flip in range(MATES)])

    def sum_loose(partial):
        blocks = sum_cores(partial).reshape(MATES, tokens, model_width)
        return scatter_mates([blocks[flip] for flip in range(MATES)])

    mine_low = pick(block_input, core)
    mine_input = mine_low.astype(wide)
    first_inverse = rms_scale(mine_input)
    grad_mine = pick(out_grad, core)
    grad_rows = loose_rows(grad_mine)
    input_rows = ordered_rows(mine_low).astype(wide)
    flat_normed = (input_rows * rms_scale(input_rows) * attn_scale).astype(low)

    lengths_here = jnp.stack([pick(lengths, core), pick(lengths, 1 - core)])
    limit = lengths_here - line_of() * span
    beta_spread = jnp.repeat(beta_full, head_size, axis=1)

    raw = matmul("rd,dc->rc", flat_normed, streams_full).astype(low)
    tails = along(raw.reshape(seq_count, span, 3 * width)[:, span - 16 :], 1)
    logits = matmul("rd,dc->rc", flat_normed, beta_spread)
    gate_values = matmul("rd,dc->rc", flat_normed, outgate_full).astype(low)
    sizes_of = (seq_count, heads, span)
    qkv, solved, wu, maps, prefix, local, ends = delta_prepare(
        limit, raw, tails, taps, logits, *sizes_of
    )
    map_matrix, map_offset = ends[:, :, :head_size], ends[:, :, head_size:]
    entering = hop_states(map_matrix, map_offset, 1)
    head_row = head_scale[None]
    state, fresh, mixed, gated = delta_mix(
        qkv, wu, prefix, local, entering, gate_values, head_row, *sizes_of
    )
    attn_out = sum_ordered(matmul("rc,dc->rd", gated, output_full).astype(low))
    middle = mine_input + attn_out
    second_inverse = rms_scale(middle)
    mlp_normed = loose_rows((middle * second_inverse * mlp_scale).astype(low))
    acts = matmul("rd,df->rf", mlp_normed, ups_full)
    gate_act, up_act = acts[:, :units], acts[:, units:]
    silu_act = jax.nn.silu(gate_act)
    hidden = (silu_act * up_act).astype(low)
    mlp_out = sum_loose(matmul("rf,df->rd", hidden, downward_full).astype(low))
    output_mine = (middle + mlp_out).astype(low)

    hidden_grad = matmul("rd,df->rf", grad_rows, downward_full)
    downward_grad = matmul("rd,rf->df", grad_rows, hidden)
    acts_grad = jnp.concatenate(
        [
            (hidden_grad * up_act * silu_slope(gate_act)).astype(low),
            (hidden_grad * silu_act).astype(low),
        ],
        axis=1,
    )
    ups_grad = matmul("rd,rf->df", mlp_normed, acts_grad)
    normed_two_grad = sum_loose(matmul("rf,df->rd", acts_grad, ups_full).astype(low))
    middle_part, mlp_gain_grad = norm_back(normed_two_grad, middle, second_inverse, mlp_scale)
    middle_grad = grad_mine.astype(wide) + middle_part
    attn_grad_rows = ordered_rows(middle_grad.astype(low))
    output_grad = matmul("rd,rc->dc", attn_grad_rows, gated)
    gated_grad = matmul("rd,dc->rc", attn_grad_rows, output_full)
    out_grads, fresh_grad, outgate_act_grad, head_gain_parts, sources, local_state = delta_turn(
        gated_grad, mixed, gate_values, head_row, qkv, wu, maps, *sizes_of
    )
    head_gain_part = jnp.sum(head_gain_parts[:, 0], axis=0)
    leaving_grad = hop_states_back(map_matrix, local_state)
    raw_grad, edge, halo, taps_grad, logit_grad = delta_unwind(
        limit, raw, tails, taps, logits, qkv, solved, wu, state, fresh, out_grads, fresh_grad,
        maps, sources, leaving_grad, *sizes_of,
    )
    returned = along(halo.astype(low), -1)
    edge = (edge + returned.astype(wide)).astype(low)
    raw_grad_low = (
        raw_grad.reshape(seq_count, span, 3 * width)
        .at[:, span - 16 :]
        .set(edge)
        .reshape(rows, 3 * width)
    )
    beta_logit_grad = logit_grad[:, ::head_size]
    last_grads = jnp.concatenate(
        [raw_grad_low, jnp.pad(beta_logit_grad, ((0, 0), (0, head_size - heads)))], axis=1
    )
    last_weights = jnp.concatenate(
        [streams_full, jnp.pad(beta_full, ((0, 0), (0, head_size - heads)))], axis=1
    )
    outgate_grad = matmul("rd,rc->dc", flat_normed, outgate_act_grad)
    last_grad = matmul("rd,rc->dc", flat_normed, last_grads)
    streams_grad, beta_grad = last_grad[:, : 3 * width], last_grad[:, 3 * width : 3 * width + heads]
    normed_part = matmul("rc,dc->rd", outgate_act_grad, outgate_full) + matmul(
        "rc,dc->rd", last_grads, last_weights
    )
    normed_grad = sum_ordered(normed_part.astype(low))
    input_part, attn_gain_grad = norm_back(normed_grad, mine_input, first_inverse, attn_scale)
    input_grad_mine = (middle_grad + input_part).astype(low)

    def both_sequences(mine):
        other = other_core(mine)
        return jnp.stack([jnp.where(core == 0, mine, other), jnp.where(core == 0, other, mine)])

    def cut_rows(grad):
        return grad.reshape(lines, MATES, depth, grad.shape[1])

    downward_sum = join_columns(scatter_grads(cut_rows(downward_grad))).T
    ups_sum = scatter_grads(cut_rows(ups_grad))
    gates_sum = scatter_grads(cut_rows(jnp.concatenate([outgate_grad, output_grad], axis=1)))
    conv_grad = (
        taps_grad[:, :CONV]
        .reshape(seq_count, heads, CONV, 3, count, gain_part)
        .sum(axis=0)
        .transpose(3, 0, 2, 1, 4)
        .reshape(count, -1)
    )
    small_grad = jnp.concatenate(
        [
            beta_grad.reshape(count, depth * heads),
            conv_grad,
            attn_gain_grad.reshape(count, depth),
            mlp_gain_grad.reshape(count, depth),
            head_gain_part.reshape(count, gain_part),
        ],
        axis=1,
    ).astype(low)
    small_grad = jnp.pad(small_grad, ((0, 0), (0, SMALL * 3 * width - small_size)))
    first_sum = scatter_grads(
        jnp.concatenate(
            [
                cut_rows(streams_grad.astype(low)),
                small_grad.reshape(lines, MATES, SMALL, 3 * width),
            ],
            axis=2,
        )
    )
    streams_sum = (
        first_sum[:, :depth]
        .reshape(MATES, depth, heads, 3, head_size)
        .transpose(3, 1, 0, 2, 4)
        .reshape(3, depth, MATES * width)
    )
    small_sum = first_sum[:, depth:].reshape(MATES, SMALL * 3 * width)
    beta_sum, conv_sum, attn_sum, mlp_sum, head_sum = (
        small_sum[:, starts[index] : starts[index + 1]] for index in range(len(sizes))
    )
    gains_sum = jnp.sum(jnp.concatenate([attn_sum, mlp_sum, head_sum], axis=1), axis=0)
    gains_sum = gains_sum + other_core(gains_sum)
    return (
        both_sequences(output_mine),
        both_sequences(input_grad_mine),
        gains_sum[:depth],
        streams_sum[0],
        streams_sum[1],
        streams_sum[2],
        join_columns(gates_sum[:, :, :width]),
        join_columns(beta_sum.reshape(MATES, depth, heads)),
        conv_sum.reshape(MATES * heads, 3, CONV, gain_part),
        gains_sum[2 * depth :],
        join_columns(gates_sum[:, :, width:]).T,
        gains_sum[depth : 2 * depth],
        join_columns(ups_sum[:, :, :units]),
        join_columns(ups_sum[:, :, units:]),
        downward_sum,
    )


def solution(mesh):
    return jax.shard_map(
        on_device,
        mesh=mesh,
        in_specs=(
            P(None, "seq", None),
            P(),
            P("seq"),
            P("seq", "tp"),
            P("seq", "tp"),
            P("seq", "tp"),
            P("seq", "tp"),
            P("seq", "tp"),
            P("tp", None, None, "seq"),
            P("seq"),
            P("tp", "seq"),
            P("seq"),
            P("seq", "tp"),
            P("seq", "tp"),
            P("tp", "seq"),
            P(None, "seq", None),
        ),
        out_specs=(
            P(None, "seq", None),
            P(None, "seq", None),
            P("seq"),
            P("seq", "tp"),
            P("seq", "tp"),
            P("seq", "tp"),
            P("seq", "tp"),
            P("seq", "tp"),
            P("tp", None, None, "seq"),
            P("seq"),
            P("tp", "seq"),
            P("seq"),
            P("seq", "tp"),
            P("seq", "tp"),
            P("tp", "seq"),
        ),
        check_vma=False,
    )
```

```python
import functools

import jax
import jax.numpy as jnp
from jax import lax
from jax.experimental import pallas as pl
from jax.experimental.layout import Layout, with_layout_constraint
from jax.experimental.pallas import tpu as pltpu
from jax.sharding import PartitionSpec as P

CONV = 4
MATES = 4
SMALL = 16


PRECISE = lax.Precision.HIGHEST
epsilon = 1e-06
low = jnp.bfloat16
wide = jnp.float32


def other_core(value):
    return lax.ppermute(value, "tp", [(0, 1), (1, 0)])


def to_mate(value, flip):
    count = lax.axis_size("seq")
    return lax.ppermute(value, "seq", [(source, source ^ flip) for source in range(count)])


def along(value, step, lines_kept=None):
    count = lax.axis_size("seq")
    lines = count // MATES
    pairs = []
    for source in range(count):
        line = source // MATES
        if 0 <= line + step < lines and (lines_kept is None or line in lines_kept):
            pairs.append((source, source + step * MATES))
    return lax.ppermute(value, "seq", pairs)


def row_major(value):
    return with_layout_constraint(value, Layout(major_to_minor=tuple(range(value.ndim))))


def mate_of():
    return lax.axis_index("seq") % MATES


def line_of():
    return lax.axis_index("seq") // MATES


def line_groups():
    lines = lax.axis_size("seq") // MATES
    return [[mate + MATES * line for line in range(lines)] for mate in range(MATES)]


def pick(blocks, index):
    return lax.dynamic_index_in_dim(blocks, index, 0, False)


def in_order(by_flip):
    mate = mate_of()
    out = row_major(jnp.zeros((MATES,) + by_flip[0].shape, by_flip[0].dtype))
    for flip, piece in enumerate(by_flip):
        out = lax.dynamic_update_index_in_dim(out, piece, mate ^ flip, 0)
    return out


def swap_blocks(blocks):
    mate = mate_of()
    pieces = [pick(blocks, mate)]
    for flip in range(1, MATES):
        pieces.append(to_mate(pick(blocks, mate ^ flip), flip))
    return in_order(pieces)


def gather_lines(block):
    lines = lax.axis_size("seq") // MATES
    if lines > 4:
        return lax.all_gather(block, "seq", axis_index_groups=line_groups())
    line = line_of()
    ups, downs = [block], [block]
    for _ in range(1, lines):
        ups.append(along(ups[-1], 1))
        downs.append(along(downs[-1], -1))
    out = jnp.zeros((lines,) + block.shape, block.dtype)
    out = lax.dynamic_update_index_in_dim(out, block, line, 0)
    for step in range(1, lines):
        out = lax.dynamic_update_index_in_dim(
            out, ups[step] + downs[lines - step], (line - step) % lines, 0
        )
    return out


def scatter_lines(blocks):
    lines = lax.axis_size("seq") // MATES
    if lines > 4:
        return lax.psum_scatter(
            blocks, "seq", scatter_dimension=0, axis_index_groups=line_groups()
        ).astype(wide)
    line = line_of()
    from_below = from_above = None
    for step in range(1, lines):
        up = pick(blocks, (line + lines - step) % lines)
        down = pick(blocks, (line + step) % lines)
        if step > 1:
            up = (up.astype(wide) + from_below.astype(wide)).astype(low)
            down = (down.astype(wide) + from_above.astype(wide)).astype(low)
        from_below = along(up, 1, range(step))
        from_above = along(down, -1, range(lines - step, lines))
    total = pick(blocks, line).astype(wide)
    if lines > 1:
        total = total + from_below.astype(wide) + from_above.astype(wide)
    return total


def hop_states(matrix, offset, step):
    lines = lax.axis_size("seq") // MATES
    state = along(offset, step)
    for _ in range(lines - 2):
        state = along(product("...ij,...jk->...ik", matrix, state) + offset, step)
    return state


def hop_states_back(matrix, offset):
    lines = lax.axis_size("seq") // MATES
    state = along(offset, -1)
    for _ in range(lines - 2):
        state = along(product("...ij,...jk->...ik", state, matrix) + offset, -1)
    return state


def product(form, left, right):
    return jnp.einsum(form, left, right, precision=PRECISE)


def matmul(form, left, right):
    return jnp.einsum(form, left, right, preferred_element_type=wide)


def silu_slope(value):
    squash = jax.nn.sigmoid(value)
    return squash * (1.0 + value * (1.0 - squash))


def rms_scale(value):
    return lax.rsqrt(jnp.mean(value * value, axis=-1, keepdims=True) + epsilon)


CHUNK = 128
TOGETHER = 4
VMEM_BYTES = 52 * 1024 * 1024
NN = (((1,), (0,)), ((), ()))
NT = (((1,), (1,)), ((), ()))


def dot(left, right, dims):
    return lax.dot_general(left, right, dims, preferred_element_type=wide)


def pair(value):
    high = value.astype(low)
    return high, (value - high.astype(wide)).astype(low)


def side(left, right):
    return jnp.concatenate([left, right], axis=1)


def over(top, bottom):
    return jnp.concatenate([top, bottom], axis=0)


def nn(left, right):
    width = right[0].shape[1]
    both = side(*right)
    out = dot(side(*left), over(both, both), NN)
    return out[:, :width] + out[:, width:]


def nt(left, right):
    width = right[0].shape[0]
    out = dot(side(*left), over(side(right[0], right[0]), side(right[1], right[1])), NT)
    return out[:, :width] + out[:, width:]


def nn_wide(left, right):
    return dot(side(*left), over(right[0], right[0]), NN) + dot(left[0], right[1], NN)


def nn_low(left, right):
    return dot(side(*left), over(right, right), NN)


def low_nn(left, right):
    return dot(side(left, left), over(*right), NN)


def low_nt(left, right):
    return dot(side(left, left), side(*right), NT)


def grid_of_rows():
    rows = lax.broadcasted_iota(jnp.int32, (CHUNK, CHUNK), 0)
    columns = lax.broadcasted_iota(jnp.int32, (CHUNK, CHUNK), 1)
    return rows, columns


def inverse_of(strict):
    rows, columns = grid_of_rows()
    one = jnp.where(rows == columns, 1.0, 0.0).astype(wide)

    def joining(shift):
        upper = columns >> shift
        return ((rows >> shift) == upper + 1) & ((upper & 1) == 0)

    solved = [one - jnp.where(joining(0), s, 0.0) for s in strict]
    shift = 1
    while (1 << shift) < CHUNK:
        mask = joining(shift)
        pairs = [pair(d) for d in solved]
        crossed = [nn(pair(jnp.where(mask, s, 0.0)), p) for s, p in zip(strict, pairs)]
        solved = [d - nn(p, pair(c)) for d, p, c in zip(solved, pairs, crossed)]
        shift += 1
    return solved


def convolved(block, taps, stream):
    columns = block[:, stream * CHUNK : (stream + 1) * CHUNK]
    total = None
    for offset in range(CONV):
        first = 16 - (CONV - 1) + offset
        term = taps[stream * CONV + offset][None, :] * columns[first : first + CHUNK]
        total = term if total is None else total + term
    return total


def silu_parts(value):
    squash = jax.nn.sigmoid(value)
    return value * squash, squash * (1.0 + value * (1.0 - squash))


def live_rows(limit, start):
    rows = lax.broadcasted_iota(jnp.int32, (CHUNK, CHUNK), 0)
    return jnp.where(rows + start < limit, 1.0, 0.0).astype(wide)


def head_squash(logits, head):
    lanes = lax.broadcasted_iota(jnp.int32, logits.shape, 1)
    column = jnp.sum(jnp.where(lanes == head, logits, 0.0), axis=1, keepdims=True)
    return jax.nn.sigmoid(jnp.broadcast_to(column, logits.shape))


def write_extended(ext, tail_ref, raw_ref):
    ext[:16] = tail_ref[0].astype(wide)
    ext[16:] = raw_ref[...].astype(wide)


def prepare_kernel(
    limit_ref, raw_ref, tail_ref, taps_ref, logit_ref,
    qkv_ref, solved_ref, wu_ref, map_ref, prefix_ref, local_ref, ends_ref,
    ext, offsets, maps,
):
    seq, head = pl.program_id(0), pl.program_id(1)
    heads = pl.num_programs(1)
    chain = seq * heads + head
    chains, chunks = prefix_ref.shape[0], prefix_ref.shape[1]
    write_extended(ext, tail_ref, raw_ref)
    taps = taps_ref[0]
    limit = limit_ref[seq]
    rows, columns = grid_of_rows()
    identity = jnp.where(rows == columns, 1.0, 0.0).astype(wide)
    head_size = CHUNK

    def group(index, carry):
        first = index * TOGETHER
        parts = []
        for step in range(TOGETHER):
            start = pl.multiple_of((first + step) * CHUNK, CHUNK)
            block = ext[pl.ds(start, CHUNK + 16)]
            query = jax.nn.silu(convolved(block, taps, 0))
            key = jax.nn.silu(convolved(block, taps, 1))
            value = jax.nn.silu(convolved(block, taps, 2)).astype(low)
            query = query * lax.rsqrt(jnp.sum(query * query, axis=1, keepdims=True) + epsilon)
            query = (query * head_size ** (-0.5)).astype(low)
            key = key * lax.rsqrt(jnp.sum(key * key, axis=1, keepdims=True) + epsilon)
            key = key.astype(low)
            beta = head_squash(logit_ref[pl.ds(start, CHUNK)], head) * live_rows(limit, start)
            qkv_ref[pl.ds(start, CHUNK)] = jnp.concatenate([query, key, value], axis=1)
            parts.append((key, value, beta))
        strict = [
            jnp.where(rows > columns, beta * dot(key, key, NT), 0.0) for key, _, beta in parts
        ]
        solved = inverse_of(strict)
        for step in range(TOGETHER):
            key, value, beta = parts[step]
            solved_ref[0, first + step] = solved[step]
            weighted = pair(solved[step] * beta.T)
            both = nn_low(weighted, side(key, value))
            wu_ref[0, first + step] = both
            moved = low_nn(key.T, pair(both))
            step_map = identity - moved[:, :head_size]
            map_ref[0, first + step] = step_map
            maps[chain, first + step] = step_map
            offsets[chain, first + step] = moved[:, head_size:]
        return carry

    lax.fori_loop(0, chunks // TOGETHER, group, 0)

    @pl.when(chain == chains - 1)
    def _():
        start = side(identity, jnp.zeros_like(identity))

        def advance(chunk, states):
            out = []
            for index in range(chains):
                state = states[index]
                prefix_ref[index, chunk] = state[:, :head_size]
                local_ref[index, chunk] = state[:, head_size:]
                moved = nn_wide(pair(maps[index, chunk]), pair(state))
                out.append(
                    side(moved[:, :head_size], moved[:, head_size:] + offsets[index, chunk])
                )
            return tuple(out)

        ends = lax.fori_loop(0, chunks, advance, (start,) * chains)
        for index in range(chains):
            ends_ref[index] = ends[index]


def mix_kernel(
    qkv_ref, wu_ref, prefix_ref, local_ref, enter_ref, gate_ref, scale_ref,
    state_ref, fresh_ref, mixed_ref, gated_ref,
):
    chunks = prefix_ref.shape[1]
    head_size = CHUNK
    rows, columns = grid_of_rows()
    enter = pair(enter_ref[0])
    scale = scale_ref[...]

    def group(index, carry):
        for step in range(TOGETHER):
            chunk = index * TOGETHER + step
            start = pl.multiple_of(chunk * CHUNK, CHUNK)
            here = pl.ds(start, CHUNK)
            state = nn(pair(prefix_ref[0, chunk]), enter) + local_ref[0, chunk]
            state_ref[0, chunk] = state
            states = pair(state)
            both = wu_ref[0, chunk]
            fresh = both[:, head_size:] - nn(pair(both[:, :head_size]), states)
            fresh_ref[0, chunk] = fresh
            query, key = qkv_ref[here, :head_size], qkv_ref[here, head_size : 2 * head_size]
            scores = jnp.where(rows >= columns, dot(query, key, NT), 0.0)
            mixed = low_nn(query, states) + nn(pair(scores), pair(fresh))
            mixed_ref[here] = mixed
            inverse = lax.rsqrt(jnp.mean(mixed * mixed, axis=1, keepdims=True) + epsilon)
            normed = mixed * inverse * scale
            gated_ref[here] = (normed * jax.nn.silu(gate_ref[here].astype(wide))).astype(low)
        return carry

    lax.fori_loop(0, chunks // TOGETHER, group, 0)


def turn_kernel(
    grad_ref, mixed_ref, gate_ref, scale_ref, qkv_ref, wu_ref, map_ref,
    out_ref, fresh_ref, gate_grad_ref, gain_ref, source_ref, end_ref,
    maps, sources,
):
    seq, head = pl.program_id(0), pl.program_id(1)
    heads = pl.num_programs(1)
    chain = seq * heads + head
    chains, chunks = maps.shape[0], maps.shape[1]
    head_size = CHUNK
    rows, columns = grid_of_rows()
    scale = scale_ref[...]

    def group(index, gain):
        for step in range(TOGETHER):
            chunk = index * TOGETHER + step
            start = pl.multiple_of(chunk * CHUNK, CHUNK)
            here = pl.ds(start, CHUNK)
            grad, mixed = grad_ref[here], mixed_ref[here]
            silu_gate, slope = silu_parts(gate_ref[here].astype(wide))
            inverse = lax.rsqrt(jnp.mean(mixed * mixed, axis=1, keepdims=True) + epsilon)
            unit = mixed * inverse
            gate_grad_ref[here] = (grad * unit * scale * slope).astype(low)
            passed = grad * silu_gate
            gain = gain + jnp.sum(passed * unit, axis=0, keepdims=True)
            scaled = passed * scale
            mixed_grad = inverse * (
                scaled - unit * inverse * jnp.mean(scaled * mixed, axis=1, keepdims=True)
            )
            out_ref[0, chunk] = mixed_grad
            query, key = qkv_ref[here, :head_size], qkv_ref[here, head_size : 2 * head_size]
            scores = jnp.where(rows >= columns, dot(query, key, NT), 0.0)
            turned = jnp.where(rows <= columns, dot(key, query, NT), 0.0)
            grads = pair(mixed_grad)
            fresh_ref[0, chunk] = nn(pair(turned), grads)
            reading = query.astype(wide) - nn(pair(scores), pair(wu_ref[0, chunk, :, :head_size]))
            source = nn(pair(mixed_grad.T), pair(reading))
            source_ref[0, chunk] = source
            sources[chain, chunk] = source
            maps[chain, chunk] = map_ref[0, chunk]
        return gain

    gain = lax.fori_loop(0, chunks // TOGETHER, group, jnp.zeros((1, head_size), wide))
    gain_ref[0] = jnp.broadcast_to(gain, (8, head_size))

    @pl.when(chain == chains - 1)
    def _():
        def advance(step, states):
            chunk = chunks - 1 - step
            return tuple(
                nn(pair(states[index]), pair(maps[index, chunk])) + sources[index, chunk]
                for index in range(chains)
            )

        ends = lax.fori_loop(
            0, chunks, advance, (jnp.zeros((head_size, head_size), wide),) * chains
        )
        for index in range(chains):
            end_ref[index] = ends[index]


def unwind_kernel(
    limit_ref, raw_ref, tail_ref, taps_ref, logit_ref, qkv_ref, solved_ref, wu_ref, state_ref,
    fresh_in_ref, out_ref, fresh_grad_ref, maps_ref, sources_ref, leave_ref, all_grads_ref,
    raw_grad_ref, edge_ref, halo_ref, taps_grad_ref, logit_grad_ref,
    ext, pre_grads, leaving,
):
    seq, head = pl.program_id(0), pl.program_id(1)
    heads = pl.num_programs(1)
    chain = seq * heads + head
    chains, chunks = maps_ref.shape[0], maps_ref.shape[1]
    head_size = CHUNK
    span = chunks * CHUNK
    rows, columns = grid_of_rows()
    write_extended(ext, tail_ref, raw_ref)
    taps = taps_ref[0]
    limit = limit_ref[seq]

    @pl.when(chain == 0)
    def _():
        def advance(step, states):
            chunk = chunks - 1 - step
            out = []
            for index in range(chains):
                leaving[index, chunk] = states[index]
                out.append(
                    nn(pair(states[index]), pair(maps_ref[index, chunk]))
                    + sources_ref[index, chunk]
                )
            return tuple(out)

        lax.fori_loop(0, chunks, advance, tuple(leave_ref[index] for index in range(chains)))

    pre_grads[:16] = jnp.zeros((16, 3 * head_size), wide)
    pre_grads[span + 16 :] = jnp.zeros((16, 3 * head_size), wide)

    def one(chunk):
        start = pl.multiple_of(chunk * CHUNK, CHUNK)
        here = pl.ds(start, CHUNK)
        query = qkv_ref[here, :head_size]
        key = qkv_ref[here, head_size : 2 * head_size]
        value = qkv_ref[here, 2 * head_size :]
        live = live_rows(limit, start)
        squash = head_squash(logit_ref[here], head)
        beta = squash * live
        grads = pair(out_ref[0, chunk])
        fresh = pair(fresh_in_ref[0, chunk])
        state = pair(state_ref[0, chunk])
        leave = pair(leaving[chain, chunk])
        both = wu_ref[0, chunk]
        fresh_grad = fresh_grad_ref[0, chunk] + low_nt(key, leave)
        fresh_grads = pair(fresh_grad)
        score_grad = jnp.where(rows >= columns, nt(grads, fresh), 0.0)
        turned_grad = jnp.where(rows <= columns, nt(fresh, grads), 0.0)
        query_grad = nt(grads, state) + nn_low(pair(score_grad), key)
        key_grad = nn_low(pair(turned_grad), query) + nn(fresh, leave)
        wkey_grad = -nt(fresh_grads, state)
        right_grad = nn_wide(pair(solved_ref[0, chunk].T), pair(side(wkey_grad, fresh_grad)))
        right = pair(right_grad)
        twos = pair(both)
        found = dot(right[0], over(*twos), NT)
        system_grad = found[:, :CHUNK] + found[:, CHUNK:] + dot(right[1], twos[0], NT)
        system_grad = jnp.where(rows > columns, -system_grad, 0.0)
        gram = dot(key, key, NT)
        gram_grad = beta * system_grad
        key_grad = key_grad + nn_low(pair(gram_grad + gram_grad.T), key)
        key_right, value_right = right_grad[:, :head_size], right_grad[:, head_size:]
        key_grad = key_grad + beta * key_right
        value_grad = beta * value_right
        beta_grad = jnp.sum(
            key_right * key.astype(wide) + value_right * value.astype(wide) + system_grad * gram,
            axis=1,
            keepdims=True,
        )
        lanes = lax.broadcasted_iota(jnp.int32, (CHUNK, head_size), 1)
        logit_grad = jnp.where(
            lanes == head, beta_grad * (live * squash * (1.0 - squash)), 0.0
        ).astype(low)

        @pl.when(head == 0)
        def _():
            logit_grad_ref[here] = logit_grad

        @pl.when(head > 0)
        def _():
            logit_grad_ref[here] = logit_grad_ref[here] + logit_grad


        block = ext[pl.ds(start, CHUNK + 16)]
        grads_pre = []
        for stream, grad in enumerate((query_grad, key_grad, value_grad)):
            act, slope = silu_parts(convolved(block, taps, stream))
            if stream < 2:
                inverse = lax.rsqrt(jnp.sum(act * act, axis=1, keepdims=True) + epsilon)
                inner = jnp.sum(act * grad, axis=1, keepdims=True)
                grad = inverse * (grad - act * (inverse * inverse * inner))
                if stream == 0:
                    grad = grad * head_size ** (-0.5)
            grads_pre.append(grad * slope)
        pre_grads[pl.ds(start + 16, CHUNK)] = jnp.concatenate(grads_pre, axis=1)

    def group(index, carry):
        for step in range(2):
            one(index * 2 + step)
        return carry

    lax.fori_loop(0, chunks // 2, group, 0)

    def back(block, offset_of_first):
        streams = []
        for stream in range(3):
            part = block[:, stream * head_size : (stream + 1) * head_size]
            total = None
            for offset in range(CONV):
                first = offset_of_first + CONV - 1 - offset
                term = taps[stream * CONV + offset][None, :] * part[first : first + CHUNK]
                total = term if total is None else total + term
            streams.append(total)
        return jnp.concatenate(streams, axis=1)

    def finish(chunk, totals):
        start = pl.multiple_of(chunk * CHUNK, CHUNK)
        block = pre_grads[pl.ds(start + 16, CHUNK + 16)]
        grad = back(block, 0)
        raw_grad_ref[pl.ds(start, CHUNK)] = grad.astype(low)
        edge_ref[0] = grad[CHUNK - 16 :]
        before = ext[pl.ds(start, CHUNK + 16)]
        pre = block[:CHUNK]
        out = []
        for offset in range(CONV):
            first = 16 - (CONV - 1) + offset
            term = jnp.sum(pre * before[first : first + CHUNK], axis=0, keepdims=True)
            out.append(totals[offset] + term)
        return tuple(out)

    zero = jnp.zeros((1, 3 * head_size), wide)
    totals = lax.fori_loop(0, chunks, finish, (zero,) * CONV)
    for offset in range(CONV):
        taps_grad_ref[0, offset : offset + 1] = totals[offset]
    halo = back(pre_grads[: CHUNK + 32], 0)
    halo_ref[0] = halo[:16]


def kernel_call(body, grid, ins, outs, scratch, aliases=None):
    return pl.pallas_call(
        body,
        grid=grid,
        in_specs=[spec for _, spec in ins],
        out_specs=[spec for _, _, spec in outs],
        out_shape=[jax.ShapeDtypeStruct(shape, dtype) for shape, dtype, _ in outs],
        scratch_shapes=scratch,
        input_output_aliases=aliases or {},
        compiler_params=pltpu.CompilerParams(
            vmem_limit_bytes=VMEM_BYTES, dimension_semantics=("arbitrary",) * len(grid)
        ),
    )(*[array for array, _ in ins])


def delta_specs(heads, span):
    head_size = CHUNK
    chunks = span // CHUNK

    def chain(s, h):
        return s * heads + h

    return {
        "scalar": pl.BlockSpec(memory_space=pltpu.SMEM),
        "three": pl.BlockSpec((span, 3 * head_size), lambda s, h: (s, h)),
        "edge": pl.BlockSpec((1, 16, 3 * head_size), lambda s, h: (s, 0, h)),
        "taps": pl.BlockSpec((1, 3 * CONV, head_size), lambda s, h: (h, 0, 0)),
        "one": pl.BlockSpec((span, head_size), lambda s, h: (s, h)),
        "gate": pl.BlockSpec((span, head_size), lambda s, h: (s, 3 * heads + h)),
        "logit": pl.BlockSpec((span, head_size), lambda s, h: (s, 0)),
        "square": pl.BlockSpec((1, chunks, CHUNK, head_size), lambda s, h: (chain(s, h), 0, 0, 0)),
        "double": pl.BlockSpec(
            (1, chunks, CHUNK, 2 * head_size), lambda s, h: (chain(s, h), 0, 0, 0)
        ),
        "state": pl.BlockSpec((1, head_size, head_size), lambda s, h: (chain(s, h), 0, 0)),
        "scale": pl.BlockSpec((1, head_size), lambda s, h: (0, 0)),
        "gain": pl.BlockSpec((1, 8, head_size), lambda s, h: (chain(s, h), 0, 0)),
        "tapped": pl.BlockSpec((1, 8, 3 * head_size), lambda s, h: (chain(s, h), 0, 0)),
        "all_squares": lambda chains: pl.BlockSpec(
            (chains, chunks, CHUNK, head_size), lambda s, h: (0, 0, 0, 0)
        ),
        "all_states": lambda chains, columns: pl.BlockSpec(
            (chains, head_size, columns), lambda s, h: (0, 0, 0)
        ),
    }


def delta_prepare(limit, raw, tails, taps, logits, seqs, heads, span):
    specs = delta_specs(heads, span)
    chains, chunks, size = seqs * heads, span // CHUNK, CHUNK
    squares = (chains, chunks, CHUNK, size)
    return kernel_call(
        prepare_kernel,
        (seqs, heads),
        [
            (limit, specs["scalar"]),
            (raw, specs["three"]),
            (tails, specs["edge"]),
            (taps, specs["taps"]),
            (logits, specs["logit"]),
        ],
        [
            ((seqs * span, 3 * heads * size), low, specs["three"]),
            (squares, wide, specs["square"]),
            ((chains, chunks, CHUNK, 2 * size), wide, specs["double"]),
            (squares, wide, specs["square"]),
            (squares, wide, specs["all_squares"](chains)),
            (squares, wide, specs["all_squares"](chains)),
            ((chains, size, 2 * size), wide, specs["all_states"](chains, 2 * size)),
        ],
        [
            pltpu.VMEM((span + 16, 3 * size), wide),
            pltpu.VMEM(squares, wide),
            pltpu.VMEM(squares, wide),
        ],
    )


def delta_mix(qkv, wu, prefix, local, enter, gate, scale, seqs, heads, span):
    specs = delta_specs(heads, span)
    chains, chunks, size = seqs * heads, span // CHUNK, CHUNK
    squares = (chains, chunks, CHUNK, size)
    return kernel_call(
        mix_kernel,
        (seqs, heads),
        [
            (qkv, specs["three"]),
            (wu, specs["double"]),
            (prefix, specs["square"]),
            (local, specs["square"]),
            (enter, specs["state"]),
            (gate, specs["gate"]),
            (scale, specs["scale"]),
        ],
        [
            (squares, wide, specs["square"]),
            (squares, wide, specs["square"]),
            ((seqs * span, heads * size), wide, specs["one"]),
            ((seqs * span, heads * size), low, specs["one"]),
        ],
        [],
    )


def delta_turn(grad, mixed, gate, scale, qkv, wu, maps, seqs, heads, span):
    specs = delta_specs(heads, span)
    chains, chunks, size = seqs * heads, span // CHUNK, CHUNK
    squares = (chains, chunks, CHUNK, size)
    return kernel_call(
        turn_kernel,
        (seqs, heads),
        [
            (grad, specs["one"]),
            (mixed, specs["one"]),
            (gate, specs["gate"]),
            (scale, specs["scale"]),
            (qkv, specs["three"]),
            (wu, specs["double"]),
            (maps, specs["square"]),
        ],
        [
            (squares, wide, specs["square"]),
            (squares, wide, specs["square"]),
            ((seqs * span, (4 * heads + 1) * size), low, specs["gate"]),
            ((chains, 8, size), wide, specs["gain"]),
            (squares, wide, specs["square"]),
            ((chains, size, size), wide, specs["all_states"](chains, size)),
        ],
        [pltpu.VMEM(squares, wide), pltpu.VMEM(squares, wide)],
    )


def delta_unwind(
    limit, raw, tails, taps, logits, qkv, solved, wu, state, fresh, out, fresh_grad, maps,
    sources, leave, all_grads, seqs, heads, span,
):
    specs = delta_specs(heads, span)
    chains, chunks, size = seqs * heads, span // CHUNK, CHUNK
    squares = (chains, chunks, CHUNK, size)
    edges = (seqs, 16, 3 * heads * size)
    return kernel_call(
        unwind_kernel,
        (seqs, heads),
        [
            (limit, specs["scalar"]),
            (raw, specs["three"]),
            (tails, specs["edge"]),
            (taps, specs["taps"]),
            (logits, specs["logit"]),
            (qkv, specs["three"]),
            (solved, specs["square"]),
            (wu, specs["double"]),
            (state, specs["square"]),
            (fresh, specs["square"]),
            (out, specs["square"]),
            (fresh_grad, specs["square"]),
            (maps, specs["all_squares"](chains)),
            (sources, specs["all_squares"](chains)),
            (leave, specs["all_states"](chains, size)),
            (all_grads, pl.BlockSpec(memory_space=pl.ANY)),
        ],
        [
            (all_grads.shape, low, specs["three"]),
            (edges, wide, specs["edge"]),
            (edges, wide, specs["edge"]),
            ((chains, 8, 3 * size), wide, specs["tapped"]),
            (logits.shape, low, specs["logit"]),
        ],
        [
            pltpu.VMEM((span + 16, 3 * size), wide),
            pltpu.VMEM((span + 32, 3 * size), wide),
            pltpu.VMEM(squares, wide),
        ],
        {15: 0},
    )


MESH = pl.DeviceIdType.MESH
STEP = 16


class Place:
    def __init__(self):
        self.seq = lax.axis_index("seq")
        self.core = lax.axis_index("tp")
        self.mate = self.seq % MATES
        self.line = self.seq // MATES
        x, y = self.mate % 2, self.mate // 2
        self.x = 2 * y + (1 - x)
        self.y = 2 * (1 - y) + x
        self.far = 2 * (1 - y) + (1 - x)
        self.base = self.seq - self.mate

    def of(self, mate):
        return (self.base + mate, self.core)

    @property
    def sibling(self):
        return (self.seq, 1 - self.core)

    def lines_away(self, step):
        return (self.seq + step * MATES, self.core)


def meet(place, far=False, lines=0):
    barrier = pltpu.get_barrier_semaphore()
    partners = [place.of(place.x), place.of(place.y), place.sibling]
    if far:
        partners.append(place.of(place.far))
    for partner in partners:
        pl.semaphore_signal(barrier, inc=1, device_id=partner, device_id_type=MESH)
    count = len(partners)
    if lines > 1:
        below, above = place.line > 0, place.line < lines - 1

        @pl.when(below)
        def _():
            pl.semaphore_signal(
                barrier, inc=1, device_id=place.lines_away(-1), device_id_type=MESH
            )

        @pl.when(above)
        def _():
            pl.semaphore_signal(barrier, inc=1, device_id=place.lines_away(1), device_id_type=MESH)

        count = count + jnp.where(below, 1, 0) + jnp.where(above, 1, 0)
    pl.semaphore_wait(barrier, count)


def sender(sems):
    send, receive = sems

    def make(index, source, target, device):
        return pltpu.make_async_remote_copy(
            src_ref=source,
            dst_ref=target,
            send_sem=send.at[index],
            recv_sem=receive.at[index],
            device_id=device,
            device_id_type=MESH,
        )

    return make


def row_steps(first, last, body):
    def one(step, carry):
        body(pl.ds(pl.multiple_of(first + step * STEP, STEP), STEP))
        return carry

    lax.fori_loop(0, (last - first) // STEP, one, 0)


class SumRows:
    SCRATCH = 4

    @staticmethod
    def scratch(rows, columns):
        return [
            pltpu.VMEM((MATES, rows, columns), low),
            pltpu.VMEM((MATES, rows, columns), low),
            pltpu.VMEM((2, rows // 2, columns), low),
            pltpu.VMEM((2, rows, columns), low),
            pltpu.SemaphoreType.DMA((MATES,)),
            pltpu.SemaphoreType.DMA((10,)),
            pltpu.SemaphoreType.DMA((10,)),
        ]

    def __init__(self, place, partial, scratch):
        self.place, self.partial = place, partial
        self.own, self.swapped, self.relay, self.arrived, self.local_sems, send, receive = scratch
        self.make = sender((send, receive))
        self.rows = self.own.shape[1]
        self.order = [place.far, place.x, place.y, place.mate]

    def begin(self):
        self.swaps, self.loads = [], []
        for slot, mate in enumerate(self.order):
            copy = self.make(
                slot, self.partial.at[1, mate], self.swapped.at[slot], self.place.sibling
            )
            copy.start()
            self.swaps.append(copy)
            load = pltpu.make_async_copy(
                self.partial.at[0, mate], self.own.at[slot], self.local_sems.at[slot]
            )
            load.start()
            self.loads.append(load)

    def add(self, target, target_slot, source, source_slot, first, last, shift=0):
        def body(here):
            there = pl.ds(pl.multiple_of(here.start - shift, STEP), STEP) if shift else here
            target[target_slot, here] = (
                target[target_slot, here].astype(wide) + source[source_slot, there].astype(wide)
            ).astype(low)

        row_steps(first, last, body)

    def sum_cores(self, slot):
        self.loads[slot].wait()
        self.swaps[slot].wait_recv()
        self.add(self.own, slot, self.swapped, slot, 0, self.rows)

    def send_far(self):
        half = self.rows // 2
        self.sum_cores(0)
        self.far_low = self.make(
            4, self.own.at[0, :half], self.relay.at[0], self.place.of(self.place.y)
        )
        self.far_high = self.make(
            5, self.own.at[0, half:], self.relay.at[1], self.place.of(self.place.x)
        )
        self.far_low.start()
        self.far_high.start()

    def send_near(self):
        half, place = self.rows // 2, self.place
        self.sum_cores(1)
        self.x_high = self.make(
            6, self.own.at[1, half:], self.arrived.at[0, half:], place.of(place.x)
        )
        self.x_high.start()
        self.sum_cores(2)
        self.y_low = self.make(
            7, self.own.at[2, :half], self.arrived.at[1, :half], place.of(place.y)
        )
        self.y_low.start()

    def send_relayed(self):
        half, place = self.rows // 2, self.place
        self.far_low.wait_recv()
        self.add(self.own, 1, self.relay, 0, 0, half)
        self.x_low = self.make(
            8, self.own.at[1, :half], self.arrived.at[0, :half], place.of(place.x)
        )
        self.x_low.start()
        self.far_high.wait_recv()
        self.add(self.own, 2, self.relay, 1, half, self.rows, shift=half)
        self.y_high = self.make(
            9, self.own.at[2, half:], self.arrived.at[1, half:], place.of(place.y)
        )
        self.y_high.start()
        self.sum_cores(3)

    def wait_half(self, upper):
        if upper:
            self.x_high.wait_recv()
            self.y_high.wait_recv()
        else:
            self.x_low.wait_recv()
            self.y_low.wait_recv()

    def total(self, here):
        return (
            self.own[3, here].astype(wide)
            + self.arrived[0, here].astype(wide)
            + self.arrived[1, here].astype(wide)
        )

    def finish(self):
        for copy in self.swaps + [
            self.far_low, self.far_high, self.x_high, self.y_low, self.x_low, self.y_high,
        ]:
            copy.wait_send()


class ShareRows:
    @staticmethod
    def scratch():
        return [
            pltpu.SemaphoreType.DMA((1,)),
            pltpu.SemaphoreType.DMA((11,)),
            pltpu.SemaphoreType.DMA((11,)),
        ]

    def __init__(self, place, source, target, scratch):
        self.place, self.source, self.target = place, source, target
        self.local_sem, send, receive = scratch
        self.make = sender((send, receive))
        self.rows = target.shape[2]
        self.copies = {}

    def put(self, index, source, target, device):
        copy = self.make(index, source, target, device)
        copy.start()
        self.copies[index] = copy

    def begin_half(self, upper):
        place, half = self.place, self.rows // 2
        rows = pl.ds(half, half) if upper else pl.ds(0, half)
        source, target = self.source.at[rows], self.target.at[0, place.mate, rows]
        if upper:
            self.put(0, source, target, place.of(place.y))
            self.put(1, source, target, place.of(place.x))
        else:
            self.put(2, source, target, place.of(place.x))
            self.put(3, source, target, place.of(place.y))

    def begin_rest(self):
        place = self.place
        self.local = pltpu.make_async_copy(
            self.source, self.target.at[0, place.mate], self.local_sem.at[0]
        )
        self.local.start()
        self.put(6, self.source, self.target.at[1, place.mate], place.sibling)

    def forward(self):
        place, half = self.place, self.rows // 2
        self.copies[2].wait_recv()
        piece = self.target.at[0, place.x, :half]
        self.put(4, piece, piece, place.of(place.y))
        self.copies[0].wait_recv()
        piece = self.target.at[0, place.y, half:]
        self.put(5, piece, piece, place.of(place.x))
        self.copies[1].wait_recv()
        self.put(7, self.target.at[0, place.x], self.target.at[1, place.x], place.sibling)
        self.copies[3].wait_recv()
        self.put(8, self.target.at[0, place.y], self.target.at[1, place.y], place.sibling)

    def forward_far(self):
        place, half = self.place, self.rows // 2
        self.copies[4].wait_recv()
        piece = self.target.at[0, place.far, :half]
        self.put(9, piece, self.target.at[1, place.far, :half], place.sibling)
        self.copies[5].wait_recv()
        piece = self.target.at[0, place.far, half:]
        self.put(10, piece, self.target.at[1, place.far, half:], place.sibling)

    def finish(self):
        self.local.wait()
        for index in range(6, 11):
            self.copies[index].wait_recv()
        for copy in self.copies.values():
            copy.wait_send()


class GatherLines:
    @staticmethod
    def scratch(lines):
        return [
            pltpu.SemaphoreType.DMA((1,)),
            pltpu.SemaphoreType.DMA((3,)),
            pltpu.SemaphoreType.DMA((3,)),
            pltpu.SemaphoreType.DMA((lines, MATES)),
            pltpu.SemaphoreType.DMA((lines, MATES)),
            pltpu.SemaphoreType.DMA((lines, MATES)),
        ]

    def __init__(self, place, blocks, target, scratch):
        self.place, self.blocks, self.target = place, blocks, target
        self.lines = target.shape[0]
        self.local_sem, send, receive, self.up_sem, self.down_sem, self.got = scratch
        self.make = sender((send, receive))
        self.order = [place.mate, place.x, place.y, place.far]

    def begin(self):
        place = self.place
        here = self.target.at[place.line, place.mate]
        self.copies = [
            pltpu.make_async_copy(self.blocks.at[place.mate], here, self.local_sem.at[0])
        ]
        for index, mate in enumerate(self.order[1:]):
            self.copies.append(self.make(index, self.blocks.at[mate], here, place.of(mate)))
        for copy in self.copies:
            copy.start()

    def hop(self, step, mate, direction):
        place = self.place
        line = place.line - step * direction
        piece = self.target.at[line, mate]
        sems = self.up_sem if direction > 0 else self.down_sem
        copy = pltpu.make_async_remote_copy(
            src_ref=piece,
            dst_ref=piece,
            send_sem=sems.at[step, mate],
            recv_sem=self.got.at[line, mate],
            device_id=place.lines_away(direction),
            device_id_type=MESH,
        )
        came = (line >= 0) & (line < self.lines)
        goes = (place.line < self.lines - 1) if direction > 0 else (place.line > 0)
        return copy, came, goes

    def leave(self):
        for slot, mate in enumerate(self.order):
            if slot == 0:
                self.copies[0].wait()
            else:
                self.copies[slot].wait_recv()
            for direction in (1, -1):
                copy, _, goes = self.hop(0, mate, direction)
                pl.when(goes)(copy.start)

    def onwards(self, step):
        for mate in self.order:
            for direction in (1, -1):
                copy, came, goes = self.hop(step, mate, direction)
                pl.when(came)(copy.wait_recv)
                if step < self.lines - 1:
                    pl.when(came & goes)(copy.start)

    def finish(self):
        for copy in self.copies[1:]:
            copy.wait_send()
        for step in range(self.lines - 1):
            for mate in self.order:
                for direction in (1, -1):
                    copy, came, goes = self.hop(step, mate, direction)
                    pl.when(came & goes)(copy.wait_send)


class SumLines:
    @staticmethod
    def scratch(lines, shape):
        return [
            pltpu.VMEM((lines,) + shape, low),
            pltpu.VMEM((2, max(lines - 1, 1)) + shape, low),
            pltpu.SemaphoreType.DMA((lines + 1,)),
            pltpu.SemaphoreType.DMA((2, lines)),
            pltpu.SemaphoreType.DMA((2, lines)),
            pltpu.SemaphoreType.DMA((3,)),
            pltpu.SemaphoreType.DMA((3,)),
        ]

    def __init__(self, place, blocks, result, scratch):
        self.place, self.blocks, self.result = place, blocks, result
        self.held, self.came, self.local_sems, self.send, self.got, send, receive = scratch
        self.lines = self.held.shape[0]
        self.make = sender((send, receive))

    def begin(self):
        self.loads = [
            pltpu.make_async_copy(self.blocks.at[line], self.held.at[line], self.local_sems.at[line])
            for line in range(self.lines)
        ]
        for load in self.loads:
            load.start()

    def wait_loads(self):
        for load in self.loads:
            load.wait()

    def put_gains(self, gains):
        lines, mates, height, lanes = self.held.shape
        top = lax.broadcasted_iota(jnp.int32, (height, lanes), 0) == 0
        for line in range(lines):
            for mate in range(mates):
                first = (line * mates + mate) * lanes
                part = jnp.broadcast_to(gains[:, first : first + lanes], (height, lanes))
                self.held[line, mate] = jnp.where(
                    top, part, self.held[line, mate].astype(wide)
                ).astype(low)

    def copy(self, turn, way):
        direction = 1 - 2 * way
        line = self.place.line + direction * (self.lines - turn)
        return line, pltpu.make_async_remote_copy(
            src_ref=self.held.at[line],
            dst_ref=self.came.at[way, turn - 1],
            send_sem=self.send.at[way, turn],
            recv_sem=self.got.at[way, turn],
            device_id=self.place.lines_away(direction),
            device_id_type=MESH,
        )

    def arrival(self, turn, way):
        slot = self.came.at[way, turn - 1]
        return pltpu.make_async_remote_copy(
            src_ref=slot,
            dst_ref=slot,
            send_sem=self.send.at[way, turn],
            recv_sem=self.got.at[way, turn],
            device_id=self.place.sibling,
            device_id_type=MESH,
        )

    def sends(self, turn, way):
        line = self.place.line
        return line <= turn - 1 if way == 0 else line >= self.lines - turn

    def inner(self, way):
        return self.place.line >= 1 if way == 0 else self.place.line <= self.lines - 2

    def add(self, line, way, turn):
        for mate in range(self.held.shape[1]):

            def body(here, mate=mate):
                self.held[line, mate, here] = (
                    self.held[line, mate, here].astype(wide)
                    + self.came[way, turn - 1, mate, here].astype(wide)
                ).astype(low)

            row_steps(0, self.held.shape[2], body)

    def round(self, turn):
        for way in (0, 1):
            line, copy = self.copy(turn, way)

            @pl.when(self.sends(turn, way))
            def _(line=line, copy=copy, way=way):
                if turn > 1:
                    before = self.arrival(turn - 1, way)

                    @pl.when(self.inner(way))
                    def _():
                        before.wait_recv()
                        self.add(line, way, turn - 1)

                copy.start()

    def exchange(self):
        place, line = self.place, self.place.line
        for way in (0, 1):
            if self.lines > 1:
                last = self.arrival(self.lines - 1, way)

                @pl.when(self.inner(way))
                def _(way=way, last=last):
                    last.wait_recv()
                    self.add(line, way, self.lines - 1)

        self.copies = []
        for index, mate in enumerate((place.x, place.y, place.far)):
            copy = self.make(
                index, self.held.at[line, mate], self.result.at[place.mate], place.of(mate)
            )
            copy.start()
            self.copies.append(copy)
        self.local = pltpu.make_async_copy(
            self.held.at[line, place.mate],
            self.result.at[place.mate],
            self.local_sems.at[self.lines],
        )
        self.local.start()

    def finish(self):
        self.local.wait()
        for copy in self.copies:
            copy.wait()
        for turn in range(1, self.lines):
            for way in (0, 1):
                _, copy = self.copy(turn, way)
                pl.when(self.sends(turn, way))(copy.wait_send)


def remote_call(body, identity, ins, outs, scratch):
    anywhere = pl.BlockSpec(memory_space=pl.ANY)
    held = pl.BlockSpec(memory_space=pltpu.VMEM)
    return pl.pallas_call(
        body,
        in_specs=[anywhere if kind == "any" else held for _, kind in ins],
        out_specs=[anywhere if kind == "any" else held for _, _, kind in outs],
        out_shape=[jax.ShapeDtypeStruct(shape, dtype) for shape, dtype, _ in outs],
        scratch_shapes=scratch,
        compiler_params=pltpu.CompilerParams(
            vmem_limit_bytes=VMEM_BYTES, collective_id=identity, has_side_effects=True
        ),
    )(*[array for array, _ in ins])


def inverse_rms(value):
    return lax.rsqrt(jnp.mean(value * value, axis=1, keepdims=True) + epsilon)


def middle_kernel(partial, input_ref, scale_ref, middle_ref, shared, normed, *scratch):
    place = Place()
    meet(place)
    rows = SumRows(place, partial, scratch[:7])
    share = ShareRows(place, normed, shared, scratch[7:])
    half = normed.shape[0] // 2
    rows.begin()
    rows.send_far()
    rows.send_near()
    rows.send_relayed()

    def body(here):
        middle = input_ref[here].astype(wide) + rows.total(here)
        middle_ref[here] = middle
        normed[here] = (middle * inverse_rms(middle) * scale_ref[...]).astype(low)

    rows.wait_half(False)
    row_steps(0, half, body)
    share.begin_half(False)
    rows.wait_half(True)
    row_steps(half, 2 * half, body)
    share.begin_half(True)
    share.begin_rest()
    rows.finish()
    share.forward()
    share.forward_far()
    share.finish()


def norm_back_rows(grad, source, scale):
    inverse = inverse_rms(source)
    scaled = grad * scale
    unit = source * inverse
    inner = jnp.mean(scaled * source, axis=1, keepdims=True)
    return inverse * (scaled - unit * (inverse * inner)), grad * unit


def turn_rows_kernel(
    partial, middle_ref, grad_ref, scale_ref, middle_grad_ref, gain_ref, shared, low_grad, *scratch
):
    place = Place()
    meet(place)
    rows = SumRows(place, partial, scratch[:7])
    share = ShareRows(place, low_grad, shared, scratch[7:])
    half = low_grad.shape[0] // 2
    rows.begin()
    gain_ref[...] = jnp.zeros_like(gain_ref)
    rows.send_far()
    rows.send_near()
    rows.send_relayed()

    def body(here):
        part, gains = norm_back_rows(rows.total(here), middle_ref[here], scale_ref[...])
        total = grad_ref[here].astype(wide) + part
        middle_grad_ref[here] = total
        low_grad[here] = total.astype(low)
        gain_ref[...] += jnp.sum(gains, axis=0, keepdims=True)

    rows.wait_half(False)
    row_steps(0, half, body)
    share.begin_half(False)
    rows.wait_half(True)
    row_steps(half, 2 * half, body)
    share.begin_half(True)
    share.begin_rest()
    rows.finish()
    share.forward()
    share.forward_far()
    share.finish()


def last_rows_kernel(
    lines, pieces, partial, mlp_partial, input_ref, middle_ref, middle_grad_ref, scale_ref, *rest
):
    place = Place()
    blocks, rest = rest[:pieces], rest[pieces:]
    input_grad, block_output, gain_ref = rest[:3]
    results, scratch = rest[3 : 3 + pieces], rest[3 + pieces :]
    low_grad, low_output = scratch[:2]
    meet(place, far=bool(pieces), lines=lines if pieces else 0)
    rows = SumRows(place, partial, scratch[2:9])
    outs = SumRows(place, mlp_partial, scratch[9:16])
    make = sender(scratch[16:18])
    local_sems = scratch[18]
    sums = [
        SumLines(place, blocks[index], results[index], scratch[19 + 7 * index : 26 + 7 * index])
        for index in range(pieces)
    ]
    whole = low_grad.shape[0]
    for each in sums:
        each.begin()
    rows.begin()
    outs.begin()
    for each in sums:
        each.wait_loads()
    for each in sums[1:]:
        if lines > 1:
            each.round(1)
    gain_ref[...] = jnp.zeros_like(gain_ref)
    rows.send_far()
    rows.send_near()
    outs.send_far()
    rows.send_relayed()
    outs.send_near()
    for each in sums[1:]:
        if lines > 2:
            each.round(2)
    outs.send_relayed()
    rows.wait_half(False)
    rows.wait_half(True)

    def body(here):
        part, gains = norm_back_rows(
            rows.total(here), input_ref[here].astype(wide), scale_ref[...]
        )
        low_grad[here] = (middle_grad_ref[here] + part).astype(low)
        gain_ref[...] += jnp.sum(gains, axis=0, keepdims=True)

    row_steps(0, whole, body)
    if sums:
        sums[0].put_gains(gain_ref)
        for turn in range(1, lines):
            sums[0].round(turn)
    first = make(0, low_grad, input_grad.at[place.core], place.sibling)
    first.start()
    first_local = pltpu.make_async_copy(low_grad, input_grad.at[place.core], local_sems.at[0])
    first_local.start()
    for turn in range(3, lines):
        for each in sums[1:]:
            each.round(turn)
    outs.wait_half(False)
    outs.wait_half(True)

    def out_body(here):
        low_output[here] = (middle_ref[here] + outs.total(here)).astype(low)

    row_steps(0, whole, out_body)
    second = make(1, low_output, block_output.at[place.core], place.sibling)
    second.start()
    second_local = pltpu.make_async_copy(low_output, block_output.at[place.core], local_sems.at[1])
    second_local.start()
    for each in sums:
        each.exchange()
    rows.finish()
    outs.finish()
    first_local.wait()
    second_local.wait()
    first.wait()
    second.wait()
    for each in sums:
        each.finish()


def first_rows_kernel(lines, pieces, input_ref, grad_ref, *rest):
    place = Place()
    ins, rest = rest[:pieces], rest[pieces:]
    inputs, grads = rest[:2]
    outs, scratch = rest[2 : 2 + pieces], rest[2 + pieces :]
    meet(place, far=bool(pieces), lines=lines if pieces else 0)
    share = ShareRows(place, input_ref.at[place.core], inputs, scratch[:3])
    other = ShareRows(place, grad_ref.at[place.core], grads, scratch[3:6])
    gathers = [
        GatherLines(place, ins[index], outs[index], scratch[6 + 6 * index : 12 + 6 * index])
        for index in range(pieces)
    ]
    for gather in gathers:
        gather.begin()
    for each in (share, other):
        each.begin_half(False)
        each.begin_half(True)
        each.begin_rest()
    for gather in gathers:
        gather.leave()
    share.forward()
    for gather in gathers:
        if lines > 1:
            gather.onwards(1)
    share.forward_far()
    other.forward()
    for step in range(2, lines):
        for gather in gathers:
            gather.onwards(step)
    other.forward_far()
    share.finish()
    other.finish()
    for gather in gathers:
        gather.finish()


def first_rows(block_input, out_grad, blocks, lines):
    seqs, rows, columns = block_input.shape
    shape = (seqs, MATES, rows, columns)
    return remote_call(
        functools.partial(first_rows_kernel, lines, len(blocks)),
        0,
        [(array, "any") for array in (block_input, out_grad, *blocks)],
        [(shape, low, "any"), (shape, low, "any")]
        + [((lines,) + block.shape, low, "any") for block in blocks],
        ShareRows.scratch() + ShareRows.scratch() + GatherLines.scratch(lines) * len(blocks),
    )


def middle_rows(partial, mine, scale):
    seqs, _, rows, columns = partial.shape
    return remote_call(
        middle_kernel,
        1,
        [(partial, "any"), (mine, "held"), (scale, "held")],
        [((rows, columns), wide, "held"), (partial.shape, low, "any")],
        [pltpu.VMEM((rows, columns), low)] + SumRows.scratch(rows, columns) + ShareRows.scratch(),
    )


def turn_rows(partial, middle, grad, scale):
    seqs, _, rows, columns = partial.shape
    return remote_call(
        turn_rows_kernel,
        2,
        [(partial, "any"), (middle, "held"), (grad, "held"), (scale, "held")],
        [
            ((rows, columns), wide, "held"),
            ((1, columns), wide, "held"),
            (partial.shape, low, "any"),
        ],
        [pltpu.VMEM((rows, columns), low)] + SumRows.scratch(rows, columns) + ShareRows.scratch(),
    )


def last_rows(partial, mlp_partial, mine, middle, middle_grad, scale, blocks, lines):
    seqs, _, rows, columns = partial.shape
    scratch = (
        [pltpu.VMEM((rows, columns), low), pltpu.VMEM((rows, columns), low)]
        + SumRows.scratch(rows, columns)
        + SumRows.scratch(rows, columns)
        + [pltpu.SemaphoreType.DMA((2,))] * 3
    )
    for block in blocks:
        scratch += SumLines.scratch(lines, block.shape[1:])
    return remote_call(
        functools.partial(last_rows_kernel, lines, len(blocks)),
        3,
        [(partial, "any"), (mlp_partial, "any")]
        + [(array, "held") for array in (mine, middle, middle_grad, scale)]
        + [(block, "any") for block in blocks],
        [
            ((seqs, rows, columns), low, "any"),
            ((seqs, rows, columns), low, "any"),
            ((1, columns), wide, "held"),
        ]
        + [(block.shape[1:], low, "any") for block in blocks],
        scratch,
    )


def cut_columns(weight):
    depth, columns = weight.shape
    return weight.reshape(depth, MATES, columns // MATES).transpose(1, 0, 2)


def join_columns(blocks):
    return blocks.transpose(1, 0, 2).reshape(blocks.shape[1], -1)


def gather_weights(blocks):
    return gather_lines(swap_blocks(blocks))


def scatter_grads(blocks):
    return swap_blocks(scatter_lines(blocks.astype(low)).astype(low)).astype(wide)


def on_device(
    block_input,
    lengths,
    attn_gain,
    query_weight,
    key_weight,
    value_weight,
    outgate_weight,
    beta_weight,
    conv_kernel,
    head_gain,
    output_weight,
    mlp_gain,
    swish_weight,
    upward_weight,
    downward_weight,
    out_grad,
):
    count = lax.axis_size("seq")
    lines = count // MATES
    core = lax.axis_index("tp")
    seq_count, tokens, model_width = block_input.shape
    depth = attn_gain.shape[0]
    gain_part = head_gain.shape[0]
    head_size = gain_part * count
    heads = beta_weight.shape[1] // MATES
    width = heads * head_size
    units = swish_weight.shape[1] // MATES

    near = lines <= 4 and depth % 128 == 0
    rows = seq_count * MATES * tokens
    span = MATES * tokens

    small_cut = jnp.concatenate(
        [
            jnp.broadcast_to(
                jnp.concatenate([attn_gain, mlp_gain, head_gain]).astype(low)[None],
                (MATES, 2 * depth + gain_part),
            ),
            conv_kernel.astype(low).reshape(MATES, -1),
        ],
        axis=1,
    )
    sizes = (depth, depth, gain_part, heads * 3 * CONV * gain_part)
    starts = [sum(sizes[:index]) for index in range(len(sizes) + 1)]
    small_cut = jnp.pad(small_cut, ((0, 0), (0, SMALL * 128 - starts[-1])))
    small_cut = small_cut.reshape(MATES, SMALL, 128)
    streams_cut = jnp.stack(
        [
            w.astype(low).reshape(depth, MATES, heads, head_size)
            for w in (query_weight, key_weight, value_weight)
        ],
        axis=3,
    )
    streams_cut = streams_cut.transpose(1, 0, 2, 3, 4).reshape(MATES, depth, 3 * width)
    beta_cut = jnp.pad(
        cut_columns(beta_weight.astype(low)), ((0, 0), (0, 0), (0, head_size - heads))
    )
    attn_cut = jnp.concatenate(
        [streams_cut, cut_columns(outgate_weight.astype(low)), beta_cut], axis=2
    )
    output_cut = cut_columns(output_weight.astype(low).T)
    cuts = (small_cut, attn_cut, output_cut)
    if near:
        input_rows, grad_rows, *gathered = first_rows(block_input, out_grad, cuts, lines)
    else:
        input_rows, grad_rows = first_rows(block_input, out_grad, (), lines)
        gathered = [gather_weights(cut) for cut in cuts]
    small, attn_full, output_full = gathered
    attn_full = attn_full.reshape(model_width, (4 * heads + 1) * head_size)
    output_full = output_full.reshape(model_width, width)
    input_rows = input_rows.reshape(rows, model_width)
    grad_rows = grad_rows.reshape(rows, model_width)
    mlp_cut = jnp.concatenate(
        [cut_columns(w.astype(low)) for w in (swish_weight, upward_weight, downward_weight.T)],
        axis=2,
    )
    mlp_full = gather_weights(row_major(mlp_cut)).reshape(model_width, 3 * units)
    ups_full, downward_full = mlp_full[:, : 2 * units], mlp_full[:, 2 * units :]
    small = small.reshape(count, SMALL * 128)
    attn_small, mlp_small, head_small, conv_small = (
        small[:, starts[index] : starts[index + 1]] for index in range(len(sizes))
    )
    taps = (
        conv_small.reshape(count, heads, 3, CONV, gain_part)
        .transpose(1, 2, 3, 0, 4)
        .reshape(heads, 3 * CONV, head_size)
        .astype(wide)
    )
    attn_scale = attn_small.reshape(1, model_width).astype(wide)
    mlp_scale = mlp_small.reshape(1, model_width).astype(wide)
    head_scale = head_small.reshape(1, head_size).astype(wide)

    mine_low = pick(block_input, core)
    grad_mine = pick(out_grad, core)
    blocked = (seq_count, MATES, tokens, model_width)
    input_wide = input_rows.astype(wide)
    flat_normed = (input_wide * rms_scale(input_wide) * attn_scale).astype(low)
    lengths_here = jnp.stack([pick(lengths, core), pick(lengths, 1 - core)])
    limit = lengths_here - line_of() * span

    streams_end, gates_end = 3 * width, 4 * width
    raw = matmul("rd,dc->rc", flat_normed, attn_full[:, :gates_end]).astype(low)
    tails = along(raw.reshape(seq_count, span, gates_end)[:, span - 16 :, :streams_end], 1)
    logits = matmul("rd,dc->rc", flat_normed, attn_full[:, gates_end:])
    sizes_of = (seq_count, heads, span)
    qkv, solved, wu, maps, prefix, local, ends = delta_prepare(
        limit, raw, tails, taps, logits, *sizes_of
    )
    map_matrix, map_offset = ends[:, :, :head_size], ends[:, :, head_size:]
    entering = hop_states(map_matrix, map_offset, 1)
    state, fresh, mixed, gated = delta_mix(
        qkv, wu, prefix, local, entering, raw, head_scale, *sizes_of
    )
    attn_part = matmul("rc,dc->rd", gated, output_full).astype(low)
    middle, mlp_normed = middle_rows(attn_part.reshape(blocked), mine_low, mlp_scale)
    mlp_normed = mlp_normed.reshape(rows, model_width)
    acts = matmul("rd,df->rf", mlp_normed, ups_full)
    gate_act, up_act = acts[:, :units], acts[:, units:]
    silu_act = jax.nn.silu(gate_act)
    hidden = (silu_act * up_act).astype(low)
    mlp_part = matmul("rf,df->rd", hidden, downward_full).astype(low)

    hidden_grad = matmul("rd,df->rf", grad_rows, downward_full)
    downward_grad = matmul("rd,rf->df", grad_rows, hidden).astype(low)
    acts_grad = jnp.concatenate(
        [
            (hidden_grad * up_act * silu_slope(gate_act)).astype(low),
            (hidden_grad * silu_act).astype(low),
        ],
        axis=1,
    )
    ups_grad = matmul("rd,rf->df", mlp_normed, acts_grad).astype(low)
    normed_two_part = matmul("rf,df->rd", acts_grad, ups_full).astype(low)
    middle_grad, mlp_gain_grad, attn_grad_rows = turn_rows(
        normed_two_part.reshape(blocked), middle, grad_mine, mlp_scale
    )
    attn_grad_rows = attn_grad_rows.reshape(rows, model_width)
    output_grad = matmul("rd,rc->dc", attn_grad_rows, gated).astype(low)
    gated_grad = matmul("rd,dc->rc", attn_grad_rows, output_full)
    out_grads, fresh_grad, all_grads, head_gain_parts, sources, local_state = delta_turn(
        gated_grad, mixed, raw, head_scale, qkv, wu, maps, *sizes_of
    )
    leaving_grad = hop_states_back(map_matrix, local_state)
    all_grads, edge, halo, taps_grad, logit_grad = delta_unwind(
        limit, raw, tails, taps, logits, qkv, solved, wu, state, fresh, out_grads, fresh_grad,
        maps, sources, leaving_grad, all_grads, *sizes_of,
    )
    returned = along(halo.astype(low), -1)
    edge = (edge + returned.astype(wide)).astype(low)
    all_grads = all_grads.at[:, gates_end:].set(logit_grad)
    for seq in range(seq_count):
        first = (seq + 1) * span
        all_grads = all_grads.at[first - 16 : first, :streams_end].set(edge[seq])
    normed_part = matmul("rc,dc->rd", all_grads, attn_full).astype(low)
    attn_grads = matmul("rd,rc->dc", flat_normed, all_grads).astype(low)

    def cut_rows(grad):
        return grad.reshape(lines, MATES, depth, grad.shape[1])

    mlp_sum = scatter_grads(row_major(cut_rows(jnp.concatenate([ups_grad, downward_grad], axis=1))))
    conv_grad = (
        taps_grad[:, :CONV]
        .reshape(seq_count, heads, CONV, 3, count, gain_part)
        .sum(axis=0)
        .transpose(3, 0, 2, 1, 4)
        .reshape(count, -1)
    )

    def small_blocks(attn_gain_grad):
        parts = [
            attn_gain_grad.reshape(count, depth),
            mlp_gain_grad.reshape(count, depth),
            jnp.sum(head_gain_parts[:, 0], axis=0).reshape(count, gain_part),
            conv_grad,
        ]
        flat = jnp.concatenate(parts, axis=1).astype(low)
        flat = jnp.pad(flat, ((0, 0), (0, SMALL * 128 - starts[-1])))
        return flat.reshape(lines, MATES, SMALL, 128)

    last_ins = (
        normed_part.reshape(blocked),
        mlp_part.reshape(blocked),
        mine_low,
        middle,
        middle_grad,
        attn_scale,
    )
    if near:
        blocks = (
            small_blocks(jnp.zeros((1, model_width), wide)),
            cut_rows(attn_grads),
            cut_rows(output_grad),
        )
        input_grad, block_output, _, small_sum, attn_sum, output_sum = last_rows(
            *last_ins, blocks, lines
        )
        attn_sum, output_sum, small_sum = (
            v.astype(wide) for v in (attn_sum, output_sum, small_sum)
        )
    else:
        input_grad, block_output, attn_gain_grad = last_rows(*last_ins, (), lines)
        small_sum, attn_sum, output_sum = (
            scatter_grads(block)
            for block in (
                small_blocks(attn_gain_grad), cut_rows(attn_grads), cut_rows(output_grad)
            )
        )
    small_sum = small_sum.reshape(MATES, SMALL * 128)
    gains_sum = jnp.sum(small_sum[:, : starts[3]], axis=0)
    gains_sum = gains_sum + other_core(gains_sum)
    conv_sum = small_sum[:, starts[3] : starts[4]]
    streams_sum = (
        attn_sum[:, :, :streams_end]
        .reshape(MATES, depth, heads, 3, head_size)
        .transpose(3, 1, 0, 2, 4)
        .reshape(3, depth, MATES * width)
    )
    return (
        block_output,
        input_grad,
        gains_sum[:depth],
        streams_sum[0],
        streams_sum[1],
        streams_sum[2],
        join_columns(attn_sum[:, :, streams_end:gates_end]),
        join_columns(attn_sum[:, :, gates_end : gates_end + heads]),
        conv_sum.reshape(MATES * heads, 3, CONV, gain_part),
        gains_sum[2 * depth :],
        join_columns(output_sum).T,
        gains_sum[depth : 2 * depth],
        join_columns(mlp_sum[:, :, :units]),
        join_columns(mlp_sum[:, :, units : 2 * units]),
        join_columns(mlp_sum[:, :, 2 * units :]).T,
    )


def solution(mesh):
    return jax.shard_map(
        on_device,
        mesh=mesh,
        in_specs=(
            P(None, "seq", None),
            P(),
            P("seq"),
            P("seq", "tp"),
            P("seq", "tp"),
            P("seq", "tp"),
            P("seq", "tp"),
            P("seq", "tp"),
            P("tp", None, None, "seq"),
            P("seq"),
            P("tp", "seq"),
            P("seq"),
            P("seq", "tp"),
            P("seq", "tp"),
            P("tp", "seq"),
            P(None, "seq", None),
        ),
        out_specs=(
            P(None, "seq", None),
            P(None, "seq", None),
            P("seq"),
            P("seq", "tp"),
            P("seq", "tp"),
            P("seq", "tp"),
            P("seq", "tp"),
            P("seq", "tp"),
            P("tp", None, None, "seq"),
            P("seq"),
            P("tp", "seq"),
            P("seq"),
            P("seq", "tp"),
            P("seq", "tp"),
            P("tp", "seq"),
        ),
        check_vma=False,
    )
```

```python
import functools

import jax
import jax.numpy as jnp
from jax import lax
from jax.experimental import pallas as pl
from jax.experimental.pallas import tpu as pltpu
from jax.sharding import PartitionSpec as P

CONV = 4
MATES = 4
SMALL = 16


epsilon = 1e-06
low = jnp.bfloat16
wide = jnp.float32


def other_core(value):
    return lax.ppermute(value, "tp", [(0, 1), (1, 0)])


def to_mate(value, flip):
    count = lax.axis_size("seq")
    return lax.ppermute(value, "seq", [(source, source ^ flip) for source in range(count)])


def mate_of():
    return lax.axis_index("seq") % MATES


def line_of():
    return lax.axis_index("seq") // MATES


def line_groups():
    lines = lax.axis_size("seq") // MATES
    return [[mate + MATES * line for line in range(lines)] for mate in range(MATES)]


def pick(blocks, index):
    return lax.dynamic_index_in_dim(blocks, index, 0, False)


def in_order(by_flip):
    mate = mate_of()
    out = jnp.zeros((MATES,) + by_flip[0].shape, by_flip[0].dtype)
    for flip, piece in enumerate(by_flip):
        out = lax.dynamic_update_index_in_dim(out, piece, mate ^ flip, 0)
    return out


def swap_blocks(blocks):
    mate = mate_of()
    pieces = [pick(blocks, mate)]
    for flip in range(1, MATES):
        pieces.append(to_mate(pick(blocks, mate ^ flip), flip))
    return in_order(pieces)


def gather_lines(block):
    return lax.all_gather(block, "seq", axis_index_groups=line_groups())


def scatter_lines(blocks):
    return lax.psum_scatter(blocks, "seq", scatter_dimension=0, axis_index_groups=line_groups())


def matmul(form, left, right):
    return jnp.einsum(form, left, right, preferred_element_type=wide)


def silu_slope(value):
    squash = jax.nn.sigmoid(value)
    return squash * (1.0 + value * (1.0 - squash))


CHUNK = 128
TOGETHER = 4
VMEM_BYTES = 58 * 1024 * 1024
NN = (((1,), (0,)), ((), ()))
NT = (((1,), (1,)), ((), ()))


def dot(left, right, dims):
    return lax.dot_general(left, right, dims, preferred_element_type=wide)


def pair(value):
    high = value.astype(low)
    return high, (value - high.astype(wide)).astype(low)


def side(left, right):
    return jnp.concatenate([left, right], axis=1)


def over(top, bottom):
    return jnp.concatenate([top, bottom], axis=0)


def nn(left, right):
    width = right[0].shape[1]
    both = side(*right)
    out = dot(side(*left), over(both, both), NN)
    return out[:, :width] + out[:, width:]


def nt(left, right):
    width = right[0].shape[0]
    out = dot(side(*left), over(side(right[0], right[0]), side(right[1], right[1])), NT)
    return out[:, :width] + out[:, width:]


def nn_wide(left, right):
    return dot(side(*left), over(right[0], right[0]), NN) + dot(left[0], right[1], NN)


def nn_low(left, right):
    return dot(side(*left), over(right, right), NN)


def low_nn(left, right):
    return dot(side(left, left), over(*right), NN)


def low_nt(left, right):
    return dot(side(left, left), side(*right), NT)


def grid_of_rows():
    rows = lax.broadcasted_iota(jnp.int32, (CHUNK, CHUNK), 0)
    columns = lax.broadcasted_iota(jnp.int32, (CHUNK, CHUNK), 1)
    return rows, columns


def inverse_of(strict):
    rows, columns = grid_of_rows()
    one = jnp.where(rows == columns, 1.0, 0.0).astype(wide)

    def joining(shift):
        upper = columns >> shift
        return ((rows >> shift) == upper + 1) & ((upper & 1) == 0)

    solved = [one - jnp.where(joining(0), s, 0.0) for s in strict]
    shift = 1
    while (1 << shift) < CHUNK:
        mask = joining(shift)
        pairs = [pair(d) for d in solved]
        crossed = [nn(pair(jnp.where(mask, s, 0.0)), p) for s, p in zip(strict, pairs)]
        solved = [d - nn(p, pair(c)) for d, p, c in zip(solved, pairs, crossed)]
        shift += 1
    return solved


def convolved(block, taps, stream):
    columns = block[:, stream * CHUNK : (stream + 1) * CHUNK]
    total = None
    for offset in range(CONV):
        first = 16 - (CONV - 1) + offset
        term = taps[stream * CONV + offset][None, :] * columns[first : first + CHUNK]
        total = term if total is None else total + term
    return total


def silu_parts(value):
    squash = jax.nn.sigmoid(value)
    return value * squash, squash * (1.0 + value * (1.0 - squash))


def live_rows(limit, start):
    rows = lax.broadcasted_iota(jnp.int32, (CHUNK, CHUNK), 0)
    return jnp.where(rows + start < limit, 1.0, 0.0).astype(wide)


def head_squash(logits, head):
    lanes = lax.broadcasted_iota(jnp.int32, logits.shape, 1)
    column = jnp.sum(jnp.where(lanes == head, logits, 0.0), axis=1, keepdims=True)
    return jax.nn.sigmoid(jnp.broadcast_to(column, logits.shape))


def front_kernel(
    lines, heads, moves, limit_ref, raw_any, raw_ref, taps_ref, logit_ref, gate_ref, scale_ref, grad_any,
    *rest,
):
    count = len(moves)
    outs = rest[count:]
    qkv_ref, solved_ref, wu_ref, map_ref, total_ref, tails_ref = outs[:6]
    state_ref, fresh_ref, mixed_ref, gated_ref, grads = outs[6:11]
    targets, scratch = outs[11 : 11 + count], outs[11 + count :]
    ext, offsets, maps, prefixes, locals_, wus, qkvs, enters, leaves, tails = scratch[:10]
    tail_sems, state_sems = scratch[10:12]
    scratch = scratch[12:]
    step = pl.program_id(0)
    chains, chunks = maps.shape[0], maps.shape[1]
    span = chunks * CHUNK
    head_size = CHUNK
    streams = 3 * heads * head_size
    place = Place()
    share = ShareRows(place, grad_any.at[place.core], grads, scratch[:3])
    gathers = [
        GatherLines(place, None, target, scratch[3 + 6 * index : 9 + 6 * index], moves[index])
        for index, target in enumerate(targets)
    ]
    below, above = place.line > 0, place.line < lines - 1
    rows, columns = grid_of_rows()
    identity = jnp.where(rows == columns, 1.0, 0.0).astype(wide)

    def tail(seq):
        return pltpu.make_async_remote_copy(
            src_ref=raw_any.at[pl.ds((seq + 1) * span - 16, 16), pl.ds(0, streams)],
            dst_ref=tails.at[seq],
            send_sem=tail_sems.at[0, seq],
            recv_sem=tail_sems.at[1, seq],
            device_id=place.lines_away(1),
            device_id_type=MESH,
        )

    state_copy = pltpu.make_async_remote_copy(
        src_ref=leaves,
        dst_ref=enters,
        send_sem=state_sems.at[0],
        recv_sem=state_sems.at[1],
        device_id=place.lines_away(1),
        device_id_type=MESH,
    )
    seqs = chains // heads

    @pl.when(step == 0)
    def _():
        meet(place, lines=lines)
        for seq in range(seqs):
            pl.when(above)(tail(seq).start)
        for gather in gathers:
            gather.leave(False)
        share.begin_half(False)
        share.begin_half(True)
        share.begin_rest()
        for seq in range(seqs):

            @pl.when(below)
            def _(seq=seq):
                tail(seq).wait_recv()

            @pl.when(place.line == 0)
            def _(seq=seq):
                tails[seq] = jnp.zeros(tails.shape[1:], low)

        tails_ref[...] = tails[...]

    def form(chain):
        seq, head = chain // heads, chain % heads
        ext[:16] = tails[seq, :, pl.ds(pl.multiple_of(head * 3 * head_size, 128), 3 * head_size)].astype(wide)
        ext[16:] = raw_ref[...].astype(wide)
        taps = taps_ref[0]
        limit = limit_ref[seq]

        def group(index, carry):
            first = index * TOGETHER
            parts = []
            for number in range(TOGETHER):
                start = pl.multiple_of((first + number) * CHUNK, CHUNK)
                block = ext[pl.ds(start, CHUNK + 16)]
                query = jax.nn.silu(convolved(block, taps, 0))
                key = jax.nn.silu(convolved(block, taps, 1))
                value = jax.nn.silu(convolved(block, taps, 2)).astype(low)
                query = query * lax.rsqrt(jnp.sum(query * query, axis=1, keepdims=True) + epsilon)
                query = (query * head_size ** (-0.5)).astype(low)
                key = key * lax.rsqrt(jnp.sum(key * key, axis=1, keepdims=True) + epsilon)
                key = key.astype(low)
                beta = head_squash(logit_ref[pl.ds(start, CHUNK)], head) * live_rows(limit, start)
                together = jnp.concatenate([query, key, value], axis=1)
                qkv_ref[pl.ds(start, CHUNK)] = together
                qkvs[chain, pl.ds(start, CHUNK)] = together
                parts.append((key, value, beta))
            strict = [
                jnp.where(rows > columns, beta * dot(key, key, NT), 0.0) for key, _, beta in parts
            ]
            solved = inverse_of(strict)
            for number in range(TOGETHER):
                key, value, beta = parts[number]
                solved_ref[0, first + number] = solved[number]
                weighted = pair(solved[number] * beta.T)
                both = nn_low(weighted, side(key, value))
                wu_ref[0, first + number] = both
                wus[chain, first + number] = both
                moved = low_nn(key.T, pair(both))
                step_map = identity - moved[:, :head_size]
                map_ref[0, first + number] = step_map
                maps[chain, first + number] = step_map
                offsets[chain, first + number] = moved[:, head_size:]
            return carry

        lax.fori_loop(0, chunks // TOGETHER, group, 0)

    @pl.when(step < chains)
    def _():
        form(step)

    @pl.when(step == chains - 2)
    def _():
        share.forward()

    @pl.when(step == chains - 1)
    def _():
        start = side(identity, jnp.zeros_like(identity))

        def advance(chunk, states):
            out = []
            for index in range(chains):
                state = states[index]
                prefixes[index, chunk] = state[:, :head_size]
                locals_[index, chunk] = state[:, head_size:]
                moved = nn_wide(pair(maps[index, chunk]), pair(state))
                out.append(
                    side(moved[:, :head_size], moved[:, head_size:] + offsets[index, chunk])
                )
            return tuple(out)

        ends = lax.fori_loop(0, chunks, advance, (start,) * chains)

        @pl.when(below)
        def _():
            state_copy.wait_recv()

        @pl.when(place.line == 0)
        def _():
            enters[...] = jnp.zeros_like(enters)

        for index in range(chains):
            total_ref[index] = ends[index][:, :head_size]
            leaving = nn_low(pair(ends[index][:, :head_size]), enters[index])
            leaves[index] = (leaving + ends[index][:, head_size:]).astype(low)
        pl.when(above)(state_copy.start)
        for gather in gathers:
            gather.onwards(1)
        share.forward_far()

    def outputs(chain):
        enter = enters[chain]
        scale = scale_ref[...]

        def group(index, carry):
            for number in range(TOGETHER):
                chunk = index * TOGETHER + number
                start = pl.multiple_of(chunk * CHUNK, CHUNK)
                here = pl.ds(start, CHUNK)
                state = nn_low(pair(prefixes[chain, chunk]), enter) + locals_[chain, chunk]
                state_ref[0, chunk] = state
                states = pair(state)
                both = wus[chain, chunk]
                fresh = both[:, head_size:] - nn(pair(both[:, :head_size]), states)
                fresh_ref[0, chunk] = fresh
                query = qkvs[chain, here, :head_size]
                key = qkvs[chain, here, head_size : 2 * head_size]
                scores = jnp.where(rows >= columns, dot(query, key, NT), 0.0)
                mixed = low_nn(query, states) + nn(pair(scores), pair(fresh))
                mixed_ref[here] = mixed
                inverse = lax.rsqrt(jnp.mean(mixed * mixed, axis=1, keepdims=True) + epsilon)
                normed = mixed * inverse * scale
                gated_ref[here] = (normed * jax.nn.silu(gate_ref[here].astype(wide))).astype(low)
            return carry

        lax.fori_loop(0, chunks // TOGETHER, group, 0)

    @pl.when(step >= chains)
    def _():
        outputs(step - chains)

    @pl.when(step == 2 * chains - 2)
    def _():
        for gather in gathers:
            gather.onwards(2)

    @pl.when(step == 2 * chains - 1)
    def _():
        for number in range(3, lines):
            for gather in gathers:
                gather.onwards(number)
        for gather in gathers:
            gather.finish_lines()
        share.finish()
        for seq in range(seqs):
            pl.when(above)(tail(seq).wait_send)
        pl.when(above)(state_copy.wait_send)


def back_kernel(
    lines, heads, parts, limit_ref, raw_ref, tails_ref, taps_ref, logit_ref, gate_ref, scale_ref, qkv_ref,
    wu_ref, map_ref, total_ref, grad_ref, mixed_ref, solved_ref, state_ref, fresh_in_ref, *rest,
):
    count = len(parts)
    blocks, rest = rest[:count], rest[count:]
    all_ref, gain_ref, taps_grad_ref = rest[:3]
    results, scratch = rest[3 : 3 + count], rest[3 + count :]
    ext, pre_grads, maps, sources, out_grads, fresh_grads, leaving, leaves, enters = scratch[:9]
    halos, edges, returned, halo_sems, state_sems = scratch[9:14]
    scratch = scratch[14:]
    step = pl.program_id(0)
    chains, chunks = maps.shape[0], maps.shape[1]
    span = chunks * CHUNK
    head_size = CHUNK
    streams = 3 * heads * head_size
    place = Place()
    sums = [
        SumLines(place, blocks[index], results[index], scratch[7 * index : 7 * index + 7], first)
        for index, (first, _) in enumerate(parts)
    ]
    below, above = place.line > 0, place.line < lines - 1
    rows, columns = grid_of_rows()

    def halo(chain):
        return pltpu.make_async_remote_copy(
            src_ref=halos.at[chain],
            dst_ref=returned.at[chain],
            send_sem=halo_sems.at[0, chain],
            recv_sem=halo_sems.at[1, chain],
            device_id=place.lines_away(-1),
            device_id_type=MESH,
        )

    state_copy = pltpu.make_async_remote_copy(
        src_ref=enters,
        dst_ref=leaves,
        send_sem=state_sems.at[0],
        recv_sem=state_sems.at[1],
        device_id=place.lines_away(-1),
        device_id_type=MESH,
    )

    @pl.when(step == 0)
    def _():
        meet(place, far=bool(parts), lines=lines)
        for each in sums:
            each.begin()
        for each in sums:
            each.wait_loads()
            each.round(1)

    def turn(chain):
        scale = scale_ref[...]

        def group(index, gain):
            for number in range(TOGETHER):
                chunk = index * TOGETHER + number
                start = pl.multiple_of(chunk * CHUNK, CHUNK)
                here = pl.ds(start, CHUNK)
                grad, mixed = grad_ref[here], mixed_ref[here]
                silu_gate, slope = silu_parts(gate_ref[here].astype(wide))
                inverse = lax.rsqrt(jnp.mean(mixed * mixed, axis=1, keepdims=True) + epsilon)
                unit = mixed * inverse
                gate_grad = (grad * unit * scale * slope).astype(low)
                there = pl.ds(pl.multiple_of(chain // heads * span + start, CHUNK), CHUNK)
                lanes = pl.ds(pl.multiple_of(streams + chain % heads * head_size, 128), head_size)
                all_ref[there, lanes] = gate_grad
                passed = grad * silu_gate
                gain = gain + jnp.sum(passed * unit, axis=0, keepdims=True)
                scaled = passed * scale
                mixed_grad = inverse * (
                    scaled - unit * inverse * jnp.mean(scaled * mixed, axis=1, keepdims=True)
                )
                out_grads[chain, chunk] = mixed_grad
                query, key = qkv_ref[here, :head_size], qkv_ref[here, head_size : 2 * head_size]
                scores = jnp.where(rows >= columns, dot(query, key, NT), 0.0)
                turned = jnp.where(rows <= columns, dot(key, query, NT), 0.0)
                grads = pair(mixed_grad)
                fresh_grads[chain, chunk] = nn(pair(turned), grads)
                reading = query.astype(wide) - nn(
                    pair(scores), pair(wu_ref[0, chunk, :, :head_size])
                )
                sources[chain, chunk] = nn(pair(mixed_grad.T), pair(reading))
                maps[chain, chunk] = map_ref[0, chunk]
            return gain

        gain = lax.fori_loop(0, chunks // TOGETHER, group, jnp.zeros((1, head_size), wide))
        gain_ref[0] = jnp.broadcast_to(gain, (8, head_size))

    @pl.when(step < chains)
    def _():
        turn(step)

    @pl.when(step == chains - 1)
    def _():
        def advance(number, states):
            chunk = chunks - 1 - number
            return tuple(
                nn(pair(states[index]), pair(maps[index, chunk])) + sources[index, chunk]
                for index in range(chains)
            )

        ends = lax.fori_loop(
            0, chunks, advance, (jnp.zeros((head_size, head_size), wide),) * chains
        )

        @pl.when(above)
        def _():
            state_copy.wait_recv()

        @pl.when(place.line == lines - 1)
        def _():
            leaves[...] = jnp.zeros_like(leaves)

        for index in range(chains):
            entering = low_nn(leaves[index], pair(total_ref[index]))
            enters[index] = (entering + ends[index]).astype(low)
        pl.when(below)(state_copy.start)

        def again(number, states):
            chunk = chunks - 1 - number
            out = []
            for index in range(chains):
                leaving[index, chunk] = states[index]
                out.append(
                    nn(pair(states[index]), pair(maps[index, chunk])) + sources[index, chunk]
                )
            return tuple(out)

        lax.fori_loop(
            0, chunks, again, tuple(leaves[index].astype(wide) for index in range(chains))
        )
        for each in sums:
            each.round(2)

    def unwind(chain):
        seq, head = chain // heads, chain % heads
        ext[:16] = tails_ref[seq, :, pl.ds(pl.multiple_of(head * 3 * head_size, 128), 3 * head_size)].astype(wide)
        ext[16:] = raw_ref[...].astype(wide)
        taps = taps_ref[0]
        limit = limit_ref[seq]
        pre_grads[:16] = jnp.zeros((16, 3 * head_size), wide)
        pre_grads[span + 16 :] = jnp.zeros((16, 3 * head_size), wide)

        def one(chunk):
            start = pl.multiple_of(chunk * CHUNK, CHUNK)
            here = pl.ds(start, CHUNK)
            query = qkv_ref[here, :head_size]
            key = qkv_ref[here, head_size : 2 * head_size]
            value = qkv_ref[here, 2 * head_size :]
            live = live_rows(limit, start)
            squash = head_squash(logit_ref[here], head)
            beta = squash * live
            grads = pair(out_grads[chain, chunk])
            fresh = pair(fresh_in_ref[0, chunk])
            state = pair(state_ref[0, chunk])
            leave = pair(leaving[chain, chunk])
            both = wu_ref[0, chunk]
            fresh_grad = fresh_grads[chain, chunk] + low_nt(key, leave)
            fresh_pair = pair(fresh_grad)
            score_grad = jnp.where(rows >= columns, nt(grads, fresh), 0.0)
            turned_grad = jnp.where(rows <= columns, nt(fresh, grads), 0.0)
            query_grad = nt(grads, state) + nn_low(pair(score_grad), key)
            key_grad = nn_low(pair(turned_grad), query) + nn(fresh, leave)
            wkey_grad = -nt(fresh_pair, state)
            right_grad = nn_wide(pair(solved_ref[0, chunk].T), pair(side(wkey_grad, fresh_grad)))
            right = pair(right_grad)
            twos = pair(both)
            found = dot(right[0], over(*twos), NT)
            system_grad = found[:, :CHUNK] + found[:, CHUNK:] + dot(right[1], twos[0], NT)
            system_grad = jnp.where(rows > columns, -system_grad, 0.0)
            gram = dot(key, key, NT)
            gram_grad = beta * system_grad
            key_grad = key_grad + nn_low(pair(gram_grad + gram_grad.T), key)
            key_right, value_right = right_grad[:, :head_size], right_grad[:, head_size:]
            key_grad = key_grad + beta * key_right
            value_grad = beta * value_right
            beta_grad = jnp.sum(
                key_right * key.astype(wide) + value_right * value.astype(wide) + system_grad * gram,
                axis=1,
                keepdims=True,
            )
            lanes = lax.broadcasted_iota(jnp.int32, (CHUNK, head_size), 1)
            logit_grad = jnp.where(
                lanes == head, beta_grad * (live * squash * (1.0 - squash)), 0.0
            ).astype(low)

            there = pl.ds(pl.multiple_of(seq * span + start, CHUNK), CHUNK)
            last_lanes = pl.ds(streams + heads * head_size, head_size)

            @pl.when(head == 0)
            def _():
                all_ref[there, last_lanes] = logit_grad

            @pl.when(head > 0)
            def _():
                all_ref[there, last_lanes] = all_ref[there, last_lanes] + logit_grad

            block = ext[pl.ds(start, CHUNK + 16)]
            grads_pre = []
            for stream, grad in enumerate((query_grad, key_grad, value_grad)):
                act, slope = silu_parts(convolved(block, taps, stream))
                if stream < 2:
                    inverse = lax.rsqrt(jnp.sum(act * act, axis=1, keepdims=True) + epsilon)
                    inner = jnp.sum(act * grad, axis=1, keepdims=True)
                    grad = inverse * (grad - act * (inverse * inverse * inner))
                    if stream == 0:
                        grad = grad * head_size ** (-0.5)
                grads_pre.append(grad * slope)
            pre_grads[pl.ds(start + 16, CHUNK)] = jnp.concatenate(grads_pre, axis=1)

        def group(index, carry):
            for number in range(2):
                one(index * 2 + number)
            return carry

        lax.fori_loop(0, chunks // 2, group, 0)

        def back(block):
            parts = []
            for stream in range(3):
                part = block[:, stream * head_size : (stream + 1) * head_size]
                total = None
                for offset in range(CONV):
                    first = CONV - 1 - offset
                    term = taps[stream * CONV + offset][None, :] * part[first : first + CHUNK]
                    total = term if total is None else total + term
                parts.append(total)
            return jnp.concatenate(parts, axis=1)

        lanes = pl.ds(pl.multiple_of(head * 3 * head_size, 128), 3 * head_size)

        def finish(chunk, totals):
            start = pl.multiple_of(chunk * CHUNK, CHUNK)
            block = pre_grads[pl.ds(start + 16, CHUNK + 16)]
            grad = back(block)
            there = pl.ds(pl.multiple_of(seq * span + start, CHUNK), CHUNK)
            all_ref[there, lanes] = grad.astype(low)
            edges[chain] = grad[CHUNK - 16 :]
            before = ext[pl.ds(start, CHUNK + 16)]
            pre = block[:CHUNK]
            out = []
            for offset in range(CONV):
                first = 16 - (CONV - 1) + offset
                term = jnp.sum(pre * before[first : first + CHUNK], axis=0, keepdims=True)
                out.append(totals[offset] + term)
            return tuple(out)

        zero = jnp.zeros((1, 3 * head_size), wide)
        totals = lax.fori_loop(0, chunks, finish, (zero,) * CONV)
        for offset in range(CONV):
            taps_grad_ref[0, offset : offset + 1] = totals[offset]
        halos[chain] = back(pre_grads[: CHUNK + 32])[:16].astype(low)
        pl.when(below)(halo(chain).start)

    @pl.when(step >= chains)
    def _():
        unwind(step - chains)

    @pl.when(step == 2 * chains - 3)
    def _():
        for each in sums:
            each.round(3)

    @pl.when(step == 2 * chains - 1)
    def _():
        for each in sums:
            for number in range(4, lines):
                each.round(number)
            each.exchange()
        for chain in range(chains):
            seq, head = chain // heads, chain % heads
            last = pl.ds((seq + 1) * span - 16, 16)
            lanes = pl.ds(head * 3 * head_size, 3 * head_size)

            @pl.when(above)
            def _(chain=chain, last=last, lanes=lanes):
                halo(chain).wait_recv()
                all_ref[last, lanes] = (edges[chain] + returned[chain].astype(wide)).astype(low)

        for chain in range(chains):
            pl.when(below)(halo(chain).wait_send)
        pl.when(below)(state_copy.wait_send)
        for each in sums:
            each.finish()


def project_kernel(input_ref, scale_ref, weight_ref, normed_ref, raw_ref, logit_ref):
    value = input_ref[...].astype(wide)
    normed = (value * inverse_rms(value) * scale_ref[...]).astype(low)
    normed_ref[...] = normed
    out = dot(normed, weight_ref[...], NN)
    width = raw_ref.shape[1]
    raw_ref[...] = out[:, :width].astype(low)
    logit_ref[...] = out[:, width:]


MESH = pl.DeviceIdType.MESH
STEP = 16


class Place:
    def __init__(self):
        self.seq = lax.axis_index("seq")
        self.core = lax.axis_index("tp")
        self.mate = self.seq % MATES
        self.line = self.seq // MATES
        x, y = self.mate % 2, self.mate // 2
        self.x = 2 * y + (1 - x)
        self.y = 2 * (1 - y) + x
        self.far = 2 * (1 - y) + (1 - x)
        self.base = self.seq - self.mate

    def of(self, mate):
        return (self.base + mate, self.core)

    @property
    def sibling(self):
        return (self.seq, 1 - self.core)

    def lines_away(self, step):
        return (self.seq + step * MATES, self.core)


def meet(place, far=False, lines=0):
    barrier = pltpu.get_barrier_semaphore()
    partners = [place.of(place.x), place.of(place.y), place.sibling]
    if far:
        partners.append(place.of(place.far))
    for partner in partners:
        pl.semaphore_signal(barrier, inc=1, device_id=partner, device_id_type=MESH)
    count = len(partners)
    if lines > 1:
        below, above = place.line > 0, place.line < lines - 1

        @pl.when(below)
        def _():
            pl.semaphore_signal(
                barrier, inc=1, device_id=place.lines_away(-1), device_id_type=MESH
            )

        @pl.when(above)
        def _():
            pl.semaphore_signal(barrier, inc=1, device_id=place.lines_away(1), device_id_type=MESH)

        count = count + jnp.where(below, 1, 0) + jnp.where(above, 1, 0)
    pl.semaphore_wait(barrier, count)


def sender(sems):
    send, receive = sems

    def make(index, source, target, device):
        return pltpu.make_async_remote_copy(
            src_ref=source,
            dst_ref=target,
            send_sem=send.at[index],
            recv_sem=receive.at[index],
            device_id=device,
            device_id_type=MESH,
        )

    return make


def row_steps(first, last, body):
    def one(step, carry):
        body(pl.ds(pl.multiple_of(first + step * STEP, STEP), STEP))
        return carry

    lax.fori_loop(0, (last - first) // STEP, one, 0)


class SumRows:
    SCRATCH = 4

    @staticmethod
    def scratch(rows, columns):
        return [
            pltpu.VMEM((MATES, rows, columns), low),
            pltpu.VMEM((MATES, rows, columns), low),
            pltpu.VMEM((2, rows // 2, columns), low),
            pltpu.VMEM((2, rows, columns), low),
            pltpu.SemaphoreType.DMA((MATES,)),
            pltpu.SemaphoreType.DMA((10,)),
            pltpu.SemaphoreType.DMA((10,)),
        ]

    def __init__(self, place, partial, scratch):
        self.place, self.partial = place, partial
        self.own, self.swapped, self.relay, self.arrived, self.local_sems, send, receive = scratch
        self.make = sender((send, receive))
        self.rows = self.own.shape[1]
        self.order = [place.far, place.x, place.y, place.mate]

    def begin(self):
        self.swaps, self.loads = [], []
        for slot, mate in enumerate(self.order):
            copy = self.make(
                slot, self.partial.at[1, mate], self.swapped.at[slot], self.place.sibling
            )
            copy.start()
            self.swaps.append(copy)
            load = pltpu.make_async_copy(
                self.partial.at[0, mate], self.own.at[slot], self.local_sems.at[slot]
            )
            load.start()
            self.loads.append(load)

    def add(self, target, target_slot, source, source_slot, first, last, shift=0):
        def body(here):
            there = pl.ds(pl.multiple_of(here.start - shift, STEP), STEP) if shift else here
            target[target_slot, here] = (
                target[target_slot, here].astype(wide) + source[source_slot, there].astype(wide)
            ).astype(low)

        row_steps(first, last, body)

    def sum_cores(self, slot):
        self.loads[slot].wait()
        self.swaps[slot].wait_recv()
        self.add(self.own, slot, self.swapped, slot, 0, self.rows)

    def send_far(self):
        half = self.rows // 2
        self.sum_cores(0)
        self.far_low = self.make(
            4, self.own.at[0, :half], self.relay.at[0], self.place.of(self.place.y)
        )
        self.far_high = self.make(
            5, self.own.at[0, half:], self.relay.at[1], self.place.of(self.place.x)
        )
        self.far_low.start()
        self.far_high.start()

    def send_near(self):
        half, place = self.rows // 2, self.place
        self.sum_cores(1)
        self.x_high = self.make(
            6, self.own.at[1, half:], self.arrived.at[0, half:], place.of(place.x)
        )
        self.x_high.start()
        self.sum_cores(2)
        self.y_low = self.make(
            7, self.own.at[2, :half], self.arrived.at[1, :half], place.of(place.y)
        )
        self.y_low.start()

    def send_relayed(self):
        half, place = self.rows // 2, self.place
        self.far_low.wait_recv()
        self.add(self.own, 1, self.relay, 0, 0, half)
        self.x_low = self.make(
            8, self.own.at[1, :half], self.arrived.at[0, :half], place.of(place.x)
        )
        self.x_low.start()
        self.far_high.wait_recv()
        self.add(self.own, 2, self.relay, 1, half, self.rows, shift=half)
        self.y_high = self.make(
            9, self.own.at[2, half:], self.arrived.at[1, half:], place.of(place.y)
        )
        self.y_high.start()
        self.sum_cores(3)

    def wait_half(self, upper):
        if upper:
            self.x_high.wait_recv()
            self.y_high.wait_recv()
        else:
            self.x_low.wait_recv()
            self.y_low.wait_recv()

    def total(self, here):
        return (
            self.own[3, here].astype(wide)
            + self.arrived[0, here].astype(wide)
            + self.arrived[1, here].astype(wide)
        )

    def finish(self):
        for copy in self.swaps + [
            self.far_low, self.far_high, self.x_high, self.y_low, self.x_low, self.y_high,
        ]:
            copy.wait_send()


class ShareRows:
    @staticmethod
    def scratch():
        return [
            pltpu.SemaphoreType.DMA((1,)),
            pltpu.SemaphoreType.DMA((11,)),
            pltpu.SemaphoreType.DMA((11,)),
        ]

    def __init__(self, place, source, target, scratch):
        self.place, self.source, self.target = place, source, target
        self.local_sem, send, receive = scratch
        self.make = sender((send, receive))
        self.rows = target.shape[2]

    def copy(self, index):
        place, half = self.place, self.rows // 2
        lower, upper, whole = pl.ds(0, half), pl.ds(half, half), pl.ds(0, self.rows)
        x, y, sibling = place.of(place.x), place.of(place.y), place.sibling

        def own(rows, device, side=0):
            return self.source.at[rows], self.target.at[side, place.mate, rows], device

        def passed(mate, rows, device, side=0):
            return self.target.at[0, mate, rows], self.target.at[side, mate, rows], device

        return self.make(
            index,
            *(
                lambda: own(upper, y),
                lambda: own(upper, x),
                lambda: own(lower, x),
                lambda: own(lower, y),
                lambda: passed(place.x, lower, y),
                lambda: passed(place.y, upper, x),
                lambda: own(whole, sibling, 1),
                lambda: passed(place.x, whole, sibling, 1),
                lambda: passed(place.y, whole, sibling, 1),
                lambda: passed(place.far, lower, sibling, 1),
                lambda: passed(place.far, upper, sibling, 1),
            )[index](),
        )

    def local(self):
        return pltpu.make_async_copy(
            self.source, self.target.at[0, self.place.mate], self.local_sem.at[0]
        )

    def begin_half(self, upper):
        for index in (0, 1) if upper else (2, 3):
            self.copy(index).start()

    def begin_rest(self):
        self.local().start()
        self.copy(6).start()

    def forward(self):
        for came, then in ((2, 4), (0, 5), (1, 7), (3, 8)):
            self.copy(came).wait_recv()
            self.copy(then).start()

    def forward_far(self):
        for came, then in ((4, 9), (5, 10)):
            self.copy(came).wait_recv()
            self.copy(then).start()

    def finish(self):
        self.local().wait()
        for index in range(6, 11):
            self.copy(index).wait_recv()
        for index in range(11):
            self.copy(index).wait_send()


class GatherLines:
    @staticmethod
    def scratch(lines):
        return [
            pltpu.SemaphoreType.DMA((1,)),
            pltpu.SemaphoreType.DMA((3,)),
            pltpu.SemaphoreType.DMA((3,)),
            pltpu.SemaphoreType.DMA((lines, MATES)),
            pltpu.SemaphoreType.DMA((lines, MATES)),
            pltpu.SemaphoreType.DMA((lines, MATES)),
        ]

    def __init__(self, place, blocks, target, scratch, rows=None):
        self.place, self.blocks, self.target = place, blocks, target
        self.lines = target.shape[0]
        self.part = pl.ds(*(rows or (0, target.shape[2])))
        self.local_sem, send, receive, self.up_sem, self.down_sem, self.got = scratch
        self.make = sender((send, receive))
        self.order = [place.mate, place.x, place.y, place.far]

    def plane(self, slot):
        place, mate = self.place, self.order[slot]
        here = self.target.at[place.line, place.mate]
        if slot == 0:
            return pltpu.make_async_copy(self.blocks.at[mate], here, self.local_sem.at[0])
        return self.make(slot - 1, self.blocks.at[mate], here, place.of(mate))

    def begin(self):
        for slot in range(MATES):
            self.plane(slot).start()

    def arrive(self, slot):
        copy = self.plane(slot)
        copy.wait_recv() if slot else copy.wait()

    def hop(self, step, mate, direction):
        place = self.place
        line = place.line - step * direction
        piece = self.target.at[line, mate, self.part]
        sems = self.up_sem if direction > 0 else self.down_sem
        copy = pltpu.make_async_remote_copy(
            src_ref=piece,
            dst_ref=piece,
            send_sem=sems.at[step, mate],
            recv_sem=self.got.at[line, mate],
            device_id=place.lines_away(direction),
            device_id_type=MESH,
        )
        came = (line >= 0) & (line < self.lines)
        goes = (place.line < self.lines - 1) if direction > 0 else (place.line > 0)
        return copy, came, goes

    def leave(self, arriving=True):
        for slot, mate in enumerate(self.order):
            if arriving:
                self.arrive(slot)
            for direction in (1, -1):
                copy, _, goes = self.hop(0, mate, direction)
                pl.when(goes)(copy.start)

    def onwards(self, step):
        if step >= self.lines:
            return
        for mate in self.order:
            for direction in (1, -1):
                copy, came, goes = self.hop(step, mate, direction)
                pl.when(came)(copy.wait_recv)
                if step < self.lines - 1:
                    pl.when(came & goes)(copy.start)

    def finish_plane(self):
        for slot in range(1, MATES):
            self.plane(slot).wait_send()

    def finish_lines(self):
        for step in range(self.lines - 1):
            for mate in self.order:
                for direction in (1, -1):
                    copy, came, goes = self.hop(step, mate, direction)
                    pl.when(came & goes)(copy.wait_send)


class SumLines:
    @staticmethod
    def scratch(lines, shape):
        return [
            pltpu.VMEM((lines,) + shape, low),
            pltpu.VMEM((2, max(lines - 1, 1)) + shape, low),
            pltpu.SemaphoreType.DMA((lines + 1,)),
            pltpu.SemaphoreType.DMA((2, lines)),
            pltpu.SemaphoreType.DMA((2, lines)),
            pltpu.SemaphoreType.DMA((3,)),
            pltpu.SemaphoreType.DMA((3,)),
        ]

    def __init__(self, place, blocks, result, scratch, first=0):
        self.place, self.blocks, self.result, self.first = place, blocks, result, first
        self.held, self.came, self.local_sems, self.send, self.got, send, receive = scratch
        self.lines = self.held.shape[0]
        self.make = sender((send, receive))

    def load(self, line):
        return pltpu.make_async_copy(
            self.blocks.at[line, :, pl.ds(self.first, self.held.shape[2])],
            self.held.at[line],
            self.local_sems.at[line],
        )

    def begin(self):
        for line in range(self.lines):
            self.load(line).start()

    def wait_loads(self):
        for line in range(self.lines):
            self.load(line).wait()

    def put_gains(self, gains):
        lines, mates, height, lanes = self.held.shape
        top = lax.broadcasted_iota(jnp.int32, (height, lanes), 0) == 0
        for line in range(lines):
            for mate in range(mates):
                first = (line * mates + mate) * lanes
                part = jnp.broadcast_to(gains[:, first : first + lanes], (height, lanes))
                self.held[line, mate] = jnp.where(
                    top, part, self.held[line, mate].astype(wide)
                ).astype(low)

    def add_top(self, other, count):
        lines, mates, height, lanes = self.held.shape
        top = lax.broadcasted_iota(jnp.int32, (height, lanes), 0) < count
        for line in range(lines):
            for mate in range(mates):
                own = self.held[line, mate].astype(wide)
                both = own + other[line, mate].astype(wide)
                self.held[line, mate] = jnp.where(top, both, own).astype(low)

    def copy(self, turn, way):
        direction = 1 - 2 * way
        line = self.place.line + direction * (self.lines - turn)
        return line, pltpu.make_async_remote_copy(
            src_ref=self.held.at[line],
            dst_ref=self.came.at[way, turn - 1],
            send_sem=self.send.at[way, turn],
            recv_sem=self.got.at[way, turn],
            device_id=self.place.lines_away(direction),
            device_id_type=MESH,
        )

    def arrival(self, turn, way):
        slot = self.came.at[way, turn - 1]
        return pltpu.make_async_remote_copy(
            src_ref=slot,
            dst_ref=slot,
            send_sem=self.send.at[way, turn],
            recv_sem=self.got.at[way, turn],
            device_id=self.place.sibling,
            device_id_type=MESH,
        )

    def sends(self, turn, way):
        line = self.place.line
        return line <= turn - 1 if way == 0 else line >= self.lines - turn

    def inner(self, way):
        return self.place.line >= 1 if way == 0 else self.place.line <= self.lines - 2

    def add(self, line, way, turn):
        def mates(mate, carry):
            def body(here):
                self.held[line, mate, here] = (
                    self.held[line, mate, here].astype(wide)
                    + self.came[way, turn - 1, mate, here].astype(wide)
                ).astype(low)

            row_steps(0, self.held.shape[2], body)
            return carry

        lax.fori_loop(0, self.held.shape[1], mates, 0)

    def round(self, turn):
        if turn >= self.lines:
            return
        for way in (0, 1):
            line, copy = self.copy(turn, way)

            @pl.when(self.sends(turn, way))
            def _(line=line, copy=copy, way=way):
                if turn > 1:

                    @pl.when(self.inner(way))
                    def _():
                        self.arrival(turn - 1, way).wait_recv()
                        self.add(line, way, turn - 1)

                copy.start()

    def plane(self, index):
        place = self.place
        mate = (place.x, place.y, place.far)[index]
        return self.make(
            index, self.held.at[place.line, mate], self.result.at[place.mate], place.of(mate)
        )

    def local(self):
        place = self.place
        return pltpu.make_async_copy(
            self.held.at[place.line, place.mate],
            self.result.at[place.mate],
            self.local_sems.at[self.lines],
        )

    def exchange(self):
        for way in (0, 1):
            if self.lines > 1:

                @pl.when(self.inner(way))
                def _(way=way):
                    self.arrival(self.lines - 1, way).wait_recv()
                    self.add(self.place.line, way, self.lines - 1)

        for index in range(3):
            self.plane(index).start()
        self.local().start()

    def finish(self):
        self.local().wait()
        for index in range(3):
            self.plane(index).wait()
        for turn in range(1, self.lines):
            for way in (0, 1):
                _, copy = self.copy(turn, way)
                pl.when(self.sends(turn, way))(copy.wait_send)


def remote_call(body, identity, ins, outs, scratch, aliases=None):
    anywhere = pl.BlockSpec(memory_space=pl.ANY)
    held = pl.BlockSpec(memory_space=pltpu.VMEM)
    return pl.pallas_call(
        body,
        in_specs=[anywhere if kind == "any" else held for _, kind in ins],
        out_specs=[anywhere if kind == "any" else held for _, _, kind in outs],
        out_shape=[jax.ShapeDtypeStruct(shape, dtype) for shape, dtype, _ in outs],
        scratch_shapes=scratch,
        input_output_aliases=aliases or {},
        compiler_params=pltpu.CompilerParams(
            vmem_limit_bytes=VMEM_BYTES, collective_id=identity, has_side_effects=True
        ),
    )(*[array for array, _ in ins])


def inverse_rms(value):
    return lax.rsqrt(jnp.mean(value * value, axis=1, keepdims=True) + epsilon)


def norm_back_rows(grad, source, scale):
    inverse = inverse_rms(source)
    scaled = grad * scale
    unit = source * inverse
    inner = jnp.mean(scaled * source, axis=1, keepdims=True)
    return inverse * (scaled - unit * (inverse * inner)), grad * unit


def sum_and_share(rows, share, body, half, during):
    begin, *steps = during
    rows.begin()
    begin()
    rows.send_far()
    rows.send_near()
    rows.send_relayed()
    rows.wait_half(False)
    row_steps(0, half, body)
    share.begin_half(False)
    rows.wait_half(True)
    row_steps(half, 2 * half, body)
    share.begin_half(True)
    share.begin_rest()
    steps[0]()
    rows.finish()
    share.forward()
    steps[1]()
    share.forward_far()
    steps[2]()
    share.finish()


def middle_kernel(lines, moves, partial, input_ref, scale_ref, *rest):
    place = Place()
    count = len(moves)
    middle_ref, shared = rest[count : count + 2]
    targets, scratch = rest[count + 2 : 2 * count + 2], rest[2 * count + 2 :]
    normed, scratch = scratch[0], scratch[1:]
    meet(place, lines=lines if moves else 0)
    rows = SumRows(place, partial, scratch[:7])
    share = ShareRows(place, normed, shared, scratch[7:10])
    gathers = [
        GatherLines(place, None, target, scratch[10 + 6 * index : 16 + 6 * index], moves[index])
        for index, target in enumerate(targets)
    ]

    def body(here):
        middle = input_ref[here].astype(wide) + rows.total(here)
        middle_ref[here] = middle
        normed[here] = (middle * inverse_rms(middle) * scale_ref[...]).astype(low)

    def leave():
        for gather in gathers:
            gather.leave(False)

    def step(number):
        def go():
            for gather in gathers:
                gather.onwards(number)

        return go

    def last():
        for number in range(3, lines):
            for gather in gathers:
                gather.onwards(number)
        for gather in gathers:
            gather.finish_lines()

    sum_and_share(rows, share, body, normed.shape[0] // 2, (leave, step(1), step(2), last))


def turn_rows_kernel(lines, parts, partial, middle_ref, grad_ref, scale_ref, *rest):
    place = Place()
    count = len(parts)
    blocks, rest = rest[:count], rest[count:]
    middle_grad_ref, gain_ref, shared = rest[:3]
    results, scratch = rest[3 : 3 + count], rest[3 + count :]
    low_grad, scratch = scratch[0], scratch[1:]
    meet(place, far=bool(parts), lines=lines if parts else 0)
    rows = SumRows(place, partial, scratch[:7])
    share = ShareRows(place, low_grad, shared, scratch[7:10])
    sums = [
        SumLines(place, blocks[index], results[index], scratch[10 + 7 * index : 17 + 7 * index], first)
        for index, (first, _) in enumerate(parts)
    ]
    for each in sums:
        each.begin()
    gain_ref[...] = jnp.zeros_like(gain_ref)

    def body(here):
        part, gains = norm_back_rows(rows.total(here), middle_ref[here], scale_ref[...])
        total = grad_ref[here].astype(wide) + part
        middle_grad_ref[here] = total
        low_grad[here] = total.astype(low)
        gain_ref[...] += jnp.sum(gains, axis=0, keepdims=True)

    def begin():
        for each in sums:
            each.wait_loads()
            each.round(1)

    def step(number):
        def go():
            for each in sums:
                each.round(number)

        return go

    def last():
        for each in sums:
            for number in range(4, lines):
                each.round(number)
            each.exchange()
        for each in sums:
            each.finish()

    sum_and_share(rows, share, body, low_grad.shape[0] // 2, (begin, step(2), step(3), last))


def last_rows_kernel(
    lines, pieces, partial, mlp_partial, input_ref, middle_ref, middle_grad_ref, scale_ref, *rest
):
    place = Place()
    blocks, rest = rest[:pieces], rest[pieces:]
    input_grad, block_output, gain_ref = rest[:3]
    results, scratch = rest[3 : 3 + pieces], rest[3 + pieces :]
    low_grad, low_output = scratch[:2]
    meet(place, far=bool(pieces), lines=lines if pieces else 0)
    rows = SumRows(place, partial, scratch[2:9])
    outs = SumRows(place, mlp_partial, scratch[9:16])
    make = sender(scratch[16:18])
    local_sems = scratch[18]
    sums = [
        SumLines(place, blocks[index], results[index], scratch[19 + 7 * index : 26 + 7 * index])
        for index in range(pieces)
    ]
    whole = low_grad.shape[0]
    for each in sums:
        each.begin()
    rows.begin()
    outs.begin()
    for each in sums:
        each.wait_loads()
    for each in sums[1:]:
        each.round(1)
    gain_ref[...] = jnp.zeros_like(gain_ref)
    rows.send_far()
    rows.send_near()
    outs.send_far()
    rows.send_relayed()
    outs.send_near()
    for each in sums[1:]:
        each.round(2)
    outs.send_relayed()
    rows.wait_half(False)
    rows.wait_half(True)

    def body(here):
        part, gains = norm_back_rows(
            rows.total(here), input_ref[here].astype(wide), scale_ref[...]
        )
        low_grad[here] = (middle_grad_ref[here] + part).astype(low)
        gain_ref[...] += jnp.sum(gains, axis=0, keepdims=True)

    row_steps(0, whole, body)
    first = make(0, low_grad, input_grad.at[place.core], place.sibling)
    first.start()
    first_local = pltpu.make_async_copy(low_grad, input_grad.at[place.core], local_sems.at[0])
    first_local.start()
    if sums:
        mine, theirs = scratch[19 + 7 * pieces :]
        small = sums[0]
        small.put_gains(gain_ref)
        mine[...] = small.held[...]
        swap = make(2, mine, theirs, place.sibling)
        swap.start()
        swap.wait_recv()
        small.add_top(theirs, 3)
        small.round(1)
        small.round(2)
    outs.wait_half(False)
    outs.wait_half(True)

    def out_body(here):
        low_output[here] = (middle_ref[here] + outs.total(here)).astype(low)

    row_steps(0, whole, out_body)
    second = make(1, low_output, block_output.at[place.core], place.sibling)
    second.start()
    second_local = pltpu.make_async_copy(low_output, block_output.at[place.core], local_sems.at[1])
    second_local.start()
    for turn in range(3, lines):
        for each in sums:
            each.round(turn)
    for each in sums:
        each.exchange()
    rows.finish()
    outs.finish()
    first_local.wait()
    second_local.wait()
    first.wait()
    second.wait()
    if sums:
        swap.wait_send()
    for each in sums:
        each.finish()


def first_rows_kernel(lines, whole, pieces, input_ref, *rest):
    place = Place()
    ins, rest = rest[:pieces], rest[pieces:]
    inputs, outs, scratch = rest[0], rest[1 : 1 + pieces], rest[1 + pieces :]
    meet(place, far=bool(pieces), lines=lines if pieces else 0)
    share = ShareRows(place, input_ref.at[place.core], inputs, scratch[:3])
    gathers = [
        GatherLines(place, ins[index], outs[index], scratch[3 + 6 * index : 9 + 6 * index])
        for index in range(pieces)
    ]
    for gather in gathers[:whole]:
        gather.begin()
    share.begin_half(False)
    share.begin_half(True)
    share.begin_rest()
    for gather in gathers[whole:]:
        gather.begin()
    for gather in gathers[:whole]:
        gather.leave()
    share.forward()
    for gather in gathers[:whole]:
        gather.onwards(1)
    share.forward_far()
    for step in range(2, lines):
        for gather in gathers[:whole]:
            gather.onwards(step)
    share.finish()
    for gather in gathers[whole:]:
        for slot in range(MATES):
            gather.arrive(slot)
    for gather in gathers:
        gather.finish_plane()
    for gather in gathers[:whole]:
        gather.finish_lines()


def first_rows(block_input, blocks, whole, lines):
    seqs, rows, columns = block_input.shape
    shape = (seqs, MATES, rows, columns)
    return remote_call(
        functools.partial(first_rows_kernel, lines, whole, len(blocks)),
        0,
        [(array, "any") for array in (block_input, *blocks)],
        [(shape, low, "any")] + [((lines,) + block.shape, low, "any") for block in blocks],
        ShareRows.scratch() + GatherLines.scratch(lines) * len(blocks),
    )


def middle_rows(partial, mine, scale, moving, lines):
    seqs, _, rows, columns = partial.shape
    arrays = [array for array, _ in moving]
    return remote_call(
        functools.partial(middle_kernel, lines, tuple(part for _, part in moving)),
        1,
        [(partial, "any"), (mine, "held"), (scale, "held")] + [(array, "any") for array in arrays],
        [((rows, columns), wide, "held"), (partial.shape, low, "any")]
        + [(array.shape, low, "any") for array in arrays],
        [pltpu.VMEM((rows, columns), low)]
        + SumRows.scratch(rows, columns)
        + ShareRows.scratch()
        + GatherLines.scratch(lines) * len(arrays),
        {3 + index: 2 + index for index in range(len(arrays))},
    )


def turn_rows(partial, middle, grad, scale, summing, lines):
    seqs, _, rows, columns = partial.shape
    scratch = (
        [pltpu.VMEM((rows, columns), low)] + SumRows.scratch(rows, columns) + ShareRows.scratch()
    )
    outs = []
    for array, (_, height) in summing:
        shape = (MATES, height, array.shape[3])
        scratch += SumLines.scratch(lines, shape)
        outs.append((shape, low, "any"))
    return remote_call(
        functools.partial(turn_rows_kernel, lines, tuple(part for _, part in summing)),
        2,
        [(partial, "any"), (middle, "held"), (grad, "held"), (scale, "held")]
        + [(array, "any") for array, _ in summing],
        [
            ((rows, columns), wide, "held"),
            ((1, columns), wide, "held"),
            (partial.shape, low, "any"),
        ]
        + outs,
        scratch,
    )


def last_rows(partial, mlp_partial, mine, middle, middle_grad, scale, blocks, lines):
    seqs, _, rows, columns = partial.shape
    scratch = (
        [pltpu.VMEM((rows, columns), low), pltpu.VMEM((rows, columns), low)]
        + SumRows.scratch(rows, columns)
        + SumRows.scratch(rows, columns)
        + [pltpu.SemaphoreType.DMA((3,))] * 3
    )
    for block in blocks:
        scratch += SumLines.scratch(lines, block.shape[1:])
    if blocks:
        scratch += [pltpu.VMEM(blocks[0].shape, low)] * 2
    return remote_call(
        functools.partial(last_rows_kernel, lines, len(blocks)),
        3,
        [(partial, "any"), (mlp_partial, "any")]
        + [(array, "held") for array in (mine, middle, middle_grad, scale)]
        + [(block, "any") for block in blocks],
        [
            ((seqs, rows, columns), low, "any"),
            ((seqs, rows, columns), low, "any"),
            ((1, columns), wide, "held"),
        ]
        + [(block.shape[1:], low, "any") for block in blocks],
        scratch,
    )


class Steps:
    def __init__(self, seqs, heads, span):
        self.seqs, self.heads, self.span = seqs, heads, span
        self.chains, self.chunks = seqs * heads, span // CHUNK

    def chain(self, step, when):
        if when == "first":
            return jnp.minimum(step, self.chains - 1)
        if when == "second":
            return jnp.maximum(step - self.chains, 0)
        return step % self.chains

    def rows(self, when, columns, place):
        def index(step):
            chain = self.chain(step, when)
            return chain // self.heads, place(chain % self.heads)

        return pl.BlockSpec((self.span, columns), index)

    def streams(self, when):
        return self.rows(when, 3 * CHUNK, lambda head: head)

    def head(self, when):
        return self.rows(when, CHUNK, lambda head: head)

    def gate(self, when):
        return self.rows(when, CHUNK, lambda head: 3 * self.heads + head)

    def logit(self, when):
        return self.rows(when, CHUNK, lambda head: 0)

    def taps(self, when):
        return pl.BlockSpec(
            (1, 3 * CONV, CHUNK), lambda step: (self.chain(step, when) % self.heads, 0, 0)
        )

    def blocks(self, when, columns=CHUNK):
        return pl.BlockSpec(
            (1, self.chunks, CHUNK, columns), lambda step: (self.chain(step, when), 0, 0, 0)
        )

    def few(self, when, columns):
        return pl.BlockSpec((1, 8, columns), lambda step: (self.chain(step, when), 0, 0))

    def whole(self, shape):
        return pl.BlockSpec(shape, lambda step: (0,) * len(shape), pipeline_mode=pl.Buffered(1))

    def call(self, body, identity, ins, outs, scratch, aliases=None):
        return pl.pallas_call(
            body,
            grid=(2 * self.chains,),
            in_specs=[spec for _, spec in ins],
            out_specs=[spec for _, _, spec in outs],
            out_shape=[jax.ShapeDtypeStruct(shape, dtype) for shape, dtype, _ in outs],
            scratch_shapes=scratch,
            input_output_aliases=aliases or {},
            compiler_params=pltpu.CompilerParams(
                vmem_limit_bytes=VMEM_BYTES,
                dimension_semantics=("arbitrary",),
                collective_id=identity,
                has_side_effects=True,
            ),
        )(*[array for array, _ in ins])


def delta_front(limit, raw, taps, logits, scale, out_grad, moving, lines, seqs, heads, span):
    steps = Steps(seqs, heads, span)
    chains, chunks, size = steps.chains, steps.chunks, CHUNK
    squares, doubles = (chains, chunks, CHUNK, size), (chains, chunks, CHUNK, 2 * size)
    states, tails = (chains, size, size), (seqs, 16, 3 * heads * size)
    tokens, model_width = out_grad.shape[1:]
    anywhere = pl.BlockSpec(memory_space=pl.ANY)
    arrays = [array for array, _ in moving]
    ins = [
        (limit, pl.BlockSpec(memory_space=pltpu.SMEM)),
        (raw, anywhere),
        (raw, steps.streams("first")),
        (taps, steps.taps("first")),
        (logits, steps.logit("first")),
        (raw, steps.gate("second")),
        (scale, steps.whole((1, size))),
        (out_grad, anywhere),
    ] + [(array, anywhere) for array in arrays]
    outs = [
        ((seqs * span, 3 * heads * size), low, steps.streams("first")),
        (squares, wide, steps.blocks("first")),
        (doubles, wide, steps.blocks("first", 2 * size)),
        (squares, wide, steps.blocks("first")),
        (states, wide, steps.whole(states)),
        (tails, low, steps.whole(tails)),
        (squares, wide, steps.blocks("second")),
        (squares, wide, steps.blocks("second")),
        ((seqs * span, heads * size), wide, steps.head("second")),
        ((seqs * span, heads * size), low, steps.head("second")),
        ((seqs, MATES, tokens, model_width), low, anywhere),
    ] + [(array.shape, low, anywhere) for array in arrays]
    scratch = [
        pltpu.VMEM((span + 16, 3 * size), wide),
        pltpu.VMEM(squares, wide),
        pltpu.VMEM(squares, wide),
        pltpu.VMEM(squares, wide),
        pltpu.VMEM(squares, wide),
        pltpu.VMEM(doubles, wide),
        pltpu.VMEM((chains, span, 3 * size), low),
        pltpu.VMEM(states, low),
        pltpu.VMEM(states, low),
        pltpu.VMEM(tails, low),
        pltpu.SemaphoreType.DMA((2, seqs)),
        pltpu.SemaphoreType.DMA((2,)),
    ]
    scratch += ShareRows.scratch() + GatherLines.scratch(lines) * len(arrays)
    moves = tuple(part for _, part in moving)
    return steps.call(
        functools.partial(front_kernel, lines, heads, moves),
        4,
        ins,
        outs,
        scratch,
        {8 + index: 11 + index for index in range(len(arrays))},
    )


def delta_back(
    limit, raw, tails, taps, logits, scale, qkv, wu, maps, total, grad, mixed, solved, state, fresh,
    summing, lines, seqs, heads, span,
):
    steps = Steps(seqs, heads, span)
    chains, chunks, size = steps.chains, steps.chunks, CHUNK
    squares, states = (chains, chunks, CHUNK, size), (chains, size, size)
    all_shape = (seqs * span, (4 * heads + 1) * size)
    anywhere = pl.BlockSpec(memory_space=pl.ANY)
    ins = [
        (limit, pl.BlockSpec(memory_space=pltpu.SMEM)),
        (raw, steps.streams("second")),
        (tails, steps.whole(tails.shape)),
        (taps, steps.taps("second")),
        (logits, steps.logit("second")),
        (raw, steps.gate("first")),
        (scale, steps.whole((1, size))),
        (qkv, steps.streams("both")),
        (wu, steps.blocks("both", 2 * size)),
        (maps, steps.blocks("first")),
        (total, steps.whole(states)),
        (grad, steps.head("first")),
        (mixed, steps.head("first")),
        (solved, steps.blocks("second")),
        (state, steps.blocks("second")),
        (fresh, steps.blocks("second")),
    ] + [(array, anywhere) for array, _ in summing]
    outs = [
        (all_shape, low, steps.whole(all_shape)),
        ((chains, 8, size), wide, steps.few("first", size)),
        ((chains, 8, 3 * size), wide, steps.few("second", 3 * size)),
    ]
    edges = (chains, 16, 3 * size)
    scratch = [
        pltpu.VMEM((span + 16, 3 * size), wide),
        pltpu.VMEM((span + 32, 3 * size), wide),
        pltpu.VMEM(squares, wide),
        pltpu.VMEM(squares, wide),
        pltpu.VMEM(squares, wide),
        pltpu.VMEM(squares, wide),
        pltpu.VMEM(squares, wide),
        pltpu.VMEM(states, low),
        pltpu.VMEM(states, low),
        pltpu.VMEM(edges, low),
        pltpu.VMEM(edges, wide),
        pltpu.VMEM(edges, low),
        pltpu.SemaphoreType.DMA((2, chains)),
        pltpu.SemaphoreType.DMA((2,)),
    ]
    for array, (_, height) in summing:
        shape = (MATES, height, array.shape[3])
        scratch += SumLines.scratch(lines, shape)
        outs.append((shape, low, anywhere))
    return steps.call(
        functools.partial(back_kernel, lines, heads, tuple(part for _, part in summing)),
        5,
        ins,
        outs,
        scratch,
    )


def project(inputs, scale, weight, raw_width):
    rows, model_width = inputs.shape
    columns = weight.shape[1]
    tile = 256

    def tall(width):
        return pl.BlockSpec((tile, width), lambda step: (step, 0))

    def whole(array):
        return pl.BlockSpec(array.shape, lambda step: (0, 0), pipeline_mode=pl.Buffered(1))

    return pl.pallas_call(
        project_kernel,
        grid=(rows // tile,),
        in_specs=[tall(model_width), whole(scale), whole(weight)],
        out_specs=[tall(model_width), tall(raw_width), tall(columns - raw_width)],
        out_shape=[
            jax.ShapeDtypeStruct((rows, model_width), low),
            jax.ShapeDtypeStruct((rows, raw_width), low),
            jax.ShapeDtypeStruct((rows, columns - raw_width), wide),
        ],
        compiler_params=pltpu.CompilerParams(vmem_limit_bytes=VMEM_BYTES),
    )(inputs, scale, weight)


def held_call(body, ins, outs):
    held = pl.BlockSpec(memory_space=pltpu.VMEM)
    return pl.pallas_call(
        body,
        in_specs=[held] * len(ins),
        out_specs=[held] * len(outs),
        out_shape=[jax.ShapeDtypeStruct(shape, dtype) for shape, dtype in outs],
        compiler_params=pltpu.CompilerParams(vmem_limit_bytes=VMEM_BYTES),
    )(*ins)


def pack_kernel(
    heads, query, key, value, outgate, beta, output, swish, upward, downward,
    attn_ref, output_ref, ups_ref, downs_ref,
):
    size = CHUNK
    width = heads * size
    units = downs_ref.shape[2]
    beta_low = beta[...].astype(low)
    for mate in range(MATES):
        first = mate * width
        for head in range(heads):
            for stream, weight in enumerate((query, key, value)):
                lanes = (3 * head + stream) * size
                attn_ref[mate, :, lanes : lanes + size] = weight[
                    :, first + head * size : first + (head + 1) * size
                ].astype(low)
        attn_ref[mate, :, 3 * width : 4 * width] = outgate[:, first : first + width].astype(low)
        shape = (beta.shape[1], size)
        rows = lax.broadcasted_iota(jnp.int32, shape, 0)
        columns = lax.broadcasted_iota(jnp.int32, shape, 1)
        chosen = (rows == columns + mate * heads) & (columns < heads)
        attn_ref[mate, :, 4 * width :] = dot(
            beta_low, jnp.where(chosen, 1.0, 0.0).astype(low), NN
        ).astype(low)
        output_ref[mate] = output[first : first + width, :].T.astype(low)
        here = mate * units
        ups_ref[mate, :, :units] = swish[:, here : here + units].astype(low)
        ups_ref[mate, :, units:] = upward[:, here : here + units].astype(low)
        downs_ref[mate] = downward[here : here + units, :].T.astype(low)


def unpack_kernel(
    heads, attn, outs, ups_low, ups_high, downs,
    query, key, value, outgate, beta, output, swish, upward, downward,
):
    size = CHUNK
    width = heads * size
    units = downs.shape[2]
    split = ups_low.shape[1]
    beta_all = None
    for mate in range(MATES):
        first = mate * width
        for head in range(heads):
            for stream, grad in enumerate((query, key, value)):
                lanes = (3 * head + stream) * size
                grad[:, first + head * size : first + (head + 1) * size] = attn[
                    mate, :, lanes : lanes + size
                ].astype(wide)
        outgate[:, first : first + width] = attn[mate, :, 3 * width : 4 * width].astype(wide)
        shape = (size, beta.shape[1])
        rows = lax.broadcasted_iota(jnp.int32, shape, 0)
        columns = lax.broadcasted_iota(jnp.int32, shape, 1)
        chosen = (columns == rows + mate * heads) & (rows < heads)
        part = dot(attn[mate, :, 4 * width :], jnp.where(chosen, 1.0, 0.0).astype(low), NN)
        beta_all = part if beta_all is None else beta_all + part
        output[first : first + width, :] = outs[mate].astype(wide).T
        here = mate * units
        for rows_here, part in ((pl.ds(0, split), ups_low), (pl.ds(split, swish.shape[0] - split), ups_high)):
            swish[rows_here, here : here + units] = part[mate, :, :units].astype(wide)
            upward[rows_here, here : here + units] = part[mate, :, units:].astype(wide)
        downward[here : here + units, :] = downs[mate].astype(wide).T
    beta[...] = beta_all


def cut_columns(weight):
    depth, columns = weight.shape
    return weight.reshape(depth, MATES, columns // MATES).transpose(1, 0, 2)


def join_columns(blocks):
    return blocks.transpose(1, 0, 2).reshape(blocks.shape[1], -1)


def gather_weights(blocks):
    return gather_lines(swap_blocks(blocks))


def scatter_grads(blocks):
    return swap_blocks(scatter_lines(blocks.astype(low))).astype(wide)


def on_device(
    block_input,
    lengths,
    attn_gain,
    query_weight,
    key_weight,
    value_weight,
    outgate_weight,
    beta_weight,
    conv_kernel,
    head_gain,
    output_weight,
    mlp_gain,
    swish_weight,
    upward_weight,
    downward_weight,
    out_grad,
):
    count = lax.axis_size("seq")
    lines = count // MATES
    core = lax.axis_index("tp")
    seq_count, tokens, model_width = block_input.shape
    depth = attn_gain.shape[0]
    gain_part = head_gain.shape[0]
    head_size = gain_part * count
    heads = beta_weight.shape[1] // MATES
    width = heads * head_size
    units = swish_weight.shape[1] // MATES

    near = lines <= 4 and depth % 128 == 0
    rows = seq_count * MATES * tokens
    span = MATES * tokens

    small_cut = jnp.concatenate(
        [
            jnp.broadcast_to(
                jnp.concatenate([attn_gain, mlp_gain, head_gain]).astype(low)[None],
                (MATES, 2 * depth + gain_part),
            ),
            jnp.zeros((MATES, -gain_part % 128), low),
            conv_kernel.astype(low).reshape(MATES, -1),
        ],
        axis=1,
    )
    sizes = (depth, depth, gain_part, -gain_part % 128, heads * 3 * CONV * gain_part)
    starts = [sum(sizes[:index]) for index in range(len(sizes) + 1)]
    small_cut = jnp.pad(small_cut, ((0, 0), (0, SMALL * 128 - starts[-1])))
    small_cut = small_cut.reshape(MATES, SMALL, 128)
    streams_end, gates_end = 3 * width, 4 * width
    attn_width = gates_end + head_size
    if near:
        cuts = held_call(
            functools.partial(pack_kernel, heads),
            (
                query_weight, key_weight, value_weight, outgate_weight, beta_weight, output_weight,
                swish_weight, upward_weight, downward_weight,
            ),
            [
                ((MATES, depth, columns), low)
                for columns in (attn_width, width, 2 * units, units)
            ],
        )
        input_rows, small, attn_full, output_full, ups_full, downward_full = first_rows(
            block_input, (small_cut, *cuts), 2, lines
        )
        ups_split = depth // 128 * 80
        front_moves = ((output_full, (0, depth)), (ups_full, (0, ups_split)))
    else:
        streams_cut = jnp.stack(
            [
                w.astype(low).reshape(depth, MATES, heads, head_size)
                for w in (query_weight, key_weight, value_weight)
            ],
            axis=3,
        )
        streams_cut = streams_cut.transpose(1, 0, 2, 3, 4).reshape(MATES, depth, streams_end)
        beta_cut = jnp.pad(
            cut_columns(beta_weight.astype(low)), ((0, 0), (0, 0), (0, head_size - heads))
        )
        cuts = (
            small_cut,
            jnp.concatenate([streams_cut, cut_columns(outgate_weight.astype(low)), beta_cut], axis=2),
            cut_columns(output_weight.astype(low).T),
            jnp.concatenate([cut_columns(w.astype(low)) for w in (swish_weight, upward_weight)], axis=2),
            cut_columns(downward_weight.astype(low).T),
        )
        input_rows, = first_rows(block_input, (), 0, lines)
        small, attn_full, output_full, ups_full, downward_full = (gather_weights(cut) for cut in cuts)
        front_moves = ()
    attn_full = attn_full.reshape(model_width, attn_width)
    input_rows = input_rows.reshape(rows, model_width)
    small = small.reshape(count, SMALL * 128)
    attn_small, mlp_small, head_small, _, conv_small = (
        small[:, starts[index] : starts[index + 1]] for index in range(len(sizes))
    )
    taps = (
        conv_small.reshape(count, heads, 3, CONV, gain_part)
        .transpose(1, 2, 3, 0, 4)
        .reshape(heads, 3 * CONV, head_size)
        .astype(wide)
    )
    attn_scale = attn_small.reshape(1, model_width).astype(wide)
    mlp_scale = mlp_small.reshape(1, model_width).astype(wide)
    head_scale = head_small.reshape(1, head_size).astype(wide)

    mine_low = pick(block_input, core)
    grad_mine = pick(out_grad, core)
    blocked = (seq_count, MATES, tokens, model_width)
    lengths_here = jnp.stack([pick(lengths, core), pick(lengths, 1 - core)])
    limit = lengths_here - line_of() * span

    flat_normed, raw, logits = project(input_rows, attn_scale, attn_full, gates_end)
    sizes_of = (lines, seq_count, heads, span)
    qkv, solved, wu, maps, total, tails, state, fresh, mixed, gated, grad_rows, *moved = delta_front(
        limit, raw, taps, logits, head_scale, out_grad, front_moves, *sizes_of
    )
    grad_rows = grad_rows.reshape(rows, model_width)
    middle_moves = ()
    if near:
        output_full, ups_full = moved
        middle_moves = (
            (ups_full, (ups_split, depth - ups_split)), (downward_full, (0, depth))
        )
    output_full = output_full.reshape(model_width, width)
    attn_part = matmul("rc,dc->rd", gated, output_full).astype(low)
    middle, mlp_normed, *moved = middle_rows(
        attn_part.reshape(blocked), mine_low, mlp_scale, middle_moves, lines
    )
    if near:
        ups_full, downward_full = moved
    ups_full = ups_full.reshape(model_width, 2 * units)
    downward_full = downward_full.reshape(model_width, units)
    mlp_normed = mlp_normed.reshape(rows, model_width)
    acts = matmul("rd,df->rf", mlp_normed, ups_full)
    gate_act, up_act = acts[:, :units], acts[:, units:]
    silu_act = jax.nn.silu(gate_act)
    hidden = (silu_act * up_act).astype(low)
    mlp_part = matmul("rf,df->rd", hidden, downward_full).astype(low)

    hidden_grad = matmul("rd,df->rf", grad_rows, downward_full)
    downward_grad = matmul("rd,rf->df", grad_rows, hidden).astype(low)
    acts_grad = jnp.concatenate(
        [
            (hidden_grad * up_act * silu_slope(gate_act)).astype(low),
            (hidden_grad * silu_act).astype(low),
        ],
        axis=1,
    )
    ups_grad = matmul("rd,rf->df", mlp_normed, acts_grad).astype(low)
    normed_two_part = matmul("rf,df->rd", acts_grad, ups_full).astype(low)

    def cut_rows(grad):
        return grad.reshape(lines, MATES, depth, grad.shape[1])

    ups_blocks, downward_blocks = cut_rows(ups_grad), cut_rows(downward_grad)
    turn_sums = back_sums = ()
    if near:
        sums_split = depth // 128 * 96
        turn_sums = ((ups_blocks, (0, sums_split)),)
    middle_grad, mlp_gain_grad, attn_grad_rows, *summed = turn_rows(
        normed_two_part.reshape(blocked), middle, grad_mine, mlp_scale, turn_sums, lines
    )
    attn_grad_rows = attn_grad_rows.reshape(rows, model_width)
    output_grad = cut_rows(matmul("rd,rc->dc", attn_grad_rows, gated).astype(low))
    gated_grad = matmul("rd,dc->rc", attn_grad_rows, output_full)
    if near:
        ups_low, = summed
        back_sums = (
            (ups_blocks, (sums_split, depth - sums_split)),
            (downward_blocks, (0, depth)),
            (output_grad, (0, depth)),
        )
    all_grads, head_gain_parts, taps_grad, *summed = delta_back(
        limit, raw, tails, taps, logits, head_scale, qkv, wu, maps, total, gated_grad, mixed, solved,
        state, fresh, back_sums, *sizes_of,
    )
    normed_part = matmul("rc,dc->rd", all_grads, attn_full).astype(low)
    attn_grads = cut_rows(matmul("rd,rc->dc", flat_normed, all_grads).astype(low))

    conv_grad = (
        taps_grad[:, :CONV]
        .reshape(seq_count, heads, CONV, 3, count, gain_part)
        .sum(axis=0)
        .transpose(3, 0, 2, 1, 4)
        .reshape(count, -1)
    )

    def small_blocks(attn_gain_grad):
        parts = [
            attn_gain_grad.reshape(count, depth),
            mlp_gain_grad.reshape(count, depth),
            jnp.sum(head_gain_parts[:, 0], axis=0).reshape(count, gain_part),
            jnp.zeros((count, -gain_part % 128), wide),
            conv_grad,
        ]
        flat = jnp.concatenate(parts, axis=1).astype(low)
        flat = jnp.pad(flat, ((0, 0), (0, SMALL * 128 - starts[-1])))
        return flat.reshape(lines, MATES, SMALL, 128)

    last_ins = (
        normed_part.reshape(blocked),
        mlp_part.reshape(blocked),
        mine_low,
        middle,
        middle_grad,
        attn_scale,
    )
    if near:
        ups_high, downward_sum, output_sum = summed
        blocks = (small_blocks(jnp.zeros((1, model_width), wide)), attn_grads)
        input_grad, block_output, _, small_sum, attn_sum = last_rows(*last_ins, blocks, lines)
        grads = held_call(
            functools.partial(unpack_kernel, heads),
            (attn_sum, output_sum, ups_low, ups_high, downward_sum),
            [
                (w.shape, wide)
                for w in (
                    query_weight, key_weight, value_weight, outgate_weight, beta_weight, output_weight,
                    swish_weight, upward_weight, downward_weight,
                )
            ],
        )
        small_sum = small_sum.reshape(MATES, SMALL * 128).astype(wide)
        gains_sum = jnp.sum(small_sum[:, : starts[3]], axis=0)
    else:
        input_grad, block_output, attn_gain_grad = last_rows(*last_ins, (), lines)
        small_sum, attn_sum, output_sum, ups_sum, downward_sum = (
            scatter_grads(block)
            for block in (
                small_blocks(attn_gain_grad), attn_grads, output_grad, ups_blocks, downward_blocks
            )
        )
        small_sum = small_sum.reshape(MATES, SMALL * 128)
        gains_sum = jnp.sum(small_sum[:, : starts[3]], axis=0)
        gains_sum = gains_sum + other_core(gains_sum)
        streams_sum = (
            attn_sum[:, :, :streams_end]
            .reshape(MATES, depth, heads, 3, head_size)
            .transpose(3, 1, 0, 2, 4)
            .reshape(3, depth, MATES * width)
        )
        grads = (
            streams_sum[0],
            streams_sum[1],
            streams_sum[2],
            join_columns(attn_sum[:, :, streams_end:gates_end]),
            join_columns(attn_sum[:, :, gates_end : gates_end + heads]),
            join_columns(output_sum).T,
            join_columns(ups_sum[:, :, :units]),
            join_columns(ups_sum[:, :, units:]),
            join_columns(downward_sum).T,
        )
    conv_sum = small_sum[:, starts[4] : starts[5]]
    return (
        block_output,
        input_grad,
        gains_sum[:depth],
        *grads[:5],
        conv_sum.reshape(MATES * heads, 3, CONV, gain_part),
        gains_sum[2 * depth :],
        grads[5],
        gains_sum[depth : 2 * depth],
        *grads[6:],
    )


def solution(mesh):
    return jax.shard_map(
        on_device,
        mesh=mesh,
        in_specs=(
            P(None, "seq", None),
            P(),
            P("seq"),
            P("seq", "tp"),
            P("seq", "tp"),
            P("seq", "tp"),
            P("seq", "tp"),
            P("seq", "tp"),
            P("tp", None, None, "seq"),
            P("seq"),
            P("tp", "seq"),
            P("seq"),
            P("seq", "tp"),
            P("seq", "tp"),
            P("tp", "seq"),
            P(None, "seq", None),
        ),
        out_specs=(
            P(None, "seq", None),
            P(None, "seq", None),
            P("seq"),
            P("seq", "tp"),
            P("seq", "tp"),
            P("seq", "tp"),
            P("seq", "tp"),
            P("seq", "tp"),
            P("tp", None, None, "seq"),
            P("seq"),
            P("tp", "seq"),
            P("seq"),
            P("seq", "tp"),
            P("seq", "tp"),
            P("tp", "seq"),
        ),
        check_vma=False,
    )
```

```python
import functools

import jax
import jax.numpy as jnp
from jax import lax
from jax.experimental import pallas as pl
from jax.experimental.pallas import tpu as pltpu
from jax.sharding import PartitionSpec as P

CONV = 4
MATES = 4
SMALL = 16


epsilon = 1e-06
low = jnp.bfloat16
wide = jnp.float32


def other_core(value):
    return lax.ppermute(value, "tp", [(0, 1), (1, 0)])


def to_mate(value, flip):
    count = lax.axis_size("seq")
    return lax.ppermute(value, "seq", [(source, source ^ flip) for source in range(count)])


def mate_of():
    return lax.axis_index("seq") % MATES


def line_of():
    return lax.axis_index("seq") // MATES


def line_groups():
    lines = lax.axis_size("seq") // MATES
    return [[mate + MATES * line for line in range(lines)] for mate in range(MATES)]


def pick(blocks, index):
    return lax.dynamic_index_in_dim(blocks, index, 0, False)


def in_order(by_flip):
    mate = mate_of()
    out = jnp.zeros((MATES,) + by_flip[0].shape, by_flip[0].dtype)
    for flip, piece in enumerate(by_flip):
        out = lax.dynamic_update_index_in_dim(out, piece, mate ^ flip, 0)
    return out


def swap_blocks(blocks):
    mate = mate_of()
    pieces = [pick(blocks, mate)]
    for flip in range(1, MATES):
        pieces.append(to_mate(pick(blocks, mate ^ flip), flip))
    return in_order(pieces)


def gather_lines(block):
    return lax.all_gather(block, "seq", axis_index_groups=line_groups())


def scatter_lines(blocks):
    return lax.psum_scatter(blocks, "seq", scatter_dimension=0, axis_index_groups=line_groups())


def matmul(form, left, right):
    return jnp.einsum(form, left, right, preferred_element_type=wide)


def silu_slope(value):
    squash = jax.nn.sigmoid(value)
    return squash * (1.0 + value * (1.0 - squash))


CHUNK = 128
TOGETHER = 4
VMEM_BYTES = 58 * 1024 * 1024
NN = (((1,), (0,)), ((), ()))
NT = (((1,), (1,)), ((), ()))


def dot(left, right, dims):
    return lax.dot_general(left, right, dims, preferred_element_type=wide)


def pair(value):
    high = value.astype(low)
    return high, (value - high.astype(wide)).astype(low)


def side(left, right):
    return jnp.concatenate([left, right], axis=1)


def over(top, bottom):
    return jnp.concatenate([top, bottom], axis=0)


def nn(left, right):
    width = right[0].shape[1]
    both = side(*right)
    out = dot(side(*left), over(both, both), NN)
    return out[:, :width] + out[:, width:]


def nt(left, right):
    width = right[0].shape[0]
    out = dot(side(*left), over(side(right[0], right[0]), side(right[1], right[1])), NT)
    return out[:, :width] + out[:, width:]


def nn_wide(left, right):
    return dot(side(*left), over(right[0], right[0]), NN) + dot(left[0], right[1], NN)


def nn_low(left, right):
    return dot(side(*left), over(right, right), NN)


def low_nn(left, right):
    return dot(side(left, left), over(*right), NN)


def low_nt(left, right):
    return dot(side(left, left), side(*right), NT)


def grid_of_rows():
    rows = lax.broadcasted_iota(jnp.int32, (CHUNK, CHUNK), 0)
    columns = lax.broadcasted_iota(jnp.int32, (CHUNK, CHUNK), 1)
    return rows, columns


def inverse_of(strict):
    rows, columns = grid_of_rows()
    one = jnp.where(rows == columns, 1.0, 0.0).astype(wide)

    def joining(shift):
        upper = columns >> shift
        return ((rows >> shift) == upper + 1) & ((upper & 1) == 0)

    solved = [one - jnp.where(joining(0), s, 0.0) for s in strict]
    shift = 1
    while (1 << shift) < CHUNK:
        mask = joining(shift)
        pairs = [pair(d) for d in solved]
        crossed = [nn(pair(jnp.where(mask, s, 0.0)), p) for s, p in zip(strict, pairs)]
        solved = [d - nn(p, pair(c)) for d, p, c in zip(solved, pairs, crossed)]
        shift += 1
    return solved


def convolved(block, taps, stream):
    columns = block[:, stream * CHUNK : (stream + 1) * CHUNK]
    total = None
    for offset in range(CONV):
        first = 16 - (CONV - 1) + offset
        term = taps[stream * CONV + offset][None, :] * columns[first : first + CHUNK]
        total = term if total is None else total + term
    return total


def silu_parts(value):
    squash = jax.nn.sigmoid(value)
    return value * squash, squash * (1.0 + value * (1.0 - squash))


def live_rows(limit, start):
    rows = lax.broadcasted_iota(jnp.int32, (CHUNK, CHUNK), 0)
    return jnp.where(rows + start < limit, 1.0, 0.0).astype(wide)


def head_squash(logits, head):
    lanes = lax.broadcasted_iota(jnp.int32, logits.shape, 1)
    column = jnp.sum(jnp.where(lanes == head, logits, 0.0), axis=1, keepdims=True)
    return jax.nn.sigmoid(jnp.broadcast_to(column, logits.shape))


def front_kernel(
    lines, heads, moves, limit_ref, raw_any, raw_ref, taps_ref, logit_ref, gate_ref, scale_ref, *rest,
):
    count = len(moves)
    outs = rest[count:]
    qkv_ref, solved_ref, wu_ref, map_ref, total_ref, tails_ref = outs[:6]
    state_ref, fresh_ref, mixed_ref, gated_ref, gathered, weights = outs[6:12]
    targets, scratch = outs[12 : 12 + count], outs[12 + count :]
    ext, offsets, maps, prefixes, locals_, wus, qkvs, enters, leaves, tails = scratch[:10]
    tail_sems, state_sems, gateds = scratch[10:13]
    scratch = scratch[13:]
    step = pl.program_id(0)
    chains, chunks = maps.shape[0], maps.shape[1]
    span = chunks * CHUNK
    head_size = CHUNK
    streams = 3 * heads * head_size
    place = Place()
    tokens = gathered.shape[2]
    share = ShareRows(place, targets[0], weights, scratch[:3])
    swap = SwapBlocks(
        place,
        lambda slot, mate: gateds.at[slot, pl.ds(pl.multiple_of(mate * tokens, 16), tokens)],
        gathered,
        scratch[3:6],
    )
    gathers = [
        GatherLines(place, None, target, scratch[6 + 6 * index : 12 + 6 * index], moves[index])
        for index, target in enumerate(targets)
        if moves[index]
    ]
    below, above = place.line > 0, place.line < lines - 1
    rows, columns = grid_of_rows()
    identity = jnp.where(rows == columns, 1.0, 0.0).astype(wide)

    def tail(seq):
        return pltpu.make_async_remote_copy(
            src_ref=raw_any.at[pl.ds((seq + 1) * span - 16, 16), pl.ds(0, streams)],
            dst_ref=tails.at[seq],
            send_sem=tail_sems.at[0, seq],
            recv_sem=tail_sems.at[1, seq],
            device_id=place.lines_away(1),
            device_id_type=MESH,
        )

    state_copy = pltpu.make_async_remote_copy(
        src_ref=leaves,
        dst_ref=enters,
        send_sem=state_sems.at[0],
        recv_sem=state_sems.at[1],
        device_id=place.lines_away(1),
        device_id_type=MESH,
    )
    seqs = chains // heads

    @pl.when(step == 0)
    def _():
        meet(place, lines=lines, cores=True)
        for seq in range(seqs):
            pl.when(above)(tail(seq).start)
        for gather in gathers:
            gather.leave(False)
        for seq in range(seqs):

            @pl.when(below)
            def _(seq=seq):
                tail(seq).wait_recv()

            @pl.when(place.line == 0)
            def _(seq=seq):
                tails[seq] = jnp.zeros(tails.shape[1:], low)

        tails_ref[...] = tails[...]

    def form(chain):
        seq, head = chain // heads, chain % heads
        ext[:16] = tails[seq, :, pl.ds(pl.multiple_of(head * 3 * head_size, 128), 3 * head_size)].astype(wide)
        ext[16:] = raw_ref[...].astype(wide)
        taps = taps_ref[0]
        limit = limit_ref[seq]

        def group(index, carry):
            first = index * TOGETHER
            parts = []
            for number in range(TOGETHER):
                start = pl.multiple_of((first + number) * CHUNK, CHUNK)
                block = ext[pl.ds(start, CHUNK + 16)]
                query = jax.nn.silu(convolved(block, taps, 0))
                key = jax.nn.silu(convolved(block, taps, 1))
                value = jax.nn.silu(convolved(block, taps, 2)).astype(low)
                query = query * lax.rsqrt(jnp.sum(query * query, axis=1, keepdims=True) + epsilon)
                query = (query * head_size ** (-0.5)).astype(low)
                key = key * lax.rsqrt(jnp.sum(key * key, axis=1, keepdims=True) + epsilon)
                key = key.astype(low)
                beta = head_squash(logit_ref[pl.ds(start, CHUNK)], head) * live_rows(limit, start)
                together = jnp.concatenate([query, key, value], axis=1)
                qkv_ref[pl.ds(start, CHUNK)] = together
                qkvs[chain, pl.ds(start, CHUNK)] = together
                parts.append((key, value, beta))
            strict = [
                jnp.where(rows > columns, beta * dot(key, key, NT), 0.0) for key, _, beta in parts
            ]
            solved = inverse_of(strict)
            for number in range(TOGETHER):
                key, value, beta = parts[number]
                solved_ref[0, first + number] = solved[number]
                weighted = pair(solved[number] * beta.T)
                both = nn_low(weighted, side(key, value))
                wu_ref[0, first + number] = both
                wus[chain, first + number] = both
                moved = low_nn(key.T, pair(both))
                step_map = identity - moved[:, :head_size]
                map_ref[0, first + number] = step_map
                maps[chain, first + number] = step_map
                offsets[chain, first + number] = moved[:, head_size:]
            return carry

        lax.fori_loop(0, chunks // TOGETHER, group, 0)

    @pl.when((step == 1) & (step < chains))
    def _():
        for gather in gathers[:1]:
            gather.onwards(1)

    @pl.when((step == 2) & (step < chains))
    def _():
        for gather in gathers[:1]:
            gather.onwards(2)

    @pl.when(step < chains)
    def _():
        form(step)

    @pl.when(step == chains - 2)
    def _():
        for gather in gathers[:1]:
            for number in range(3, lines):
                gather.onwards(number)
        share.begin_half(False)
        share.begin_half(True)
        share.begin_rest()
        for gather in gathers[1:]:
            gather.onwards(1)

    @pl.when(step == chains - 1)
    def _():
        start = side(identity, jnp.zeros_like(identity))

        def advance(chunk, states):
            out = []
            for index in range(chains):
                state = states[index]
                prefixes[index, chunk] = state[:, :head_size]
                locals_[index, chunk] = state[:, head_size:]
                moved = nn_wide(pair(maps[index, chunk]), pair(state))
                out.append(
                    side(moved[:, :head_size], moved[:, head_size:] + offsets[index, chunk])
                )
            return tuple(out)

        ends = lax.fori_loop(0, chunks, advance, (start,) * chains)

        @pl.when(below)
        def _():
            state_copy.wait_recv()

        @pl.when(place.line == 0)
        def _():
            enters[...] = jnp.zeros_like(enters)

        for index in range(chains):
            total_ref[index] = ends[index][:, :head_size]
            leaving = nn_low(pair(ends[index][:, :head_size]), enters[index])
            leaves[index] = (leaving + ends[index][:, head_size:]).astype(low)
        pl.when(above)(state_copy.start)

    def outputs(chain):
        enter = enters[chain]
        scale = scale_ref[...]

        def group(index, carry):
            for number in range(TOGETHER):
                chunk = index * TOGETHER + number
                start = pl.multiple_of(chunk * CHUNK, CHUNK)
                here = pl.ds(start, CHUNK)
                state = nn_low(pair(prefixes[chain, chunk]), enter) + locals_[chain, chunk]
                state_ref[0, chunk] = state
                states = pair(state)
                both = wus[chain, chunk]
                fresh = both[:, head_size:] - nn(pair(both[:, :head_size]), states)
                fresh_ref[0, chunk] = fresh
                query = qkvs[chain, here, :head_size]
                key = qkvs[chain, here, head_size : 2 * head_size]
                scores = jnp.where(rows >= columns, dot(query, key, NT), 0.0)
                mixed = low_nn(query, states) + nn(pair(scores), pair(fresh))
                mixed_ref[here] = mixed
                inverse = lax.rsqrt(jnp.mean(mixed * mixed, axis=1, keepdims=True) + epsilon)
                normed = mixed * inverse * scale
                gated = (normed * jax.nn.silu(gate_ref[here].astype(wide))).astype(low)
                gated_ref[here] = gated
                lanes = pl.ds(pl.multiple_of(chain % heads * head_size, 128), head_size)
                gateds[chain // heads, here, lanes] = gated
            return carry

        lax.fori_loop(0, chunks // TOGETHER, group, 0)

    @pl.when(step >= chains)
    def _():
        outputs(step - chains)

    @pl.when(step == chains + heads - 1)
    def _():
        swap.begin(0)
        share.forward()

    @pl.when(step == 2 * chains - 2)
    def _():
        for gather in gathers[1:]:
            gather.onwards(2)

    @pl.when(step == 2 * chains - 1)
    def _():
        swap.begin(1)
        share.forward_far()
        for gather in gathers[1:]:
            for number in range(3, lines):
                gather.onwards(number)
        for gather in gathers:
            gather.finish_lines()
        share.finish()
        swap.finish()
        for seq in range(seqs):
            pl.when(above)(tail(seq).wait_send)
        pl.when(above)(state_copy.wait_send)


def back_kernel(
    lines, heads, parts, limit_ref, raw_ref, tails_ref, taps_ref, logit_ref, gate_ref, scale_ref, qkv_ref,
    wu_ref, map_ref, total_ref, grad_ref, mixed_ref, solved_ref, state_ref, fresh_in_ref, row_grad, *rest,
):
    count = len(parts)
    blocks, rest = rest[:count], rest[count:]
    all_ref, gain_ref, taps_grad_ref, row_grads = rest[:4]
    results, scratch = rest[4 : 4 + count], rest[4 + count :]
    ext, pre_grads, maps, sources, out_grads, fresh_grads, leaving, leaves, enters = scratch[:9]
    halos, edges, returned, halo_sems, state_sems = scratch[9:14]
    share_scratch, scratch = scratch[14:17], scratch[17:]
    step = pl.program_id(0)
    chains, chunks = maps.shape[0], maps.shape[1]
    span = chunks * CHUNK
    head_size = CHUNK
    streams = 3 * heads * head_size
    place = Place()
    sums = [
        SumLines(place, blocks[index], results[index], scratch[7 * index : 7 * index + 7], first)
        for index, (first, _) in enumerate(parts)
    ]
    share = ShareRows(place, row_grad, row_grads, share_scratch)
    below, above = place.line > 0, place.line < lines - 1
    rows, columns = grid_of_rows()

    def halo(chain):
        return pltpu.make_async_remote_copy(
            src_ref=halos.at[chain],
            dst_ref=returned.at[chain],
            send_sem=halo_sems.at[0, chain],
            recv_sem=halo_sems.at[1, chain],
            device_id=place.lines_away(-1),
            device_id_type=MESH,
        )

    state_copy = pltpu.make_async_remote_copy(
        src_ref=enters,
        dst_ref=leaves,
        send_sem=state_sems.at[0],
        recv_sem=state_sems.at[1],
        device_id=place.lines_away(-1),
        device_id_type=MESH,
    )

    @pl.when(step == 0)
    def _():
        meet(place, far=bool(parts), lines=lines)
        share.begin_half(False)
        share.begin_half(True)
        share.begin_rest()
        for each in sums:
            each.begin()
        for each in sums:
            each.wait_loads()
            each.round(1)

    def turn(chain):
        scale = scale_ref[...]

        def group(index, gain):
            for number in range(TOGETHER):
                chunk = index * TOGETHER + number
                start = pl.multiple_of(chunk * CHUNK, CHUNK)
                here = pl.ds(start, CHUNK)
                grad, mixed = grad_ref[here].astype(wide), mixed_ref[here]
                silu_gate, slope = silu_parts(gate_ref[here].astype(wide))
                inverse = lax.rsqrt(jnp.mean(mixed * mixed, axis=1, keepdims=True) + epsilon)
                unit = mixed * inverse
                gate_grad = (grad * unit * scale * slope).astype(low)
                there = pl.ds(pl.multiple_of(chain // heads * span + start, CHUNK), CHUNK)
                lanes = pl.ds(pl.multiple_of(streams + chain % heads * head_size, 128), head_size)
                all_ref[there, lanes] = gate_grad
                passed = grad * silu_gate
                gain = gain + jnp.sum(passed * unit, axis=0, keepdims=True)
                scaled = passed * scale
                mixed_grad = inverse * (
                    scaled - unit * inverse * jnp.mean(scaled * mixed, axis=1, keepdims=True)
                )
                out_grads[chain, chunk] = mixed_grad
                query, key = qkv_ref[here, :head_size], qkv_ref[here, head_size : 2 * head_size]
                scores = jnp.where(rows >= columns, dot(query, key, NT), 0.0)
                turned = jnp.where(rows <= columns, dot(key, query, NT), 0.0)
                grads = pair(mixed_grad)
                fresh_grads[chain, chunk] = nn(pair(turned), grads)
                reading = query.astype(wide) - nn(
                    pair(scores), pair(wu_ref[0, chunk, :, :head_size])
                )
                sources[chain, chunk] = nn(pair(mixed_grad.T), pair(reading))
                maps[chain, chunk] = map_ref[0, chunk]
            return gain

        gain = lax.fori_loop(0, chunks // TOGETHER, group, jnp.zeros((1, head_size), wide))
        gain_ref[0] = jnp.broadcast_to(gain, (8, head_size))

    @pl.when(step < chains)
    def _():
        turn(step)

    @pl.when(step == chains - 1)
    def _():
        def advance(number, states):
            chunk = chunks - 1 - number
            return tuple(
                nn(pair(states[index]), pair(maps[index, chunk])) + sources[index, chunk]
                for index in range(chains)
            )

        ends = lax.fori_loop(
            0, chunks, advance, (jnp.zeros((head_size, head_size), wide),) * chains
        )

        @pl.when(above)
        def _():
            state_copy.wait_recv()

        @pl.when(place.line == lines - 1)
        def _():
            leaves[...] = jnp.zeros_like(leaves)

        for index in range(chains):
            entering = low_nn(leaves[index], pair(total_ref[index]))
            enters[index] = (entering + ends[index]).astype(low)
        pl.when(below)(state_copy.start)

        def again(number, states):
            chunk = chunks - 1 - number
            out = []
            for index in range(chains):
                leaving[index, chunk] = states[index]
                out.append(
                    nn(pair(states[index]), pair(maps[index, chunk])) + sources[index, chunk]
                )
            return tuple(out)

        lax.fori_loop(
            0, chunks, again, tuple(leaves[index].astype(wide) for index in range(chains))
        )
        for each in sums:
            each.round(2)

    def unwind(chain):
        seq, head = chain // heads, chain % heads
        ext[:16] = tails_ref[seq, :, pl.ds(pl.multiple_of(head * 3 * head_size, 128), 3 * head_size)].astype(wide)
        ext[16:] = raw_ref[...].astype(wide)
        taps = taps_ref[0]
        limit = limit_ref[seq]
        pre_grads[:16] = jnp.zeros((16, 3 * head_size), wide)
        pre_grads[span + 16 :] = jnp.zeros((16, 3 * head_size), wide)

        def one(chunk):
            start = pl.multiple_of(chunk * CHUNK, CHUNK)
            here = pl.ds(start, CHUNK)
            query = qkv_ref[here, :head_size]
            key = qkv_ref[here, head_size : 2 * head_size]
            value = qkv_ref[here, 2 * head_size :]
            live = live_rows(limit, start)
            squash = head_squash(logit_ref[here], head)
            beta = squash * live
            grads = pair(out_grads[chain, chunk])
            fresh = pair(fresh_in_ref[0, chunk])
            state = pair(state_ref[0, chunk])
            leave = pair(leaving[chain, chunk])
            both = wu_ref[0, chunk]
            fresh_grad = fresh_grads[chain, chunk] + low_nt(key, leave)
            fresh_pair = pair(fresh_grad)
            score_grad = jnp.where(rows >= columns, nt(grads, fresh), 0.0)
            turned_grad = jnp.where(rows <= columns, nt(fresh, grads), 0.0)
            query_grad = nt(grads, state) + nn_low(pair(score_grad), key)
            key_grad = nn_low(pair(turned_grad), query) + nn(fresh, leave)
            wkey_grad = -nt(fresh_pair, state)
            right_grad = nn_wide(pair(solved_ref[0, chunk].T), pair(side(wkey_grad, fresh_grad)))
            right = pair(right_grad)
            twos = pair(both)
            found = dot(right[0], over(*twos), NT)
            system_grad = found[:, :CHUNK] + found[:, CHUNK:] + dot(right[1], twos[0], NT)
            system_grad = jnp.where(rows > columns, -system_grad, 0.0)
            gram = dot(key, key, NT)
            gram_grad = beta * system_grad
            key_grad = key_grad + nn_low(pair(gram_grad + gram_grad.T), key)
            key_right, value_right = right_grad[:, :head_size], right_grad[:, head_size:]
            key_grad = key_grad + beta * key_right
            value_grad = beta * value_right
            beta_grad = jnp.sum(
                key_right * key.astype(wide) + value_right * value.astype(wide) + system_grad * gram,
                axis=1,
                keepdims=True,
            )
            lanes = lax.broadcasted_iota(jnp.int32, (CHUNK, head_size), 1)
            logit_grad = jnp.where(
                lanes == head, beta_grad * (live * squash * (1.0 - squash)), 0.0
            ).astype(low)

            there = pl.ds(pl.multiple_of(seq * span + start, CHUNK), CHUNK)
            last_lanes = pl.ds(streams + heads * head_size, head_size)

            @pl.when(head == 0)
            def _():
                all_ref[there, last_lanes] = logit_grad

            @pl.when(head > 0)
            def _():
                all_ref[there, last_lanes] = all_ref[there, last_lanes] + logit_grad

            block = ext[pl.ds(start, CHUNK + 16)]
            grads_pre = []
            for stream, grad in enumerate((query_grad, key_grad, value_grad)):
                act, slope = silu_parts(convolved(block, taps, stream))
                if stream < 2:
                    inverse = lax.rsqrt(jnp.sum(act * act, axis=1, keepdims=True) + epsilon)
                    inner = jnp.sum(act * grad, axis=1, keepdims=True)
                    grad = inverse * (grad - act * (inverse * inverse * inner))
                    if stream == 0:
                        grad = grad * head_size ** (-0.5)
                grads_pre.append(grad * slope)
            pre_grads[pl.ds(start + 16, CHUNK)] = jnp.concatenate(grads_pre, axis=1)

        def group(index, carry):
            for number in range(2):
                one(index * 2 + number)
            return carry

        lax.fori_loop(0, chunks // 2, group, 0)

        def back(block):
            parts = []
            for stream in range(3):
                part = block[:, stream * head_size : (stream + 1) * head_size]
                total = None
                for offset in range(CONV):
                    first = CONV - 1 - offset
                    term = taps[stream * CONV + offset][None, :] * part[first : first + CHUNK]
                    total = term if total is None else total + term
                parts.append(total)
            return jnp.concatenate(parts, axis=1)

        lanes = pl.ds(pl.multiple_of(head * 3 * head_size, 128), 3 * head_size)

        def finish(chunk, totals):
            start = pl.multiple_of(chunk * CHUNK, CHUNK)
            block = pre_grads[pl.ds(start + 16, CHUNK + 16)]
            grad = back(block)
            there = pl.ds(pl.multiple_of(seq * span + start, CHUNK), CHUNK)
            all_ref[there, lanes] = grad.astype(low)
            edges[chain] = grad[CHUNK - 16 :]
            before = ext[pl.ds(start, CHUNK + 16)]
            pre = block[:CHUNK]
            out = []
            for offset in range(CONV):
                first = 16 - (CONV - 1) + offset
                term = jnp.sum(pre * before[first : first + CHUNK], axis=0, keepdims=True)
                out.append(totals[offset] + term)
            return tuple(out)

        zero = jnp.zeros((1, 3 * head_size), wide)
        totals = lax.fori_loop(0, chunks, finish, (zero,) * CONV)
        for offset in range(CONV):
            taps_grad_ref[0, offset : offset + 1] = totals[offset]
        halos[chain] = back(pre_grads[: CHUNK + 32])[:16].astype(low)
        pl.when(below)(halo(chain).start)

    @pl.when(step >= chains)
    def _():
        unwind(step - chains)

    @pl.when(step == chains)
    def _():
        share.forward()

    @pl.when(step == 2 * chains - 3)
    def _():
        share.forward_far()
        for each in sums:
            each.round(3)

    @pl.when(step == 2 * chains - 1)
    def _():
        for each in sums:
            for number in range(4, lines):
                each.round(number)
            each.exchange()
        for chain in range(chains):
            seq, head = chain // heads, chain % heads
            last = pl.ds((seq + 1) * span - 16, 16)
            lanes = pl.ds(head * 3 * head_size, 3 * head_size)

            @pl.when(above)
            def _(chain=chain, last=last, lanes=lanes):
                halo(chain).wait_recv()
                all_ref[last, lanes] = (edges[chain] + returned[chain].astype(wide)).astype(low)

        for chain in range(chains):
            pl.when(below)(halo(chain).wait_send)
        pl.when(below)(state_copy.wait_send)
        share.finish()
        for each in sums:
            each.finish()


def project_kernel(input_ref, scale_ref, weight_ref, normed_ref, raw_ref, logit_ref):
    value = input_ref[...].astype(wide)
    normed = (value * inverse_rms(value) * scale_ref[...]).astype(low)
    normed_ref[...] = normed
    out = dot(normed, weight_ref[...], NN)
    width = raw_ref.shape[1]
    raw_ref[...] = out[:, :width].astype(low)
    logit_ref[...] = out[:, width:]


MESH = pl.DeviceIdType.MESH
STEP = 16


class Place:
    def __init__(self):
        self.seq = lax.axis_index("seq")
        self.core = lax.axis_index("tp")
        self.mate = self.seq % MATES
        self.line = self.seq // MATES
        x, y = self.mate % 2, self.mate // 2
        self.x = 2 * y + (1 - x)
        self.y = 2 * (1 - y) + x
        self.far = 2 * (1 - y) + (1 - x)
        self.base = self.seq - self.mate

    def of(self, mate, other=0):
        return (self.base + mate, 1 - self.core if other else self.core)

    @property
    def sibling(self):
        return (self.seq, 1 - self.core)

    def lines_away(self, step):
        return (self.seq + step * MATES, self.core)


def meet(place, far=False, lines=0, cores=False, straight=False):
    barrier = pltpu.get_barrier_semaphore()
    partners = [place.of(place.x), place.of(place.y), place.sibling]
    if far or cores:
        partners.append(place.of(place.far))
    if cores:
        partners += [place.of(mate, 1) for mate in (place.x, place.y, place.far)]
    for partner in partners:
        pl.semaphore_signal(barrier, inc=1, device_id=partner, device_id_type=MESH)
    count = len(partners)
    if straight:
        for step in range(1, lines):
            line = (place.line + step) % lines
            pl.semaphore_signal(
                barrier,
                inc=1,
                device_id=(line * MATES + place.mate, place.core),
                device_id_type=MESH,
            )
        count = count + max(lines - 1, 0)
    elif lines > 1:
        below, above = place.line > 0, place.line < lines - 1

        @pl.when(below)
        def _():
            pl.semaphore_signal(
                barrier, inc=1, device_id=place.lines_away(-1), device_id_type=MESH
            )

        @pl.when(above)
        def _():
            pl.semaphore_signal(barrier, inc=1, device_id=place.lines_away(1), device_id_type=MESH)

        count = count + jnp.where(below, 1, 0) + jnp.where(above, 1, 0)
    pl.semaphore_wait(barrier, count)


def sender(sems):
    send, receive = sems

    def make(index, source, target, device):
        return pltpu.make_async_remote_copy(
            src_ref=source,
            dst_ref=target,
            send_sem=send.at[index],
            recv_sem=receive.at[index],
            device_id=device,
            device_id_type=MESH,
        )

    return make


def row_steps(first, last, body):
    def one(step, carry):
        body(pl.ds(pl.multiple_of(first + step * STEP, STEP), STEP))
        return carry

    lax.fori_loop(0, (last - first) // STEP, one, 0)


class SumRows:
    SCRATCH = 4

    @staticmethod
    def scratch(rows, columns):
        return [
            pltpu.VMEM((MATES, rows, columns), low),
            pltpu.VMEM((MATES, rows, columns), low),
            pltpu.VMEM((2, rows // 2, columns), low),
            pltpu.VMEM((2, rows, columns), low),
            pltpu.SemaphoreType.DMA((MATES,)),
            pltpu.SemaphoreType.DMA((10,)),
            pltpu.SemaphoreType.DMA((10,)),
        ]

    def __init__(self, place, partial, scratch):
        self.place, self.partial = place, partial
        self.own, self.swapped, self.relay, self.arrived, self.local_sems, send, receive = scratch
        self.make = sender((send, receive))
        self.rows = self.own.shape[1]
        self.order = [place.far, place.x, place.y, place.mate]

    def begin(self):
        self.swaps, self.loads = [], []
        for slot, mate in enumerate(self.order):
            copy = self.make(
                slot, self.partial.at[1, mate], self.swapped.at[slot], self.place.sibling
            )
            copy.start()
            self.swaps.append(copy)
            load = pltpu.make_async_copy(
                self.partial.at[0, mate], self.own.at[slot], self.local_sems.at[slot]
            )
            load.start()
            self.loads.append(load)

    def add(self, target, target_slot, source, source_slot, first, last, shift=0):
        def body(here):
            there = pl.ds(pl.multiple_of(here.start - shift, STEP), STEP) if shift else here
            target[target_slot, here] = (
                target[target_slot, here].astype(wide) + source[source_slot, there].astype(wide)
            ).astype(low)

        row_steps(first, last, body)

    def sum_cores(self, slot):
        self.loads[slot].wait()
        self.swaps[slot].wait_recv()
        self.add(self.own, slot, self.swapped, slot, 0, self.rows)

    def send_far(self):
        half = self.rows // 2
        self.sum_cores(0)
        self.far_low = self.make(
            4, self.own.at[0, :half], self.relay.at[0], self.place.of(self.place.y)
        )
        self.far_high = self.make(
            5, self.own.at[0, half:], self.relay.at[1], self.place.of(self.place.x)
        )
        self.far_low.start()
        self.far_high.start()

    def send_near(self):
        half, place = self.rows // 2, self.place
        self.sum_cores(1)
        self.x_high = self.make(
            6, self.own.at[1, half:], self.arrived.at[0, half:], place.of(place.x)
        )
        self.x_high.start()
        self.sum_cores(2)
        self.y_low = self.make(
            7, self.own.at[2, :half], self.arrived.at[1, :half], place.of(place.y)
        )
        self.y_low.start()

    def send_relayed(self):
        half, place = self.rows // 2, self.place
        self.far_low.wait_recv()
        self.add(self.own, 1, self.relay, 0, 0, half)
        self.x_low = self.make(
            8, self.own.at[1, :half], self.arrived.at[0, :half], place.of(place.x)
        )
        self.x_low.start()
        self.far_high.wait_recv()
        self.add(self.own, 2, self.relay, 1, half, self.rows, shift=half)
        self.y_high = self.make(
            9, self.own.at[2, half:], self.arrived.at[1, half:], place.of(place.y)
        )
        self.y_high.start()
        self.sum_cores(3)

    def wait_half(self, upper):
        if upper:
            self.x_high.wait_recv()
            self.y_high.wait_recv()
        else:
            self.x_low.wait_recv()
            self.y_low.wait_recv()

    def total(self, here):
        return (
            self.own[3, here].astype(wide)
            + self.arrived[0, here].astype(wide)
            + self.arrived[1, here].astype(wide)
        )

    def finish(self):
        for copy in self.swaps + [
            self.far_low, self.far_high, self.x_high, self.y_low, self.x_low, self.y_high,
        ]:
            copy.wait_send()


class ShareRows:
    @staticmethod
    def scratch():
        return [
            pltpu.SemaphoreType.DMA((1,)),
            pltpu.SemaphoreType.DMA((11,)),
            pltpu.SemaphoreType.DMA((11,)),
        ]

    def __init__(self, place, source, target, scratch):
        self.place, self.source, self.target = place, source, target
        self.local_sem, send, receive = scratch
        self.make = sender((send, receive))
        self.rows = target.shape[2]

    def copy(self, index):
        place, half = self.place, self.rows // 2
        lower, upper, whole = pl.ds(0, half), pl.ds(half, half), pl.ds(0, self.rows)
        x, y, sibling = place.of(place.x), place.of(place.y), place.sibling

        def own(rows, device, side=0):
            return self.source.at[rows], self.target.at[side, place.mate, rows], device

        def passed(mate, rows, device, side=0):
            return self.target.at[0, mate, rows], self.target.at[side, mate, rows], device

        return self.make(
            index,
            *(
                lambda: own(upper, y),
                lambda: own(upper, x),
                lambda: own(lower, x),
                lambda: own(lower, y),
                lambda: passed(place.x, lower, y),
                lambda: passed(place.y, upper, x),
                lambda: own(whole, sibling, 1),
                lambda: passed(place.x, whole, sibling, 1),
                lambda: passed(place.y, whole, sibling, 1),
                lambda: passed(place.far, lower, sibling, 1),
                lambda: passed(place.far, upper, sibling, 1),
            )[index](),
        )

    def local(self):
        return pltpu.make_async_copy(
            self.source, self.target.at[0, self.place.mate], self.local_sem.at[0]
        )

    def begin_half(self, upper):
        for index in (0, 1) if upper else (2, 3):
            self.copy(index).start()

    def begin_rest(self):
        self.local().start()
        self.copy(6).start()

    def forward(self):
        for came, then in ((2, 4), (0, 5), (1, 7), (3, 8)):
            self.copy(came).wait_recv()
            self.copy(then).start()

    def forward_far(self):
        for came, then in ((4, 9), (5, 10)):
            self.copy(came).wait_recv()
            self.copy(then).start()

    def finish(self):
        self.local().wait()
        for index in range(6, 11):
            self.copy(index).wait_recv()
        for index in range(11):
            self.copy(index).wait_send()


class GatherLines:
    @staticmethod
    def scratch(lines):
        return [
            pltpu.SemaphoreType.DMA((1,)),
            pltpu.SemaphoreType.DMA((3,)),
            pltpu.SemaphoreType.DMA((3,)),
            pltpu.SemaphoreType.DMA((lines, MATES)),
            pltpu.SemaphoreType.DMA((lines, MATES)),
            pltpu.SemaphoreType.DMA((lines, MATES)),
        ]

    def __init__(self, place, blocks, target, scratch, rows=None):
        self.place, self.blocks, self.target = place, blocks, target
        self.lines = target.shape[0]
        self.part = pl.ds(*(rows or (0, target.shape[2])))
        self.local_sem, send, receive, self.up_sem, self.down_sem, self.got = scratch
        self.make = sender((send, receive))
        self.order = [place.mate, place.x, place.y, place.far]

    def plane(self, slot):
        place, mate = self.place, self.order[slot]
        here = self.target.at[place.line, place.mate]
        if slot == 0:
            return pltpu.make_async_copy(self.blocks.at[mate], here, self.local_sem.at[0])
        return self.make(slot - 1, self.blocks.at[mate], here, place.of(mate))

    def begin(self):
        for slot in range(MATES):
            self.plane(slot).start()

    def arrive(self, slot):
        copy = self.plane(slot)
        copy.wait_recv() if slot else copy.wait()

    def hop(self, step, mate, direction):
        place = self.place
        line = place.line - step * direction
        piece = self.target.at[line, mate, self.part]
        sems = self.up_sem if direction > 0 else self.down_sem
        copy = pltpu.make_async_remote_copy(
            src_ref=piece,
            dst_ref=piece,
            send_sem=sems.at[step, mate],
            recv_sem=self.got.at[line, mate],
            device_id=place.lines_away(direction),
            device_id_type=MESH,
        )
        came = (line >= 0) & (line < self.lines)
        goes = (place.line < self.lines - 1) if direction > 0 else (place.line > 0)
        return copy, came, goes

    def leave(self, arriving=True):
        for slot, mate in enumerate(self.order):
            if arriving:
                self.arrive(slot)
            for direction in (1, -1):
                copy, _, goes = self.hop(0, mate, direction)
                pl.when(goes)(copy.start)

    def onwards(self, step):
        if step >= self.lines:
            return
        for mate in self.order:
            for direction in (1, -1):
                copy, came, goes = self.hop(step, mate, direction)
                pl.when(came)(copy.wait_recv)
                if step < self.lines - 1:
                    pl.when(came & goes)(copy.start)

    def finish_plane(self):
        for slot in range(1, MATES):
            self.plane(slot).wait_send()

    def finish_lines(self):
        for step in range(self.lines - 1):
            for mate in self.order:
                for direction in (1, -1):
                    copy, came, goes = self.hop(step, mate, direction)
                    pl.when(came & goes)(copy.wait_send)


class SwapBlocks:
    @staticmethod
    def scratch():
        return [
            pltpu.SemaphoreType.DMA((1,)),
            pltpu.SemaphoreType.DMA((2 * MATES,)),
            pltpu.SemaphoreType.DMA((2 * MATES,)),
        ]

    def __init__(self, place, piece, target, scratch):
        self.place, self.piece, self.target = place, piece, target
        self.local_sem, send, receive = scratch
        self.make = sender((send, receive))
        self.order = [place.far, place.x, place.y, place.mate]

    def copy(self, slot, index):
        place, mate = self.place, self.order[index]
        source, target = self.piece(slot, mate), self.target.at[slot, place.mate]
        if slot == 0 and index == MATES - 1:
            return pltpu.make_async_copy(source, target, self.local_sem.at[0]), True
        return self.make(slot * MATES + index, source, target, place.of(mate, slot)), False

    def begin(self, slot, index=None):
        for each in range(MATES) if index is None else (index,):
            self.copy(slot, each)[0].start()

    def finish(self):
        for slot in range(2):
            for index in range(MATES):
                self.copy(slot, index)[0].wait()


class SumLines:
    @staticmethod
    def scratch(lines, shape):
        return [
            pltpu.VMEM((lines,) + shape, low),
            pltpu.VMEM((2, max(lines - 1, 1)) + shape, low),
            pltpu.SemaphoreType.DMA((lines + 1,)),
            pltpu.SemaphoreType.DMA((2, lines)),
            pltpu.SemaphoreType.DMA((2, lines)),
            pltpu.SemaphoreType.DMA((3,)),
            pltpu.SemaphoreType.DMA((3,)),
        ]

    def __init__(self, place, blocks, result, scratch, first=0):
        self.place, self.blocks, self.result, self.first = place, blocks, result, first
        self.held, self.came, self.local_sems, self.send, self.got, send, receive = scratch
        self.lines = self.held.shape[0]
        self.make = sender((send, receive))

    def load(self, line):
        return pltpu.make_async_copy(
            self.blocks.at[line, :, pl.ds(self.first, self.held.shape[2])],
            self.held.at[line],
            self.local_sems.at[line],
        )

    def begin(self):
        for line in range(self.lines):
            self.load(line).start()

    def wait_loads(self):
        for line in range(self.lines):
            self.load(line).wait()

    def put_gains(self, gains):
        lines, mates, height, lanes = self.held.shape
        top = lax.broadcasted_iota(jnp.int32, (height, lanes), 0) == 0
        for line in range(lines):
            for mate in range(mates):
                first = (line * mates + mate) * lanes
                part = jnp.broadcast_to(gains[:, first : first + lanes], (height, lanes))
                self.held[line, mate] = jnp.where(
                    top, part, self.held[line, mate].astype(wide)
                ).astype(low)

    def add_top(self, other, count):
        lines, mates, height, lanes = self.held.shape
        top = lax.broadcasted_iota(jnp.int32, (height, lanes), 0) < count
        for line in range(lines):
            for mate in range(mates):
                own = self.held[line, mate].astype(wide)
                both = own + other[line, mate].astype(wide)
                self.held[line, mate] = jnp.where(top, both, own).astype(low)

    def copy(self, turn, way):
        direction = 1 - 2 * way
        line = self.place.line + direction * (self.lines - turn)
        return line, pltpu.make_async_remote_copy(
            src_ref=self.held.at[line],
            dst_ref=self.came.at[way, turn - 1],
            send_sem=self.send.at[way, turn],
            recv_sem=self.got.at[way, turn],
            device_id=self.place.lines_away(direction),
            device_id_type=MESH,
        )

    def arrival(self, turn, way):
        slot = self.came.at[way, turn - 1]
        return pltpu.make_async_remote_copy(
            src_ref=slot,
            dst_ref=slot,
            send_sem=self.send.at[way, turn],
            recv_sem=self.got.at[way, turn],
            device_id=self.place.sibling,
            device_id_type=MESH,
        )

    def sends(self, turn, way):
        line = self.place.line
        return line <= turn - 1 if way == 0 else line >= self.lines - turn

    def inner(self, way):
        return self.place.line >= 1 if way == 0 else self.place.line <= self.lines - 2

    def add(self, line, way, turn):
        def mates(mate, carry):
            def body(here):
                self.held[line, mate, here] = (
                    self.held[line, mate, here].astype(wide)
                    + self.came[way, turn - 1, mate, here].astype(wide)
                ).astype(low)

            row_steps(0, self.held.shape[2], body)
            return carry

        lax.fori_loop(0, self.held.shape[1], mates, 0)

    def round(self, turn):
        if turn >= self.lines:
            return
        for way in (0, 1):
            line, copy = self.copy(turn, way)

            @pl.when(self.sends(turn, way))
            def _(line=line, copy=copy, way=way):
                if turn > 1:

                    @pl.when(self.inner(way))
                    def _():
                        self.arrival(turn - 1, way).wait_recv()
                        self.add(line, way, turn - 1)

                copy.start()

    def plane(self, index):
        place = self.place
        mate = (place.x, place.y, place.far)[index]
        return self.make(
            index, self.held.at[place.line, mate], self.result.at[place.mate], place.of(mate)
        )

    def local(self):
        place = self.place
        return pltpu.make_async_copy(
            self.held.at[place.line, place.mate],
            self.result.at[place.mate],
            self.local_sems.at[self.lines],
        )

    def exchange(self):
        for way in (0, 1):
            if self.lines > 1:

                @pl.when(self.inner(way))
                def _(way=way):
                    self.arrival(self.lines - 1, way).wait_recv()
                    self.add(self.place.line, way, self.lines - 1)

        for index in range(3):
            self.plane(index).start()
        self.local().start()

    def straight(self, step):
        line = (self.place.line + step) % self.lines
        return pltpu.make_async_remote_copy(
            src_ref=self.held.at[line],
            dst_ref=self.came.at[0, step - 1],
            send_sem=self.send.at[0, step],
            recv_sem=self.got.at[0, step],
            device_id=(line * MATES + self.place.mate, self.place.core),
            device_id_type=MESH,
        )

    def direct(self):
        for step in range(1, self.lines):
            self.straight(step).start()

    def exchange_direct(self):
        for step in range(1, self.lines):
            self.straight(step).wait_recv()
            self.add(self.place.line, 0, step)
        for index in range(3):
            self.plane(index).start()
        self.local().start()

    def finish(self, direct=False):
        self.local().wait()
        for index in range(3):
            self.plane(index).wait()
        if direct:
            for step in range(1, self.lines):
                self.straight(step).wait_send()
            return
        for turn in range(1, self.lines):
            for way in (0, 1):
                _, copy = self.copy(turn, way)
                pl.when(self.sends(turn, way))(copy.wait_send)


def remote_call(body, identity, ins, outs, scratch, aliases=None):
    anywhere = pl.BlockSpec(memory_space=pl.ANY)
    held = pl.BlockSpec(memory_space=pltpu.VMEM)
    return pl.pallas_call(
        body,
        in_specs=[anywhere if kind == "any" else held for _, kind in ins],
        out_specs=[anywhere if kind == "any" else held for _, _, kind in outs],
        out_shape=[jax.ShapeDtypeStruct(shape, dtype) for shape, dtype, _ in outs],
        scratch_shapes=scratch,
        input_output_aliases=aliases or {},
        compiler_params=pltpu.CompilerParams(
            vmem_limit_bytes=VMEM_BYTES, collective_id=identity, has_side_effects=True
        ),
    )(*[array for array, _ in ins])


def inverse_rms(value):
    return lax.rsqrt(jnp.mean(value * value, axis=1, keepdims=True) + epsilon)


def norm_back_rows(grad, source, scale):
    inverse = inverse_rms(source)
    scaled = grad * scale
    unit = source * inverse
    inner = jnp.mean(scaled * source, axis=1, keepdims=True)
    return inverse * (scaled - unit * (inverse * inner)), grad * unit


def load_weights(weights, held, sems):
    return [
        pltpu.make_async_copy(weights.at[slot, mate], held.at[slot, mate], sems.at[slot, mate])
        for slot in range(2)
        for mate in range(MATES)
    ]


def middle_kernel(lines, moves, gathered, weights, input_ref, scale_ref, grad_any, *rest):
    place = Place()
    count = len(moves)
    middle_ref, shared, grads = rest[count : count + 3]
    targets, scratch = rest[count + 3 : 2 * count + 3], rest[2 * count + 3 :]
    normed, held, weight_sems = scratch[:3]
    share = ShareRows(place, normed, shared, scratch[3:6])
    other = ShareRows(place, grad_any.at[place.core], grads, scratch[6:9])
    gathers = [
        GatherLines(place, None, target, scratch[9 + 6 * index : 15 + 6 * index], moves[index])
        for index, target in enumerate(targets)
    ]
    meet(place, lines=lines if moves else 0)
    loads = load_weights(weights, held, weight_sems)
    for load in loads:
        load.start()
    for gather in gathers:
        gather.leave(False)
    for load in loads:
        load.wait()
    rows = normed.shape[0]
    half = rows // 2
    _, _, all_lines, _, depth, width = held.shape

    height = MATES * depth
    some = max(1, 512 // height)

    def product(step, carry):
        columns = pl.ds(pl.multiple_of(step * some * height, 128), some * height)
        part = pl.ds(step * some, some)
        for first in (0, half):
            total = None
            for slot in range(2):
                for mate in range(MATES):
                    term = dot(
                        gathered[slot, mate, first : first + half],
                        held[slot, mate, part].reshape(some * height, width),
                        NT,
                    )
                    total = term if total is None else total + term
            here = pl.ds(first, half)
            middle_ref[here, columns] = input_ref[here, columns].astype(wide) + total
        return carry

    def body(here):
        middle = middle_ref[here]
        normed[here] = (middle * inverse_rms(middle) * scale_ref[...]).astype(low)

    lax.fori_loop(0, all_lines // some, product, 0)
    row_steps(0, half, body)
    share.begin_half(False)
    row_steps(half, rows, body)
    share.begin_half(True)
    share.begin_rest()
    for gather in gathers:
        gather.onwards(1)
    share.forward()
    other.begin_half(False)
    other.begin_half(True)
    other.begin_rest()
    share.forward_far()
    for gather in gathers:
        gather.onwards(2)
    other.forward()
    other.forward_far()
    for number in range(3, lines):
        for gather in gathers:
            gather.onwards(number)
    for gather in gathers:
        gather.finish_lines()
    share.finish()
    other.finish()


def turn_rows_kernel(
    lines, parts, partial, weights, middle_ref, grad_ref, scale_ref, *rest
):
    place = Place()
    count = len(parts)
    blocks, rest = rest[:count], rest[count:]
    middle_grad_ref, gain_ref, low_grad, gated_grads = rest[:4]
    results, scratch = rest[4 : 4 + count], rest[4 + count :]
    held, weight_sems, sent = scratch[:3]
    rows = SumRows(place, partial, scratch[3:10])
    swap = SwapBlocks(place, lambda slot, mate: sent.at[slot, mate], gated_grads, scratch[10:13])
    sums = [
        SumLines(place, blocks[index], results[index], scratch[13 + 7 * index : 20 + 7 * index], first)
        for index, (first, _) in enumerate(parts)
    ]
    meet(place, lines=lines if parts else 0, cores=True)
    rows.begin()
    for each in sums:
        each.begin()
    loads = load_weights(weights, held, weight_sems)
    for load in loads:
        load.start()
    gain_ref[...] = jnp.zeros_like(gain_ref)
    rows.send_far()
    for each in sums:
        each.wait_loads()
        each.round(1)
    rows.send_near()
    rows.send_relayed()
    for load in loads:
        load.wait()
    rows.wait_half(False)
    rows.wait_half(True)

    def body(here):
        part, gains = norm_back_rows(rows.total(here), middle_ref[here], scale_ref[...])
        total = grad_ref[here].astype(wide) + part
        middle_grad_ref[here] = total
        low_grad[here] = total.astype(low)
        gain_ref[...] += jnp.sum(gains, axis=0, keepdims=True)

    row_steps(0, low_grad.shape[0], body)
    _, _, all_lines, _, depth, width = held.shape
    for slot in range(2):
        for index, mate in enumerate(swap.order):
            weight = held[slot, mate].reshape(all_lines * MATES * depth, width)
            sent[slot, mate] = dot(low_grad[...], weight, NN).astype(low)
            swap.begin(slot, index)
    rows.finish()
    for each in sums:
        each.round(2)
        each.round(3)
    swap.finish()
    for each in sums:
        for number in range(4, lines):
            each.round(number)
        each.exchange()
    for each in sums:
        each.finish()


def last_rows_kernel(
    lines, pieces, partial, mlp_partial, input_ref, middle_ref, middle_grad_ref, scale_ref, *rest
):
    place = Place()
    blocks, rest = rest[:pieces], rest[pieces:]
    input_grad, block_output, gain_ref = rest[:3]
    results, scratch = rest[3 : 3 + pieces], rest[3 + pieces :]
    low_grad, low_output = scratch[:2]
    meet(place, far=bool(pieces), lines=lines if pieces else 0, straight=True)
    rows = SumRows(place, partial, scratch[2:9])
    outs = SumRows(place, mlp_partial, scratch[9:16])
    make = sender(scratch[16:18])
    local_sems = scratch[18]
    sums = [
        SumLines(place, blocks[index], results[index], scratch[19 + 7 * index : 26 + 7 * index])
        for index in range(pieces)
    ]
    whole = low_grad.shape[0]
    for each in sums:
        each.begin()
    rows.begin()
    outs.begin()
    for each in sums:
        each.wait_loads()
    for each in sums[1:]:
        each.round(1)
    gain_ref[...] = jnp.zeros_like(gain_ref)
    rows.send_far()
    rows.send_near()
    outs.send_far()
    rows.send_relayed()
    outs.send_near()
    for each in sums[1:]:
        each.round(2)
    outs.send_relayed()
    rows.wait_half(False)
    rows.wait_half(True)

    def body(here):
        part, gains = norm_back_rows(
            rows.total(here), input_ref[here].astype(wide), scale_ref[...]
        )
        low_grad[here] = (middle_grad_ref[here] + part).astype(low)
        gain_ref[...] += jnp.sum(gains, axis=0, keepdims=True)

    row_steps(0, whole, body)
    first = make(0, low_grad, input_grad.at[place.core], place.sibling)
    first.start()
    first_local = pltpu.make_async_copy(low_grad, input_grad.at[place.core], local_sems.at[0])
    first_local.start()
    if sums:
        mine, theirs = scratch[19 + 7 * pieces :]
        small = sums[0]
        small.put_gains(gain_ref)
        mine[...] = small.held[...]
        swap = make(2, mine, theirs, place.sibling)
        swap.start()
        swap.wait_recv()
        small.add_top(theirs, 3)
        small.direct()
    outs.wait_half(False)
    outs.wait_half(True)

    def out_body(here):
        low_output[here] = (middle_ref[here] + outs.total(here)).astype(low)

    row_steps(0, whole, out_body)
    second = make(1, low_output, block_output.at[place.core], place.sibling)
    second.start()
    second_local = pltpu.make_async_copy(low_output, block_output.at[place.core], local_sems.at[1])
    second_local.start()
    for turn in range(3, lines):
        for each in sums[1:]:
            each.round(turn)
    for each in sums[:1]:
        each.exchange_direct()
    for each in sums[1:]:
        each.exchange()
    rows.finish()
    outs.finish()
    first_local.wait()
    second_local.wait()
    first.wait()
    second.wait()
    if sums:
        swap.wait_send()
    for each in sums:
        each.finish(direct=each is sums[0])


def first_rows_kernel(lines, whole, pieces, input_ref, *rest):
    place = Place()
    ins, rest = rest[:pieces], rest[pieces:]
    inputs, outs, scratch = rest[0], rest[1 : 1 + pieces], rest[1 + pieces :]
    meet(place, far=bool(pieces), lines=lines if pieces else 0)
    share = ShareRows(place, input_ref.at[place.core], inputs, scratch[:3])
    gathers = [
        GatherLines(place, ins[index], outs[index], scratch[3 + 6 * index : 9 + 6 * index])
        for index in range(pieces)
    ]
    for gather in gathers[:whole]:
        gather.begin()
    for gather in gathers[:whole]:
        gather.leave()
    share.begin_half(False)
    share.begin_half(True)
    share.begin_rest()
    for gather in gathers[whole:]:
        gather.begin()
    share.forward()
    for gather in gathers[:whole]:
        gather.onwards(1)
    share.forward_far()
    for step in range(2, lines):
        for gather in gathers[:whole]:
            gather.onwards(step)
    share.finish()
    for gather in gathers[whole:]:
        for slot in range(MATES):
            gather.arrive(slot)
    for gather in gathers:
        gather.finish_plane()
    for gather in gathers[:whole]:
        gather.finish_lines()


def first_rows(block_input, blocks, whole, lines):
    seqs, rows, columns = block_input.shape
    shape = (seqs, MATES, rows, columns)
    return remote_call(
        functools.partial(first_rows_kernel, lines, whole, len(blocks)),
        0,
        [(array, "any") for array in (block_input, *blocks)],
        [(shape, low, "any")] + [((lines,) + block.shape, low, "any") for block in blocks],
        ShareRows.scratch() + GatherLines.scratch(lines) * len(blocks),
    )


def middle_rows(gathered, weights, mine, scale, out_grad, moving, lines):
    rows, columns = mine.shape
    shared = (2, MATES, rows, columns)
    arrays = [array for array, _ in moving]
    return remote_call(
        functools.partial(middle_kernel, lines, tuple(part for _, part in moving)),
        1,
        [(gathered, "held"), (weights, "any"), (mine, "held"), (scale, "held"), (out_grad, "any")]
        + [(array, "any") for array in arrays],
        [((rows, columns), wide, "held"), (shared, low, "any"), (shared, low, "any")]
        + [(array.shape, low, "any") for array in arrays],
        [
            pltpu.VMEM((rows, columns), low),
            pltpu.VMEM(weights.shape, low),
            pltpu.SemaphoreType.DMA((2, MATES)),
        ]
        + ShareRows.scratch() * 2
        + GatherLines.scratch(lines) * len(arrays),
        {5 + index: 3 + index for index in range(len(arrays))},
    )


def turn_rows(partial, weights, middle, grad, scale, summing, lines):
    seqs, _, rows, columns = partial.shape
    width = weights.shape[-1]
    blocks = (2, MATES, rows, width)
    scratch = [
        pltpu.VMEM(weights.shape, low),
        pltpu.SemaphoreType.DMA((2, MATES)),
        pltpu.VMEM(blocks, low),
    ]
    scratch += SumRows.scratch(rows, columns) + SwapBlocks.scratch()
    outs = []
    for array, (_, height) in summing:
        shape = (MATES, height, array.shape[3])
        scratch += SumLines.scratch(lines, shape)
        outs.append((shape, low, "any"))
    return remote_call(
        functools.partial(turn_rows_kernel, lines, tuple(part for _, part in summing)),
        2,
        [(partial, "any"), (weights, "any"), (middle, "held"), (grad, "held"), (scale, "held")]
        + [(array, "any") for array, _ in summing],
        [
            ((rows, columns), wide, "held"),
            ((1, columns), wide, "held"),
            ((rows, columns), low, "held"),
            (blocks, low, "any"),
        ]
        + outs,
        scratch,
    )


def last_rows(partial, mlp_partial, mine, middle, middle_grad, scale, blocks, lines):
    seqs, _, rows, columns = partial.shape
    scratch = (
        [pltpu.VMEM((rows, columns), low), pltpu.VMEM((rows, columns), low)]
        + SumRows.scratch(rows, columns)
        + SumRows.scratch(rows, columns)
        + [pltpu.SemaphoreType.DMA((3,))] * 3
    )
    for block in blocks:
        scratch += SumLines.scratch(lines, block.shape[1:])
    if blocks:
        scratch += [pltpu.VMEM(blocks[0].shape, low)] * 2
    return remote_call(
        functools.partial(last_rows_kernel, lines, len(blocks)),
        3,
        [(partial, "any"), (mlp_partial, "any")]
        + [(array, "held") for array in (mine, middle, middle_grad, scale)]
        + [(block, "any") for block in blocks],
        [
            ((seqs, rows, columns), low, "any"),
            ((seqs, rows, columns), low, "any"),
            ((1, columns), wide, "held"),
        ]
        + [(block.shape[1:], low, "any") for block in blocks],
        scratch,
    )


class Steps:
    def __init__(self, seqs, heads, span):
        self.seqs, self.heads, self.span = seqs, heads, span
        self.chains, self.chunks = seqs * heads, span // CHUNK

    def chain(self, step, when):
        if when == "first":
            return jnp.minimum(step, self.chains - 1)
        if when == "second":
            return jnp.maximum(step - self.chains, 0)
        return step % self.chains

    def rows(self, when, columns, place):
        def index(step):
            chain = self.chain(step, when)
            return chain // self.heads, place(chain % self.heads)

        return pl.BlockSpec((self.span, columns), index)

    def streams(self, when):
        return self.rows(when, 3 * CHUNK, lambda head: head)

    def head(self, when):
        return self.rows(when, CHUNK, lambda head: head)

    def gate(self, when):
        return self.rows(when, CHUNK, lambda head: 3 * self.heads + head)

    def logit(self, when):
        return self.rows(when, CHUNK, lambda head: 0)

    def taps(self, when):
        return pl.BlockSpec(
            (1, 3 * CONV, CHUNK), lambda step: (self.chain(step, when) % self.heads, 0, 0)
        )

    def blocks(self, when, columns=CHUNK):
        return pl.BlockSpec(
            (1, self.chunks, CHUNK, columns), lambda step: (self.chain(step, when), 0, 0, 0)
        )

    def few(self, when, columns):
        return pl.BlockSpec((1, 8, columns), lambda step: (self.chain(step, when), 0, 0))

    def whole(self, shape):
        return pl.BlockSpec(shape, lambda step: (0,) * len(shape), pipeline_mode=pl.Buffered(1))

    def call(self, body, identity, ins, outs, scratch, aliases=None):
        return pl.pallas_call(
            body,
            grid=(2 * self.chains,),
            in_specs=[spec for _, spec in ins],
            out_specs=[spec for _, _, spec in outs],
            out_shape=[jax.ShapeDtypeStruct(shape, dtype) for shape, dtype, _ in outs],
            scratch_shapes=scratch,
            input_output_aliases=aliases or {},
            compiler_params=pltpu.CompilerParams(
                vmem_limit_bytes=VMEM_BYTES,
                dimension_semantics=("arbitrary",),
                collective_id=identity,
                has_side_effects=True,
            ),
        )(*[array for array, _ in ins])


def delta_front(limit, raw, taps, logits, scale, moving, lines, seqs, heads, span):
    steps = Steps(seqs, heads, span)
    chains, chunks, size = steps.chains, steps.chunks, CHUNK
    squares, doubles = (chains, chunks, CHUNK, size), (chains, chunks, CHUNK, 2 * size)
    states, tails = (chains, size, size), (seqs, 16, 3 * heads * size)
    tokens = span // MATES
    anywhere = pl.BlockSpec(memory_space=pl.ANY)
    arrays = [array for array, _ in moving]
    ins = [
        (limit, pl.BlockSpec(memory_space=pltpu.SMEM)),
        (raw, anywhere),
        (raw, steps.streams("first")),
        (taps, steps.taps("first")),
        (logits, steps.logit("first")),
        (raw, steps.gate("second")),
        (scale, steps.whole((1, size))),
    ] + [(array, anywhere) for array in arrays]
    outs = [
        ((seqs * span, 3 * heads * size), low, steps.streams("first")),
        (squares, wide, steps.blocks("first")),
        (doubles, wide, steps.blocks("first", 2 * size)),
        (squares, wide, steps.blocks("first")),
        (states, wide, steps.whole(states)),
        (tails, low, steps.whole(tails)),
        (squares, wide, steps.blocks("second")),
        (squares, wide, steps.blocks("second")),
        ((seqs * span, heads * size), wide, steps.head("second")),
        ((seqs * span, heads * size), low, steps.head("second")),
        ((seqs, MATES, tokens, heads * size), low, anywhere),
        ((seqs, MATES) + arrays[0].shape, low, anywhere),
    ] + [(array.shape, low, anywhere) for array in arrays]
    scratch = [
        pltpu.VMEM((span + 16, 3 * size), wide),
        pltpu.VMEM(squares, wide),
        pltpu.VMEM(squares, wide),
        pltpu.VMEM(squares, wide),
        pltpu.VMEM(squares, wide),
        pltpu.VMEM(doubles, wide),
        pltpu.VMEM((chains, span, 3 * size), low),
        pltpu.VMEM(states, low),
        pltpu.VMEM(states, low),
        pltpu.VMEM(tails, low),
        pltpu.SemaphoreType.DMA((2, seqs)),
        pltpu.SemaphoreType.DMA((2,)),
        pltpu.VMEM((seqs, span, heads * size), low),
    ]
    scratch += ShareRows.scratch() + SwapBlocks.scratch()
    scratch += GatherLines.scratch(lines) * len(arrays)
    moves = tuple(part for _, part in moving)
    return steps.call(
        functools.partial(front_kernel, lines, heads, moves),
        4,
        ins,
        outs,
        scratch,
        {7 + index: 12 + index for index in range(len(arrays))},
    )


def delta_back(
    limit, raw, tails, taps, logits, scale, qkv, wu, maps, total, grad, mixed, solved, state, fresh,
    row_grad, summing, lines, seqs, heads, span,
):
    steps = Steps(seqs, heads, span)
    chains, chunks, size = steps.chains, steps.chunks, CHUNK
    squares, states = (chains, chunks, CHUNK, size), (chains, size, size)
    all_shape = (seqs * span, (4 * heads + 1) * size)
    anywhere = pl.BlockSpec(memory_space=pl.ANY)
    ins = [
        (limit, pl.BlockSpec(memory_space=pltpu.SMEM)),
        (raw, steps.streams("second")),
        (tails, steps.whole(tails.shape)),
        (taps, steps.taps("second")),
        (logits, steps.logit("second")),
        (raw, steps.gate("first")),
        (scale, steps.whole((1, size))),
        (qkv, steps.streams("both")),
        (wu, steps.blocks("both", 2 * size)),
        (maps, steps.blocks("first")),
        (total, steps.whole(states)),
        (grad, steps.head("first")),
        (mixed, steps.head("first")),
        (solved, steps.blocks("second")),
        (state, steps.blocks("second")),
        (fresh, steps.blocks("second")),
        (row_grad, anywhere),
    ] + [(array, anywhere) for array, _ in summing]
    outs = [
        (all_shape, low, steps.whole(all_shape)),
        ((chains, 8, size), wide, steps.few("first", size)),
        ((chains, 8, 3 * size), wide, steps.few("second", 3 * size)),
        ((seqs, MATES) + row_grad.shape, low, anywhere),
    ]
    edges = (chains, 16, 3 * size)
    scratch = [
        pltpu.VMEM((span + 16, 3 * size), wide),
        pltpu.VMEM((span + 32, 3 * size), wide),
        pltpu.VMEM(squares, wide),
        pltpu.VMEM(squares, wide),
        pltpu.VMEM(squares, wide),
        pltpu.VMEM(squares, wide),
        pltpu.VMEM(squares, wide),
        pltpu.VMEM(states, low),
        pltpu.VMEM(states, low),
        pltpu.VMEM(edges, low),
        pltpu.VMEM(edges, wide),
        pltpu.VMEM(edges, low),
        pltpu.SemaphoreType.DMA((2, chains)),
        pltpu.SemaphoreType.DMA((2,)),
    ] + ShareRows.scratch()
    for array, (_, height) in summing:
        shape = (MATES, height, array.shape[3])
        scratch += SumLines.scratch(lines, shape)
        outs.append((shape, low, anywhere))
    return steps.call(
        functools.partial(back_kernel, lines, heads, tuple(part for _, part in summing)),
        5,
        ins,
        outs,
        scratch,
    )


def project(inputs, scale, weight, raw_width):
    rows, model_width = inputs.shape
    columns = weight.shape[1]
    tile = 256

    def tall(width):
        return pl.BlockSpec((tile, width), lambda step: (step, 0))

    def whole(array):
        return pl.BlockSpec(array.shape, lambda step: (0, 0), pipeline_mode=pl.Buffered(1))

    return pl.pallas_call(
        project_kernel,
        grid=(rows // tile,),
        in_specs=[tall(model_width), whole(scale), whole(weight)],
        out_specs=[tall(model_width), tall(raw_width), tall(columns - raw_width)],
        out_shape=[
            jax.ShapeDtypeStruct((rows, model_width), low),
            jax.ShapeDtypeStruct((rows, raw_width), low),
            jax.ShapeDtypeStruct((rows, columns - raw_width), wide),
        ],
        compiler_params=pltpu.CompilerParams(vmem_limit_bytes=VMEM_BYTES),
    )(inputs, scale, weight)


def held_call(body, ins, outs):
    held = pl.BlockSpec(memory_space=pltpu.VMEM)
    return pl.pallas_call(
        body,
        in_specs=[held] * len(ins),
        out_specs=[held] * len(outs),
        out_shape=[jax.ShapeDtypeStruct(shape, dtype) for shape, dtype in outs],
        compiler_params=pltpu.CompilerParams(vmem_limit_bytes=VMEM_BYTES),
    )(*ins)


def pack_kernel(
    heads, query, key, value, outgate, beta, output, swish, upward, downward,
    attn_ref, output_ref, ups_ref, downs_ref,
):
    size = CHUNK
    width = heads * size
    units = downs_ref.shape[2]
    beta_low = beta[...].astype(low)
    for mate in range(MATES):
        first = mate * width
        for head in range(heads):
            for stream, weight in enumerate((query, key, value)):
                lanes = (3 * head + stream) * size
                attn_ref[mate, :, lanes : lanes + size] = weight[
                    :, first + head * size : first + (head + 1) * size
                ].astype(low)
        attn_ref[mate, :, 3 * width : 4 * width] = outgate[:, first : first + width].astype(low)
        shape = (beta.shape[1], size)
        rows = lax.broadcasted_iota(jnp.int32, shape, 0)
        columns = lax.broadcasted_iota(jnp.int32, shape, 1)
        chosen = (rows == columns + mate * heads) & (columns < heads)
        attn_ref[mate, :, 4 * width :] = dot(
            beta_low, jnp.where(chosen, 1.0, 0.0).astype(low), NN
        ).astype(low)
        output_ref[mate] = output[first : first + width, :].T.astype(low)
        here = mate * units
        ups_ref[mate, :, :units] = swish[:, here : here + units].astype(low)
        ups_ref[mate, :, units:] = upward[:, here : here + units].astype(low)
        downs_ref[mate] = downward[here : here + units, :].T.astype(low)


def unpack_kernel(
    heads, attn, outs, ups_low, ups_high, downs,
    query, key, value, outgate, beta, output, swish, upward, downward,
):
    size = CHUNK
    width = heads * size
    units = downs.shape[2]
    split = ups_low.shape[1]
    beta_all = None
    for mate in range(MATES):
        first = mate * width
        for head in range(heads):
            for stream, grad in enumerate((query, key, value)):
                lanes = (3 * head + stream) * size
                grad[:, first + head * size : first + (head + 1) * size] = attn[
                    mate, :, lanes : lanes + size
                ].astype(wide)
        outgate[:, first : first + width] = attn[mate, :, 3 * width : 4 * width].astype(wide)
        shape = (size, beta.shape[1])
        rows = lax.broadcasted_iota(jnp.int32, shape, 0)
        columns = lax.broadcasted_iota(jnp.int32, shape, 1)
        chosen = (columns == rows + mate * heads) & (rows < heads)
        part = dot(attn[mate, :, 4 * width :], jnp.where(chosen, 1.0, 0.0).astype(low), NN)
        beta_all = part if beta_all is None else beta_all + part
        output[first : first + width, :] = outs[mate].astype(wide).T
        here = mate * units
        for rows_here, part in ((pl.ds(0, split), ups_low), (pl.ds(split, swish.shape[0] - split), ups_high)):
            swish[rows_here, here : here + units] = part[mate, :, :units].astype(wide)
            upward[rows_here, here : here + units] = part[mate, :, units:].astype(wide)
        downward[here : here + units, :] = downs[mate].astype(wide).T
    beta[...] = beta_all


def cut_columns(weight):
    depth, columns = weight.shape
    return weight.reshape(depth, MATES, columns // MATES).transpose(1, 0, 2)


def join_columns(blocks):
    return blocks.transpose(1, 0, 2).reshape(blocks.shape[1], -1)


def gather_weights(blocks):
    return gather_lines(swap_blocks(blocks))


def scatter_grads(blocks):
    return swap_blocks(scatter_lines(blocks.astype(low))).astype(wide)


def on_device(
    block_input,
    lengths,
    attn_gain,
    query_weight,
    key_weight,
    value_weight,
    outgate_weight,
    beta_weight,
    conv_kernel,
    head_gain,
    output_weight,
    mlp_gain,
    swish_weight,
    upward_weight,
    downward_weight,
    out_grad,
):
    count = lax.axis_size("seq")
    lines = count // MATES
    core = lax.axis_index("tp")
    seq_count, tokens, model_width = block_input.shape
    depth = attn_gain.shape[0]
    gain_part = head_gain.shape[0]
    head_size = gain_part * count
    heads = beta_weight.shape[1] // MATES
    width = heads * head_size
    units = swish_weight.shape[1] // MATES

    near = lines <= 4 and depth % 128 == 0
    rows = seq_count * MATES * tokens
    span = MATES * tokens

    small_cut = jnp.concatenate(
        [
            jnp.broadcast_to(
                jnp.concatenate([attn_gain, mlp_gain, head_gain]).astype(low)[None],
                (MATES, 2 * depth + gain_part),
            ),
            jnp.zeros((MATES, -gain_part % 128), low),
            conv_kernel.astype(low).reshape(MATES, -1),
        ],
        axis=1,
    )
    sizes = (depth, depth, gain_part, -gain_part % 128, heads * 3 * CONV * gain_part)
    starts = [sum(sizes[:index]) for index in range(len(sizes) + 1)]
    small_cut = jnp.pad(small_cut, ((0, 0), (0, SMALL * 128 - starts[-1])))
    small_cut = small_cut.reshape(MATES, SMALL, 128)
    streams_end, gates_end = 3 * width, 4 * width
    attn_width = gates_end + head_size
    if near:
        cuts = held_call(
            functools.partial(pack_kernel, heads),
            (
                query_weight, key_weight, value_weight, outgate_weight, beta_weight, output_weight,
                swish_weight, upward_weight, downward_weight,
            ),
            [
                ((MATES, depth, columns), low)
                for columns in (attn_width, width, 2 * units, units)
            ],
        )
        input_rows, small, attn_full, output_full, ups_full, downward_full = first_rows(
            block_input, (small_cut, *cuts), 2, lines
        )
        ups_split = depth // 128 * 80
        front_moves = ((output_full, (0, depth)), (ups_full, (0, ups_split)))
    else:
        streams_cut = jnp.stack(
            [
                w.astype(low).reshape(depth, MATES, heads, head_size)
                for w in (query_weight, key_weight, value_weight)
            ],
            axis=3,
        )
        streams_cut = streams_cut.transpose(1, 0, 2, 3, 4).reshape(MATES, depth, streams_end)
        beta_cut = jnp.pad(
            cut_columns(beta_weight.astype(low)), ((0, 0), (0, 0), (0, head_size - heads))
        )
        cuts = (
            small_cut,
            jnp.concatenate([streams_cut, cut_columns(outgate_weight.astype(low)), beta_cut], axis=2),
            cut_columns(output_weight.astype(low).T),
            jnp.concatenate([cut_columns(w.astype(low)) for w in (swish_weight, upward_weight)], axis=2),
            cut_columns(downward_weight.astype(low).T),
        )
        input_rows, = first_rows(block_input, (), 0, lines)
        small, attn_full, output_full, ups_full, downward_full = (gather_weights(cut) for cut in cuts)
        front_moves = ((output_full, None),)
    attn_full = attn_full.reshape(model_width, attn_width)
    input_rows = input_rows.reshape(rows, model_width)
    small = small.reshape(count, SMALL * 128)
    attn_small, mlp_small, head_small, _, conv_small = (
        small[:, starts[index] : starts[index + 1]] for index in range(len(sizes))
    )
    taps = (
        conv_small.reshape(count, heads, 3, CONV, gain_part)
        .transpose(1, 2, 3, 0, 4)
        .reshape(heads, 3 * CONV, head_size)
        .astype(wide)
    )
    attn_scale = attn_small.reshape(1, model_width).astype(wide)
    mlp_scale = mlp_small.reshape(1, model_width).astype(wide)
    head_scale = head_small.reshape(1, head_size).astype(wide)

    mine_low = pick(block_input, core)
    grad_mine = pick(out_grad, core)
    blocked = (seq_count, MATES, tokens, model_width)
    lengths_here = jnp.stack([pick(lengths, core), pick(lengths, 1 - core)])
    limit = lengths_here - line_of() * span

    flat_normed, raw, logits = project(input_rows, attn_scale, attn_full, gates_end)
    sizes_of = (lines, seq_count, heads, span)
    (
        qkv, solved, wu, maps, total, tails, state, fresh, mixed, gated, gathered, output_all, *moved
    ) = delta_front(limit, raw, taps, logits, head_scale, front_moves, *sizes_of)
    middle_moves = ()
    if near:
        ups_full = moved[1]
        middle_moves = (
            (ups_full, (ups_split, depth - ups_split)), (downward_full, (0, depth))
        )
    middle, mlp_normed, grad_rows, *moved = middle_rows(
        gathered, output_all, mine_low, mlp_scale, out_grad, middle_moves, lines
    )
    grad_rows = grad_rows.reshape(rows, model_width)
    if near:
        ups_full, downward_full = moved
    ups_full = ups_full.reshape(model_width, 2 * units)
    downward_full = downward_full.reshape(model_width, units)
    mlp_normed = mlp_normed.reshape(rows, model_width)
    acts = matmul("rd,df->rf", mlp_normed, ups_full)
    gate_act, up_act = acts[:, :units], acts[:, units:]
    silu_act = jax.nn.silu(gate_act)
    hidden = (silu_act * up_act).astype(low)
    mlp_part = matmul("rf,df->rd", hidden, downward_full).astype(low)

    hidden_grad = matmul("rd,df->rf", grad_rows, downward_full)
    downward_grad = matmul("rd,rf->df", grad_rows, hidden).astype(low)
    acts_grad = jnp.concatenate(
        [
            (hidden_grad * up_act * silu_slope(gate_act)).astype(low),
            (hidden_grad * silu_act).astype(low),
        ],
        axis=1,
    )
    ups_grad = matmul("rd,rf->df", mlp_normed, acts_grad).astype(low)
    normed_two_part = matmul("rf,df->rd", acts_grad, ups_full).astype(low)

    def cut_rows(grad):
        return grad.reshape(lines, MATES, depth, grad.shape[1])

    ups_blocks, downward_blocks = cut_rows(ups_grad), cut_rows(downward_grad)
    turn_sums = back_sums = ()
    if near:
        sums_split = depth // 128 * 80
        turn_sums = ((ups_blocks, (0, sums_split)),)
    middle_grad, mlp_gain_grad, attn_grad_mine, gated_grad, *summed = turn_rows(
        normed_two_part.reshape(blocked), output_all, middle, grad_mine, mlp_scale, turn_sums, lines
    )
    if near:
        ups_low, = summed
        back_sums = (
            (ups_blocks, (sums_split, depth - sums_split)),
            (downward_blocks, (0, depth)),
        )
    all_grads, head_gain_parts, taps_grad, attn_grad_rows, *summed = delta_back(
        limit, raw, tails, taps, logits, head_scale, qkv, wu, maps, total,
        gated_grad.reshape(rows, width), mixed, solved, state, fresh, attn_grad_mine, back_sums,
        *sizes_of,
    )
    attn_grad_rows = attn_grad_rows.reshape(rows, model_width)
    output_grad = cut_rows(matmul("rd,rc->dc", attn_grad_rows, gated).astype(low))
    normed_part = matmul("rc,dc->rd", all_grads, attn_full).astype(low)
    attn_grads = cut_rows(matmul("rd,rc->dc", flat_normed, all_grads).astype(low))

    conv_grad = (
        taps_grad[:, :CONV]
        .reshape(seq_count, heads, CONV, 3, count, gain_part)
        .sum(axis=0)
        .transpose(3, 0, 2, 1, 4)
        .reshape(count, -1)
    )

    def small_blocks(attn_gain_grad):
        parts = [
            attn_gain_grad.reshape(count, depth),
            mlp_gain_grad.reshape(count, depth),
            jnp.sum(head_gain_parts[:, 0], axis=0).reshape(count, gain_part),
            jnp.zeros((count, -gain_part % 128), wide),
            conv_grad,
        ]
        flat = jnp.concatenate(parts, axis=1).astype(low)
        flat = jnp.pad(flat, ((0, 0), (0, SMALL * 128 - starts[-1])))
        return flat.reshape(lines, MATES, SMALL, 128)

    last_ins = (
        normed_part.reshape(blocked),
        mlp_part.reshape(blocked),
        mine_low,
        middle,
        middle_grad,
        attn_scale,
    )
    if near:
        ups_high, downward_sum = summed
        blocks = (small_blocks(jnp.zeros((1, model_width), wide)), attn_grads, output_grad)
        input_grad, block_output, _, small_sum, attn_sum, output_sum = last_rows(
            *last_ins, blocks, lines
        )
        grads = held_call(
            functools.partial(unpack_kernel, heads),
            (attn_sum, output_sum, ups_low, ups_high, downward_sum),
            [
                (w.shape, wide)
                for w in (
                    query_weight, key_weight, value_weight, outgate_weight, beta_weight, output_weight,
                    swish_weight, upward_weight, downward_weight,
                )
            ],
        )
        small_sum = small_sum.reshape(MATES, SMALL * 128).astype(wide)
        gains_sum = jnp.sum(small_sum[:, : starts[3]], axis=0)
    else:
        input_grad, block_output, attn_gain_grad = last_rows(*last_ins, (), lines)
        small_sum, attn_sum, output_sum, ups_sum, downward_sum = (
            scatter_grads(block)
            for block in (
                small_blocks(attn_gain_grad), attn_grads, output_grad, ups_blocks, downward_blocks
            )
        )
        small_sum = small_sum.reshape(MATES, SMALL * 128)
        gains_sum = jnp.sum(small_sum[:, : starts[3]], axis=0)
        gains_sum = gains_sum + other_core(gains_sum)
        streams_sum = (
            attn_sum[:, :, :streams_end]
            .reshape(MATES, depth, heads, 3, head_size)
            .transpose(3, 1, 0, 2, 4)
            .reshape(3, depth, MATES * width)
        )
        grads = (
            streams_sum[0],
            streams_sum[1],
            streams_sum[2],
            join_columns(attn_sum[:, :, streams_end:gates_end]),
            join_columns(attn_sum[:, :, gates_end : gates_end + heads]),
            join_columns(output_sum).T,
            join_columns(ups_sum[:, :, :units]),
            join_columns(ups_sum[:, :, units:]),
            join_columns(downward_sum).T,
        )
    conv_sum = small_sum[:, starts[4] : starts[5]]
    return (
        block_output,
        input_grad,
        gains_sum[:depth],
        *grads[:5],
        conv_sum.reshape(MATES * heads, 3, CONV, gain_part),
        gains_sum[2 * depth :],
        grads[5],
        gains_sum[depth : 2 * depth],
        *grads[6:],
    )


def solution(mesh):
    return jax.shard_map(
        on_device,
        mesh=mesh,
        in_specs=(
            P(None, "seq", None),
            P(),
            P("seq"),
            P("seq", "tp"),
            P("seq", "tp"),
            P("seq", "tp"),
            P("seq", "tp"),
            P("seq", "tp"),
            P("tp", None, None, "seq"),
            P("seq"),
            P("tp", "seq"),
            P("seq"),
            P("seq", "tp"),
            P("seq", "tp"),
            P("tp", "seq"),
            P(None, "seq", None),
        ),
        out_specs=(
            P(None, "seq", None),
            P(None, "seq", None),
            P("seq"),
            P("seq", "tp"),
            P("seq", "tp"),
            P("seq", "tp"),
            P("seq", "tp"),
            P("seq", "tp"),
            P("tp", None, None, "seq"),
            P("seq"),
            P("tp", "seq"),
            P("seq"),
            P("seq", "tp"),
            P("seq", "tp"),
            P("tp", "seq"),
        ),
        check_vma=False,
    )
```

```python
import functools

import jax
import jax.numpy as jnp
from jax import lax
from jax.experimental import pallas as pl
from jax.experimental.pallas import tpu as pltpu
from jax.sharding import PartitionSpec as P

CONV = 4
MATES = 4
SMALL = 16
CONV_ROW = 3
BETA_ROW = 5


epsilon = 1e-06
low = jnp.bfloat16
wide = jnp.float32


def other_core(value):
    return lax.ppermute(value, "tp", [(0, 1), (1, 0)])


def to_mate(value, flip):
    count = lax.axis_size("seq")
    return lax.ppermute(value, "seq", [(source, source ^ flip) for source in range(count)])


def mate_of():
    return lax.axis_index("seq") % MATES


def line_of():
    return lax.axis_index("seq") // MATES


def line_groups():
    lines = lax.axis_size("seq") // MATES
    return [[mate + MATES * line for line in range(lines)] for mate in range(MATES)]


def pick(blocks, index):
    return lax.dynamic_index_in_dim(blocks, index, 0, False)


def in_order(by_flip):
    mate = mate_of()
    out = jnp.zeros((MATES,) + by_flip[0].shape, by_flip[0].dtype)
    for flip, piece in enumerate(by_flip):
        out = lax.dynamic_update_index_in_dim(out, piece, mate ^ flip, 0)
    return out


def swap_blocks(blocks):
    mate = mate_of()
    pieces = [pick(blocks, mate)]
    for flip in range(1, MATES):
        pieces.append(to_mate(pick(blocks, mate ^ flip), flip))
    return in_order(pieces)


def gather_lines(block):
    return lax.all_gather(block, "seq", axis_index_groups=line_groups())


def scatter_lines(blocks):
    return lax.psum_scatter(blocks, "seq", scatter_dimension=0, axis_index_groups=line_groups())


def matmul(form, left, right):
    return jnp.einsum(form, left, right, preferred_element_type=wide)


def silu_slope(value):
    squash = jax.nn.sigmoid(value)
    return squash * (1.0 + value * (1.0 - squash))


CHUNK = 128
TOGETHER = 4
VMEM_BYTES = 58 * 1024 * 1024
NN = (((1,), (0,)), ((), ()))
NT = (((1,), (1,)), ((), ()))


def dot(left, right, dims):
    return lax.dot_general(left, right, dims, preferred_element_type=wide)


def pair(value):
    high = value.astype(low)
    return high, (value - high.astype(wide)).astype(low)


def side(left, right):
    return jnp.concatenate([left, right], axis=1)


def over(top, bottom):
    return jnp.concatenate([top, bottom], axis=0)


def nn(left, right):
    width = right[0].shape[1]
    both = side(*right)
    out = dot(side(*left), over(both, both), NN)
    return out[:, :width] + out[:, width:]


def nt(left, right):
    width = right[0].shape[0]
    out = dot(side(*left), over(side(right[0], right[0]), side(right[1], right[1])), NT)
    return out[:, :width] + out[:, width:]


def nn_wide(left, right):
    return dot(side(*left), over(right[0], right[0]), NN) + dot(left[0], right[1], NN)


def nn_low(left, right):
    return dot(side(*left), over(right, right), NN)


def low_nn(left, right):
    return dot(side(left, left), over(*right), NN)


def low_nt(left, right):
    return dot(side(left, left), side(*right), NT)


def grid_of_rows():
    rows = lax.broadcasted_iota(jnp.int32, (CHUNK, CHUNK), 0)
    columns = lax.broadcasted_iota(jnp.int32, (CHUNK, CHUNK), 1)
    return rows, columns


def inverse_of(strict):
    rows, columns = grid_of_rows()
    one = jnp.where(rows == columns, 1.0, 0.0).astype(wide)

    def joining(shift):
        upper = columns >> shift
        return ((rows >> shift) == upper + 1) & ((upper & 1) == 0)

    solved = [one - jnp.where(joining(0), s, 0.0) for s in strict]
    shift = 1
    while (1 << shift) < CHUNK:
        mask = joining(shift)
        pairs = [pair(d) for d in solved]
        crossed = [nn(pair(jnp.where(mask, s, 0.0)), p) for s, p in zip(strict, pairs)]
        solved = [d - nn(p, pair(c)) for d, p, c in zip(solved, pairs, crossed)]
        shift += 1
    return solved


def convolved(block, taps, stream):
    columns = block[:, stream * CHUNK : (stream + 1) * CHUNK]
    total = None
    for offset in range(CONV):
        first = 16 - (CONV - 1) + offset
        term = taps[stream * CONV + offset][None, :] * columns[first : first + CHUNK]
        total = term if total is None else total + term
    return total


def silu_parts(value):
    squash = jax.nn.sigmoid(value)
    return value * squash, squash * (1.0 + value * (1.0 - squash))


def live_rows(limit, start):
    rows = lax.broadcasted_iota(jnp.int32, (CHUNK, CHUNK), 0)
    return jnp.where(rows + start < limit, 1.0, 0.0).astype(wide)


def head_squash(logits, head):
    lanes = lax.broadcasted_iota(jnp.int32, logits.shape, 1)
    column = jnp.sum(jnp.where(lanes == BETA_ROW + head, logits, 0.0), axis=1, keepdims=True)
    return jax.nn.sigmoid(jnp.broadcast_to(column, logits.shape))


def front_kernel(
    lines, heads, moves, limit_ref, raw_any, raw_ref, taps_ref, logit_ref, gate_ref, scale_ref, *rest,
):
    count = len(moves)
    outs = rest[count:]
    qkv_ref, solved_ref, wu_ref, map_ref, total_ref, tails_ref = outs[:6]
    state_ref, fresh_ref, mixed_ref, gated_ref, gathered, weights = outs[6:12]
    targets, scratch = outs[12 : 12 + count], outs[12 + count :]
    ext, offsets, maps, prefixes, locals_, wus, qkvs, enters, leaves, tails = scratch[:10]
    tail_sems, state_sems, gateds = scratch[10:13]
    scratch = scratch[13:]
    step = pl.program_id(0)
    chains, chunks = maps.shape[0], maps.shape[1]
    span = chunks * CHUNK
    head_size = CHUNK
    streams = 3 * heads * head_size
    place = Place()
    tokens = gathered.shape[2]
    share = ShareRows(place, targets[0], weights, scratch[:3])
    swap = SwapBlocks(
        place,
        lambda slot, mate: gateds.at[slot, pl.ds(pl.multiple_of(mate * tokens, 16), tokens)],
        gathered,
        scratch[3:6],
    )
    gathers = [
        GatherLines(place, None, target, scratch[6 + 6 * index : 12 + 6 * index], moves[index])
        for index, target in enumerate(targets)
        if moves[index]
    ]
    below, above = place.line > 0, place.line < lines - 1
    rows, columns = grid_of_rows()
    identity = jnp.where(rows == columns, 1.0, 0.0).astype(wide)

    def tail(seq):
        return pltpu.make_async_remote_copy(
            src_ref=raw_any.at[pl.ds((seq + 1) * span - 16, 16), pl.ds(0, streams)],
            dst_ref=tails.at[seq],
            send_sem=tail_sems.at[0, seq],
            recv_sem=tail_sems.at[1, seq],
            device_id=place.lines_away(1),
            device_id_type=MESH,
        )

    state_copy = pltpu.make_async_remote_copy(
        src_ref=leaves,
        dst_ref=enters,
        send_sem=state_sems.at[0],
        recv_sem=state_sems.at[1],
        device_id=place.lines_away(1),
        device_id_type=MESH,
    )
    seqs = chains // heads

    @pl.when(step == 0)
    def _():
        meet(place, lines=lines, cores=True)
        for seq in range(seqs):
            pl.when(above)(tail(seq).start)
        for gather in gathers:
            gather.leave(False)
        for seq in range(seqs):

            @pl.when(below)
            def _(seq=seq):
                tail(seq).wait_recv()

            @pl.when(place.line == 0)
            def _(seq=seq):
                tails[seq] = jnp.zeros(tails.shape[1:], low)

        tails_ref[...] = tails[...]

    def form(chain):
        seq, head = chain // heads, chain % heads
        ext[:16] = tails[seq, :, pl.ds(pl.multiple_of(head * 3 * head_size, 128), 3 * head_size)].astype(wide)
        ext[16:] = raw_ref[...].astype(wide)
        taps = taps_ref[0]
        limit = limit_ref[seq]

        def group(index, carry):
            first = index * TOGETHER
            parts = []
            for number in range(TOGETHER):
                start = pl.multiple_of((first + number) * CHUNK, CHUNK)
                block = ext[pl.ds(start, CHUNK + 16)]
                query = jax.nn.silu(convolved(block, taps, 0))
                key = jax.nn.silu(convolved(block, taps, 1))
                value = jax.nn.silu(convolved(block, taps, 2)).astype(low)
                query = query * lax.rsqrt(jnp.sum(query * query, axis=1, keepdims=True) + epsilon)
                query = (query * head_size ** (-0.5)).astype(low)
                key = key * lax.rsqrt(jnp.sum(key * key, axis=1, keepdims=True) + epsilon)
                key = key.astype(low)
                beta = head_squash(logit_ref[pl.ds(start, CHUNK)], head) * live_rows(limit, start)
                together = jnp.concatenate([query, key, value], axis=1)
                qkv_ref[pl.ds(start, CHUNK)] = together
                qkvs[chain, pl.ds(start, CHUNK)] = together
                parts.append((key, value, beta))
            strict = [
                jnp.where(rows > columns, beta * dot(key, key, NT), 0.0) for key, _, beta in parts
            ]
            solved = inverse_of(strict)
            for number in range(TOGETHER):
                key, value, beta = parts[number]
                solved_ref[0, first + number] = solved[number]
                weighted = pair(solved[number] * beta.T)
                both = nn_low(weighted, side(key, value))
                wu_ref[0, first + number] = both
                wus[chain, first + number] = both
                moved = low_nn(key.T, pair(both))
                step_map = identity - moved[:, :head_size]
                map_ref[0, first + number] = step_map
                maps[chain, first + number] = step_map
                offsets[chain, first + number] = moved[:, head_size:]
            return carry

        lax.fori_loop(0, chunks // TOGETHER, group, 0)

    @pl.when((step == 1) & (step < chains))
    def _():
        for gather in gathers[:1]:
            gather.onwards(1)

    @pl.when((step == 2) & (step < chains))
    def _():
        for gather in gathers[:1]:
            gather.onwards(2)

    @pl.when(step < chains)
    def _():
        form(step)

    @pl.when(step == chains - 2)
    def _():
        for gather in gathers[:1]:
            for number in range(3, lines):
                gather.onwards(number)
        share.begin_half(False)
        share.begin_half(True)
        share.begin_rest()
        for gather in gathers[1:]:
            gather.onwards(1)

    @pl.when(step == chains - 1)
    def _():
        start = side(identity, jnp.zeros_like(identity))

        def advance(chunk, states):
            out = []
            for index in range(chains):
                state = states[index]
                prefixes[index, chunk] = state[:, :head_size]
                locals_[index, chunk] = state[:, head_size:]
                moved = nn_wide(pair(maps[index, chunk]), pair(state))
                out.append(
                    side(moved[:, :head_size], moved[:, head_size:] + offsets[index, chunk])
                )
            return tuple(out)

        ends = lax.fori_loop(0, chunks, advance, (start,) * chains)

        @pl.when(below)
        def _():
            state_copy.wait_recv()

        @pl.when(place.line == 0)
        def _():
            enters[...] = jnp.zeros_like(enters)

        for index in range(chains):
            total_ref[index] = ends[index][:, :head_size]
            leaving = nn_low(pair(ends[index][:, :head_size]), enters[index])
            leaves[index] = (leaving + ends[index][:, head_size:]).astype(low)
        pl.when(above)(state_copy.start)

    def outputs(chain):
        enter = enters[chain]
        scale = scale_ref[...]

        def group(index, carry):
            for number in range(TOGETHER):
                chunk = index * TOGETHER + number
                start = pl.multiple_of(chunk * CHUNK, CHUNK)
                here = pl.ds(start, CHUNK)
                state = nn_low(pair(prefixes[chain, chunk]), enter) + locals_[chain, chunk]
                state_ref[0, chunk] = state
                states = pair(state)
                both = wus[chain, chunk]
                fresh = both[:, head_size:] - nn(pair(both[:, :head_size]), states)
                fresh_ref[0, chunk] = fresh
                query = qkvs[chain, here, :head_size]
                key = qkvs[chain, here, head_size : 2 * head_size]
                scores = jnp.where(rows >= columns, dot(query, key, NT), 0.0)
                mixed = low_nn(query, states) + nn(pair(scores), pair(fresh))
                mixed_ref[here] = mixed
                inverse = lax.rsqrt(jnp.mean(mixed * mixed, axis=1, keepdims=True) + epsilon)
                normed = mixed * inverse * scale
                gated = (normed * jax.nn.silu(gate_ref[here].astype(wide))).astype(low)
                gated_ref[here] = gated
                lanes = pl.ds(pl.multiple_of(chain % heads * head_size, 128), head_size)
                gateds[chain // heads, here, lanes] = gated
            return carry

        lax.fori_loop(0, chunks // TOGETHER, group, 0)

    @pl.when(step >= chains)
    def _():
        outputs(step - chains)

    @pl.when(step == chains + heads - 1)
    def _():
        swap.begin(0)
        share.forward()

    @pl.when(step == 2 * chains - 2)
    def _():
        for gather in gathers[1:]:
            gather.onwards(2)

    @pl.when(step == 2 * chains - 1)
    def _():
        swap.begin(1)
        share.forward_far()
        for gather in gathers[1:]:
            for number in range(3, lines):
                gather.onwards(number)
        for gather in gathers:
            gather.finish_lines()
        share.finish()
        swap.finish()
        for seq in range(seqs):
            pl.when(above)(tail(seq).wait_send)
        pl.when(above)(state_copy.wait_send)


def back_kernel(
    lines, heads, parts, limit_ref, raw_ref, tails_ref, taps_ref, logit_ref, gate_ref, scale_ref, qkv_ref,
    wu_ref, map_ref, total_ref, grad_ref, mixed_ref, solved_ref, state_ref, fresh_in_ref, row_grad, *rest,
):
    count = len(parts)
    blocks, rest = rest[:count], rest[count:]
    all_ref, gain_ref, taps_grad_ref, row_grads = rest[:4]
    results, scratch = rest[4 : 4 + count], rest[4 + count :]
    ext, pre_grads, maps, sources, out_grads, fresh_grads, leaving, leaves, enters = scratch[:9]
    halos, edges, returned, halo_sems, state_sems = scratch[9:14]
    share_scratch, scratch = scratch[14:17], scratch[17:]
    step = pl.program_id(0)
    chains, chunks = maps.shape[0], maps.shape[1]
    span = chunks * CHUNK
    head_size = CHUNK
    streams = 3 * heads * head_size
    place = Place()
    sums = [
        SumLines(place, blocks[index], results[index], scratch[7 * index : 7 * index + 7], first)
        for index, (first, _) in enumerate(parts)
    ]
    share = ShareRows(place, row_grad, row_grads, share_scratch)
    below, above = place.line > 0, place.line < lines - 1
    rows, columns = grid_of_rows()

    def halo(chain):
        return pltpu.make_async_remote_copy(
            src_ref=halos.at[chain],
            dst_ref=returned.at[chain],
            send_sem=halo_sems.at[0, chain],
            recv_sem=halo_sems.at[1, chain],
            device_id=place.lines_away(-1),
            device_id_type=MESH,
        )

    state_copy = pltpu.make_async_remote_copy(
        src_ref=enters,
        dst_ref=leaves,
        send_sem=state_sems.at[0],
        recv_sem=state_sems.at[1],
        device_id=place.lines_away(-1),
        device_id_type=MESH,
    )

    @pl.when(step == 0)
    def _():
        meet(place, far=bool(parts), lines=lines)
        share.begin_half(False)
        share.begin_half(True)
        share.begin_rest()
        for each in sums:
            each.begin()
        for each in sums:
            each.wait_loads()
            each.round(1)

    def turn(chain):
        scale = scale_ref[...]

        def group(index, gain):
            for number in range(TOGETHER):
                chunk = index * TOGETHER + number
                start = pl.multiple_of(chunk * CHUNK, CHUNK)
                here = pl.ds(start, CHUNK)
                grad, mixed = grad_ref[here].astype(wide), mixed_ref[here]
                silu_gate, slope = silu_parts(gate_ref[here].astype(wide))
                inverse = lax.rsqrt(jnp.mean(mixed * mixed, axis=1, keepdims=True) + epsilon)
                unit = mixed * inverse
                gate_grad = (grad * unit * scale * slope).astype(low)
                there = pl.ds(pl.multiple_of(chain // heads * span + start, CHUNK), CHUNK)
                lanes = pl.ds(pl.multiple_of(streams + chain % heads * head_size, 128), head_size)
                all_ref[there, lanes] = gate_grad
                passed = grad * silu_gate
                gain = gain + jnp.sum(passed * unit, axis=0, keepdims=True)
                scaled = passed * scale
                mixed_grad = inverse * (
                    scaled - unit * inverse * jnp.mean(scaled * mixed, axis=1, keepdims=True)
                )
                out_grads[chain, chunk] = mixed_grad
                query, key = qkv_ref[here, :head_size], qkv_ref[here, head_size : 2 * head_size]
                scores = jnp.where(rows >= columns, dot(query, key, NT), 0.0)
                turned = jnp.where(rows <= columns, dot(key, query, NT), 0.0)
                grads = pair(mixed_grad)
                fresh_grads[chain, chunk] = nn(pair(turned), grads)
                reading = query.astype(wide) - nn(
                    pair(scores), pair(wu_ref[0, chunk, :, :head_size])
                )
                sources[chain, chunk] = nn(pair(mixed_grad.T), pair(reading))
                maps[chain, chunk] = map_ref[0, chunk]
            return gain

        gain = lax.fori_loop(0, chunks // TOGETHER, group, jnp.zeros((1, head_size), wide))
        gain_ref[0] = jnp.broadcast_to(gain, (8, head_size))

    @pl.when(step < chains)
    def _():
        turn(step)

    @pl.when(step == chains - 1)
    def _():
        def advance(number, states):
            chunk = chunks - 1 - number
            return tuple(
                nn(pair(states[index]), pair(maps[index, chunk])) + sources[index, chunk]
                for index in range(chains)
            )

        ends = lax.fori_loop(
            0, chunks, advance, (jnp.zeros((head_size, head_size), wide),) * chains
        )

        @pl.when(above)
        def _():
            state_copy.wait_recv()

        @pl.when(place.line == lines - 1)
        def _():
            leaves[...] = jnp.zeros_like(leaves)

        for index in range(chains):
            entering = low_nn(leaves[index], pair(total_ref[index]))
            enters[index] = (entering + ends[index]).astype(low)
        pl.when(below)(state_copy.start)

        def again(number, states):
            chunk = chunks - 1 - number
            out = []
            for index in range(chains):
                leaving[index, chunk] = states[index]
                out.append(
                    nn(pair(states[index]), pair(maps[index, chunk])) + sources[index, chunk]
                )
            return tuple(out)

        lax.fori_loop(
            0, chunks, again, tuple(leaves[index].astype(wide) for index in range(chains))
        )
        for each in sums:
            each.round(2)

    def unwind(chain):
        seq, head = chain // heads, chain % heads
        ext[:16] = tails_ref[seq, :, pl.ds(pl.multiple_of(head * 3 * head_size, 128), 3 * head_size)].astype(wide)
        ext[16:] = raw_ref[...].astype(wide)
        taps = taps_ref[0]
        limit = limit_ref[seq]
        pre_grads[:16] = jnp.zeros((16, 3 * head_size), wide)
        pre_grads[span + 16 :] = jnp.zeros((16, 3 * head_size), wide)

        def one(chunk):
            start = pl.multiple_of(chunk * CHUNK, CHUNK)
            here = pl.ds(start, CHUNK)
            query = qkv_ref[here, :head_size]
            key = qkv_ref[here, head_size : 2 * head_size]
            value = qkv_ref[here, 2 * head_size :]
            live = live_rows(limit, start)
            squash = head_squash(logit_ref[here], head)
            beta = squash * live
            grads = pair(out_grads[chain, chunk])
            fresh = pair(fresh_in_ref[0, chunk])
            state = pair(state_ref[0, chunk])
            leave = pair(leaving[chain, chunk])
            both = wu_ref[0, chunk]
            fresh_grad = fresh_grads[chain, chunk] + low_nt(key, leave)
            fresh_pair = pair(fresh_grad)
            score_grad = jnp.where(rows >= columns, nt(grads, fresh), 0.0)
            turned_grad = jnp.where(rows <= columns, nt(fresh, grads), 0.0)
            query_grad = nt(grads, state) + nn_low(pair(score_grad), key)
            key_grad = nn_low(pair(turned_grad), query) + nn(fresh, leave)
            wkey_grad = -nt(fresh_pair, state)
            right_grad = nn_wide(pair(solved_ref[0, chunk].T), pair(side(wkey_grad, fresh_grad)))
            right = pair(right_grad)
            twos = pair(both)
            found = dot(right[0], over(*twos), NT)
            system_grad = found[:, :CHUNK] + found[:, CHUNK:] + dot(right[1], twos[0], NT)
            system_grad = jnp.where(rows > columns, -system_grad, 0.0)
            gram = dot(key, key, NT)
            gram_grad = beta * system_grad
            key_grad = key_grad + nn_low(pair(gram_grad + gram_grad.T), key)
            key_right, value_right = right_grad[:, :head_size], right_grad[:, head_size:]
            key_grad = key_grad + beta * key_right
            value_grad = beta * value_right
            beta_grad = jnp.sum(
                key_right * key.astype(wide) + value_right * value.astype(wide) + system_grad * gram,
                axis=1,
                keepdims=True,
            )
            lanes = lax.broadcasted_iota(jnp.int32, (CHUNK, head_size), 1)
            logit_grad = jnp.where(
                lanes == BETA_ROW + head, beta_grad * (live * squash * (1.0 - squash)), 0.0
            ).astype(low)

            there = pl.ds(pl.multiple_of(seq * span + start, CHUNK), CHUNK)
            last_lanes = pl.ds(streams + heads * head_size, head_size)

            @pl.when(head == 0)
            def _():
                all_ref[there, last_lanes] = logit_grad

            @pl.when(head > 0)
            def _():
                all_ref[there, last_lanes] = all_ref[there, last_lanes] + logit_grad

            block = ext[pl.ds(start, CHUNK + 16)]
            grads_pre = []
            for stream, grad in enumerate((query_grad, key_grad, value_grad)):
                act, slope = silu_parts(convolved(block, taps, stream))
                if stream < 2:
                    inverse = lax.rsqrt(jnp.sum(act * act, axis=1, keepdims=True) + epsilon)
                    inner = jnp.sum(act * grad, axis=1, keepdims=True)
                    grad = inverse * (grad - act * (inverse * inverse * inner))
                    if stream == 0:
                        grad = grad * head_size ** (-0.5)
                grads_pre.append(grad * slope)
            pre_grads[pl.ds(start + 16, CHUNK)] = jnp.concatenate(grads_pre, axis=1)

        def group(index, carry):
            for number in range(2):
                one(index * 2 + number)
            return carry

        lax.fori_loop(0, chunks // 2, group, 0)

        def back(block):
            parts = []
            for stream in range(3):
                part = block[:, stream * head_size : (stream + 1) * head_size]
                total = None
                for offset in range(CONV):
                    first = CONV - 1 - offset
                    term = taps[stream * CONV + offset][None, :] * part[first : first + CHUNK]
                    total = term if total is None else total + term
                parts.append(total)
            return jnp.concatenate(parts, axis=1)

        lanes = pl.ds(pl.multiple_of(head * 3 * head_size, 128), 3 * head_size)

        def finish(chunk, totals):
            start = pl.multiple_of(chunk * CHUNK, CHUNK)
            block = pre_grads[pl.ds(start + 16, CHUNK + 16)]
            grad = back(block)
            there = pl.ds(pl.multiple_of(seq * span + start, CHUNK), CHUNK)
            all_ref[there, lanes] = grad.astype(low)
            edges[chain] = grad[CHUNK - 16 :]
            before = ext[pl.ds(start, CHUNK + 16)]
            pre = block[:CHUNK]
            out = []
            for offset in range(CONV):
                first = 16 - (CONV - 1) + offset
                term = jnp.sum(pre * before[first : first + CHUNK], axis=0, keepdims=True)
                out.append(totals[offset] + term)
            return tuple(out)

        zero = jnp.zeros((1, 3 * head_size), wide)
        totals = lax.fori_loop(0, chunks, finish, (zero,) * CONV)
        for offset in range(CONV):
            taps_grad_ref[0, offset : offset + 1] = totals[offset]
        halos[chain] = back(pre_grads[: CHUNK + 32])[:16].astype(low)
        pl.when(below)(halo(chain).start)

    @pl.when(step >= chains)
    def _():
        unwind(step - chains)

    @pl.when(step == chains)
    def _():
        share.forward()

    @pl.when(step == chains + 1)
    def _():
        share.forward_far()

    @pl.when(step == 2 * chains - 3)
    def _():
        for each in sums:
            each.round(3)

    @pl.when(step == 2 * chains - 1)
    def _():
        for each in sums:
            for number in range(4, lines):
                each.round(number)
            each.exchange()
        for chain in range(chains):
            seq, head = chain // heads, chain % heads
            last = pl.ds((seq + 1) * span - 16, 16)
            lanes = pl.ds(head * 3 * head_size, 3 * head_size)

            @pl.when(above)
            def _(chain=chain, last=last, lanes=lanes):
                halo(chain).wait_recv()
                all_ref[last, lanes] = (edges[chain] + returned[chain].astype(wide)).astype(low)

        for chain in range(chains):
            pl.when(below)(halo(chain).wait_send)
        pl.when(below)(state_copy.wait_send)
        share.finish()
        for each in sums:
            each.finish()


def project_kernel(input_ref, scale_ref, weight_ref, beta_ref, normed_ref, raw_ref, logit_ref):
    value = input_ref[...].astype(wide)
    normed = (value * inverse_rms(value) * scale_ref[...]).astype(low)
    normed_ref[...] = normed
    raw_ref[...] = dot(normed, weight_ref[...], NN).astype(low)
    logit_ref[...] = dot(normed, beta_ref[...], NT)


def back_project_kernel(grad_ref, weight_ref, beta_ref, out_ref):
    width = weight_ref.shape[1]
    total = dot(grad_ref[:, :width], weight_ref[...], NT)
    out_ref[...] = (total + dot(grad_ref[:, width:], beta_ref[...], NN)).astype(low)


MESH = pl.DeviceIdType.MESH
STEP = 16


class Place:
    def __init__(self):
        self.seq = lax.axis_index("seq")
        self.core = lax.axis_index("tp")
        self.mate = self.seq % MATES
        self.line = self.seq // MATES
        x, y = self.mate % 2, self.mate // 2
        self.x = 2 * y + (1 - x)
        self.y = 2 * (1 - y) + x
        self.far = 2 * (1 - y) + (1 - x)
        self.base = self.seq - self.mate

    def of(self, mate, other=0):
        return (self.base + mate, 1 - self.core if other else self.core)

    @property
    def sibling(self):
        return (self.seq, 1 - self.core)

    def lines_away(self, step):
        return (self.seq + step * MATES, self.core)


def meet(place, far=False, lines=0, cores=False, straight=False):
    barrier = pltpu.get_barrier_semaphore()
    partners = [place.of(place.x), place.of(place.y), place.sibling]
    if far or cores:
        partners.append(place.of(place.far))
    if cores:
        partners += [place.of(mate, 1) for mate in (place.x, place.y, place.far)]
    for partner in partners:
        pl.semaphore_signal(barrier, inc=1, device_id=partner, device_id_type=MESH)
    count = len(partners)
    if straight:
        for step in range(1, lines):
            line = (place.line + step) % lines
            pl.semaphore_signal(
                barrier,
                inc=1,
                device_id=(line * MATES + place.mate, place.core),
                device_id_type=MESH,
            )
        count = count + max(lines - 1, 0)
    elif lines > 1:
        below, above = place.line > 0, place.line < lines - 1

        @pl.when(below)
        def _():
            pl.semaphore_signal(
                barrier, inc=1, device_id=place.lines_away(-1), device_id_type=MESH
            )

        @pl.when(above)
        def _():
            pl.semaphore_signal(barrier, inc=1, device_id=place.lines_away(1), device_id_type=MESH)

        count = count + jnp.where(below, 1, 0) + jnp.where(above, 1, 0)
    pl.semaphore_wait(barrier, count)


def sender(sems):
    send, receive = sems

    def make(index, source, target, device):
        return pltpu.make_async_remote_copy(
            src_ref=source,
            dst_ref=target,
            send_sem=send.at[index],
            recv_sem=receive.at[index],
            device_id=device,
            device_id_type=MESH,
        )

    return make


def row_steps(first, last, body):
    def one(step, carry):
        body(pl.ds(pl.multiple_of(first + step * STEP, STEP), STEP))
        return carry

    lax.fori_loop(0, (last - first) // STEP, one, 0)


class SumRows:
    SCRATCH = 4

    @staticmethod
    def scratch(rows, columns):
        return [
            pltpu.VMEM((MATES, rows, columns), low),
            pltpu.VMEM((MATES, rows, columns), low),
            pltpu.VMEM((2, rows // 2, columns), low),
            pltpu.VMEM((2, rows, columns), low),
            pltpu.SemaphoreType.DMA((MATES,)),
            pltpu.SemaphoreType.DMA((10,)),
            pltpu.SemaphoreType.DMA((10,)),
        ]

    def __init__(self, place, partial, scratch):
        self.place, self.partial = place, partial
        self.own, self.swapped, self.relay, self.arrived, self.local_sems, send, receive = scratch
        self.make = sender((send, receive))
        self.rows = self.own.shape[1]
        self.order = [place.far, place.x, place.y, place.mate]

    def begin(self):
        self.swaps, self.loads = [], []
        for slot, mate in enumerate(self.order):
            copy = self.make(
                slot, self.partial.at[1, mate], self.swapped.at[slot], self.place.sibling
            )
            copy.start()
            self.swaps.append(copy)
            load = pltpu.make_async_copy(
                self.partial.at[0, mate], self.own.at[slot], self.local_sems.at[slot]
            )
            load.start()
            self.loads.append(load)

    def add(self, target, target_slot, source, source_slot, first, last, shift=0):
        def body(here):
            there = pl.ds(pl.multiple_of(here.start - shift, STEP), STEP) if shift else here
            target[target_slot, here] = (
                target[target_slot, here].astype(wide) + source[source_slot, there].astype(wide)
            ).astype(low)

        row_steps(first, last, body)

    def sum_cores(self, slot):
        self.loads[slot].wait()
        self.swaps[slot].wait_recv()
        self.add(self.own, slot, self.swapped, slot, 0, self.rows)

    def send_far(self):
        half = self.rows // 2
        self.sum_cores(0)
        self.far_low = self.make(
            4, self.own.at[0, :half], self.relay.at[0], self.place.of(self.place.y)
        )
        self.far_high = self.make(
            5, self.own.at[0, half:], self.relay.at[1], self.place.of(self.place.x)
        )
        self.far_low.start()
        self.far_high.start()

    def send_near(self):
        half, place = self.rows // 2, self.place
        self.sum_cores(1)
        self.x_high = self.make(
            6, self.own.at[1, half:], self.arrived.at[0, half:], place.of(place.x)
        )
        self.x_high.start()
        self.sum_cores(2)
        self.y_low = self.make(
            7, self.own.at[2, :half], self.arrived.at[1, :half], place.of(place.y)
        )
        self.y_low.start()

    def send_relayed(self):
        half, place = self.rows // 2, self.place
        self.far_low.wait_recv()
        self.add(self.own, 1, self.relay, 0, 0, half)
        self.x_low = self.make(
            8, self.own.at[1, :half], self.arrived.at[0, :half], place.of(place.x)
        )
        self.x_low.start()
        self.far_high.wait_recv()
        self.add(self.own, 2, self.relay, 1, half, self.rows, shift=half)
        self.y_high = self.make(
            9, self.own.at[2, half:], self.arrived.at[1, half:], place.of(place.y)
        )
        self.y_high.start()
        self.sum_cores(3)

    def wait_half(self, upper):
        if upper:
            self.x_high.wait_recv()
            self.y_high.wait_recv()
        else:
            self.x_low.wait_recv()
            self.y_low.wait_recv()

    def total(self, here):
        return (
            self.own[3, here].astype(wide)
            + self.arrived[0, here].astype(wide)
            + self.arrived[1, here].astype(wide)
        )

    def finish(self):
        for copy in self.swaps + [
            self.far_low, self.far_high, self.x_high, self.y_low, self.x_low, self.y_high,
        ]:
            copy.wait_send()


class ShareRows:
    @staticmethod
    def scratch():
        return [
            pltpu.SemaphoreType.DMA((1,)),
            pltpu.SemaphoreType.DMA((11,)),
            pltpu.SemaphoreType.DMA((11,)),
        ]

    def __init__(self, place, source, target, scratch):
        self.place, self.source, self.target = place, source, target
        self.local_sem, send, receive = scratch
        self.make = sender((send, receive))
        self.rows = target.shape[2]

    def copy(self, index):
        place, half = self.place, self.rows // 2
        lower, upper, whole = pl.ds(0, half), pl.ds(half, half), pl.ds(0, self.rows)
        x, y, sibling = place.of(place.x), place.of(place.y), place.sibling

        def own(rows, device, side=0):
            return self.source.at[rows], self.target.at[side, place.mate, rows], device

        def passed(mate, rows, device, side=0):
            return self.target.at[0, mate, rows], self.target.at[side, mate, rows], device

        return self.make(
            index,
            *(
                lambda: own(upper, y),
                lambda: own(upper, x),
                lambda: own(lower, x),
                lambda: own(lower, y),
                lambda: passed(place.x, lower, y),
                lambda: passed(place.y, upper, x),
                lambda: own(whole, sibling, 1),
                lambda: passed(place.x, whole, sibling, 1),
                lambda: passed(place.y, whole, sibling, 1),
                lambda: passed(place.far, lower, sibling, 1),
                lambda: passed(place.far, upper, sibling, 1),
            )[index](),
        )

    def local(self):
        return pltpu.make_async_copy(
            self.source, self.target.at[0, self.place.mate], self.local_sem.at[0]
        )

    def begin_half(self, upper):
        for index in (0, 1) if upper else (2, 3):
            self.copy(index).start()

    def begin_rest(self):
        self.local().start()
        self.copy(6).start()

    def forward(self):
        for came, then in ((2, 4), (0, 5), (1, 7), (3, 8)):
            self.copy(came).wait_recv()
            self.copy(then).start()

    def forward_far(self):
        for came, then in ((4, 9), (5, 10)):
            self.copy(came).wait_recv()
            self.copy(then).start()

    def finish(self):
        self.local().wait()
        for index in range(6, 11):
            self.copy(index).wait_recv()
        for index in range(11):
            self.copy(index).wait_send()


class GatherLines:
    @staticmethod
    def scratch(lines):
        return [
            pltpu.SemaphoreType.DMA((1,)),
            pltpu.SemaphoreType.DMA((3,)),
            pltpu.SemaphoreType.DMA((3,)),
            pltpu.SemaphoreType.DMA((lines, MATES)),
            pltpu.SemaphoreType.DMA((lines, MATES)),
            pltpu.SemaphoreType.DMA((lines, MATES)),
        ]

    def __init__(self, place, blocks, target, scratch, rows=None):
        self.place, self.blocks, self.target = place, blocks, target
        self.lines = target.shape[0]
        self.part = pl.ds(*(rows or (0, target.shape[2])))
        self.local_sem, send, receive, self.up_sem, self.down_sem, self.got = scratch
        self.make = sender((send, receive))
        self.order = [place.mate, place.x, place.y, place.far]

    def plane(self, slot):
        place, mate = self.place, self.order[slot]
        here = self.target.at[place.line, place.mate]
        if slot == 0:
            return pltpu.make_async_copy(self.blocks.at[mate], here, self.local_sem.at[0])
        return self.make(slot - 1, self.blocks.at[mate], here, place.of(mate))

    def begin(self):
        for slot in range(MATES):
            self.plane(slot).start()

    def arrive(self, slot):
        copy = self.plane(slot)
        copy.wait_recv() if slot else copy.wait()

    def hop(self, step, mate, direction):
        place = self.place
        line = place.line - step * direction
        piece = self.target.at[line, mate, self.part]
        sems = self.up_sem if direction > 0 else self.down_sem
        copy = pltpu.make_async_remote_copy(
            src_ref=piece,
            dst_ref=piece,
            send_sem=sems.at[step, mate],
            recv_sem=self.got.at[line, mate],
            device_id=place.lines_away(direction),
            device_id_type=MESH,
        )
        came = (line >= 0) & (line < self.lines)
        goes = (place.line < self.lines - 1) if direction > 0 else (place.line > 0)
        return copy, came, goes

    def leave(self, arriving=True):
        for slot, mate in enumerate(self.order):
            if arriving:
                self.arrive(slot)
            for direction in (1, -1):
                copy, _, goes = self.hop(0, mate, direction)
                pl.when(goes)(copy.start)

    def onwards(self, step):
        if step >= self.lines:
            return
        for mate in self.order:
            for direction in (1, -1):
                copy, came, goes = self.hop(step, mate, direction)
                pl.when(came)(copy.wait_recv)
                if step < self.lines - 1:
                    pl.when(came & goes)(copy.start)

    def finish_plane(self):
        for slot in range(1, MATES):
            self.plane(slot).wait_send()

    def finish_lines(self):
        for step in range(self.lines - 1):
            for mate in self.order:
                for direction in (1, -1):
                    copy, came, goes = self.hop(step, mate, direction)
                    pl.when(came & goes)(copy.wait_send)


class SwapBlocks:
    @staticmethod
    def scratch():
        return [
            pltpu.SemaphoreType.DMA((1,)),
            pltpu.SemaphoreType.DMA((2 * MATES,)),
            pltpu.SemaphoreType.DMA((2 * MATES,)),
        ]

    def __init__(self, place, piece, target, scratch):
        self.place, self.piece, self.target = place, piece, target
        self.local_sem, send, receive = scratch
        self.make = sender((send, receive))
        self.order = [place.far, place.x, place.y, place.mate]

    def copy(self, slot, index):
        place, mate = self.place, self.order[index]
        source, target = self.piece(slot, mate), self.target.at[slot, place.mate]
        if slot == 0 and index == MATES - 1:
            return pltpu.make_async_copy(source, target, self.local_sem.at[0]), True
        return self.make(slot * MATES + index, source, target, place.of(mate, slot)), False

    def begin(self, slot, index=None):
        for each in range(MATES) if index is None else (index,):
            self.copy(slot, each)[0].start()

    def finish(self):
        for slot in range(2):
            for index in range(MATES):
                self.copy(slot, index)[0].wait()


class SumLines:
    @staticmethod
    def scratch(lines, shape):
        return [
            pltpu.VMEM((lines,) + shape, low),
            pltpu.VMEM((2, max(lines - 1, 1)) + shape, low),
            pltpu.SemaphoreType.DMA((lines + 1,)),
            pltpu.SemaphoreType.DMA((2, lines)),
            pltpu.SemaphoreType.DMA((2, lines)),
            pltpu.SemaphoreType.DMA((3,)),
            pltpu.SemaphoreType.DMA((3,)),
        ]

    def __init__(self, place, blocks, result, scratch, first=0):
        self.place, self.blocks, self.result, self.first = place, blocks, result, first
        self.held, self.came, self.local_sems, self.send, self.got, send, receive = scratch
        self.lines = self.held.shape[0]
        self.make = sender((send, receive))

    def load(self, line):
        return pltpu.make_async_copy(
            self.blocks.at[
                line, :, pl.ds(self.first, self.held.shape[2]), pl.ds(0, self.held.shape[3])
            ],
            self.held.at[line],
            self.local_sems.at[line],
        )

    def begin(self):
        for line in range(self.lines):
            self.load(line).start()

    def wait_loads(self):
        for line in range(self.lines):
            self.load(line).wait()

    def put_gains(self, gains):
        lines, mates, height, lanes = self.held.shape
        top = lax.broadcasted_iota(jnp.int32, (height, lanes), 0) == 0
        for line in range(lines):
            for mate in range(mates):
                first = (line * mates + mate) * lanes
                part = jnp.broadcast_to(gains[:, first : first + lanes], (height, lanes))
                self.held[line, mate] = jnp.where(
                    top, part, self.held[line, mate].astype(wide)
                ).astype(low)

    def add_top(self, other, count):
        lines, mates, height, lanes = self.held.shape
        top = lax.broadcasted_iota(jnp.int32, (height, lanes), 0) < count
        for line in range(lines):
            for mate in range(mates):
                own = self.held[line, mate].astype(wide)
                both = own + other[line, mate].astype(wide)
                self.held[line, mate] = jnp.where(top, both, own).astype(low)

    def copy(self, turn, way):
        direction = 1 - 2 * way
        line = self.place.line + direction * (self.lines - turn)
        return line, pltpu.make_async_remote_copy(
            src_ref=self.held.at[line],
            dst_ref=self.came.at[way, turn - 1],
            send_sem=self.send.at[way, turn],
            recv_sem=self.got.at[way, turn],
            device_id=self.place.lines_away(direction),
            device_id_type=MESH,
        )

    def arrival(self, turn, way):
        slot = self.came.at[way, turn - 1]
        return pltpu.make_async_remote_copy(
            src_ref=slot,
            dst_ref=slot,
            send_sem=self.send.at[way, turn],
            recv_sem=self.got.at[way, turn],
            device_id=self.place.sibling,
            device_id_type=MESH,
        )

    def sends(self, turn, way):
        line = self.place.line
        return line <= turn - 1 if way == 0 else line >= self.lines - turn

    def inner(self, way):
        return self.place.line >= 1 if way == 0 else self.place.line <= self.lines - 2

    def add(self, line, way, turn):
        def mates(mate, carry):
            def body(here):
                self.held[line, mate, here] = (
                    self.held[line, mate, here].astype(wide)
                    + self.came[way, turn - 1, mate, here].astype(wide)
                ).astype(low)

            row_steps(0, self.held.shape[2], body)
            return carry

        lax.fori_loop(0, self.held.shape[1], mates, 0)

    def round(self, turn):
        if turn >= self.lines:
            return
        for way in (0, 1):
            line, copy = self.copy(turn, way)

            @pl.when(self.sends(turn, way))
            def _(line=line, copy=copy, way=way):
                if turn > 1:

                    @pl.when(self.inner(way))
                    def _():
                        self.arrival(turn - 1, way).wait_recv()
                        self.add(line, way, turn - 1)

                copy.start()

    def plane(self, index):
        place = self.place
        mate = (place.x, place.y, place.far)[index]
        return self.make(
            index, self.held.at[place.line, mate], self.result.at[place.mate], place.of(mate)
        )

    def local(self):
        place = self.place
        return pltpu.make_async_copy(
            self.held.at[place.line, place.mate],
            self.result.at[place.mate],
            self.local_sems.at[self.lines],
        )

    def exchange(self):
        for way in (0, 1):
            if self.lines > 1:

                @pl.when(self.inner(way))
                def _(way=way):
                    self.arrival(self.lines - 1, way).wait_recv()
                    self.add(self.place.line, way, self.lines - 1)

        for index in range(3):
            self.plane(index).start()
        self.local().start()

    def straight(self, step):
        line = (self.place.line + step) % self.lines
        return pltpu.make_async_remote_copy(
            src_ref=self.held.at[line],
            dst_ref=self.came.at[0, step - 1],
            send_sem=self.send.at[0, step],
            recv_sem=self.got.at[0, step],
            device_id=(line * MATES + self.place.mate, self.place.core),
            device_id_type=MESH,
        )

    def direct(self):
        for step in range(1, self.lines):
            self.straight(step).start()

    def exchange_direct(self):
        for step in range(1, self.lines):
            self.straight(step).wait_recv()
            self.add(self.place.line, 0, step)
        for index in range(3):
            self.plane(index).start()
        self.local().start()

    def finish(self, direct=False):
        self.local().wait()
        for index in range(3):
            self.plane(index).wait()
        if direct:
            for step in range(1, self.lines):
                self.straight(step).wait_send()
            return
        for turn in range(1, self.lines):
            for way in (0, 1):
                _, copy = self.copy(turn, way)
                pl.when(self.sends(turn, way))(copy.wait_send)


def remote_call(body, identity, ins, outs, scratch, aliases=None):
    anywhere = pl.BlockSpec(memory_space=pl.ANY)
    held = pl.BlockSpec(memory_space=pltpu.VMEM)
    return pl.pallas_call(
        body,
        in_specs=[anywhere if kind == "any" else held for _, kind in ins],
        out_specs=[anywhere if kind == "any" else held for _, _, kind in outs],
        out_shape=[jax.ShapeDtypeStruct(shape, dtype) for shape, dtype, _ in outs],
        scratch_shapes=scratch,
        input_output_aliases=aliases or {},
        compiler_params=pltpu.CompilerParams(
            vmem_limit_bytes=VMEM_BYTES, collective_id=identity, has_side_effects=True
        ),
    )(*[array for array, _ in ins])


def inverse_rms(value):
    return lax.rsqrt(jnp.mean(value * value, axis=1, keepdims=True) + epsilon)


def norm_back_rows(grad, source, scale):
    inverse = inverse_rms(source)
    scaled = grad * scale
    unit = source * inverse
    inner = jnp.mean(scaled * source, axis=1, keepdims=True)
    return inverse * (scaled - unit * (inverse * inner)), grad * unit


def load_weights(weights, held, sems):
    return [
        pltpu.make_async_copy(weights.at[slot, mate], held.at[slot, mate], sems.at[slot, mate])
        for slot in range(2)
        for mate in range(MATES)
    ]


def middle_kernel(lines, moves, gathered, weights, input_ref, scale_ref, grad_any, *rest):
    place = Place()
    count = len(moves)
    middle_ref, shared, grads = rest[count : count + 3]
    targets, scratch = rest[count + 3 : 2 * count + 3], rest[2 * count + 3 :]
    normed, held, weight_sems = scratch[:3]
    share = ShareRows(place, normed, shared, scratch[3:6])
    other = ShareRows(place, grad_any.at[place.core], grads, scratch[6:9])
    gathers = [
        GatherLines(place, None, target, scratch[9 + 6 * index : 15 + 6 * index], moves[index])
        for index, target in enumerate(targets)
    ]
    meet(place, lines=lines if moves else 0)
    loads = load_weights(weights, held, weight_sems)
    for load in loads:
        load.start()
    for gather in gathers:
        gather.leave(False)
    for load in loads:
        load.wait()
    rows = normed.shape[0]
    half = rows // 2
    _, _, all_lines, _, depth, width = held.shape

    height = MATES * depth
    some = max(1, 512 // height)

    def product(step, carry):
        columns = pl.ds(pl.multiple_of(step * some * height, 128), some * height)
        part = pl.ds(step * some, some)
        for first in (0, half):
            total = None
            for slot in range(2):
                for mate in range(MATES):
                    term = dot(
                        gathered[slot, mate, first : first + half],
                        held[slot, mate, part].reshape(some * height, width),
                        NT,
                    )
                    total = term if total is None else total + term
            here = pl.ds(first, half)
            middle_ref[here, columns] = input_ref[here, columns].astype(wide) + total
        return carry

    def body(here):
        middle = middle_ref[here]
        normed[here] = (middle * inverse_rms(middle) * scale_ref[...]).astype(low)

    lax.fori_loop(0, all_lines // some, product, 0)
    row_steps(0, half, body)
    share.begin_half(False)
    row_steps(half, rows, body)
    share.begin_half(True)
    share.begin_rest()
    for gather in gathers:
        gather.onwards(1)
    share.forward()
    other.begin_half(False)
    other.begin_half(True)
    other.begin_rest()
    share.forward_far()
    for gather in gathers:
        gather.onwards(2)
    other.forward()
    other.forward_far()
    for number in range(3, lines):
        for gather in gathers:
            gather.onwards(number)
    for gather in gathers:
        gather.finish_lines()
    share.finish()
    other.finish()


def turn_rows_kernel(
    lines, parts, partial, weights, middle_ref, grad_ref, scale_ref, *rest
):
    place = Place()
    count = len(parts)
    blocks, rest = rest[:count], rest[count:]
    middle_grad_ref, gain_ref, low_grad, gated_grads = rest[:4]
    results, scratch = rest[4 : 4 + count], rest[4 + count :]
    held, weight_sems, sent = scratch[:3]
    rows = SumRows(place, partial, scratch[3:10])
    swap = SwapBlocks(place, lambda slot, mate: sent.at[slot, mate], gated_grads, scratch[10:13])
    sums = [
        SumLines(place, blocks[index], results[index], scratch[13 + 7 * index : 20 + 7 * index], first)
        for index, (first, _) in enumerate(parts)
    ]
    meet(place, lines=lines if parts else 0, cores=True)
    rows.begin()
    for each in sums:
        each.begin()
    loads = load_weights(weights, held, weight_sems)
    for load in loads:
        load.start()
    gain_ref[...] = jnp.zeros_like(gain_ref)
    rows.send_far()
    for each in sums:
        each.wait_loads()
        each.round(1)
    rows.send_near()
    rows.send_relayed()
    for load in loads:
        load.wait()
    for each in sums:
        each.round(2)
    rows.wait_half(False)
    rows.wait_half(True)

    def body(here):
        part, gains = norm_back_rows(rows.total(here), middle_ref[here], scale_ref[...])
        total = grad_ref[here].astype(wide) + part
        middle_grad_ref[here] = total
        low_grad[here] = total.astype(low)
        gain_ref[...] += jnp.sum(gains, axis=0, keepdims=True)

    row_steps(0, low_grad.shape[0], body)
    _, _, all_lines, _, depth, width = held.shape
    for slot in range(2):
        for index, mate in enumerate(swap.order):
            weight = held[slot, mate].reshape(all_lines * MATES * depth, width)
            sent[slot, mate] = dot(low_grad[...], weight, NN).astype(low)
            swap.begin(slot, index)
    rows.finish()
    for each in sums:
        each.round(3)
    swap.finish()
    for each in sums:
        for number in range(4, lines):
            each.round(number)
        each.exchange()
    for each in sums:
        each.finish()


def last_rows_kernel(
    lines, pieces, partial, mlp_partial, input_ref, middle_ref, middle_grad_ref, scale_ref, *rest
):
    place = Place()
    blocks, rest = rest[:pieces], rest[pieces:]
    input_grad, block_output, gain_ref = rest[:3]
    results, scratch = rest[3 : 3 + pieces], rest[3 + pieces :]
    low_grad, low_output = scratch[:2]
    meet(place, far=bool(pieces), lines=lines if pieces else 0, straight=True)
    rows = SumRows(place, partial, scratch[2:9])
    outs = SumRows(place, mlp_partial, scratch[9:16])
    make = sender(scratch[16:18])
    local_sems = scratch[18]
    sums = [
        SumLines(place, blocks[index], results[index], scratch[19 + 7 * index : 26 + 7 * index])
        for index in range(pieces)
    ]
    whole = low_grad.shape[0]
    for each in sums:
        each.begin()
    rows.begin()
    outs.begin()
    for each in sums:
        each.wait_loads()
    for each in sums[1:]:
        each.round(1)
    gain_ref[...] = jnp.zeros_like(gain_ref)
    rows.send_far()
    rows.send_near()
    rows.send_relayed()
    outs.send_far()
    outs.send_near()
    for each in sums[1:]:
        each.round(2)
    rows.wait_half(False)
    rows.wait_half(True)

    def body(here):
        part, gains = norm_back_rows(
            rows.total(here), input_ref[here].astype(wide), scale_ref[...]
        )
        low_grad[here] = (middle_grad_ref[here] + part).astype(low)
        gain_ref[...] += jnp.sum(gains, axis=0, keepdims=True)

    row_steps(0, whole, body)
    first = make(0, low_grad, input_grad.at[place.core], place.sibling)
    first.start()
    first_local = pltpu.make_async_copy(low_grad, input_grad.at[place.core], local_sems.at[0])
    first_local.start()
    if sums:
        mine, theirs = scratch[19 + 7 * pieces :]
        small = sums[0]
        small.put_gains(gain_ref)
        mine[...] = small.held[...]
        swap = make(2, mine, theirs, place.sibling)
        swap.start()
        swap.wait_recv()
        small.add_top(theirs, CONV_ROW)
        small.direct()
    outs.send_relayed()
    for each in sums[1:]:
        each.round(3)
    outs.wait_half(False)
    outs.wait_half(True)

    def out_body(here):
        low_output[here] = (middle_ref[here] + outs.total(here)).astype(low)

    row_steps(0, whole, out_body)
    second = make(1, low_output, block_output.at[place.core], place.sibling)
    second.start()
    second_local = pltpu.make_async_copy(low_output, block_output.at[place.core], local_sems.at[1])
    second_local.start()
    for turn in range(4, lines):
        for each in sums[1:]:
            each.round(turn)
    for each in sums[:1]:
        each.exchange_direct()
    for each in sums[1:]:
        each.exchange()
    rows.finish()
    outs.finish()
    first_local.wait()
    second_local.wait()
    first.wait()
    second.wait()
    if sums:
        swap.wait_send()
    for each in sums:
        each.finish(direct=each is sums[0])


def first_rows_kernel(input_ref, inputs, *scratch):
    place = Place()
    meet(place)
    share = ShareRows(place, input_ref.at[place.core], inputs, scratch)
    share.begin_half(False)
    share.begin_half(True)
    share.begin_rest()
    share.forward()
    share.forward_far()
    share.finish()


def first_rows(block_input):
    seqs, rows, columns = block_input.shape
    return remote_call(
        first_rows_kernel,
        0,
        [(block_input, "any")],
        [((seqs, MATES, rows, columns), low, "any")],
        ShareRows.scratch(),
    )[0]


def first_kernel(lines, pieces, input_ref, *rest):
    place = Place()
    blocks, rest = rest[:pieces], rest[pieces:]
    normed_out, raw_ref, logit_ref, small_ref, attn_out = rest[:5]
    others, scratch = rest[5 : 3 + pieces], rest[3 + pieces :]
    inputs, normed, small, attn, scale, out_sems = scratch[:6]
    scratch = scratch[6:]
    targets = (small, attn) + tuple(others)
    meet(place, far=True, lines=lines)
    share = ShareRows(place, input_ref.at[place.core], inputs, scratch[:3])
    gathers = [
        GatherLines(place, blocks[index], targets[index], scratch[3 + 6 * index : 9 + 6 * index])
        for index in range(pieces)
    ]
    few, main = gathers[:2]
    for gather in (few, main):
        gather.begin()
    for gather in (few, main):
        gather.leave()
    share.begin_half(False)
    share.begin_half(True)
    share.begin_rest()
    for gather in (few, main):
        gather.onwards(1)
    share.forward()
    for gather in gathers[2:]:
        gather.begin()
    few.onwards(2)
    main.onwards(2)
    for step in range(3, lines):
        few.onwards(step)
    share.forward_far()
    share.finish()
    small_ref[...] = small[...]
    _, _, tokens, model_width = inputs.shape
    depth = small.shape[3]
    parts = [(line, mate) for line in range(lines) for mate in range(MATES)]
    for index, (line, mate) in enumerate(parts):
        scale[:, index * depth : (index + 1) * depth] = small[line, mate, :1].astype(wide)
    beta = jnp.concatenate([small[line, mate] for line, mate in parts], axis=1)
    beta = over(beta, jnp.zeros((CHUNK - beta.shape[0], model_width), low))
    outs = []
    for slot in range(2):
        for mate in range(MATES):
            first = (slot * MATES + mate) * tokens

            def body(here, slot=slot, mate=mate, first=first):
                value = inputs[slot, mate, here].astype(wide)
                there = pl.ds(pl.multiple_of(first + here.start, STEP), STEP)
                normed[there] = (value * inverse_rms(value) * scale[...]).astype(low)

            row_steps(0, tokens, body)
            block = pl.ds(first, tokens)
            logit_ref[block] = dot(normed[block], beta, NT)
            outs.append(
                pltpu.make_async_copy(
                    normed.at[block], normed_out.at[block], out_sems.at[slot * MATES + mate]
                )
            )
            outs[-1].start()
    for step in range(3, lines):
        main.onwards(step)
    outs.append(pltpu.make_async_copy(attn, attn_out, out_sems.at[2 * MATES]))
    outs[-1].start()
    weight = attn[...].reshape(model_width, attn.shape[3])

    def product(index, carry):
        here = pl.ds(pl.multiple_of(index * tokens, STEP), tokens)
        raw_ref[here] = dot(normed[here], weight, NN).astype(low)
        return carry

    lax.fori_loop(0, 2 * MATES, product, 0)
    for gather in gathers[2:]:
        for slot in range(MATES):
            gather.arrive(slot)
    for out in outs:
        out.wait()
    for gather in gathers:
        gather.finish_plane()
    for gather in (few, main):
        gather.finish_lines()


def first_call(block_input, blocks, lines):
    seqs, tokens, model_width = block_input.shape
    rows = seqs * MATES * tokens
    small, attn = ((lines,) + block.shape for block in blocks[:2])
    shared = (seqs, MATES, tokens, model_width)
    return remote_call(
        functools.partial(first_kernel, lines, len(blocks)),
        0,
        [(array, "any") for array in (block_input, *blocks)],
        [
            ((rows, model_width), low, "any"),
            ((rows, attn[3]), low, "held"),
            ((rows, CHUNK), wide, "held"),
            (small, low, "held"),
            (attn, low, "any"),
        ]
        + [((lines,) + block.shape, low, "any") for block in blocks[2:]],
        [
            pltpu.VMEM(shared, low),
            pltpu.VMEM((rows, model_width), low),
            pltpu.VMEM(small, low),
            pltpu.VMEM(attn, low),
            pltpu.VMEM((1, model_width), wide),
            pltpu.SemaphoreType.DMA((2 * MATES + 1,)),
        ]
        + ShareRows.scratch()
        + GatherLines.scratch(lines) * len(blocks),
    )


def middle_rows(gathered, weights, mine, scale, out_grad, moving, lines):
    rows, columns = mine.shape
    shared = (2, MATES, rows, columns)
    arrays = [array for array, _ in moving]
    return remote_call(
        functools.partial(middle_kernel, lines, tuple(part for _, part in moving)),
        1,
        [(gathered, "held"), (weights, "any"), (mine, "held"), (scale, "held"), (out_grad, "any")]
        + [(array, "any") for array in arrays],
        [((rows, columns), wide, "held"), (shared, low, "any"), (shared, low, "any")]
        + [(array.shape, low, "any") for array in arrays],
        [
            pltpu.VMEM((rows, columns), low),
            pltpu.VMEM(weights.shape, low),
            pltpu.SemaphoreType.DMA((2, MATES)),
        ]
        + ShareRows.scratch() * 2
        + GatherLines.scratch(lines) * len(arrays),
        {5 + index: 3 + index for index in range(len(arrays))},
    )


def turn_rows(partial, weights, middle, grad, scale, summing, lines):
    seqs, _, rows, columns = partial.shape
    width = weights.shape[-1]
    blocks = (2, MATES, rows, width)
    scratch = [
        pltpu.VMEM(weights.shape, low),
        pltpu.SemaphoreType.DMA((2, MATES)),
        pltpu.VMEM(blocks, low),
    ]
    scratch += SumRows.scratch(rows, columns) + SwapBlocks.scratch()
    outs = []
    for array, (_, height) in summing:
        shape = (MATES, height, array.shape[3])
        scratch += SumLines.scratch(lines, shape)
        outs.append((shape, low, "any"))
    return remote_call(
        functools.partial(turn_rows_kernel, lines, tuple(part for _, part in summing)),
        2,
        [(partial, "any"), (weights, "any"), (middle, "held"), (grad, "held"), (scale, "held")]
        + [(array, "any") for array, _ in summing],
        [
            ((rows, columns), wide, "held"),
            ((1, columns), wide, "held"),
            ((rows, columns), low, "held"),
            (blocks, low, "any"),
        ]
        + outs,
        scratch,
    )


def last_rows(partial, mlp_partial, mine, middle, middle_grad, scale, blocks, lines):
    seqs, _, rows, columns = partial.shape
    scratch = (
        [pltpu.VMEM((rows, columns), low), pltpu.VMEM((rows, columns), low)]
        + SumRows.scratch(rows, columns)
        + SumRows.scratch(rows, columns)
        + [pltpu.SemaphoreType.DMA((3,))] * 3
    )
    for block, kept in blocks:
        scratch += SumLines.scratch(lines, block.shape[1:3] + (kept,))
    if blocks:
        scratch += [pltpu.VMEM(blocks[0][0].shape, low)] * 2
    return remote_call(
        functools.partial(last_rows_kernel, lines, len(blocks)),
        3,
        [(partial, "any"), (mlp_partial, "any")]
        + [(array, "held") for array in (mine, middle, middle_grad, scale)]
        + [(block, "any") for block, _ in blocks],
        [
            ((seqs, rows, columns), low, "any"),
            ((seqs, rows, columns), low, "any"),
            ((1, columns), wide, "held"),
        ]
        + [(block.shape[1:3] + (kept,), low, "any") for block, kept in blocks],
        scratch,
    )


class Steps:
    def __init__(self, seqs, heads, span):
        self.seqs, self.heads, self.span = seqs, heads, span
        self.chains, self.chunks = seqs * heads, span // CHUNK

    def chain(self, step, when):
        if when == "first":
            return jnp.minimum(step, self.chains - 1)
        if when == "second":
            return jnp.maximum(step - self.chains, 0)
        return step % self.chains

    def rows(self, when, columns, place):
        def index(step):
            chain = self.chain(step, when)
            return chain // self.heads, place(chain % self.heads)

        return pl.BlockSpec((self.span, columns), index)

    def streams(self, when):
        return self.rows(when, 3 * CHUNK, lambda head: head)

    def head(self, when):
        return self.rows(when, CHUNK, lambda head: head)

    def gate(self, when):
        return self.rows(when, CHUNK, lambda head: 3 * self.heads + head)

    def logit(self, when):
        return self.rows(when, CHUNK, lambda head: 0)

    def taps(self, when):
        return pl.BlockSpec(
            (1, 3 * CONV, CHUNK), lambda step: (self.chain(step, when) % self.heads, 0, 0)
        )

    def blocks(self, when, columns=CHUNK):
        return pl.BlockSpec(
            (1, self.chunks, CHUNK, columns), lambda step: (self.chain(step, when), 0, 0, 0)
        )

    def few(self, when, columns):
        return pl.BlockSpec((1, 8, columns), lambda step: (self.chain(step, when), 0, 0))

    def whole(self, shape):
        return pl.BlockSpec(shape, lambda step: (0,) * len(shape), pipeline_mode=pl.Buffered(1))

    def call(self, body, identity, ins, outs, scratch, aliases=None):
        return pl.pallas_call(
            body,
            grid=(2 * self.chains,),
            in_specs=[spec for _, spec in ins],
            out_specs=[spec for _, _, spec in outs],
            out_shape=[jax.ShapeDtypeStruct(shape, dtype) for shape, dtype, _ in outs],
            scratch_shapes=scratch,
            input_output_aliases=aliases or {},
            compiler_params=pltpu.CompilerParams(
                vmem_limit_bytes=VMEM_BYTES,
                dimension_semantics=("arbitrary",),
                collective_id=identity,
                has_side_effects=True,
            ),
        )(*[array for array, _ in ins])


def delta_front(limit, raw, taps, logits, scale, moving, lines, seqs, heads, span):
    steps = Steps(seqs, heads, span)
    chains, chunks, size = steps.chains, steps.chunks, CHUNK
    squares, doubles = (chains, chunks, CHUNK, size), (chains, chunks, CHUNK, 2 * size)
    states, tails = (chains, size, size), (seqs, 16, 3 * heads * size)
    tokens = span // MATES
    anywhere = pl.BlockSpec(memory_space=pl.ANY)
    arrays = [array for array, _ in moving]
    ins = [
        (limit, pl.BlockSpec(memory_space=pltpu.SMEM)),
        (raw, anywhere),
        (raw, steps.streams("first")),
        (taps, steps.taps("first")),
        (logits, steps.logit("first")),
        (raw, steps.gate("second")),
        (scale, steps.whole((1, size))),
    ] + [(array, anywhere) for array in arrays]
    outs = [
        ((seqs * span, 3 * heads * size), low, steps.streams("first")),
        (squares, wide, steps.blocks("first")),
        (doubles, wide, steps.blocks("first", 2 * size)),
        (squares, wide, steps.blocks("first")),
        (states, wide, steps.whole(states)),
        (tails, low, steps.whole(tails)),
        (squares, wide, steps.blocks("second")),
        (squares, wide, steps.blocks("second")),
        ((seqs * span, heads * size), wide, steps.head("second")),
        ((seqs * span, heads * size), low, steps.head("second")),
        ((seqs, MATES, tokens, heads * size), low, anywhere),
        ((seqs, MATES) + arrays[0].shape, low, anywhere),
    ] + [(array.shape, low, anywhere) for array in arrays]
    scratch = [
        pltpu.VMEM((span + 16, 3 * size), wide),
        pltpu.VMEM(squares, wide),
        pltpu.VMEM(squares, wide),
        pltpu.VMEM(squares, wide),
        pltpu.VMEM(squares, wide),
        pltpu.VMEM(doubles, wide),
        pltpu.VMEM((chains, span, 3 * size), low),
        pltpu.VMEM(states, low),
        pltpu.VMEM(states, low),
        pltpu.VMEM(tails, low),
        pltpu.SemaphoreType.DMA((2, seqs)),
        pltpu.SemaphoreType.DMA((2,)),
        pltpu.VMEM((seqs, span, heads * size), low),
    ]
    scratch += ShareRows.scratch() + SwapBlocks.scratch()
    scratch += GatherLines.scratch(lines) * len(arrays)
    moves = tuple(part for _, part in moving)
    return steps.call(
        functools.partial(front_kernel, lines, heads, moves),
        4,
        ins,
        outs,
        scratch,
        {7 + index: 12 + index for index in range(len(arrays))},
    )


def delta_back(
    limit, raw, tails, taps, logits, scale, qkv, wu, maps, total, grad, mixed, solved, state, fresh,
    row_grad, summing, lines, seqs, heads, span,
):
    steps = Steps(seqs, heads, span)
    chains, chunks, size = steps.chains, steps.chunks, CHUNK
    squares, states = (chains, chunks, CHUNK, size), (chains, size, size)
    all_shape = (seqs * span, (4 * heads + 1) * size)
    anywhere = pl.BlockSpec(memory_space=pl.ANY)
    ins = [
        (limit, pl.BlockSpec(memory_space=pltpu.SMEM)),
        (raw, steps.streams("second")),
        (tails, steps.whole(tails.shape)),
        (taps, steps.taps("second")),
        (logits, steps.logit("second")),
        (raw, steps.gate("first")),
        (scale, steps.whole((1, size))),
        (qkv, steps.streams("both")),
        (wu, steps.blocks("both", 2 * size)),
        (maps, steps.blocks("first")),
        (total, steps.whole(states)),
        (grad, steps.head("first")),
        (mixed, steps.head("first")),
        (solved, steps.blocks("second")),
        (state, steps.blocks("second")),
        (fresh, steps.blocks("second")),
        (row_grad, anywhere),
    ] + [(array, anywhere) for array, _ in summing]
    outs = [
        (all_shape, low, steps.whole(all_shape)),
        ((chains, 8, size), wide, steps.few("first", size)),
        ((chains, 8, 3 * size), wide, steps.few("second", 3 * size)),
        ((seqs, MATES) + row_grad.shape, low, anywhere),
    ]
    edges = (chains, 16, 3 * size)
    scratch = [
        pltpu.VMEM((span + 16, 3 * size), wide),
        pltpu.VMEM((span + 32, 3 * size), wide),
        pltpu.VMEM(squares, wide),
        pltpu.VMEM(squares, wide),
        pltpu.VMEM(squares, wide),
        pltpu.VMEM(squares, wide),
        pltpu.VMEM(squares, wide),
        pltpu.VMEM(states, low),
        pltpu.VMEM(states, low),
        pltpu.VMEM(edges, low),
        pltpu.VMEM(edges, wide),
        pltpu.VMEM(edges, low),
        pltpu.SemaphoreType.DMA((2, chains)),
        pltpu.SemaphoreType.DMA((2,)),
    ] + ShareRows.scratch()
    for array, (_, height) in summing:
        shape = (MATES, height, array.shape[3])
        scratch += SumLines.scratch(lines, shape)
        outs.append((shape, low, anywhere))
    return steps.call(
        functools.partial(back_kernel, lines, heads, tuple(part for _, part in summing)),
        5,
        ins,
        outs,
        scratch,
    )


def tiled_call(body, ins, wholes, outs):
    tile = 256

    def tall(shape):
        return pl.BlockSpec((tile, shape[1]), lambda step: (step, 0))

    def whole(array):
        return pl.BlockSpec(array.shape, lambda step: (0, 0), pipeline_mode=pl.Buffered(1))

    return pl.pallas_call(
        body,
        grid=(ins[0].shape[0] // tile,),
        in_specs=[tall(array.shape) for array in ins] + [whole(array) for array in wholes],
        out_specs=[tall(shape) for shape, _ in outs],
        out_shape=[jax.ShapeDtypeStruct(shape, dtype) for shape, dtype in outs],
        compiler_params=pltpu.CompilerParams(vmem_limit_bytes=VMEM_BYTES),
    )(*ins, *wholes)


def project(inputs, scale, weight, beta):
    rows, model_width = inputs.shape
    return tiled_call(
        project_kernel,
        (inputs,),
        (scale, weight, beta),
        [((rows, model_width), low), ((rows, weight.shape[1]), low), ((rows, beta.shape[0]), wide)],
    )


def back_project(grads, weight, beta):
    return tiled_call(
        back_project_kernel, (grads,), (weight, beta), [((grads.shape[0], weight.shape[0]), low)]
    )[0]


def held_call(body, ins, outs):
    held = pl.BlockSpec(memory_space=pltpu.VMEM)
    return pl.pallas_call(
        body,
        in_specs=[held] * len(ins),
        out_specs=[held] * len(outs),
        out_shape=[jax.ShapeDtypeStruct(shape, dtype) for shape, dtype in outs],
        compiler_params=pltpu.CompilerParams(vmem_limit_bytes=VMEM_BYTES),
    )(*ins)


def pack_kernel(
    heads, query, key, value, outgate, output, swish, upward, downward,
    attn_ref, output_ref, ups_ref, downs_ref,
):
    size = CHUNK
    width = heads * size
    units = downs_ref.shape[2]
    for mate in range(MATES):
        first = mate * width
        for head in range(heads):
            for stream, weight in enumerate((query, key, value)):
                lanes = (3 * head + stream) * size
                attn_ref[mate, :, lanes : lanes + size] = weight[
                    :, first + head * size : first + (head + 1) * size
                ].astype(low)
        attn_ref[mate, :, 3 * width : 4 * width] = outgate[:, first : first + width].astype(low)
        output_ref[mate] = output[first : first + width, :].T.astype(low)
        here = mate * units
        ups_ref[mate, :, :units] = swish[:, here : here + units].astype(low)
        ups_ref[mate, :, units:] = upward[:, here : here + units].astype(low)
        downs_ref[mate] = downward[here : here + units, :].T.astype(low)


def unpack_kernel(
    heads, attn, outs, ups_low, ups_high, downs,
    query, key, value, outgate, output, swish, upward, downward,
):
    size = CHUNK
    width = heads * size
    units = downs.shape[2]
    split = ups_low.shape[1]
    for mate in range(MATES):
        first = mate * width
        for head in range(heads):
            for stream, grad in enumerate((query, key, value)):
                lanes = (3 * head + stream) * size
                grad[:, first + head * size : first + (head + 1) * size] = attn[
                    mate, :, lanes : lanes + size
                ].astype(wide)
        outgate[:, first : first + width] = attn[mate, :, 3 * width : 4 * width].astype(wide)
        output[first : first + width, :] = outs[mate].astype(wide).T
        here = mate * units
        for rows_here, part in ((pl.ds(0, split), ups_low), (pl.ds(split, swish.shape[0] - split), ups_high)):
            swish[rows_here, here : here + units] = part[mate, :, :units].astype(wide)
            upward[rows_here, here : here + units] = part[mate, :, units:].astype(wide)
        downward[here : here + units, :] = downs[mate].astype(wide).T


def cut_columns(weight):
    depth, columns = weight.shape
    return weight.reshape(depth, MATES, columns // MATES).transpose(1, 0, 2)


def join_columns(blocks):
    return blocks.transpose(1, 0, 2).reshape(blocks.shape[1], -1)


def gather_weights(blocks):
    return gather_lines(swap_blocks(blocks))


def scatter_grads(blocks):
    return swap_blocks(scatter_lines(blocks.astype(low))).astype(wide)


def on_device(
    block_input,
    lengths,
    attn_gain,
    query_weight,
    key_weight,
    value_weight,
    outgate_weight,
    beta_weight,
    conv_kernel,
    head_gain,
    output_weight,
    mlp_gain,
    swish_weight,
    upward_weight,
    downward_weight,
    out_grad,
):
    count = lax.axis_size("seq")
    lines = count // MATES
    core = lax.axis_index("tp")
    seq_count, tokens, model_width = block_input.shape
    depth = attn_gain.shape[0]
    gain_part = head_gain.shape[0]
    head_size = gain_part * count
    heads = beta_weight.shape[1] // MATES
    width = heads * head_size
    units = swish_weight.shape[1] // MATES

    conv_rows = -(-heads * 3 * CONV * gain_part // CHUNK)
    near = 1 < lines <= 4 and depth == CHUNK and conv_rows == BETA_ROW - CONV_ROW
    rows = seq_count * MATES * tokens
    span = MATES * tokens

    def in_rows(array):
        return jnp.pad(array, ((0, 0), (0, -array.shape[1] % 128)))

    def gains_of(attn, mlp, head):
        return jnp.concatenate([attn, mlp, in_rows(head)], axis=1)

    gains_cut = gains_of(attn_gain[None], mlp_gain[None], head_gain[None]).astype(low)
    conv_cut = in_rows(conv_kernel.astype(low).reshape(MATES, -1))
    beta_cut = beta_weight.astype(low).reshape(depth, MATES, heads).transpose(1, 2, 0)
    small_cut = jnp.concatenate(
        [jnp.broadcast_to(gains_cut, (MATES, gains_cut.shape[1])), conv_cut], axis=1
    )
    conv_start, conv_size = gains_cut.shape[1], heads * 3 * CONV * gain_part
    beta_start = small_cut.shape[1]
    small_cut = jnp.concatenate([small_cut, beta_cut.reshape(MATES, -1)], axis=1)
    small_size = small_cut.shape[1]
    small_cut = jnp.pad(small_cut, ((0, 0), (0, SMALL * 128 - small_size)))
    small_cut = small_cut.reshape(MATES, SMALL, 128)
    streams_end, gates_end = 3 * width, 4 * width
    if near:
        cuts = held_call(
            functools.partial(pack_kernel, heads),
            (
                query_weight, key_weight, value_weight, outgate_weight, output_weight,
                swish_weight, upward_weight, downward_weight,
            ),
            [
                ((MATES, depth, columns), low)
                for columns in (gates_end, width, 2 * units, units)
            ],
        )
        flat_normed, raw, logits, small, attn_full, output_full, ups_full, downward_full = first_call(
            block_input, (small_cut, *cuts), lines
        )
        ups_split = depth // 128 * 80
        front_moves = ((output_full, (0, depth)), (ups_full, (0, ups_split)))
    else:
        streams_cut = jnp.stack(
            [
                w.astype(low).reshape(depth, MATES, heads, head_size)
                for w in (query_weight, key_weight, value_weight)
            ],
            axis=3,
        )
        streams_cut = streams_cut.transpose(1, 0, 2, 3, 4).reshape(MATES, depth, streams_end)
        cuts = (
            small_cut,
            jnp.concatenate([streams_cut, cut_columns(outgate_weight.astype(low))], axis=2),
            cut_columns(output_weight.astype(low).T),
            jnp.concatenate([cut_columns(w.astype(low)) for w in (swish_weight, upward_weight)], axis=2),
            cut_columns(downward_weight.astype(low).T),
        )
        input_rows = first_rows(block_input).reshape(rows, model_width)
        small, attn_full, output_full, ups_full, downward_full = (gather_weights(cut) for cut in cuts)
        front_moves = ((output_full, None),)
    attn_full = attn_full.reshape(model_width, gates_end)
    small = small.reshape(count, SMALL * 128)
    attn_scale = small[:, :depth].reshape(1, model_width).astype(wide)
    mlp_scale = small[:, depth : 2 * depth].reshape(1, model_width).astype(wide)
    head_scale = small[:, 2 * depth : 2 * depth + gain_part].reshape(1, head_size).astype(wide)
    taps = (
        small[:, conv_start : conv_start + conv_size]
        .reshape(count, heads, 3, CONV, gain_part)
        .transpose(1, 2, 3, 0, 4)
        .reshape(heads, 3 * CONV, head_size)
        .astype(wide)
    )
    beta_rows = (
        small[:, beta_start:small_size]
        .reshape(count, heads, depth)
        .transpose(1, 0, 2)
        .reshape(heads, model_width)
    )
    beta_rows = jnp.pad(beta_rows, ((BETA_ROW, CHUNK - BETA_ROW - heads), (0, 0)))

    mine_low = pick(block_input, core)
    grad_mine = pick(out_grad, core)
    blocked = (seq_count, MATES, tokens, model_width)
    lengths_here = jnp.stack([pick(lengths, core), pick(lengths, 1 - core)])
    limit = lengths_here - line_of() * span

    if not near:
        flat_normed, raw, logits = project(input_rows, attn_scale, attn_full, beta_rows)
    sizes_of = (lines, seq_count, heads, span)
    (
        qkv, solved, wu, maps, total, tails, state, fresh, mixed, gated, gathered, output_all, *moved
    ) = delta_front(limit, raw, taps, logits, head_scale, front_moves, *sizes_of)
    middle_moves = ()
    if near:
        ups_full = moved[1]
        middle_moves = (
            (ups_full, (ups_split, depth - ups_split)), (downward_full, (0, depth))
        )
    middle, mlp_normed, grad_rows, *moved = middle_rows(
        gathered, output_all, mine_low, mlp_scale, out_grad, middle_moves, lines
    )
    grad_rows = grad_rows.reshape(rows, model_width)
    if near:
        ups_full, downward_full = moved
    ups_full = ups_full.reshape(model_width, 2 * units)
    downward_full = downward_full.reshape(model_width, units)
    mlp_normed = mlp_normed.reshape(rows, model_width)
    acts = matmul("rd,df->rf", mlp_normed, ups_full)
    gate_act, up_act = acts[:, :units], acts[:, units:]
    silu_act = jax.nn.silu(gate_act)
    hidden = (silu_act * up_act).astype(low)
    mlp_part = matmul("rf,df->rd", hidden, downward_full).astype(low)

    hidden_grad = matmul("rd,df->rf", grad_rows, downward_full)
    downward_grad = matmul("rd,rf->df", grad_rows, hidden).astype(low)
    acts_grad = jnp.concatenate(
        [
            (hidden_grad * up_act * silu_slope(gate_act)).astype(low),
            (hidden_grad * silu_act).astype(low),
        ],
        axis=1,
    )
    ups_grad = matmul("rd,rf->df", mlp_normed, acts_grad).astype(low)
    normed_two_part = matmul("rf,df->rd", acts_grad, ups_full).astype(low)

    def cut_rows(grad):
        return grad.reshape(lines, MATES, depth, grad.shape[1])

    ups_blocks, downward_blocks = cut_rows(ups_grad), cut_rows(downward_grad)
    turn_sums = back_sums = ()
    if near:
        sums_split = depth // 128 * 80
        turn_sums = ((ups_blocks, (0, sums_split)),)
    middle_grad, mlp_gain_grad, attn_grad_mine, gated_grad, *summed = turn_rows(
        normed_two_part.reshape(blocked), output_all, middle, grad_mine, mlp_scale, turn_sums, lines
    )
    if near:
        ups_low, = summed
        back_sums = (
            (ups_blocks, (sums_split, depth - sums_split)),
            (downward_blocks, (0, depth)),
        )
    all_grads, head_gain_parts, taps_grad, attn_grad_rows, *summed = delta_back(
        limit, raw, tails, taps, logits, head_scale, qkv, wu, maps, total,
        gated_grad.reshape(rows, width), mixed, solved, state, fresh, attn_grad_mine, back_sums,
        *sizes_of,
    )
    attn_grad_rows = attn_grad_rows.reshape(rows, model_width)
    output_grad = cut_rows(matmul("rd,rc->dc", attn_grad_rows, gated).astype(low))
    normed_part = back_project(all_grads, attn_full, beta_rows)
    attn_grads = matmul("rd,rc->dc", flat_normed, all_grads).astype(low)
    beta_grad = attn_grads[:, gates_end + BETA_ROW : gates_end + BETA_ROW + heads]
    attn_grads = cut_rows(attn_grads)

    conv_grad = (
        taps_grad[:, :CONV]
        .reshape(seq_count, heads, CONV, 3, count, gain_part)
        .sum(axis=0)
        .transpose(3, 0, 2, 1, 4)
        .reshape(count, -1)
    )

    def small_blocks(attn_gain_grad):
        gains = gains_of(
            attn_gain_grad.reshape(count, depth),
            mlp_gain_grad.reshape(count, depth),
            jnp.sum(head_gain_parts[:, 0], axis=0).reshape(count, gain_part),
        )
        beta = beta_grad.reshape(count, depth, heads).transpose(0, 2, 1).reshape(count, -1)
        flat = jnp.concatenate([gains.astype(low), in_rows(conv_grad.astype(low)), beta], axis=1)
        flat = jnp.pad(flat, ((0, 0), (0, SMALL * 128 - small_size)))
        return flat.reshape(lines, MATES, SMALL, 128)

    last_ins = (
        normed_part.reshape(blocked),
        mlp_part.reshape(blocked),
        mine_low,
        middle,
        middle_grad,
        attn_scale,
    )
    if near:
        ups_high, downward_sum = summed
        blocks = (
            (small_blocks(jnp.zeros((1, model_width), wide)), 128),
            (attn_grads, gates_end),
            (output_grad, width),
        )
        input_grad, block_output, _, small_sum, attn_sum, output_sum = last_rows(
            *last_ins, blocks, lines
        )
        grads = held_call(
            functools.partial(unpack_kernel, heads),
            (attn_sum, output_sum, ups_low, ups_high, downward_sum),
            [
                (w.shape, wide)
                for w in (
                    query_weight, key_weight, value_weight, outgate_weight, output_weight,
                    swish_weight, upward_weight, downward_weight,
                )
            ],
        )
        small_sum = small_sum.reshape(MATES, SMALL * 128).astype(wide)
        gains_sum = jnp.sum(small_sum[:, :conv_start], axis=0)
    else:
        input_grad, block_output, attn_gain_grad = last_rows(*last_ins, (), lines)
        small_sum, attn_sum, output_sum, ups_sum, downward_sum = (
            scatter_grads(block)
            for block in (
                small_blocks(attn_gain_grad), attn_grads[..., :gates_end], output_grad, ups_blocks, downward_blocks
            )
        )
        small_sum = small_sum.reshape(MATES, SMALL * 128)
        gains_sum = jnp.sum(small_sum[:, :conv_start], axis=0)
        gains_sum = gains_sum + other_core(gains_sum)
        streams_sum = (
            attn_sum[:, :, :streams_end]
            .reshape(MATES, depth, heads, 3, head_size)
            .transpose(3, 1, 0, 2, 4)
            .reshape(3, depth, MATES * width)
        )
        grads = (
            streams_sum[0],
            streams_sum[1],
            streams_sum[2],
            join_columns(attn_sum[:, :, streams_end:gates_end]),
            join_columns(output_sum).T,
            join_columns(ups_sum[:, :, :units]),
            join_columns(ups_sum[:, :, units:]),
            join_columns(downward_sum).T,
        )
    conv_sum = small_sum[:, conv_start : conv_start + conv_size]
    beta_sum = small_sum[:, beta_start:small_size].reshape(MATES * heads, depth).T
    return (
        block_output,
        input_grad,
        gains_sum[:depth],
        *grads[:4],
        beta_sum,
        conv_sum.reshape(MATES * heads, 3, CONV, gain_part),
        gains_sum[2 * depth : 2 * depth + gain_part],
        grads[4],
        gains_sum[depth : 2 * depth],
        *grads[5:],
    )


def solution(mesh):
    return jax.shard_map(
        on_device,
        mesh=mesh,
        in_specs=(
            P(None, "seq", None),
            P(),
            P("seq"),
            P("seq", "tp"),
            P("seq", "tp"),
            P("seq", "tp"),
            P("seq", "tp"),
            P("seq", "tp"),
            P("tp", None, None, "seq"),
            P("seq"),
            P("tp", "seq"),
            P("seq"),
            P("seq", "tp"),
            P("seq", "tp"),
            P("tp", "seq"),
            P(None, "seq", None),
        ),
        out_specs=(
            P(None, "seq", None),
            P(None, "seq", None),
            P("seq"),
            P("seq", "tp"),
            P("seq", "tp"),
            P("seq", "tp"),
            P("seq", "tp"),
            P("seq", "tp"),
            P("tp", None, None, "seq"),
            P("seq"),
            P("tp", "seq"),
            P("seq"),
            P("seq", "tp"),
            P("seq", "tp"),
            P("tp", "seq"),
        ),
        check_vma=False,
    )
```

```python
import functools

import jax
import jax.numpy as jnp
from jax import lax
from jax.experimental import pallas as pl
from jax.experimental.pallas import tpu as pltpu
from jax.sharding import PartitionSpec as P

CONV = 4
MATES = 4
SMALL = 16
CONV_ROW = 3
BETA_ROW = 5


epsilon = 1e-06
low = jnp.bfloat16
wide = jnp.float32


def other_core(value):
    return lax.ppermute(value, "tp", [(0, 1), (1, 0)])


def to_mate(value, flip):
    count = lax.axis_size("seq")
    return lax.ppermute(value, "seq", [(source, source ^ flip) for source in range(count)])


def mate_of():
    return lax.axis_index("seq") % MATES


def line_of():
    return lax.axis_index("seq") // MATES


def line_groups():
    lines = lax.axis_size("seq") // MATES
    return [[mate + MATES * line for line in range(lines)] for mate in range(MATES)]


def pick(blocks, index):
    return lax.dynamic_index_in_dim(blocks, index, 0, False)


def in_order(by_flip):
    mate = mate_of()
    out = jnp.zeros((MATES,) + by_flip[0].shape, by_flip[0].dtype)
    for flip, piece in enumerate(by_flip):
        out = lax.dynamic_update_index_in_dim(out, piece, mate ^ flip, 0)
    return out


def swap_blocks(blocks):
    mate = mate_of()
    pieces = [pick(blocks, mate)]
    for flip in range(1, MATES):
        pieces.append(to_mate(pick(blocks, mate ^ flip), flip))
    return in_order(pieces)


def gather_lines(block):
    return lax.all_gather(block, "seq", axis_index_groups=line_groups())


def scatter_lines(blocks):
    return lax.psum_scatter(blocks, "seq", scatter_dimension=0, axis_index_groups=line_groups())


def matmul(form, left, right):
    return jnp.einsum(form, left, right, preferred_element_type=wide)


def silu_slope(value):
    squash = jax.nn.sigmoid(value)
    return squash * (1.0 + value * (1.0 - squash))


CHUNK = 128
TOGETHER = 4
VMEM_BYTES = 58 * 1024 * 1024
NN = (((1,), (0,)), ((), ()))
NT = (((1,), (1,)), ((), ()))


def dot(left, right, dims):
    return lax.dot_general(left, right, dims, preferred_element_type=wide)


def pair(value):
    high = value.astype(low)
    return high, (value - high.astype(wide)).astype(low)


def side(left, right):
    return jnp.concatenate([left, right], axis=1)


def over(top, bottom):
    return jnp.concatenate([top, bottom], axis=0)


def nn(left, right):
    width = right[0].shape[1]
    both = side(*right)
    out = dot(side(*left), over(both, both), NN)
    return out[:, :width] + out[:, width:]


def nt(left, right):
    width = right[0].shape[0]
    out = dot(side(*left), over(side(right[0], right[0]), side(right[1], right[1])), NT)
    return out[:, :width] + out[:, width:]


def nn_wide(left, right):
    return dot(side(*left), over(right[0], right[0]), NN) + dot(left[0], right[1], NN)


def nn_low(left, right):
    return dot(side(*left), over(right, right), NN)


def low_nn(left, right):
    return dot(side(left, left), over(*right), NN)


def low_nt(left, right):
    return dot(side(left, left), side(*right), NT)


def grid_of_rows():
    rows = lax.broadcasted_iota(jnp.int32, (CHUNK, CHUNK), 0)
    columns = lax.broadcasted_iota(jnp.int32, (CHUNK, CHUNK), 1)
    return rows, columns


def inverse_of(strict):
    rows, columns = grid_of_rows()
    one = jnp.where(rows == columns, 1.0, 0.0).astype(wide)

    def joining(shift):
        upper = columns >> shift
        return ((rows >> shift) == upper + 1) & ((upper & 1) == 0)

    solved = [one - jnp.where(joining(0), s, 0.0) for s in strict]
    shift = 1
    while (1 << shift) < CHUNK:
        mask = joining(shift)
        pairs = [pair(d) for d in solved]
        crossed = [nn(pair(jnp.where(mask, s, 0.0)), p) for s, p in zip(strict, pairs)]
        solved = [d - nn(p, pair(c)) for d, p, c in zip(solved, pairs, crossed)]
        shift += 1
    return solved


def convolved(block, taps, stream):
    columns = block[:, stream * CHUNK : (stream + 1) * CHUNK]
    total = None
    for offset in range(CONV):
        first = 16 - (CONV - 1) + offset
        term = taps[stream * CONV + offset][None, :] * columns[first : first + CHUNK]
        total = term if total is None else total + term
    return total


def silu_parts(value):
    squash = jax.nn.sigmoid(value)
    return value * squash, squash * (1.0 + value * (1.0 - squash))


def live_rows(limit, start):
    rows = lax.broadcasted_iota(jnp.int32, (CHUNK, CHUNK), 0)
    return jnp.where(rows + start < limit, 1.0, 0.0).astype(wide)


def head_squash(logits, head):
    lanes = lax.broadcasted_iota(jnp.int32, logits.shape, 1)
    column = jnp.sum(jnp.where(lanes == BETA_ROW + head, logits, 0.0), axis=1, keepdims=True)
    return jax.nn.sigmoid(jnp.broadcast_to(column, logits.shape))


def front_kernel(
    lines, heads, moves, limit_ref, raw_any, raw_ref, taps_ref, logit_ref, gate_ref, scale_ref, *rest,
):
    count = len(moves)
    outs = rest[count:]
    qkv_ref, solved_ref, wu_ref, map_ref, total_ref, tails_ref = outs[:6]
    state_ref, fresh_ref, mixed_ref, gated_ref, gathered, weights = outs[6:12]
    targets, scratch = outs[12 : 12 + count], outs[12 + count :]
    ext, offsets, maps, prefixes, locals_, wus, qkvs, enters, leaves, tails = scratch[:10]
    tail_sems, state_sems, gateds = scratch[10:13]
    scratch = scratch[13:]
    step = pl.program_id(0)
    chains, chunks = maps.shape[0], maps.shape[1]
    span = chunks * CHUNK
    head_size = CHUNK
    streams = 3 * heads * head_size
    place = Place()
    tokens = gathered.shape[2]
    share = ShareRows(place, targets[0], weights, scratch[:3])
    swap = SwapBlocks(
        place,
        lambda slot, mate: gateds.at[slot, pl.ds(pl.multiple_of(mate * tokens, 16), tokens)],
        gathered,
        scratch[3:6],
    )
    gathers = [
        GatherLines(place, None, target, scratch[6 + 6 * index : 12 + 6 * index], moves[index])
        for index, target in enumerate(targets)
        if moves[index]
    ]
    below, above = place.line > 0, place.line < lines - 1
    rows, columns = grid_of_rows()
    identity = jnp.where(rows == columns, 1.0, 0.0).astype(wide)

    def tail(seq):
        return pltpu.make_async_remote_copy(
            src_ref=raw_any.at[pl.ds((seq + 1) * span - 16, 16), pl.ds(0, streams)],
            dst_ref=tails.at[seq],
            send_sem=tail_sems.at[0, seq],
            recv_sem=tail_sems.at[1, seq],
            device_id=place.lines_away(1),
            device_id_type=MESH,
        )

    state_copy = pltpu.make_async_remote_copy(
        src_ref=leaves,
        dst_ref=enters,
        send_sem=state_sems.at[0],
        recv_sem=state_sems.at[1],
        device_id=place.lines_away(1),
        device_id_type=MESH,
    )
    seqs = chains // heads

    @pl.when(step == 0)
    def _():
        meet(place, lines=lines, cores=True)
        for seq in range(seqs):
            pl.when(above)(tail(seq).start)
        for gather in gathers:
            gather.leave(False)
        share.begin_half(False)
        share.begin_half(True)
        share.begin_rest()
        for seq in range(seqs):

            @pl.when(below)
            def _(seq=seq):
                tail(seq).wait_recv()

            @pl.when(place.line == 0)
            def _(seq=seq):
                tails[seq] = jnp.zeros(tails.shape[1:], low)

        tails_ref[...] = tails[...]

    def form(chain):
        seq, head = chain // heads, chain % heads
        ext[:16] = tails[seq, :, pl.ds(pl.multiple_of(head * 3 * head_size, 128), 3 * head_size)].astype(wide)
        ext[16:] = raw_ref[...].astype(wide)
        taps = taps_ref[0]
        limit = limit_ref[seq]

        def group(index, carry):
            first = index * TOGETHER
            parts = []
            for number in range(TOGETHER):
                start = pl.multiple_of((first + number) * CHUNK, CHUNK)
                block = ext[pl.ds(start, CHUNK + 16)]
                query = jax.nn.silu(convolved(block, taps, 0))
                key = jax.nn.silu(convolved(block, taps, 1))
                value = jax.nn.silu(convolved(block, taps, 2)).astype(low)
                query = query * lax.rsqrt(jnp.sum(query * query, axis=1, keepdims=True) + epsilon)
                query = (query * head_size ** (-0.5)).astype(low)
                key = key * lax.rsqrt(jnp.sum(key * key, axis=1, keepdims=True) + epsilon)
                key = key.astype(low)
                beta = head_squash(logit_ref[pl.ds(start, CHUNK)], head) * live_rows(limit, start)
                together = jnp.concatenate([query, key, value], axis=1)
                qkv_ref[pl.ds(start, CHUNK)] = together
                qkvs[chain, pl.ds(start, CHUNK)] = together
                parts.append((key, value, beta))
            strict = [
                jnp.where(rows > columns, beta * dot(key, key, NT), 0.0) for key, _, beta in parts
            ]
            solved = inverse_of(strict)
            for number in range(TOGETHER):
                key, value, beta = parts[number]
                solved_ref[0, first + number] = solved[number]
                weighted = pair(solved[number] * beta.T)
                both = nn_low(weighted, side(key, value))
                wu_ref[0, first + number] = both
                wus[chain, first + number] = both
                moved = low_nn(key.T, pair(both))
                step_map = identity - moved[:, :head_size]
                map_ref[0, first + number] = step_map
                maps[chain, first + number] = step_map
                offsets[chain, first + number] = moved[:, head_size:]
            return carry

        lax.fori_loop(0, chunks // TOGETHER, group, 0)

    @pl.when(step < chains)
    def _():
        form(step)

    @pl.when(step == chains - 2)
    def _():
        for gather in gathers:
            gather.onwards(1)

    @pl.when(step == chains - 1)
    def _():
        start = side(identity, jnp.zeros_like(identity))

        def advance(chunk, states):
            out = []
            for index in range(chains):
                state = states[index]
                prefixes[index, chunk] = state[:, :head_size]
                locals_[index, chunk] = state[:, head_size:]
                moved = nn_wide(pair(maps[index, chunk]), pair(state))
                out.append(
                    side(moved[:, :head_size], moved[:, head_size:] + offsets[index, chunk])
                )
            return tuple(out)

        ends = lax.fori_loop(0, chunks, advance, (start,) * chains)

        @pl.when(below)
        def _():
            state_copy.wait_recv()

        @pl.when(place.line == 0)
        def _():
            enters[...] = jnp.zeros_like(enters)

        for index in range(chains):
            total_ref[index] = ends[index][:, :head_size]
            leaving = nn_low(pair(ends[index][:, :head_size]), enters[index])
            leaves[index] = (leaving + ends[index][:, head_size:]).astype(low)
        pl.when(above)(state_copy.start)
        share.forward()

    def outputs(chain):
        enter = enters[chain]
        scale = scale_ref[...]

        def group(index, carry):
            for number in range(TOGETHER):
                chunk = index * TOGETHER + number
                start = pl.multiple_of(chunk * CHUNK, CHUNK)
                here = pl.ds(start, CHUNK)
                state = nn_low(pair(prefixes[chain, chunk]), enter) + locals_[chain, chunk]
                state_ref[0, chunk] = state
                states = pair(state)
                both = wus[chain, chunk]
                fresh = both[:, head_size:] - nn(pair(both[:, :head_size]), states)
                fresh_ref[0, chunk] = fresh
                query = qkvs[chain, here, :head_size]
                key = qkvs[chain, here, head_size : 2 * head_size]
                scores = jnp.where(rows >= columns, dot(query, key, NT), 0.0)
                mixed = low_nn(query, states) + nn(pair(scores), pair(fresh))
                mixed_ref[here] = mixed
                inverse = lax.rsqrt(jnp.mean(mixed * mixed, axis=1, keepdims=True) + epsilon)
                normed = mixed * inverse * scale
                gated = (normed * jax.nn.silu(gate_ref[here].astype(wide))).astype(low)
                gated_ref[here] = gated
                lanes = pl.ds(pl.multiple_of(chain % heads * head_size, 128), head_size)
                gateds[chain // heads, here, lanes] = gated
            return carry

        lax.fori_loop(0, chunks // TOGETHER, group, 0)

    @pl.when(step >= chains)
    def _():
        outputs(step - chains)

    @pl.when(step == chains + heads - 1)
    def _():
        swap.begin(0)
        share.forward_far()
        for gather in gathers:
            gather.onwards(2)

    @pl.when(step == 2 * chains - 1)
    def _():
        swap.begin(1)
        for gather in gathers:
            for number in range(3, lines):
                gather.onwards(number)
        for gather in gathers:
            gather.finish_lines()
        share.finish()
        swap.finish()
        for seq in range(seqs):
            pl.when(above)(tail(seq).wait_send)
        pl.when(above)(state_copy.wait_send)


def back_kernel(
    lines, heads, parts, limit_ref, raw_ref, tails_ref, taps_ref, logit_ref, gate_ref, scale_ref, qkv_ref,
    wu_ref, map_ref, total_ref, grad_ref, mixed_ref, solved_ref, state_ref, fresh_in_ref, row_grad, mlp_partial,
    middle_ref, *rest,
):
    count = len(parts)
    blocks, rest = rest[:count], rest[count:]
    all_ref, gain_ref, taps_grad_ref, row_grads, block_output = rest[:5]
    results, scratch = rest[5 : 5 + count], rest[5 + count :]
    ext, pre_grads, maps, sources, out_grads, fresh_grads, leaving, leaves, enters = scratch[:9]
    halos, edges, returned, halo_sems, state_sems = scratch[9:14]
    share_scratch, scratch = scratch[14:17], scratch[17:]
    low_output, out_sems = scratch[0], scratch[1:4]
    outs_scratch, scratch = scratch[4:11], scratch[11:]
    step = pl.program_id(0)
    chains, chunks = maps.shape[0], maps.shape[1]
    span = chunks * CHUNK
    head_size = CHUNK
    streams = 3 * heads * head_size
    place = Place()
    sums = [
        SumLines(place, blocks[index], results[index], scratch[7 * index : 7 * index + 7], first)
        for index, (first, _) in enumerate(parts)
    ]
    share = ShareRows(place, row_grad, row_grads, share_scratch)
    outs = SumRows(place, mlp_partial, outs_scratch)
    to_sibling = sender(out_sems[:2])(
        0, low_output, block_output.at[place.core], place.sibling
    )
    to_self = pltpu.make_async_copy(low_output, block_output.at[place.core], out_sems[2].at[0])
    below, above = place.line > 0, place.line < lines - 1
    rows, columns = grid_of_rows()

    def halo(chain):
        return pltpu.make_async_remote_copy(
            src_ref=halos.at[chain],
            dst_ref=returned.at[chain],
            send_sem=halo_sems.at[0, chain],
            recv_sem=halo_sems.at[1, chain],
            device_id=place.lines_away(-1),
            device_id_type=MESH,
        )

    state_copy = pltpu.make_async_remote_copy(
        src_ref=enters,
        dst_ref=leaves,
        send_sem=state_sems.at[0],
        recv_sem=state_sems.at[1],
        device_id=place.lines_away(-1),
        device_id_type=MESH,
    )

    @pl.when(step == 0)
    def _():
        meet(place, far=bool(parts), lines=lines)
        share.begin_half(False)
        share.begin_half(True)
        share.begin_rest()
        outs.begin()
        for each in sums:
            each.begin()
        for each in sums:
            each.wait_loads()
            each.round(1)

    def turn(chain):
        scale = scale_ref[...]

        def group(index, gain):
            for number in range(TOGETHER):
                chunk = index * TOGETHER + number
                start = pl.multiple_of(chunk * CHUNK, CHUNK)
                here = pl.ds(start, CHUNK)
                grad, mixed = grad_ref[here].astype(wide), mixed_ref[here]
                silu_gate, slope = silu_parts(gate_ref[here].astype(wide))
                inverse = lax.rsqrt(jnp.mean(mixed * mixed, axis=1, keepdims=True) + epsilon)
                unit = mixed * inverse
                gate_grad = (grad * unit * scale * slope).astype(low)
                there = pl.ds(pl.multiple_of(chain // heads * span + start, CHUNK), CHUNK)
                lanes = pl.ds(pl.multiple_of(streams + chain % heads * head_size, 128), head_size)
                all_ref[there, lanes] = gate_grad
                passed = grad * silu_gate
                gain = gain + jnp.sum(passed * unit, axis=0, keepdims=True)
                scaled = passed * scale
                mixed_grad = inverse * (
                    scaled - unit * inverse * jnp.mean(scaled * mixed, axis=1, keepdims=True)
                )
                out_grads[chain, chunk] = mixed_grad
                query, key = qkv_ref[here, :head_size], qkv_ref[here, head_size : 2 * head_size]
                scores = jnp.where(rows >= columns, dot(query, key, NT), 0.0)
                turned = jnp.where(rows <= columns, dot(key, query, NT), 0.0)
                grads = pair(mixed_grad)
                fresh_grads[chain, chunk] = nn(pair(turned), grads)
                reading = query.astype(wide) - nn(
                    pair(scores), pair(wu_ref[0, chunk, :, :head_size])
                )
                sources[chain, chunk] = nn(pair(mixed_grad.T), pair(reading))
                maps[chain, chunk] = map_ref[0, chunk]
            return gain

        gain = lax.fori_loop(0, chunks // TOGETHER, group, jnp.zeros((1, head_size), wide))
        gain_ref[0] = jnp.broadcast_to(gain, (8, head_size))

    @pl.when(step == 1)
    def _():
        outs.send_far()

    @pl.when(step == 2)
    def _():
        outs.send_near()

    @pl.when(step < chains)
    def _():
        turn(step)

    @pl.when(step == chains - 1)
    def _():
        def advance(number, states):
            chunk = chunks - 1 - number
            return tuple(
                nn(pair(states[index]), pair(maps[index, chunk])) + sources[index, chunk]
                for index in range(chains)
            )

        ends = lax.fori_loop(
            0, chunks, advance, (jnp.zeros((head_size, head_size), wide),) * chains
        )

        @pl.when(above)
        def _():
            state_copy.wait_recv()

        @pl.when(place.line == lines - 1)
        def _():
            leaves[...] = jnp.zeros_like(leaves)

        for index in range(chains):
            entering = low_nn(leaves[index], pair(total_ref[index]))
            enters[index] = (entering + ends[index]).astype(low)
        pl.when(below)(state_copy.start)

        def again(number, states):
            chunk = chunks - 1 - number
            out = []
            for index in range(chains):
                leaving[index, chunk] = states[index]
                out.append(
                    nn(pair(states[index]), pair(maps[index, chunk])) + sources[index, chunk]
                )
            return tuple(out)

        lax.fori_loop(
            0, chunks, again, tuple(leaves[index].astype(wide) for index in range(chains))
        )
        for each in sums:
            each.round(2)

    def unwind(chain):
        seq, head = chain // heads, chain % heads
        ext[:16] = tails_ref[seq, :, pl.ds(pl.multiple_of(head * 3 * head_size, 128), 3 * head_size)].astype(wide)
        ext[16:] = raw_ref[...].astype(wide)
        taps = taps_ref[0]
        limit = limit_ref[seq]
        pre_grads[:16] = jnp.zeros((16, 3 * head_size), wide)
        pre_grads[span + 16 :] = jnp.zeros((16, 3 * head_size), wide)

        def one(chunk):
            start = pl.multiple_of(chunk * CHUNK, CHUNK)
            here = pl.ds(start, CHUNK)
            query = qkv_ref[here, :head_size]
            key = qkv_ref[here, head_size : 2 * head_size]
            value = qkv_ref[here, 2 * head_size :]
            live = live_rows(limit, start)
            squash = head_squash(logit_ref[here], head)
            beta = squash * live
            grads = pair(out_grads[chain, chunk])
            fresh = pair(fresh_in_ref[0, chunk])
            state = pair(state_ref[0, chunk])
            leave = pair(leaving[chain, chunk])
            both = wu_ref[0, chunk]
            fresh_grad = fresh_grads[chain, chunk] + low_nt(key, leave)
            fresh_pair = pair(fresh_grad)
            score_grad = jnp.where(rows >= columns, nt(grads, fresh), 0.0)
            turned_grad = jnp.where(rows <= columns, nt(fresh, grads), 0.0)
            query_grad = nt(grads, state) + nn_low(pair(score_grad), key)
            key_grad = nn_low(pair(turned_grad), query) + nn(fresh, leave)
            wkey_grad = -nt(fresh_pair, state)
            right_grad = nn_wide(pair(solved_ref[0, chunk].T), pair(side(wkey_grad, fresh_grad)))
            right = pair(right_grad)
            twos = pair(both)
            found = dot(right[0], over(*twos), NT)
            system_grad = found[:, :CHUNK] + found[:, CHUNK:] + dot(right[1], twos[0], NT)
            system_grad = jnp.where(rows > columns, -system_grad, 0.0)
            gram = dot(key, key, NT)
            gram_grad = beta * system_grad
            key_grad = key_grad + nn_low(pair(gram_grad + gram_grad.T), key)
            key_right, value_right = right_grad[:, :head_size], right_grad[:, head_size:]
            key_grad = key_grad + beta * key_right
            value_grad = beta * value_right
            beta_grad = jnp.sum(
                key_right * key.astype(wide) + value_right * value.astype(wide) + system_grad * gram,
                axis=1,
                keepdims=True,
            )
            lanes = lax.broadcasted_iota(jnp.int32, (CHUNK, head_size), 1)
            logit_grad = jnp.where(
                lanes == BETA_ROW + head, beta_grad * (live * squash * (1.0 - squash)), 0.0
            ).astype(low)

            there = pl.ds(pl.multiple_of(seq * span + start, CHUNK), CHUNK)
            last_lanes = pl.ds(streams + heads * head_size, head_size)

            @pl.when(head == 0)
            def _():
                all_ref[there, last_lanes] = logit_grad

            @pl.when(head > 0)
            def _():
                all_ref[there, last_lanes] = all_ref[there, last_lanes] + logit_grad

            block = ext[pl.ds(start, CHUNK + 16)]
            grads_pre = []
            for stream, grad in enumerate((query_grad, key_grad, value_grad)):
                act, slope = silu_parts(convolved(block, taps, stream))
                if stream < 2:
                    inverse = lax.rsqrt(jnp.sum(act * act, axis=1, keepdims=True) + epsilon)
                    inner = jnp.sum(act * grad, axis=1, keepdims=True)
                    grad = inverse * (grad - act * (inverse * inverse * inner))
                    if stream == 0:
                        grad = grad * head_size ** (-0.5)
                grads_pre.append(grad * slope)
            pre_grads[pl.ds(start + 16, CHUNK)] = jnp.concatenate(grads_pre, axis=1)

        def group(index, carry):
            for number in range(2):
                one(index * 2 + number)
            return carry

        lax.fori_loop(0, chunks // 2, group, 0)

        def back(block):
            parts = []
            for stream in range(3):
                part = block[:, stream * head_size : (stream + 1) * head_size]
                total = None
                for offset in range(CONV):
                    first = CONV - 1 - offset
                    term = taps[stream * CONV + offset][None, :] * part[first : first + CHUNK]
                    total = term if total is None else total + term
                parts.append(total)
            return jnp.concatenate(parts, axis=1)

        lanes = pl.ds(pl.multiple_of(head * 3 * head_size, 128), 3 * head_size)

        def finish(chunk, totals):
            start = pl.multiple_of(chunk * CHUNK, CHUNK)
            block = pre_grads[pl.ds(start + 16, CHUNK + 16)]
            grad = back(block)
            there = pl.ds(pl.multiple_of(seq * span + start, CHUNK), CHUNK)
            all_ref[there, lanes] = grad.astype(low)
            edges[chain] = grad[CHUNK - 16 :]
            before = ext[pl.ds(start, CHUNK + 16)]
            pre = block[:CHUNK]
            out = []
            for offset in range(CONV):
                first = 16 - (CONV - 1) + offset
                term = jnp.sum(pre * before[first : first + CHUNK], axis=0, keepdims=True)
                out.append(totals[offset] + term)
            return tuple(out)

        zero = jnp.zeros((1, 3 * head_size), wide)
        totals = lax.fori_loop(0, chunks, finish, (zero,) * CONV)
        for offset in range(CONV):
            taps_grad_ref[0, offset : offset + 1] = totals[offset]
        halos[chain] = back(pre_grads[: CHUNK + 32])[:16].astype(low)
        pl.when(below)(halo(chain).start)

    @pl.when(step >= chains)
    def _():
        unwind(step - chains)

    @pl.when(step == chains)
    def _():
        share.forward()

    @pl.when(step == chains + 1)
    def _():
        outs.send_relayed()

    @pl.when(step == chains + 2)
    def _():
        share.forward_far()
        for each in sums:
            each.round(3)

    @pl.when(step == chains + 3)
    def _():
        outs.wait_half(False)
        outs.wait_half(True)

        def out_body(here):
            low_output[here] = (middle_ref[here] + outs.total(here)).astype(low)

        row_steps(0, low_output.shape[0], out_body)
        to_sibling.start()
        to_self.start()

    @pl.when(step == 2 * chains - 1)
    def _():
        for each in sums:
            for number in range(4, lines):
                each.round(number)
            each.exchange()
        for chain in range(chains):
            seq, head = chain // heads, chain % heads
            last = pl.ds((seq + 1) * span - 16, 16)
            lanes = pl.ds(head * 3 * head_size, 3 * head_size)

            @pl.when(above)
            def _(chain=chain, last=last, lanes=lanes):
                halo(chain).wait_recv()
                all_ref[last, lanes] = (edges[chain] + returned[chain].astype(wide)).astype(low)

        for chain in range(chains):
            pl.when(below)(halo(chain).wait_send)
        pl.when(below)(state_copy.wait_send)
        share.finish()
        outs.finish()
        to_self.wait()
        to_sibling.wait()
        for each in sums:
            each.finish()


def project_kernel(input_ref, scale_ref, weight_ref, beta_ref, normed_ref, raw_ref, logit_ref):
    value = input_ref[...].astype(wide)
    normed = (value * inverse_rms(value) * scale_ref[...]).astype(low)
    normed_ref[...] = normed
    raw_ref[...] = dot(normed, weight_ref[...], NN).astype(low)
    logit_ref[...] = dot(normed, beta_ref[...], NT)


MESH = pl.DeviceIdType.MESH
STEP = 16


class Place:
    def __init__(self):
        self.seq = lax.axis_index("seq")
        self.core = lax.axis_index("tp")
        self.mate = self.seq % MATES
        self.line = self.seq // MATES
        x, y = self.mate % 2, self.mate // 2
        self.x = 2 * y + (1 - x)
        self.y = 2 * (1 - y) + x
        self.far = 2 * (1 - y) + (1 - x)
        self.base = self.seq - self.mate

    def of(self, mate, other=0):
        return (self.base + mate, 1 - self.core if other else self.core)

    @property
    def sibling(self):
        return (self.seq, 1 - self.core)

    def lines_away(self, step):
        return (self.seq + step * MATES, self.core)


def meet(place, far=False, lines=0, cores=False, straight=False):
    barrier = pltpu.get_barrier_semaphore()
    partners = [place.of(place.x), place.of(place.y), place.sibling]
    if far or cores:
        partners.append(place.of(place.far))
    if cores:
        partners += [place.of(mate, 1) for mate in (place.x, place.y, place.far)]
    for partner in partners:
        pl.semaphore_signal(barrier, inc=1, device_id=partner, device_id_type=MESH)
    count = len(partners)
    if straight:
        for step in range(1, lines):
            line = (place.line + step) % lines
            pl.semaphore_signal(
                barrier,
                inc=1,
                device_id=(line * MATES + place.mate, place.core),
                device_id_type=MESH,
            )
        count = count + max(lines - 1, 0)
    elif lines > 1:
        below, above = place.line > 0, place.line < lines - 1

        @pl.when(below)
        def _():
            pl.semaphore_signal(
                barrier, inc=1, device_id=place.lines_away(-1), device_id_type=MESH
            )

        @pl.when(above)
        def _():
            pl.semaphore_signal(barrier, inc=1, device_id=place.lines_away(1), device_id_type=MESH)

        count = count + jnp.where(below, 1, 0) + jnp.where(above, 1, 0)
    pl.semaphore_wait(barrier, count)


def sender(sems):
    send, receive = sems

    def make(index, source, target, device):
        return pltpu.make_async_remote_copy(
            src_ref=source,
            dst_ref=target,
            send_sem=send.at[index],
            recv_sem=receive.at[index],
            device_id=device,
            device_id_type=MESH,
        )

    return make


def row_steps(first, last, body):
    def one(step, carry):
        body(pl.ds(pl.multiple_of(first + step * STEP, STEP), STEP))
        return carry

    lax.fori_loop(0, (last - first) // STEP, one, 0)


class SumRows:
    @staticmethod
    def scratch(rows, columns, computed=False):
        return [
            pltpu.VMEM((MATES, rows, columns), low),
            pltpu.VMEM((MATES, rows, columns), low),
            pltpu.VMEM((2, rows // 2, columns), low),
            pltpu.VMEM((2, rows, columns), low),
            pltpu.SemaphoreType.DMA((MATES,)),
            pltpu.SemaphoreType.DMA((10,)),
            pltpu.SemaphoreType.DMA((10,)),
        ] + [pltpu.VMEM((MATES, rows, columns), low)] * computed

    def __init__(self, place, partial, scratch, compute=None):
        self.place, self.partial, self.compute = place, partial, compute
        self.own, self.swapped, self.relay, self.arrived, self.local_sems, send, receive = scratch[:7]
        if compute:
            self.other = scratch[7]
        self.make = sender((send, receive))
        self.rows = self.own.shape[1]
        self.order = [place.far, place.x, place.y, place.mate]
        half, x, y = self.rows // 2, place.of(place.x), place.of(place.y)
        own, relay, arrived = self.own, self.relay, self.arrived
        self.far_low = self.make(4, own.at[0, :half], relay.at[0], y)
        self.far_high = self.make(5, own.at[0, half:], relay.at[1], x)
        self.x_high = self.make(6, own.at[1, half:], arrived.at[0, half:], x)
        self.y_low = self.make(7, own.at[2, :half], arrived.at[1, :half], y)
        self.x_low = self.make(8, own.at[1, :half], arrived.at[0, :half], x)
        self.y_high = self.make(9, own.at[2, half:], arrived.at[1, half:], y)
        self.swaps = [
            self.make(
                slot,
                self.other.at[slot] if compute else partial.at[1, mate],
                self.swapped.at[slot],
                place.sibling,
            )
            for slot, mate in enumerate(self.order)
        ]

    def load(self, slot):
        return pltpu.make_async_copy(
            self.partial.at[0, self.order[slot]], self.own.at[slot], self.local_sems.at[slot]
        )

    def begin(self):
        for slot, mate in enumerate(self.order):
            if self.compute:
                self.compute(1, mate, self.other, slot)
            else:
                self.load(slot).start()
            self.swaps[slot].start()

    def add(self, target, target_slot, source, source_slot, first, last, shift=0):
        def body(here):
            there = pl.ds(pl.multiple_of(here.start - shift, STEP), STEP) if shift else here
            target[target_slot, here] = (
                target[target_slot, here].astype(wide) + source[source_slot, there].astype(wide)
            ).astype(low)

        row_steps(first, last, body)

    def sum_cores(self, slot):
        if self.compute:
            self.compute(0, self.order[slot], self.own, slot)
        else:
            self.load(slot).wait()
        self.swaps[slot].wait_recv()
        self.add(self.own, slot, self.swapped, slot, 0, self.rows)

    def send_far(self):
        self.sum_cores(0)
        self.far_low.start()
        self.far_high.start()

    def send_near(self):
        self.sum_cores(1)
        self.x_high.start()
        self.sum_cores(2)
        self.y_low.start()

    def send_relayed(self):
        half = self.rows // 2
        self.far_low.wait_recv()
        self.add(self.own, 1, self.relay, 0, 0, half)
        self.x_low.start()
        self.far_high.wait_recv()
        self.add(self.own, 2, self.relay, 1, half, self.rows, shift=half)
        self.y_high.start()
        self.sum_cores(3)

    def wait_half(self, upper):
        if upper:
            self.x_high.wait_recv()
            self.y_high.wait_recv()
        else:
            self.x_low.wait_recv()
            self.y_low.wait_recv()

    def total(self, here):
        return (
            self.own[3, here].astype(wide)
            + self.arrived[0, here].astype(wide)
            + self.arrived[1, here].astype(wide)
        )

    def finish(self):
        for copy in self.swaps + [
            self.far_low, self.far_high, self.x_high, self.y_low, self.x_low, self.y_high,
        ]:
            copy.wait_send()


class ShareRows:
    @staticmethod
    def scratch():
        return [
            pltpu.SemaphoreType.DMA((1,)),
            pltpu.SemaphoreType.DMA((11,)),
            pltpu.SemaphoreType.DMA((11,)),
        ]

    def __init__(self, place, source, target, scratch):
        self.place, self.source, self.target = place, source, target
        self.local_sem, send, receive = scratch
        self.make = sender((send, receive))
        self.rows = target.shape[2]

    def copy(self, index):
        place, half = self.place, self.rows // 2
        lower, upper, whole = pl.ds(0, half), pl.ds(half, half), pl.ds(0, self.rows)
        x, y, sibling = place.of(place.x), place.of(place.y), place.sibling

        def own(rows, device, side=0):
            return self.source.at[rows], self.target.at[side, place.mate, rows], device

        def passed(mate, rows, device, side=0):
            return self.target.at[0, mate, rows], self.target.at[side, mate, rows], device

        return self.make(
            index,
            *(
                lambda: own(upper, y),
                lambda: own(upper, x),
                lambda: own(lower, x),
                lambda: own(lower, y),
                lambda: passed(place.x, lower, y),
                lambda: passed(place.y, upper, x),
                lambda: own(whole, sibling, 1),
                lambda: passed(place.x, whole, sibling, 1),
                lambda: passed(place.y, whole, sibling, 1),
                lambda: passed(place.far, lower, sibling, 1),
                lambda: passed(place.far, upper, sibling, 1),
            )[index](),
        )

    def local(self):
        return pltpu.make_async_copy(
            self.source, self.target.at[0, self.place.mate], self.local_sem.at[0]
        )

    def begin_half(self, upper):
        for index in (0, 1) if upper else (2, 3):
            self.copy(index).start()

    def begin_rest(self):
        self.local().start()
        self.copy(6).start()

    def forward(self):
        for came, then in ((2, 4), (0, 5), (1, 7), (3, 8)):
            self.copy(came).wait_recv()
            self.copy(then).start()

    def forward_far(self):
        for came, then in ((4, 9), (5, 10)):
            self.copy(came).wait_recv()
            self.copy(then).start()

    def finish(self):
        self.local().wait()
        for index in range(6, 11):
            self.copy(index).wait_recv()
        for index in range(11):
            self.copy(index).wait_send()


class GatherLines:
    @staticmethod
    def scratch(lines):
        return [
            pltpu.SemaphoreType.DMA((1,)),
            pltpu.SemaphoreType.DMA((3,)),
            pltpu.SemaphoreType.DMA((3,)),
            pltpu.SemaphoreType.DMA((lines, MATES)),
            pltpu.SemaphoreType.DMA((lines, MATES)),
            pltpu.SemaphoreType.DMA((lines, MATES)),
        ]

    def __init__(self, place, blocks, target, scratch, rows=None):
        self.place, self.blocks, self.target = place, blocks, target
        self.lines = target.shape[0]
        self.part = pl.ds(*(rows or (0, target.shape[2])))
        self.local_sem, send, receive, self.up_sem, self.down_sem, self.got = scratch
        self.make = sender((send, receive))
        self.order = [place.mate, place.x, place.y, place.far]

    def plane(self, slot):
        place, mate = self.place, self.order[slot]
        here = self.target.at[place.line, place.mate]
        if slot == 0:
            return pltpu.make_async_copy(self.blocks.at[mate], here, self.local_sem.at[0])
        return self.make(slot - 1, self.blocks.at[mate], here, place.of(mate))

    def begin(self):
        for slot in range(MATES):
            self.plane(slot).start()

    def arrive(self, slot):
        copy = self.plane(slot)
        copy.wait_recv() if slot else copy.wait()

    def hop(self, step, mate, direction):
        place = self.place
        line = place.line - step * direction
        piece = self.target.at[line, mate, self.part]
        sems = self.up_sem if direction > 0 else self.down_sem
        copy = pltpu.make_async_remote_copy(
            src_ref=piece,
            dst_ref=piece,
            send_sem=sems.at[step, mate],
            recv_sem=self.got.at[line, mate],
            device_id=place.lines_away(direction),
            device_id_type=MESH,
        )
        came = (line >= 0) & (line < self.lines)
        goes = (place.line < self.lines - 1) if direction > 0 else (place.line > 0)
        return copy, came, goes

    def leave(self, arriving=True):
        for slot, mate in enumerate(self.order):
            if arriving:
                self.arrive(slot)
            for direction in (1, -1):
                copy, _, goes = self.hop(0, mate, direction)
                pl.when(goes)(copy.start)

    def onwards(self, step):
        if step >= self.lines:
            return
        for mate in self.order:
            for direction in (1, -1):
                copy, came, goes = self.hop(step, mate, direction)
                pl.when(came)(copy.wait_recv)
                if step < self.lines - 1:
                    pl.when(came & goes)(copy.start)

    def finish_plane(self):
        for slot in range(1, MATES):
            self.plane(slot).wait_send()

    def finish_lines(self):
        for step in range(self.lines - 1):
            for mate in self.order:
                for direction in (1, -1):
                    copy, came, goes = self.hop(step, mate, direction)
                    pl.when(came & goes)(copy.wait_send)


class SwapBlocks:
    @staticmethod
    def scratch():
        return [
            pltpu.SemaphoreType.DMA((1,)),
            pltpu.SemaphoreType.DMA((2 * MATES,)),
            pltpu.SemaphoreType.DMA((2 * MATES,)),
        ]

    def __init__(self, place, piece, target, scratch):
        self.place, self.piece, self.target = place, piece, target
        self.local_sem, send, receive = scratch
        self.make = sender((send, receive))
        self.order = [place.far, place.x, place.y, place.mate]

    def copy(self, slot, index):
        place, mate = self.place, self.order[index]
        source, target = self.piece(slot, mate), self.target.at[slot, place.mate]
        if slot == 0 and index == MATES - 1:
            return pltpu.make_async_copy(source, target, self.local_sem.at[0]), True
        return self.make(slot * MATES + index, source, target, place.of(mate, slot)), False

    def begin(self, slot, index=None):
        for each in range(MATES) if index is None else (index,):
            self.copy(slot, each)[0].start()

    def finish(self):
        for slot in range(2):
            for index in range(MATES):
                self.copy(slot, index)[0].wait()


class SumLines:
    @staticmethod
    def scratch(lines, shape):
        return [
            pltpu.VMEM((lines,) + shape, low),
            pltpu.VMEM((2, max(lines - 1, 1)) + shape, low),
            pltpu.SemaphoreType.DMA((lines + 1,)),
            pltpu.SemaphoreType.DMA((2, lines)),
            pltpu.SemaphoreType.DMA((2, lines)),
            pltpu.SemaphoreType.DMA((3,)),
            pltpu.SemaphoreType.DMA((3,)),
        ]

    def __init__(self, place, blocks, result, scratch, first=0):
        self.place, self.blocks, self.result, self.first = place, blocks, result, first
        self.held, self.came, self.local_sems, self.send, self.got, send, receive = scratch
        self.lines = self.held.shape[0]
        self.make = sender((send, receive))

    def load(self, line):
        return pltpu.make_async_copy(
            self.blocks.at[
                line, :, pl.ds(self.first, self.held.shape[2]), pl.ds(0, self.held.shape[3])
            ],
            self.held.at[line],
            self.local_sems.at[line],
        )

    def begin(self):
        for line in range(self.lines):
            self.load(line).start()

    def wait_loads(self):
        for line in range(self.lines):
            self.load(line).wait()

    def put_gains(self, gains):
        lines, mates, height, lanes = self.held.shape
        top = lax.broadcasted_iota(jnp.int32, (height, lanes), 0) == 0
        for line in range(lines):
            for mate in range(mates):
                first = (line * mates + mate) * lanes
                part = jnp.broadcast_to(gains[:, first : first + lanes], (height, lanes))
                self.held[line, mate] = jnp.where(
                    top, part, self.held[line, mate].astype(wide)
                ).astype(low)

    def add_top(self, other, count):
        lines, mates, height, lanes = self.held.shape
        top = lax.broadcasted_iota(jnp.int32, (height, lanes), 0) < count
        for line in range(lines):
            for mate in range(mates):
                own = self.held[line, mate].astype(wide)
                both = own + other[line, mate].astype(wide)
                self.held[line, mate] = jnp.where(top, both, own).astype(low)

    def copy(self, turn, way):
        direction = 1 - 2 * way
        line = self.place.line + direction * (self.lines - turn)
        return line, pltpu.make_async_remote_copy(
            src_ref=self.held.at[line],
            dst_ref=self.came.at[way, turn - 1],
            send_sem=self.send.at[way, turn],
            recv_sem=self.got.at[way, turn],
            device_id=self.place.lines_away(direction),
            device_id_type=MESH,
        )

    def arrival(self, turn, way):
        slot = self.came.at[way, turn - 1]
        return pltpu.make_async_remote_copy(
            src_ref=slot,
            dst_ref=slot,
            send_sem=self.send.at[way, turn],
            recv_sem=self.got.at[way, turn],
            device_id=self.place.sibling,
            device_id_type=MESH,
        )

    def sends(self, turn, way):
        line = self.place.line
        return line <= turn - 1 if way == 0 else line >= self.lines - turn

    def inner(self, way):
        return self.place.line >= 1 if way == 0 else self.place.line <= self.lines - 2

    def add(self, line, way, turn):
        def mates(mate, carry):
            def body(here):
                self.held[line, mate, here] = (
                    self.held[line, mate, here].astype(wide)
                    + self.came[way, turn - 1, mate, here].astype(wide)
                ).astype(low)

            row_steps(0, self.held.shape[2], body)
            return carry

        lax.fori_loop(0, self.held.shape[1], mates, 0)

    def round(self, turn):
        if turn >= self.lines:
            return
        for way in (0, 1):
            line, copy = self.copy(turn, way)

            @pl.when(self.sends(turn, way))
            def _(line=line, copy=copy, way=way):
                if turn > 1:

                    @pl.when(self.inner(way))
                    def _():
                        self.arrival(turn - 1, way).wait_recv()
                        self.add(line, way, turn - 1)

                copy.start()

    def plane(self, index):
        place = self.place
        mate = (place.x, place.y, place.far)[index]
        return self.make(
            index, self.held.at[place.line, mate], self.result.at[place.mate], place.of(mate)
        )

    def local(self):
        place = self.place
        return pltpu.make_async_copy(
            self.held.at[place.line, place.mate],
            self.result.at[place.mate],
            self.local_sems.at[self.lines],
        )

    def exchange(self):
        for way in (0, 1):
            if self.lines > 1:

                @pl.when(self.inner(way))
                def _(way=way):
                    self.arrival(self.lines - 1, way).wait_recv()
                    self.add(self.place.line, way, self.lines - 1)

        for index in range(3):
            self.plane(index).start()
        self.local().start()

    def straight(self, step):
        line = (self.place.line + step) % self.lines
        return pltpu.make_async_remote_copy(
            src_ref=self.held.at[line],
            dst_ref=self.came.at[0, step - 1],
            send_sem=self.send.at[0, step],
            recv_sem=self.got.at[0, step],
            device_id=(line * MATES + self.place.mate, self.place.core),
            device_id_type=MESH,
        )

    def direct(self):
        for step in range(1, self.lines):
            self.straight(step).start()

    def exchange_direct(self):
        for step in range(1, self.lines):
            self.straight(step).wait_recv()
            self.add(self.place.line, 0, step)
        for index in range(3):
            self.plane(index).start()
        self.local().start()

    def finish(self, direct=False):
        self.local().wait()
        for index in range(3):
            self.plane(index).wait()
        if direct:
            for step in range(1, self.lines):
                self.straight(step).wait_send()
            return
        for turn in range(1, self.lines):
            for way in (0, 1):
                _, copy = self.copy(turn, way)
                pl.when(self.sends(turn, way))(copy.wait_send)


def remote_call(body, identity, ins, outs, scratch, aliases=None):
    anywhere = pl.BlockSpec(memory_space=pl.ANY)
    held = pl.BlockSpec(memory_space=pltpu.VMEM)
    return pl.pallas_call(
        body,
        in_specs=[anywhere if kind == "any" else held for _, kind in ins],
        out_specs=[anywhere if kind == "any" else held for _, _, kind in outs],
        out_shape=[jax.ShapeDtypeStruct(shape, dtype) for shape, dtype, _ in outs],
        scratch_shapes=scratch,
        input_output_aliases=aliases or {},
        compiler_params=pltpu.CompilerParams(
            vmem_limit_bytes=VMEM_BYTES, collective_id=identity, has_side_effects=True
        ),
    )(*[array for array, _ in ins])


def inverse_rms(value):
    return lax.rsqrt(jnp.mean(value * value, axis=1, keepdims=True) + epsilon)


def norm_back_rows(grad, source, scale):
    inverse = inverse_rms(source)
    scaled = grad * scale
    unit = source * inverse
    inner = jnp.mean(scaled * source, axis=1, keepdims=True)
    return inverse * (scaled - unit * (inverse * inner)), grad * unit


def load_weights(weights, held, sems):
    return [
        pltpu.make_async_copy(weights.at[slot, mate], held.at[slot, mate], sems.at[slot, mate])
        for slot in range(2)
        for mate in range(MATES)
    ]


def middle_kernel(lines, moves, gathered, weights, input_ref, scale_ref, grad_any, *rest):
    place = Place()
    count = len(moves)
    middle_ref, shared, grads, acts_out, hidden_out = rest[count : count + 5]
    targets, scratch = rest[count + 5 : 2 * count + 5], rest[2 * count + 5 :]
    normed, held, weight_sems, all_normed, ups, acts, hidden, out_sems, load_sems = scratch[:9]
    scratch = scratch[9:]
    share = ShareRows(place, normed, all_normed, scratch[:3])
    other = ShareRows(place, grad_any.at[place.core], grads, scratch[3:6])
    gathers = [
        GatherLines(place, None, target, scratch[6 + 6 * index : 12 + 6 * index], moves[index])
        for index, target in enumerate(targets)
        if moves[index]
    ]
    meet(place, lines=lines if gathers else 0)
    loads = load_weights(weights, held, weight_sems)
    for load in loads:
        load.start()
    other.begin_half(False)
    other.begin_half(True)
    other.begin_rest()
    for gather in gathers[:1]:
        gather.leave(False)
    _, _, all_lines, _, depth, width = held.shape
    early = moves[0][0] if gathers else depth

    def load_ups(index):
        part = (pl.ds(0, early), pl.ds(early, depth - early))[index]
        return pltpu.make_async_copy(
            targets[0].at[:, :, part], ups.at[:, :, part], load_sems.at[index]
        )

    load_ups(0).start()
    for load in loads:
        load.wait()
    rows, model_width = normed.shape
    half = rows // 2
    height = MATES * depth
    some = max(1, 512 // height)

    def product(step, carry):
        columns = pl.ds(pl.multiple_of(step * some * height, 128), some * height)
        part = pl.ds(step * some, some)
        for first in (0, half):
            total = None
            for slot in range(2):
                for mate in range(MATES):
                    term = dot(
                        gathered[slot, mate, first : first + half],
                        held[slot, mate, part].reshape(some * height, width),
                        NT,
                    )
                    total = term if total is None else total + term
            here = pl.ds(first, half)
            middle_ref[here, columns] = input_ref[here, columns].astype(wide) + total
        return carry

    def body(here):
        middle = middle_ref[here]
        normed[here] = (middle * inverse_rms(middle) * scale_ref[...]).astype(low)

    lax.fori_loop(0, all_lines // some, product, 0)
    row_steps(0, half, body)
    share.begin_half(False)
    row_steps(half, rows, body)
    share.begin_half(True)
    share.begin_rest()
    for gather in gathers[:1]:
        gather.onwards(1)
    for gather in gathers[1:]:
        gather.leave(False)
    for gather in gathers[:1]:
        gather.onwards(2)
    share.forward()
    for gather in gathers[:1]:
        for number in range(3, lines):
            gather.onwards(number)
    if early < depth:
        load_ups(1).start()
    for gather in gathers[1:]:
        gather.onwards(1)
    other.forward()
    share.forward_far()
    share.finish()
    load_ups(0).wait()
    if early < depth:
        load_ups(1).wait()
    weight = ups[...].reshape(model_width, ups.shape[3])
    units = hidden.shape[2]
    outs = []
    for slot in range(2):
        for mate in range(MATES):
            index = slot * MATES + mate
            values = dot(all_normed[slot, mate], weight, NN)
            acts[index] = values.astype(low)
            gate, up = values[:, :units], values[:, units:]
            hidden[index] = (gate * jax.nn.sigmoid(gate) * up).astype(low)
            here = pl.ds(index * rows, rows)
            outs += [
                pltpu.make_async_copy(acts.at[index], acts_out.at[here], out_sems.at[0, index]),
                pltpu.make_async_copy(hidden.at[index], hidden_out.at[here], out_sems.at[1, index]),
                pltpu.make_async_copy(
                    all_normed.at[slot, mate], shared.at[slot, mate], out_sems.at[2, index]
                ),
            ]
            for out in outs[-3:]:
                out.start()
        if slot == 0:
            for gather in gathers[1:]:
                gather.onwards(2)
            other.forward_far()
    for number in range(3, lines):
        for gather in gathers[1:]:
            gather.onwards(number)
    for gather in gathers:
        gather.finish_lines()
    other.finish()
    for out in outs:
        out.wait()


def columns_in_steps(lines, depth, body):
    height = MATES * depth
    some = max(1, 512 // height)

    def one(step, carry):
        body(
            pl.ds(pl.multiple_of(step * some * height, 128), some * height),
            pl.ds(step * some, some),
            some * height,
        )
        return carry

    lax.fori_loop(0, lines // some, one, 0)


def turn_rows_kernel(
    lines, parts, acts_grad, ups_any, weights, middle_ref, grad_ref, scale_ref, *rest
):
    place = Place()
    count = len(parts)
    blocks, rest = rest[:count], rest[count:]
    middle_grad_ref, gain_ref, low_grad, gated_grads = rest[:4]
    results, scratch = rest[4 : 4 + count], rest[4 + count :]
    held, load_sems, sent, acts, ups = scratch[:5]
    all_lines, _, depth, units = ups.shape
    tokens = low_grad.shape[0]

    def compute(side_of, mate, target, slot):
        first = pl.ds(pl.multiple_of((side_of * MATES + mate) * tokens, STEP), tokens)

        def step(columns, part, size):
            target[slot, :, columns] = dot(
                acts[first], ups[part].reshape(size, units), NT
            ).astype(low)

        columns_in_steps(all_lines, depth, step)

    rows = SumRows(place, None, scratch[5:13], compute)
    swap = SwapBlocks(place, lambda slot, mate: sent.at[slot, mate], gated_grads, scratch[13:16])
    sums = [
        SumLines(place, blocks[index], results[index], scratch[16 + 7 * index : 23 + 7 * index], first)
        for index, (first, _) in enumerate(parts)
    ]
    meet(place, lines=lines if parts else 0, cores=True)
    loads = [
        pltpu.make_async_copy(acts_grad, acts, load_sems.at[0]),
        pltpu.make_async_copy(ups_any, ups, load_sems.at[1]),
    ]
    for load in loads:
        load.start()
    for each in sums:
        each.begin()

    def load_weight(slot):
        return pltpu.make_async_copy(weights.at[slot], held, load_sems.at[2])

    load_weight(0).start()
    gain_ref[...] = jnp.zeros_like(gain_ref)
    for each in sums:
        each.wait_loads()
        each.round(1)
    for load in loads:
        load.wait()
    rows.begin()
    rows.send_far()
    rows.send_near()
    rows.send_relayed()
    for each in sums:
        each.round(2)
    rows.wait_half(False)
    rows.wait_half(True)

    def body(here):
        part, gains = norm_back_rows(rows.total(here), middle_ref[here], scale_ref[...])
        total = grad_ref[here].astype(wide) + part
        middle_grad_ref[here] = total
        low_grad[here] = total.astype(low)
        gain_ref[...] += jnp.sum(gains, axis=0, keepdims=True)

    row_steps(0, tokens, body)
    width = held.shape[-1]
    for slot in range(2):
        load_weight(slot).wait()
        for index, mate in enumerate(swap.order):
            weight = held[mate].reshape(all_lines * MATES * depth, width)
            sent[slot, mate] = dot(low_grad[...], weight, NN).astype(low)
            swap.begin(slot, index)
        if slot == 0:
            load_weight(1).start()
    rows.finish()
    for each in sums:
        each.round(3)
    swap.finish()
    for each in sums:
        for number in range(4, lines):
            each.round(number)
        each.exchange()
    for each in sums:
        each.finish()


def last_rows_kernel(
    lines, pieces, all_grads, attn_any, beta_ref, input_ref, middle_grad_ref, scale_ref, *rest
):
    place = Place()
    blocks, rest = rest[:pieces], rest[pieces:]
    input_grad, gain_ref = rest[:2]
    results, scratch = rest[2 : 2 + pieces], rest[2 + pieces :]
    low_grad, grads, attn, load_sems = scratch[:4]
    all_lines, _, depth, width = attn.shape
    tokens = low_grad.shape[0]

    def compute(side_of, mate, target, slot):
        first = pl.ds(pl.multiple_of((side_of * MATES + mate) * tokens, STEP), tokens)

        def step(columns, part, size):
            total = dot(grads[first, :width], attn[part].reshape(size, width), NT)
            total = total + dot(grads[first, width:], beta_ref[:, columns], NN)
            target[slot, :, columns] = total.astype(low)

        columns_in_steps(all_lines, depth, step)

    meet(place, far=bool(pieces), lines=lines if pieces else 0, straight=True)
    rows = SumRows(place, None, scratch[4:12], compute)
    make = sender(scratch[12:14])
    scratch = scratch[14:]
    sums = [
        SumLines(place, blocks[index], results[index], scratch[7 * index : 7 * index + 7])
        for index in range(pieces)
    ]
    loads = [
        pltpu.make_async_copy(all_grads, grads, load_sems.at[0]),
        pltpu.make_async_copy(attn_any, attn, load_sems.at[1]),
    ]
    for each in sums:
        each.begin()
    for load in loads:
        load.start()
    for each in sums:
        each.wait_loads()
    for each in sums[1:]:
        each.round(1)
    gain_ref[...] = jnp.zeros_like(gain_ref)
    for load in loads:
        load.wait()
    rows.begin()
    rows.send_far()
    rows.send_near()
    rows.send_relayed()
    for each in sums[1:]:
        each.round(2)
    rows.wait_half(False)
    rows.wait_half(True)

    def body(here):
        part, gains = norm_back_rows(
            rows.total(here), input_ref[here].astype(wide), scale_ref[...]
        )
        low_grad[here] = (middle_grad_ref[here] + part).astype(low)
        gain_ref[...] += jnp.sum(gains, axis=0, keepdims=True)

    row_steps(0, tokens, body)
    first = make(0, low_grad, input_grad.at[place.core], place.sibling)
    first.start()
    first_local = pltpu.make_async_copy(low_grad, input_grad.at[place.core], load_sems.at[2])
    first_local.start()
    if sums:
        mine, theirs = scratch[7 * pieces :]
        small = sums[0]
        small.put_gains(gain_ref)
        mine[...] = small.held[...]
        swap = make(1, mine, theirs, place.sibling)
        swap.start()
        swap.wait_recv()
        small.add_top(theirs, CONV_ROW)
        small.direct()
    for each in sums[1:]:
        each.round(3)
    for each in sums[:1]:
        each.exchange_direct()
    for turn in range(4, lines):
        for each in sums[1:]:
            each.round(turn)
    for each in sums[1:]:
        each.exchange()
    rows.finish()
    first_local.wait()
    first.wait()
    if sums:
        swap.wait_send()
    for each in sums:
        each.finish(direct=each is sums[0])


def first_rows_kernel(input_ref, inputs, *scratch):
    place = Place()
    meet(place)
    share = ShareRows(place, input_ref.at[place.core], inputs, scratch)
    share.begin_half(False)
    share.begin_half(True)
    share.begin_rest()
    share.forward()
    share.forward_far()
    share.finish()


def first_rows(block_input):
    seqs, rows, columns = block_input.shape
    return remote_call(
        first_rows_kernel,
        0,
        [(block_input, "any")],
        [((seqs, MATES, rows, columns), low, "any")],
        ShareRows.scratch(),
    )[0]


def first_kernel(lines, pieces, input_ref, *rest):
    place = Place()
    blocks, rest = rest[:pieces], rest[pieces:]
    normed_out, raw_ref, logit_ref, small_ref, attn_out = rest[:5]
    others, scratch = rest[5 : 3 + pieces], rest[3 + pieces :]
    inputs, normed, small, attn, scale, out_sems = scratch[:6]
    scratch = scratch[6:]
    targets = (small, attn) + tuple(others)
    meet(place, far=True, lines=lines)
    share = ShareRows(place, input_ref.at[place.core], inputs, scratch[:3])
    gathers = [
        GatherLines(place, blocks[index], targets[index], scratch[3 + 6 * index : 9 + 6 * index])
        for index in range(pieces)
    ]
    few, main, later = gathers[:3]
    for gather in gathers[:3]:
        gather.begin()
    for gather in gathers[:3]:
        gather.leave()
    share.begin_half(False)
    share.begin_half(True)
    share.begin_rest()
    for gather in (few, main):
        gather.onwards(1)
    share.forward()
    later.onwards(1)
    for gather in gathers[3:]:
        gather.begin()
    few.onwards(2)
    main.onwards(2)
    for step in range(3, lines):
        few.onwards(step)
    share.forward_far()
    later.onwards(2)
    share.finish()
    small_ref[...] = small[...]
    _, _, tokens, model_width = inputs.shape
    depth = small.shape[3]
    parts = [(line, mate) for line in range(lines) for mate in range(MATES)]
    for index, (line, mate) in enumerate(parts):
        scale[:, index * depth : (index + 1) * depth] = small[line, mate, :1].astype(wide)
    beta = jnp.concatenate([small[line, mate] for line, mate in parts], axis=1)
    beta = over(beta, jnp.zeros((CHUNK - beta.shape[0], model_width), low))
    outs = []
    for slot in range(2):
        for mate in range(MATES):
            first = (slot * MATES + mate) * tokens

            def body(here, slot=slot, mate=mate, first=first):
                value = inputs[slot, mate, here].astype(wide)
                there = pl.ds(pl.multiple_of(first + here.start, STEP), STEP)
                normed[there] = (value * inverse_rms(value) * scale[...]).astype(low)

            row_steps(0, tokens, body)
            block = pl.ds(first, tokens)
            logit_ref[block] = dot(normed[block], beta, NT)
            outs.append(
                pltpu.make_async_copy(
                    normed.at[block], normed_out.at[block], out_sems.at[slot * MATES + mate]
                )
            )
            outs[-1].start()
    for step in range(3, lines):
        main.onwards(step)
    outs.append(pltpu.make_async_copy(attn, attn_out, out_sems.at[2 * MATES]))
    outs[-1].start()
    weight = attn[...].reshape(model_width, attn.shape[3])

    def product(index, carry):
        here = pl.ds(pl.multiple_of(index * tokens, STEP), tokens)
        raw_ref[here] = dot(normed[here], weight, NN).astype(low)
        return carry

    lax.fori_loop(0, 2 * MATES, product, 0)
    for step in range(3, lines):
        later.onwards(step)
    for gather in gathers[3:]:
        for slot in range(MATES):
            gather.arrive(slot)
    for out in outs:
        out.wait()
    for gather in gathers:
        gather.finish_plane()
    for gather in gathers[:3]:
        gather.finish_lines()


def first_call(block_input, blocks, lines):
    seqs, tokens, model_width = block_input.shape
    rows = seqs * MATES * tokens
    small, attn = ((lines,) + block.shape for block in blocks[:2])
    shared = (seqs, MATES, tokens, model_width)
    return remote_call(
        functools.partial(first_kernel, lines, len(blocks)),
        0,
        [(array, "any") for array in (block_input, *blocks)],
        [
            ((rows, model_width), low, "any"),
            ((rows, attn[3]), low, "held"),
            ((rows, CHUNK), wide, "held"),
            (small, low, "held"),
            (attn, low, "any"),
        ]
        + [((lines,) + block.shape, low, "any") for block in blocks[2:]],
        [
            pltpu.VMEM(shared, low),
            pltpu.VMEM((rows, model_width), low),
            pltpu.VMEM(small, low),
            pltpu.VMEM(attn, low),
            pltpu.VMEM((1, model_width), wide),
            pltpu.SemaphoreType.DMA((2 * MATES + 1,)),
        ]
        + ShareRows.scratch()
        + GatherLines.scratch(lines) * len(blocks),
    )


def middle_rows(gathered, weights, mine, scale, out_grad, moving, lines):
    rows, columns = mine.shape
    shared = (2, MATES, rows, columns)
    arrays = [array for array, _ in moving]
    ups, downs = arrays
    several = 2 * MATES
    return remote_call(
        functools.partial(middle_kernel, lines, tuple(part for _, part in moving)),
        1,
        [(gathered, "held"), (weights, "any"), (mine, "held"), (scale, "held"), (out_grad, "any")]
        + [(array, "any") for array in arrays],
        [
            ((rows, columns), wide, "held"),
            (shared, low, "any"),
            (shared, low, "any"),
            ((several * rows, ups.shape[3]), low, "any"),
            ((several * rows, downs.shape[3]), low, "any"),
        ]
        + [(array.shape, low, "any") for array in arrays],
        [
            pltpu.VMEM((rows, columns), low),
            pltpu.VMEM(weights.shape, low),
            pltpu.SemaphoreType.DMA((2, MATES)),
            pltpu.VMEM(shared, low),
            pltpu.VMEM(ups.shape, low),
            pltpu.VMEM((several, rows, ups.shape[3]), low),
            pltpu.VMEM((several, rows, downs.shape[3]), low),
            pltpu.SemaphoreType.DMA((3, several)),
            pltpu.SemaphoreType.DMA((2,)),
        ]
        + ShareRows.scratch() * 2
        + GatherLines.scratch(lines) * len(arrays),
        {5 + index: 5 + index for index in range(len(arrays))},
    )


def turn_rows(acts_grad, ups, weights, middle, grad, scale, summing, lines):
    rows, columns = middle.shape
    width = weights.shape[-1]
    blocks = (2, MATES, rows, width)
    scratch = [
        pltpu.VMEM(weights.shape[1:], low),
        pltpu.SemaphoreType.DMA((3,)),
        pltpu.VMEM(blocks, low),
        pltpu.VMEM(acts_grad.shape, low),
        pltpu.VMEM(ups.shape, low),
    ]
    scratch += SumRows.scratch(rows, columns, True) + SwapBlocks.scratch()
    outs = []
    for array, (_, height) in summing:
        shape = (MATES, height, array.shape[3])
        scratch += SumLines.scratch(lines, shape)
        outs.append((shape, low, "any"))
    return remote_call(
        functools.partial(turn_rows_kernel, lines, tuple(part for _, part in summing)),
        2,
        [(array, "any") for array in (acts_grad, ups, weights)]
        + [(array, "held") for array in (middle, grad, scale)]
        + [(array, "any") for array, _ in summing],
        [
            ((rows, columns), wide, "held"),
            ((1, columns), wide, "held"),
            ((rows, columns), low, "held"),
            (blocks, low, "any"),
        ]
        + outs,
        scratch,
    )


def last_rows(all_grads, attn, beta, mine, middle_grad, scale, blocks, lines):
    rows, columns = mine.shape
    scratch = [
        pltpu.VMEM((rows, columns), low),
        pltpu.VMEM(all_grads.shape, low),
        pltpu.VMEM(attn.shape, low),
        pltpu.SemaphoreType.DMA((3,)),
    ]
    scratch += SumRows.scratch(rows, columns, True) + [pltpu.SemaphoreType.DMA((2,))] * 2
    for block, kept in blocks:
        scratch += SumLines.scratch(lines, block.shape[1:3] + (kept,))
    if blocks:
        scratch += [pltpu.VMEM(blocks[0][0].shape, low)] * 2
    return remote_call(
        functools.partial(last_rows_kernel, lines, len(blocks)),
        3,
        [(all_grads, "any"), (attn, "any")]
        + [(array, "held") for array in (beta, mine, middle_grad, scale)]
        + [(block, "any") for block, _ in blocks],
        [((2, rows, columns), low, "any"), ((1, columns), wide, "held")]
        + [(block.shape[1:3] + (kept,), low, "any") for block, kept in blocks],
        scratch,
    )


class Steps:
    def __init__(self, seqs, heads, span):
        self.seqs, self.heads, self.span = seqs, heads, span
        self.chains, self.chunks = seqs * heads, span // CHUNK

    def chain(self, step, when):
        if when == "first":
            return jnp.minimum(step, self.chains - 1)
        if when == "second":
            return jnp.maximum(step - self.chains, 0)
        return step % self.chains

    def rows(self, when, columns, place):
        def index(step):
            chain = self.chain(step, when)
            return chain // self.heads, place(chain % self.heads)

        return pl.BlockSpec((self.span, columns), index)

    def streams(self, when):
        return self.rows(when, 3 * CHUNK, lambda head: head)

    def head(self, when):
        return self.rows(when, CHUNK, lambda head: head)

    def gate(self, when):
        return self.rows(when, CHUNK, lambda head: 3 * self.heads + head)

    def logit(self, when):
        return self.rows(when, CHUNK, lambda head: 0)

    def taps(self, when):
        return pl.BlockSpec(
            (1, 3 * CONV, CHUNK), lambda step: (self.chain(step, when) % self.heads, 0, 0)
        )

    def blocks(self, when, columns=CHUNK):
        return pl.BlockSpec(
            (1, self.chunks, CHUNK, columns), lambda step: (self.chain(step, when), 0, 0, 0)
        )

    def few(self, when, columns):
        return pl.BlockSpec((1, 8, columns), lambda step: (self.chain(step, when), 0, 0))

    def whole(self, shape):
        return pl.BlockSpec(shape, lambda step: (0,) * len(shape), pipeline_mode=pl.Buffered(1))

    def call(self, body, identity, ins, outs, scratch, aliases=None):
        return pl.pallas_call(
            body,
            grid=(2 * self.chains,),
            in_specs=[spec for _, spec in ins],
            out_specs=[spec for _, _, spec in outs],
            out_shape=[jax.ShapeDtypeStruct(shape, dtype) for shape, dtype, _ in outs],
            scratch_shapes=scratch,
            input_output_aliases=aliases or {},
            compiler_params=pltpu.CompilerParams(
                vmem_limit_bytes=VMEM_BYTES,
                dimension_semantics=("arbitrary",),
                collective_id=identity,
                has_side_effects=True,
            ),
        )(*[array for array, _ in ins])


def delta_front(limit, raw, taps, logits, scale, moving, lines, seqs, heads, span):
    steps = Steps(seqs, heads, span)
    chains, chunks, size = steps.chains, steps.chunks, CHUNK
    squares, doubles = (chains, chunks, CHUNK, size), (chains, chunks, CHUNK, 2 * size)
    states, tails = (chains, size, size), (seqs, 16, 3 * heads * size)
    tokens = span // MATES
    anywhere = pl.BlockSpec(memory_space=pl.ANY)
    arrays = [array for array, _ in moving]
    ins = [
        (limit, pl.BlockSpec(memory_space=pltpu.SMEM)),
        (raw, anywhere),
        (raw, steps.streams("first")),
        (taps, steps.taps("first")),
        (logits, steps.logit("first")),
        (raw, steps.gate("second")),
        (scale, steps.whole((1, size))),
    ] + [(array, anywhere) for array in arrays]
    outs = [
        ((seqs * span, 3 * heads * size), low, steps.streams("first")),
        (squares, wide, steps.blocks("first")),
        (doubles, wide, steps.blocks("first", 2 * size)),
        (squares, wide, steps.blocks("first")),
        (states, wide, steps.whole(states)),
        (tails, low, steps.whole(tails)),
        (squares, wide, steps.blocks("second")),
        (squares, wide, steps.blocks("second")),
        ((seqs * span, heads * size), wide, steps.head("second")),
        ((seqs * span, heads * size), low, steps.head("second")),
        ((seqs, MATES, tokens, heads * size), low, anywhere),
        ((seqs, MATES) + arrays[0].shape, low, anywhere),
    ] + [(array.shape, low, anywhere) for array in arrays]
    scratch = [
        pltpu.VMEM((span + 16, 3 * size), wide),
        pltpu.VMEM(squares, wide),
        pltpu.VMEM(squares, wide),
        pltpu.VMEM(squares, wide),
        pltpu.VMEM(squares, wide),
        pltpu.VMEM(doubles, wide),
        pltpu.VMEM((chains, span, 3 * size), low),
        pltpu.VMEM(states, low),
        pltpu.VMEM(states, low),
        pltpu.VMEM(tails, low),
        pltpu.SemaphoreType.DMA((2, seqs)),
        pltpu.SemaphoreType.DMA((2,)),
        pltpu.VMEM((seqs, span, heads * size), low),
    ]
    scratch += ShareRows.scratch() + SwapBlocks.scratch()
    scratch += GatherLines.scratch(lines) * len(arrays)
    moves = tuple(part for _, part in moving)
    return steps.call(
        functools.partial(front_kernel, lines, heads, moves),
        4,
        ins,
        outs,
        scratch,
        {7 + index: 12 + index for index in range(len(arrays))},
    )


def delta_back(
    limit, raw, tails, taps, logits, scale, qkv, wu, maps, total, grad, mixed, solved, state, fresh,
    row_grad, mlp_partial, middle, summing, lines, seqs, heads, span,
):
    steps = Steps(seqs, heads, span)
    chains, chunks, size = steps.chains, steps.chunks, CHUNK
    squares, states = (chains, chunks, CHUNK, size), (chains, size, size)
    all_shape = (seqs * span, (4 * heads + 1) * size)
    anywhere = pl.BlockSpec(memory_space=pl.ANY)
    ins = [
        (limit, pl.BlockSpec(memory_space=pltpu.SMEM)),
        (raw, steps.streams("second")),
        (tails, steps.whole(tails.shape)),
        (taps, steps.taps("second")),
        (logits, steps.logit("second")),
        (raw, steps.gate("first")),
        (scale, steps.whole((1, size))),
        (qkv, steps.streams("both")),
        (wu, steps.blocks("both", 2 * size)),
        (maps, steps.blocks("first")),
        (total, steps.whole(states)),
        (grad, steps.head("first")),
        (mixed, steps.head("first")),
        (solved, steps.blocks("second")),
        (state, steps.blocks("second")),
        (fresh, steps.blocks("second")),
        (row_grad, anywhere),
        (mlp_partial, anywhere),
        (middle, steps.whole(middle.shape)),
    ] + [(array, anywhere) for array, _ in summing]
    outs = [
        (all_shape, low, steps.whole(all_shape)),
        ((chains, 8, size), wide, steps.few("first", size)),
        ((chains, 8, 3 * size), wide, steps.few("second", 3 * size)),
        ((seqs, MATES) + row_grad.shape, low, anywhere),
        ((seqs,) + row_grad.shape, low, anywhere),
    ]
    edges = (chains, 16, 3 * size)
    scratch = [
        pltpu.VMEM((span + 16, 3 * size), wide),
        pltpu.VMEM((span + 32, 3 * size), wide),
        pltpu.VMEM(squares, wide),
        pltpu.VMEM(squares, wide),
        pltpu.VMEM(squares, wide),
        pltpu.VMEM(squares, wide),
        pltpu.VMEM(squares, wide),
        pltpu.VMEM(states, low),
        pltpu.VMEM(states, low),
        pltpu.VMEM(edges, low),
        pltpu.VMEM(edges, wide),
        pltpu.VMEM(edges, low),
        pltpu.SemaphoreType.DMA((2, chains)),
        pltpu.SemaphoreType.DMA((2,)),
    ] + ShareRows.scratch()
    scratch += [pltpu.VMEM(row_grad.shape, low)] + [pltpu.SemaphoreType.DMA((1,))] * 3
    scratch += SumRows.scratch(*row_grad.shape)
    for array, (_, height) in summing:
        shape = (MATES, height, array.shape[3])
        scratch += SumLines.scratch(lines, shape)
        outs.append((shape, low, anywhere))
    return steps.call(
        functools.partial(back_kernel, lines, heads, tuple(part for _, part in summing)),
        5,
        ins,
        outs,
        scratch,
    )


def tiled_call(body, ins, wholes, outs):
    tile = 256

    def tall(shape):
        return pl.BlockSpec((tile, shape[1]), lambda step: (step, 0))

    def whole(array):
        return pl.BlockSpec(array.shape, lambda step: (0, 0), pipeline_mode=pl.Buffered(1))

    return pl.pallas_call(
        body,
        grid=(ins[0].shape[0] // tile,),
        in_specs=[tall(array.shape) for array in ins] + [whole(array) for array in wholes],
        out_specs=[tall(shape) for shape, _ in outs],
        out_shape=[jax.ShapeDtypeStruct(shape, dtype) for shape, dtype in outs],
        compiler_params=pltpu.CompilerParams(vmem_limit_bytes=VMEM_BYTES),
    )(*ins, *wholes)


def project(inputs, scale, weight, beta):
    rows, model_width = inputs.shape
    return tiled_call(
        project_kernel,
        (inputs,),
        (scale, weight, beta),
        [((rows, model_width), low), ((rows, weight.shape[1]), low), ((rows, beta.shape[0]), wide)],
    )


def held_call(body, ins, outs):
    held = pl.BlockSpec(memory_space=pltpu.VMEM)
    return pl.pallas_call(
        body,
        in_specs=[held] * len(ins),
        out_specs=[held] * len(outs),
        out_shape=[jax.ShapeDtypeStruct(shape, dtype) for shape, dtype in outs],
        compiler_params=pltpu.CompilerParams(vmem_limit_bytes=VMEM_BYTES),
    )(*ins)


def pack_kernel(
    heads, query, key, value, outgate, output, swish, upward, downward,
    attn_ref, output_ref, ups_ref, downs_ref,
):
    size = CHUNK
    width = heads * size
    units = downs_ref.shape[2]
    for mate in range(MATES):
        first = mate * width
        for head in range(heads):
            for stream, weight in enumerate((query, key, value)):
                lanes = (3 * head + stream) * size
                attn_ref[mate, :, lanes : lanes + size] = weight[
                    :, first + head * size : first + (head + 1) * size
                ].astype(low)
        attn_ref[mate, :, 3 * width : 4 * width] = outgate[:, first : first + width].astype(low)
        output_ref[mate] = output[first : first + width, :].T.astype(low)
        here = mate * units
        ups_ref[mate, :, :units] = swish[:, here : here + units].astype(low)
        ups_ref[mate, :, units:] = upward[:, here : here + units].astype(low)
        downs_ref[mate] = downward[here : here + units, :].T.astype(low)


def unpack_kernel(
    heads, attn, outs, ups_low, ups_high, downs,
    query, key, value, outgate, output, swish, upward, downward,
):
    size = CHUNK
    width = heads * size
    units = downs.shape[2]
    split = ups_low.shape[1]
    for mate in range(MATES):
        first = mate * width
        for head in range(heads):
            for stream, grad in enumerate((query, key, value)):
                lanes = (3 * head + stream) * size
                grad[:, first + head * size : first + (head + 1) * size] = attn[
                    mate, :, lanes : lanes + size
                ].astype(wide)
        outgate[:, first : first + width] = attn[mate, :, 3 * width : 4 * width].astype(wide)
        output[first : first + width, :] = outs[mate].astype(wide).T
        here = mate * units
        for rows_here, part in ((pl.ds(0, split), ups_low), (pl.ds(split, swish.shape[0] - split), ups_high)):
            swish[rows_here, here : here + units] = part[mate, :, :units].astype(wide)
            upward[rows_here, here : here + units] = part[mate, :, units:].astype(wide)
        downward[here : here + units, :] = downs[mate].astype(wide).T


def cut_columns(weight):
    depth, columns = weight.shape
    return weight.reshape(depth, MATES, columns // MATES).transpose(1, 0, 2)


def join_columns(blocks):
    return blocks.transpose(1, 0, 2).reshape(blocks.shape[1], -1)


def gather_weights(blocks):
    return gather_lines(swap_blocks(blocks))


def scatter_grads(blocks):
    return swap_blocks(scatter_lines(blocks.astype(low))).astype(wide)


def on_device(
    block_input,
    lengths,
    attn_gain,
    query_weight,
    key_weight,
    value_weight,
    outgate_weight,
    beta_weight,
    conv_kernel,
    head_gain,
    output_weight,
    mlp_gain,
    swish_weight,
    upward_weight,
    downward_weight,
    out_grad,
):
    count = lax.axis_size("seq")
    lines = count // MATES
    core = lax.axis_index("tp")
    seq_count, tokens, model_width = block_input.shape
    depth = attn_gain.shape[0]
    gain_part = head_gain.shape[0]
    head_size = gain_part * count
    heads = beta_weight.shape[1] // MATES
    width = heads * head_size
    units = swish_weight.shape[1] // MATES

    conv_rows = -(-heads * 3 * CONV * gain_part // CHUNK)
    near = 1 < lines <= 4 and depth == CHUNK and conv_rows == BETA_ROW - CONV_ROW
    rows = seq_count * MATES * tokens
    span = MATES * tokens

    def in_rows(array):
        return jnp.pad(array, ((0, 0), (0, -array.shape[1] % 128)))

    def gains_of(attn, mlp, head):
        return jnp.concatenate([attn, mlp, in_rows(head)], axis=1)

    gains_cut = gains_of(attn_gain[None], mlp_gain[None], head_gain[None]).astype(low)
    conv_cut = in_rows(conv_kernel.astype(low).reshape(MATES, -1))
    beta_cut = beta_weight.astype(low).reshape(depth, MATES, heads).transpose(1, 2, 0)
    small_cut = jnp.concatenate(
        [jnp.broadcast_to(gains_cut, (MATES, gains_cut.shape[1])), conv_cut], axis=1
    )
    conv_start, conv_size = gains_cut.shape[1], heads * 3 * CONV * gain_part
    beta_start = small_cut.shape[1]
    small_cut = jnp.concatenate([small_cut, beta_cut.reshape(MATES, -1)], axis=1)
    small_size = small_cut.shape[1]
    small_cut = jnp.pad(small_cut, ((0, 0), (0, SMALL * 128 - small_size)))
    small_cut = small_cut.reshape(MATES, SMALL, 128)
    streams_end, gates_end = 3 * width, 4 * width
    if near:
        cuts = held_call(
            functools.partial(pack_kernel, heads),
            (
                query_weight, key_weight, value_weight, outgate_weight, output_weight,
                swish_weight, upward_weight, downward_weight,
            ),
            [
                ((MATES, depth, columns), low)
                for columns in (gates_end, width, 2 * units, units)
            ],
        )
        flat_normed, raw, logits, small, attn_full, output_full, ups_full, downward_full = first_call(
            block_input, (small_cut, *cuts), lines
        )
        ups_split = depth // 128 * 96
        front_moves = ((output_full, None), (ups_full, (0, ups_split)))
    else:
        streams_cut = jnp.stack(
            [
                w.astype(low).reshape(depth, MATES, heads, head_size)
                for w in (query_weight, key_weight, value_weight)
            ],
            axis=3,
        )
        streams_cut = streams_cut.transpose(1, 0, 2, 3, 4).reshape(MATES, depth, streams_end)
        cuts = (
            small_cut,
            jnp.concatenate([streams_cut, cut_columns(outgate_weight.astype(low))], axis=2),
            cut_columns(output_weight.astype(low).T),
            jnp.concatenate([cut_columns(w.astype(low)) for w in (swish_weight, upward_weight)], axis=2),
            cut_columns(downward_weight.astype(low).T),
        )
        input_rows = first_rows(block_input).reshape(rows, model_width)
        small, attn_full, output_full, ups_full, downward_full = (gather_weights(cut) for cut in cuts)
        front_moves = ((output_full, None),)
    attn_blocks = attn_full
    attn_full = attn_full.reshape(model_width, gates_end)
    small = small.reshape(count, SMALL * 128)
    attn_scale = small[:, :depth].reshape(1, model_width).astype(wide)
    mlp_scale = small[:, depth : 2 * depth].reshape(1, model_width).astype(wide)
    head_scale = small[:, 2 * depth : 2 * depth + gain_part].reshape(1, head_size).astype(wide)
    taps = (
        small[:, conv_start : conv_start + conv_size]
        .reshape(count, heads, 3, CONV, gain_part)
        .transpose(1, 2, 3, 0, 4)
        .reshape(heads, 3 * CONV, head_size)
        .astype(wide)
    )
    beta_rows = (
        small[:, beta_start:small_size]
        .reshape(count, heads, depth)
        .transpose(1, 0, 2)
        .reshape(heads, model_width)
    )
    beta_rows = jnp.pad(beta_rows, ((BETA_ROW, CHUNK - BETA_ROW - heads), (0, 0)))

    mine_low = pick(block_input, core)
    grad_mine = pick(out_grad, core)
    blocked = (seq_count, MATES, tokens, model_width)
    lengths_here = jnp.stack([pick(lengths, core), pick(lengths, 1 - core)])
    limit = lengths_here - line_of() * span

    if not near:
        flat_normed, raw, logits = project(input_rows, attn_scale, attn_full, beta_rows)
    sizes_of = (lines, seq_count, heads, span)
    (
        qkv, solved, wu, maps, total, tails, state, fresh, mixed, gated, gathered, output_all, *moved
    ) = delta_front(limit, raw, taps, logits, head_scale, front_moves, *sizes_of)
    middle_moves = ((ups_full, None), (downward_full, None))
    if near:
        middle_moves = ((moved[1], (ups_split, depth - ups_split)), (downward_full, (0, depth)))
    middle, mlp_normed, grad_rows, acts, hidden, ups_full, downward_full = middle_rows(
        gathered, output_all, mine_low, mlp_scale, out_grad, middle_moves, lines
    )
    grad_rows = grad_rows.reshape(rows, model_width)
    downward_full = downward_full.reshape(model_width, units)
    mlp_normed = mlp_normed.reshape(rows, model_width)
    gate_act, up_act = acts[:, :units].astype(wide), acts[:, units:].astype(wide)
    mlp_part = matmul("rf,df->rd", hidden, downward_full).astype(low)

    hidden_grad = matmul("rd,df->rf", grad_rows, downward_full)
    downward_grad = matmul("rd,rf->df", grad_rows, hidden).astype(low)
    acts_grad = jnp.concatenate(
        [
            (hidden_grad * up_act * silu_slope(gate_act)).astype(low),
            (hidden_grad * jax.nn.silu(gate_act)).astype(low),
        ],
        axis=1,
    )
    ups_grad = matmul("rd,rf->df", mlp_normed, acts_grad).astype(low)

    def cut_rows(grad):
        return grad.reshape(lines, MATES, depth, grad.shape[1])

    ups_blocks, downward_blocks = cut_rows(ups_grad), cut_rows(downward_grad)
    turn_sums = back_sums = ()
    if near:
        sums_split = depth // 128 * 32
        turn_sums = ((downward_blocks, (0, depth)), (ups_blocks, (0, sums_split)))
    middle_grad, mlp_gain_grad, attn_grad_mine, gated_grad, *summed = turn_rows(
        acts_grad, ups_full, output_all, middle, grad_mine, mlp_scale, turn_sums, lines
    )
    if near:
        downward_sum, ups_low = summed
        back_sums = ((ups_blocks, (sums_split, depth - sums_split)),)
    all_grads, head_gain_parts, taps_grad, attn_grad_rows, block_output, *summed = delta_back(
        limit, raw, tails, taps, logits, head_scale, qkv, wu, maps, total,
        gated_grad.reshape(rows, width), mixed, solved, state, fresh, attn_grad_mine, mlp_part.reshape(blocked), middle,
        back_sums, *sizes_of,
    )
    attn_grad_rows = attn_grad_rows.reshape(rows, model_width)
    output_grad = cut_rows(matmul("rd,rc->dc", attn_grad_rows, gated).astype(low))
    attn_grads = matmul("rd,rc->dc", flat_normed, all_grads).astype(low)
    beta_grad = attn_grads[:, gates_end + BETA_ROW : gates_end + BETA_ROW + heads]
    attn_grads = cut_rows(attn_grads)

    conv_grad = (
        taps_grad[:, :CONV]
        .reshape(seq_count, heads, CONV, 3, count, gain_part)
        .sum(axis=0)
        .transpose(3, 0, 2, 1, 4)
        .reshape(count, -1)
    )

    def small_blocks(attn_gain_grad):
        gains = gains_of(
            attn_gain_grad.reshape(count, depth),
            mlp_gain_grad.reshape(count, depth),
            jnp.sum(head_gain_parts[:, 0], axis=0).reshape(count, gain_part),
        )
        beta = beta_grad.reshape(count, depth, heads).transpose(0, 2, 1).reshape(count, -1)
        flat = jnp.concatenate([gains.astype(low), in_rows(conv_grad.astype(low)), beta], axis=1)
        flat = jnp.pad(flat, ((0, 0), (0, SMALL * 128 - small_size)))
        return flat.reshape(lines, MATES, SMALL, 128)

    last_ins = (all_grads, attn_blocks, beta_rows, mine_low, middle_grad, attn_scale)
    if near:
        ups_high, = summed
        blocks = (
            (small_blocks(jnp.zeros((1, model_width), wide)), 128),
            (attn_grads, gates_end),
            (output_grad, width),
        )
        input_grad, _, small_sum, attn_sum, output_sum = last_rows(*last_ins, blocks, lines)
        grads = held_call(
            functools.partial(unpack_kernel, heads),
            (attn_sum, output_sum, ups_low, ups_high, downward_sum),
            [
                (w.shape, wide)
                for w in (
                    query_weight, key_weight, value_weight, outgate_weight, output_weight,
                    swish_weight, upward_weight, downward_weight,
                )
            ],
        )
        small_sum = small_sum.reshape(MATES, SMALL * 128).astype(wide)
        gains_sum = jnp.sum(small_sum[:, :conv_start], axis=0)
    else:
        input_grad, attn_gain_grad = last_rows(*last_ins, (), lines)
        small_sum, attn_sum, output_sum, ups_sum, downward_sum = (
            scatter_grads(block)
            for block in (
                small_blocks(attn_gain_grad), attn_grads[..., :gates_end], output_grad, ups_blocks, downward_blocks
            )
        )
        small_sum = small_sum.reshape(MATES, SMALL * 128)
        gains_sum = jnp.sum(small_sum[:, :conv_start], axis=0)
        gains_sum = gains_sum + other_core(gains_sum)
        streams_sum = (
            attn_sum[:, :, :streams_end]
            .reshape(MATES, depth, heads, 3, head_size)
            .transpose(3, 1, 0, 2, 4)
            .reshape(3, depth, MATES * width)
        )
        grads = (
            streams_sum[0],
            streams_sum[1],
            streams_sum[2],
            join_columns(attn_sum[:, :, streams_end:gates_end]),
            join_columns(output_sum).T,
            join_columns(ups_sum[:, :, :units]),
            join_columns(ups_sum[:, :, units:]),
            join_columns(downward_sum).T,
        )
    conv_sum = small_sum[:, conv_start : conv_start + conv_size]
    beta_sum = small_sum[:, beta_start:small_size].reshape(MATES * heads, depth).T
    return (
        block_output,
        input_grad,
        gains_sum[:depth],
        *grads[:4],
        beta_sum,
        conv_sum.reshape(MATES * heads, 3, CONV, gain_part),
        gains_sum[2 * depth : 2 * depth + gain_part],
        grads[4],
        gains_sum[depth : 2 * depth],
        *grads[5:],
    )


def solution(mesh):
    return jax.shard_map(
        on_device,
        mesh=mesh,
        in_specs=(
            P(None, "seq", None),
            P(),
            P("seq"),
            P("seq", "tp"),
            P("seq", "tp"),
            P("seq", "tp"),
            P("seq", "tp"),
            P("seq", "tp"),
            P("tp", None, None, "seq"),
            P("seq"),
            P("tp", "seq"),
            P("seq"),
            P("seq", "tp"),
            P("seq", "tp"),
            P("tp", "seq"),
            P(None, "seq", None),
        ),
        out_specs=(
            P(None, "seq", None),
            P(None, "seq", None),
            P("seq"),
            P("seq", "tp"),
            P("seq", "tp"),
            P("seq", "tp"),
            P("seq", "tp"),
            P("seq", "tp"),
            P("tp", None, None, "seq"),
            P("seq"),
            P("tp", "seq"),
            P("seq"),
            P("seq", "tp"),
            P("seq", "tp"),
            P("tp", "seq"),
        ),
        check_vma=False,
    )
```

```python
import functools

import jax
import jax.numpy as jnp
from jax import lax
from jax.experimental import pallas as pl
from jax.experimental.pallas import tpu as pltpu
from jax.sharding import PartitionSpec as P

CONV = 4
MATES = 4
SMALL = 16
CONV_ROW = 3
BETA_ROW = 5


epsilon = 1e-06
low = jnp.bfloat16
wide = jnp.float32


def other_core(value):
    return lax.ppermute(value, "tp", [(0, 1), (1, 0)])


def to_mate(value, flip):
    count = lax.axis_size("seq")
    return lax.ppermute(value, "seq", [(source, source ^ flip) for source in range(count)])


def mate_of():
    return lax.axis_index("seq") % MATES


def line_of():
    return lax.axis_index("seq") // MATES


def line_groups():
    lines = lax.axis_size("seq") // MATES
    return [[mate + MATES * line for line in range(lines)] for mate in range(MATES)]


def pick(blocks, index):
    return lax.dynamic_index_in_dim(blocks, index, 0, False)


def in_order(by_flip):
    mate = mate_of()
    out = jnp.zeros((MATES,) + by_flip[0].shape, by_flip[0].dtype)
    for flip, piece in enumerate(by_flip):
        out = lax.dynamic_update_index_in_dim(out, piece, mate ^ flip, 0)
    return out


def swap_blocks(blocks):
    mate = mate_of()
    pieces = [pick(blocks, mate)]
    for flip in range(1, MATES):
        pieces.append(to_mate(pick(blocks, mate ^ flip), flip))
    return in_order(pieces)


def gather_lines(block):
    return lax.all_gather(block, "seq", axis_index_groups=line_groups())


def scatter_lines(blocks):
    return lax.psum_scatter(blocks, "seq", scatter_dimension=0, axis_index_groups=line_groups())


def matmul(form, left, right):
    return jnp.einsum(form, left, right, preferred_element_type=wide)


CHUNK = 128
TOGETHER = 4
VMEM_BYTES = 60 * 1024 * 1024
NN = (((1,), (0,)), ((), ()))
NT = (((1,), (1,)), ((), ()))


def dot(left, right, dims):
    return lax.dot_general(left, right, dims, preferred_element_type=wide)


def pair(value):
    high = value.astype(low)
    return high, (value - high.astype(wide)).astype(low)


def side(left, right):
    return jnp.concatenate([left, right], axis=1)


def over(top, bottom):
    return jnp.concatenate([top, bottom], axis=0)


def nn(left, right):
    width = right[0].shape[1]
    both = side(*right)
    out = dot(side(*left), over(both, both), NN)
    return out[:, :width] + out[:, width:]


def nt(left, right):
    width = right[0].shape[0]
    out = dot(side(*left), over(side(right[0], right[0]), side(right[1], right[1])), NT)
    return out[:, :width] + out[:, width:]


def nn_wide(left, right):
    return dot(side(*left), over(right[0], right[0]), NN) + dot(left[0], right[1], NN)


def nn_low(left, right):
    return dot(side(*left), over(right, right), NN)


def low_nn(left, right):
    return dot(side(left, left), over(*right), NN)


def low_nt(left, right):
    return dot(side(left, left), side(*right), NT)


def grid_of_rows():
    rows = lax.broadcasted_iota(jnp.int32, (CHUNK, CHUNK), 0)
    columns = lax.broadcasted_iota(jnp.int32, (CHUNK, CHUNK), 1)
    return rows, columns


def inverse_of(strict):
    rows, columns = grid_of_rows()
    one = jnp.where(rows == columns, 1.0, 0.0).astype(wide)

    def joining(shift):
        upper = columns >> shift
        return ((rows >> shift) == upper + 1) & ((upper & 1) == 0)

    solved = [one - jnp.where(joining(0), s, 0.0) for s in strict]
    shift = 1
    while (1 << shift) < CHUNK:
        mask = joining(shift)
        pairs = [pair(d) for d in solved]
        crossed = [nn(pair(jnp.where(mask, s, 0.0)), p) for s, p in zip(strict, pairs)]
        solved = [d - nn(p, pair(c)) for d, p, c in zip(solved, pairs, crossed)]
        shift += 1
    return solved


def convolved(block, taps, stream):
    columns = block[:, stream * CHUNK : (stream + 1) * CHUNK]
    total = None
    for offset in range(CONV):
        first = 16 - (CONV - 1) + offset
        term = taps[stream * CONV + offset][None, :] * columns[first : first + CHUNK]
        total = term if total is None else total + term
    return total


def silu_parts(value):
    squash = jax.nn.sigmoid(value)
    return value * squash, squash * (1.0 + value * (1.0 - squash))


def live_rows(limit, start):
    rows = lax.broadcasted_iota(jnp.int32, (CHUNK, CHUNK), 0)
    return jnp.where(rows + start < limit, 1.0, 0.0).astype(wide)


def head_squash(logits, head):
    lanes = lax.broadcasted_iota(jnp.int32, logits.shape, 1)
    column = jnp.sum(jnp.where(lanes == BETA_ROW + head, logits, 0.0), axis=1, keepdims=True)
    return jax.nn.sigmoid(jnp.broadcast_to(column, logits.shape))


def front_kernel(
    lines, heads, moves, limit_ref, raw_any, raw_ref, taps_ref, logit_ref, gate_ref, scale_ref, *rest,
):
    count = len(moves)
    outs = rest[count:]
    qkv_ref, solved_ref, wu_ref, map_ref, total_ref, tails_ref = outs[:6]
    state_ref, fresh_ref, mixed_ref, gated_ref, gathered, weights = outs[6:12]
    targets, scratch = outs[12 : 12 + count], outs[12 + count :]
    ext, offsets, maps, prefixes, locals_, wus, qkvs, enters, leaves, tails = scratch[:10]
    tail_sems, state_sems, gateds = scratch[10:13]
    scratch = scratch[13:]
    step = pl.program_id(0)
    chains, chunks = maps.shape[0], maps.shape[1]
    span = chunks * CHUNK
    head_size = CHUNK
    streams = 3 * heads * head_size
    place = Place()
    tokens = gathered.shape[2]
    share = ShareRows(place, targets[0], weights, scratch[:3])
    swap = SwapBlocks(
        place,
        lambda slot, mate: gateds.at[slot, pl.ds(pl.multiple_of(mate * tokens, 16), tokens)],
        gathered,
        scratch[3:6],
    )
    gathers = [
        GatherLines(place, None, target, scratch[6 + 6 * index : 12 + 6 * index], moves[index])
        for index, target in enumerate(targets)
        if moves[index]
    ]
    below, above = place.line > 0, place.line < lines - 1
    rows, columns = grid_of_rows()
    identity = jnp.where(rows == columns, 1.0, 0.0).astype(wide)

    def tail(seq):
        return pltpu.make_async_remote_copy(
            src_ref=raw_any.at[pl.ds((seq + 1) * span - 16, 16), pl.ds(0, streams)],
            dst_ref=tails.at[seq],
            send_sem=tail_sems.at[0, seq],
            recv_sem=tail_sems.at[1, seq],
            device_id=place.lines_away(1),
            device_id_type=MESH,
        )

    state_copy = pltpu.make_async_remote_copy(
        src_ref=leaves,
        dst_ref=enters,
        send_sem=state_sems.at[0],
        recv_sem=state_sems.at[1],
        device_id=place.lines_away(1),
        device_id_type=MESH,
    )
    seqs = chains // heads

    @pl.when(step == 0)
    def _():
        meet(place, lines=lines, cores=True)
        for seq in range(seqs):
            pl.when(above)(tail(seq).start)
        for gather in gathers:
            gather.leave(False)
        share.begin_half(False)
        share.begin_half(True)
        share.begin_rest()
        for seq in range(seqs):

            @pl.when(below)
            def _(seq=seq):
                tail(seq).wait_recv()

            @pl.when(place.line == 0)
            def _(seq=seq):
                tails[seq] = jnp.zeros(tails.shape[1:], low)

        tails_ref[...] = tails[...]

    def form(chain):
        seq, head = chain // heads, chain % heads
        ext[:16] = tails[seq, :, pl.ds(pl.multiple_of(head * 3 * head_size, 128), 3 * head_size)].astype(wide)
        ext[16:] = raw_ref[...].astype(wide)
        taps = taps_ref[0]
        limit = limit_ref[seq]

        def group(index, carry):
            first = index * TOGETHER
            parts = []
            for number in range(TOGETHER):
                start = pl.multiple_of((first + number) * CHUNK, CHUNK)
                block = ext[pl.ds(start, CHUNK + 16)]
                query = jax.nn.silu(convolved(block, taps, 0))
                key = jax.nn.silu(convolved(block, taps, 1))
                value = jax.nn.silu(convolved(block, taps, 2)).astype(low)
                query = query * lax.rsqrt(jnp.sum(query * query, axis=1, keepdims=True) + epsilon)
                query = (query * head_size ** (-0.5)).astype(low)
                key = key * lax.rsqrt(jnp.sum(key * key, axis=1, keepdims=True) + epsilon)
                key = key.astype(low)
                beta = head_squash(logit_ref[pl.ds(start, CHUNK)], head) * live_rows(limit, start)
                together = jnp.concatenate([query, key, value], axis=1)
                qkv_ref[pl.ds(start, CHUNK)] = together
                qkvs[chain, pl.ds(start, CHUNK)] = together
                parts.append((key, value, beta))
            strict = [
                jnp.where(rows > columns, beta * dot(key, key, NT), 0.0) for key, _, beta in parts
            ]
            solved = inverse_of(strict)
            for number in range(TOGETHER):
                key, value, beta = parts[number]
                solved_ref[0, first + number] = solved[number]
                weighted = pair(solved[number] * beta.T)
                both = nn_low(weighted, side(key, value))
                wu_ref[0, first + number] = both
                wus[chain, first + number] = both
                moved = low_nn(key.T, pair(both))
                step_map = identity - moved[:, :head_size]
                map_ref[0, first + number] = step_map
                maps[chain, first + number] = step_map
                offsets[chain, first + number] = moved[:, head_size:]
            return carry

        lax.fori_loop(0, chunks // TOGETHER, group, 0)

    @pl.when(step < chains)
    def _():
        form(step)

    @pl.when(step == chains - 2)
    def _():
        for gather in gathers:
            gather.onwards(1)

    @pl.when(step == chains - 1)
    def _():
        start = side(identity, jnp.zeros_like(identity))

        def advance(chunk, states):
            out = []
            for index in range(chains):
                state = states[index]
                prefixes[index, chunk] = state[:, :head_size]
                locals_[index, chunk] = state[:, head_size:]
                moved = nn_wide(pair(maps[index, chunk]), pair(state))
                out.append(
                    side(moved[:, :head_size], moved[:, head_size:] + offsets[index, chunk])
                )
            return tuple(out)

        ends = lax.fori_loop(0, chunks, advance, (start,) * chains)

        @pl.when(below)
        def _():
            state_copy.wait_recv()

        @pl.when(place.line == 0)
        def _():
            enters[...] = jnp.zeros_like(enters)

        for index in range(chains):
            total_ref[index] = ends[index][:, :head_size]
            leaving = nn_low(pair(ends[index][:, :head_size]), enters[index])
            leaves[index] = (leaving + ends[index][:, head_size:]).astype(low)
        pl.when(above)(state_copy.start)
        share.forward()

    def outputs(chain):
        enter = enters[chain]
        scale = scale_ref[...]

        def group(index, carry):
            for number in range(TOGETHER):
                chunk = index * TOGETHER + number
                start = pl.multiple_of(chunk * CHUNK, CHUNK)
                here = pl.ds(start, CHUNK)
                state = nn_low(pair(prefixes[chain, chunk]), enter) + locals_[chain, chunk]
                state_ref[0, chunk] = state
                states = pair(state)
                both = wus[chain, chunk]
                fresh = both[:, head_size:] - nn(pair(both[:, :head_size]), states)
                fresh_ref[0, chunk] = fresh
                query = qkvs[chain, here, :head_size]
                key = qkvs[chain, here, head_size : 2 * head_size]
                scores = jnp.where(rows >= columns, dot(query, key, NT), 0.0)
                mixed = low_nn(query, states) + nn(pair(scores), pair(fresh))
                mixed_ref[here] = mixed
                inverse = lax.rsqrt(jnp.mean(mixed * mixed, axis=1, keepdims=True) + epsilon)
                normed = mixed * inverse * scale
                gated = (normed * jax.nn.silu(gate_ref[here].astype(wide))).astype(low)
                gated_ref[here] = gated
                lanes = pl.ds(pl.multiple_of(chain % heads * head_size, 128), head_size)
                gateds[chain // heads, here, lanes] = gated
            return carry

        lax.fori_loop(0, chunks // TOGETHER, group, 0)

    @pl.when(step >= chains)
    def _():
        outputs(step - chains)

    @pl.when(step == chains + heads - 1)
    def _():
        swap.begin(0)
        share.forward_far()
        for gather in gathers:
            gather.onwards(2)

    @pl.when(step == 2 * chains - 1)
    def _():
        swap.begin(1)
        for gather in gathers:
            for number in range(3, lines):
                gather.onwards(number)
        for gather in gathers:
            gather.finish_lines()
        share.finish()
        swap.finish()
        for seq in range(seqs):
            pl.when(above)(tail(seq).wait_send)
        pl.when(above)(state_copy.wait_send)


def back_kernel(
    lines, heads, parts, limit_ref, raw_ref, tails_ref, taps_ref, logit_ref, gate_ref, scale_ref, qkv_ref,
    wu_ref, map_ref, total_ref, grad_ref, mixed_ref, solved_ref, state_ref, fresh_in_ref, row_grad, mlp_partial,
    middle_ref, *rest,
):
    count = len(parts)
    blocks, rest = rest[:count], rest[count:]
    all_ref, gain_ref, taps_grad_ref, row_grads, block_output = rest[:5]
    results, scratch = rest[5 : 5 + count], rest[5 + count :]
    ext, pre_grads, maps, sources, out_grads, fresh_grads, leaving, leaves, enters = scratch[:9]
    halos, edges, returned, halo_sems, state_sems = scratch[9:14]
    share_scratch, scratch = scratch[14:17], scratch[17:]
    low_output, out_sems = scratch[0], scratch[1:4]
    outs_scratch, scratch = scratch[4:11], scratch[11:]
    step = pl.program_id(0)
    chains, chunks = maps.shape[0], maps.shape[1]
    span = chunks * CHUNK
    head_size = CHUNK
    streams = 3 * heads * head_size
    place = Place()
    sums = [
        SumLines(place, blocks[index], results[index], scratch[7 * index : 7 * index + 7], first)
        for index, (first, _) in enumerate(parts)
    ]
    share = ShareRows(place, row_grad, row_grads, share_scratch)
    outs = SumRows(place, mlp_partial, outs_scratch)
    to_sibling = sender(out_sems[:2])(
        0, low_output, block_output.at[place.core], place.sibling
    )
    to_self = pltpu.make_async_copy(low_output, block_output.at[place.core], out_sems[2].at[0])
    below, above = place.line > 0, place.line < lines - 1
    rows, columns = grid_of_rows()

    def halo(chain):
        return pltpu.make_async_remote_copy(
            src_ref=halos.at[chain],
            dst_ref=returned.at[chain],
            send_sem=halo_sems.at[0, chain],
            recv_sem=halo_sems.at[1, chain],
            device_id=place.lines_away(-1),
            device_id_type=MESH,
        )

    state_copy = pltpu.make_async_remote_copy(
        src_ref=enters,
        dst_ref=leaves,
        send_sem=state_sems.at[0],
        recv_sem=state_sems.at[1],
        device_id=place.lines_away(-1),
        device_id_type=MESH,
    )

    @pl.when(step == 0)
    def _():
        meet(place, far=bool(parts), lines=lines)
        share.begin_half(False)
        share.begin_half(True)
        share.begin_rest()
        outs.begin()
        for each in sums:
            each.begin()
        for each in sums:
            each.wait_loads()
            each.round(1)

    def turn(chain):
        scale = scale_ref[...]

        def group(index, gain):
            for number in range(TOGETHER):
                chunk = index * TOGETHER + number
                start = pl.multiple_of(chunk * CHUNK, CHUNK)
                here = pl.ds(start, CHUNK)
                grad, mixed = grad_ref[here].astype(wide), mixed_ref[here]
                silu_gate, slope = silu_parts(gate_ref[here].astype(wide))
                inverse = lax.rsqrt(jnp.mean(mixed * mixed, axis=1, keepdims=True) + epsilon)
                unit = mixed * inverse
                gate_grad = (grad * unit * scale * slope).astype(low)
                there = pl.ds(pl.multiple_of(chain // heads * span + start, CHUNK), CHUNK)
                lanes = pl.ds(pl.multiple_of(streams + chain % heads * head_size, 128), head_size)
                all_ref[there, lanes] = gate_grad
                passed = grad * silu_gate
                gain = gain + jnp.sum(passed * unit, axis=0, keepdims=True)
                scaled = passed * scale
                mixed_grad = inverse * (
                    scaled - unit * inverse * jnp.mean(scaled * mixed, axis=1, keepdims=True)
                )
                out_grads[chain, chunk] = mixed_grad
                query, key = qkv_ref[here, :head_size], qkv_ref[here, head_size : 2 * head_size]
                scores = jnp.where(rows >= columns, dot(query, key, NT), 0.0)
                turned = jnp.where(rows <= columns, dot(key, query, NT), 0.0)
                grads = pair(mixed_grad)
                fresh_grads[chain, chunk] = nn(pair(turned), grads)
                reading = query.astype(wide) - nn(
                    pair(scores), pair(wu_ref[0, chunk, :, :head_size])
                )
                sources[chain, chunk] = nn(pair(mixed_grad.T), pair(reading))
                maps[chain, chunk] = map_ref[0, chunk]
            return gain

        gain = lax.fori_loop(0, chunks // TOGETHER, group, jnp.zeros((1, head_size), wide))
        gain_ref[0] = jnp.broadcast_to(gain, (8, head_size))

    @pl.when(step == 1)
    def _():
        outs.send_far()

    @pl.when(step == 2)
    def _():
        outs.send_near()

    @pl.when(step < chains)
    def _():
        turn(step)

    @pl.when(step == chains - 1)
    def _():
        def advance(number, states):
            chunk = chunks - 1 - number
            return tuple(
                nn(pair(states[index]), pair(maps[index, chunk])) + sources[index, chunk]
                for index in range(chains)
            )

        ends = lax.fori_loop(
            0, chunks, advance, (jnp.zeros((head_size, head_size), wide),) * chains
        )

        @pl.when(above)
        def _():
            state_copy.wait_recv()

        @pl.when(place.line == lines - 1)
        def _():
            leaves[...] = jnp.zeros_like(leaves)

        for index in range(chains):
            entering = low_nn(leaves[index], pair(total_ref[index]))
            enters[index] = (entering + ends[index]).astype(low)
        pl.when(below)(state_copy.start)

        def again(number, states):
            chunk = chunks - 1 - number
            out = []
            for index in range(chains):
                leaving[index, chunk] = states[index]
                out.append(
                    nn(pair(states[index]), pair(maps[index, chunk])) + sources[index, chunk]
                )
            return tuple(out)

        lax.fori_loop(
            0, chunks, again, tuple(leaves[index].astype(wide) for index in range(chains))
        )
        for each in sums:
            each.round(2)

    def unwind(chain):
        seq, head = chain // heads, chain % heads
        ext[:16] = tails_ref[seq, :, pl.ds(pl.multiple_of(head * 3 * head_size, 128), 3 * head_size)].astype(wide)
        ext[16:] = raw_ref[...].astype(wide)
        taps = taps_ref[0]
        limit = limit_ref[seq]
        pre_grads[:16] = jnp.zeros((16, 3 * head_size), wide)
        pre_grads[span + 16 :] = jnp.zeros((16, 3 * head_size), wide)

        def one(chunk):
            start = pl.multiple_of(chunk * CHUNK, CHUNK)
            here = pl.ds(start, CHUNK)
            query = qkv_ref[here, :head_size]
            key = qkv_ref[here, head_size : 2 * head_size]
            value = qkv_ref[here, 2 * head_size :]
            live = live_rows(limit, start)
            squash = head_squash(logit_ref[here], head)
            beta = squash * live
            grads = pair(out_grads[chain, chunk])
            fresh = pair(fresh_in_ref[0, chunk])
            state = pair(state_ref[0, chunk])
            leave = pair(leaving[chain, chunk])
            both = wu_ref[0, chunk]
            fresh_grad = fresh_grads[chain, chunk] + low_nt(key, leave)
            fresh_pair = pair(fresh_grad)
            score_grad = jnp.where(rows >= columns, nt(grads, fresh), 0.0)
            turned_grad = jnp.where(rows <= columns, nt(fresh, grads), 0.0)
            query_grad = nt(grads, state) + nn_low(pair(score_grad), key)
            key_grad = nn_low(pair(turned_grad), query) + nn(fresh, leave)
            wkey_grad = -nt(fresh_pair, state)
            right_grad = nn_wide(pair(solved_ref[0, chunk].T), pair(side(wkey_grad, fresh_grad)))
            right = pair(right_grad)
            twos = pair(both)
            found = dot(right[0], over(*twos), NT)
            system_grad = found[:, :CHUNK] + found[:, CHUNK:] + dot(right[1], twos[0], NT)
            system_grad = jnp.where(rows > columns, -system_grad, 0.0)
            gram = dot(key, key, NT)
            gram_grad = beta * system_grad
            key_grad = key_grad + nn_low(pair(gram_grad + gram_grad.T), key)
            key_right, value_right = right_grad[:, :head_size], right_grad[:, head_size:]
            key_grad = key_grad + beta * key_right
            value_grad = beta * value_right
            beta_grad = jnp.sum(
                key_right * key.astype(wide) + value_right * value.astype(wide) + system_grad * gram,
                axis=1,
                keepdims=True,
            )
            lanes = lax.broadcasted_iota(jnp.int32, (CHUNK, head_size), 1)
            logit_grad = jnp.where(
                lanes == BETA_ROW + head, beta_grad * (live * squash * (1.0 - squash)), 0.0
            ).astype(low)

            there = pl.ds(pl.multiple_of(seq * span + start, CHUNK), CHUNK)
            last_lanes = pl.ds(streams + heads * head_size, head_size)

            @pl.when(head == 0)
            def _():
                all_ref[there, last_lanes] = logit_grad

            @pl.when(head > 0)
            def _():
                all_ref[there, last_lanes] = all_ref[there, last_lanes] + logit_grad

            block = ext[pl.ds(start, CHUNK + 16)]
            grads_pre = []
            for stream, grad in enumerate((query_grad, key_grad, value_grad)):
                act, slope = silu_parts(convolved(block, taps, stream))
                if stream < 2:
                    inverse = lax.rsqrt(jnp.sum(act * act, axis=1, keepdims=True) + epsilon)
                    inner = jnp.sum(act * grad, axis=1, keepdims=True)
                    grad = inverse * (grad - act * (inverse * inverse * inner))
                    if stream == 0:
                        grad = grad * head_size ** (-0.5)
                grads_pre.append(grad * slope)
            pre_grads[pl.ds(start + 16, CHUNK)] = jnp.concatenate(grads_pre, axis=1)

        def group(index, carry):
            for number in range(2):
                one(index * 2 + number)
            return carry

        lax.fori_loop(0, chunks // 2, group, 0)

        def back(block):
            parts = []
            for stream in range(3):
                part = block[:, stream * head_size : (stream + 1) * head_size]
                total = None
                for offset in range(CONV):
                    first = CONV - 1 - offset
                    term = taps[stream * CONV + offset][None, :] * part[first : first + CHUNK]
                    total = term if total is None else total + term
                parts.append(total)
            return jnp.concatenate(parts, axis=1)

        lanes = pl.ds(pl.multiple_of(head * 3 * head_size, 128), 3 * head_size)

        def finish(chunk, totals):
            start = pl.multiple_of(chunk * CHUNK, CHUNK)
            block = pre_grads[pl.ds(start + 16, CHUNK + 16)]
            grad = back(block)
            there = pl.ds(pl.multiple_of(seq * span + start, CHUNK), CHUNK)
            all_ref[there, lanes] = grad.astype(low)
            edges[chain] = grad[CHUNK - 16 :]
            before = ext[pl.ds(start, CHUNK + 16)]
            pre = block[:CHUNK]
            out = []
            for offset in range(CONV):
                first = 16 - (CONV - 1) + offset
                term = jnp.sum(pre * before[first : first + CHUNK], axis=0, keepdims=True)
                out.append(totals[offset] + term)
            return tuple(out)

        zero = jnp.zeros((1, 3 * head_size), wide)
        totals = lax.fori_loop(0, chunks, finish, (zero,) * CONV)
        for offset in range(CONV):
            taps_grad_ref[0, offset : offset + 1] = totals[offset]
        halos[chain] = back(pre_grads[: CHUNK + 32])[:16].astype(low)
        pl.when(below)(halo(chain).start)

    @pl.when(step >= chains)
    def _():
        unwind(step - chains)

    @pl.when(step == chains)
    def _():
        share.forward()

    @pl.when(step == chains + 1)
    def _():
        outs.send_relayed()

    @pl.when(step == chains + 2)
    def _():
        share.forward_far()
        for each in sums:
            each.round(3)

    @pl.when(step == chains + 3)
    def _():
        outs.wait_half(False)
        outs.wait_half(True)

        def out_body(here):
            low_output[here] = (middle_ref[here] + outs.total(here)).astype(low)

        row_steps(0, low_output.shape[0], out_body)
        to_sibling.start()
        to_self.start()

    @pl.when(step == 2 * chains - 1)
    def _():
        for each in sums:
            for number in range(4, lines):
                each.round(number)
            each.exchange()
        for chain in range(chains):
            seq, head = chain // heads, chain % heads
            last = pl.ds((seq + 1) * span - 16, 16)
            lanes = pl.ds(head * 3 * head_size, 3 * head_size)

            @pl.when(above)
            def _(chain=chain, last=last, lanes=lanes):
                halo(chain).wait_recv()
                all_ref[last, lanes] = (edges[chain] + returned[chain].astype(wide)).astype(low)

        for chain in range(chains):
            pl.when(below)(halo(chain).wait_send)
        pl.when(below)(state_copy.wait_send)
        share.finish()
        outs.finish()
        to_self.wait()
        to_sibling.wait()
        for each in sums:
            each.finish()


def project_kernel(input_ref, scale_ref, weight_ref, beta_ref, normed_ref, raw_ref, logit_ref):
    value = input_ref[...].astype(wide)
    normed = (value * inverse_rms(value) * scale_ref[...]).astype(low)
    normed_ref[...] = normed
    raw_ref[...] = dot(normed, weight_ref[...], NN).astype(low)
    logit_ref[...] = dot(normed, beta_ref[...], NT)


MESH = pl.DeviceIdType.MESH
STEP = 16


class Place:
    def __init__(self):
        self.seq = lax.axis_index("seq")
        self.core = lax.axis_index("tp")
        self.mate = self.seq % MATES
        self.line = self.seq // MATES
        x, y = self.mate % 2, self.mate // 2
        self.x = 2 * y + (1 - x)
        self.y = 2 * (1 - y) + x
        self.far = 2 * (1 - y) + (1 - x)
        self.base = self.seq - self.mate

    def of(self, mate, other=0):
        return (self.base + mate, 1 - self.core if other else self.core)

    @property
    def sibling(self):
        return (self.seq, 1 - self.core)

    def lines_away(self, step):
        return (self.seq + step * MATES, self.core)


def meet(place, far=False, lines=0, cores=False, straight=False):
    barrier = pltpu.get_barrier_semaphore()
    partners = [place.of(place.x), place.of(place.y), place.sibling]
    if far or cores:
        partners.append(place.of(place.far))
    if cores:
        partners += [place.of(mate, 1) for mate in (place.x, place.y, place.far)]
    for partner in partners:
        pl.semaphore_signal(barrier, inc=1, device_id=partner, device_id_type=MESH)
    count = len(partners)
    if straight:
        for step in range(1, lines):
            line = (place.line + step) % lines
            pl.semaphore_signal(
                barrier,
                inc=1,
                device_id=(line * MATES + place.mate, place.core),
                device_id_type=MESH,
            )
        count = count + max(lines - 1, 0)
    elif lines > 1:
        below, above = place.line > 0, place.line < lines - 1

        @pl.when(below)
        def _():
            pl.semaphore_signal(
                barrier, inc=1, device_id=place.lines_away(-1), device_id_type=MESH
            )

        @pl.when(above)
        def _():
            pl.semaphore_signal(barrier, inc=1, device_id=place.lines_away(1), device_id_type=MESH)

        count = count + jnp.where(below, 1, 0) + jnp.where(above, 1, 0)
    pl.semaphore_wait(barrier, count)


def sender(sems):
    send, receive = sems

    def make(index, source, target, device):
        return pltpu.make_async_remote_copy(
            src_ref=source,
            dst_ref=target,
            send_sem=send.at[index],
            recv_sem=receive.at[index],
            device_id=device,
            device_id_type=MESH,
        )

    return make


def row_steps(first, last, body):
    def one(step, carry):
        body(pl.ds(pl.multiple_of(first + step * STEP, STEP), STEP))
        return carry

    lax.fori_loop(0, (last - first) // STEP, one, 0)


class SumRows:
    @staticmethod
    def scratch(rows, columns, computed=False):
        return [
            pltpu.VMEM((MATES, rows, columns), low),
            pltpu.VMEM((MATES, rows, columns), low),
            pltpu.VMEM((2, rows // 2, columns), low),
            pltpu.VMEM((2, rows, columns), low),
            pltpu.SemaphoreType.DMA((MATES,)),
            pltpu.SemaphoreType.DMA((10,)),
            pltpu.SemaphoreType.DMA((10,)),
        ] + [pltpu.VMEM((MATES, rows, columns), low)] * computed

    def __init__(self, place, partial, scratch, compute=None):
        self.place, self.partial, self.compute = place, partial, compute
        self.own, self.swapped, self.relay, self.arrived, self.local_sems, send, receive = scratch[:7]
        if compute:
            self.other = scratch[7]
        self.make = sender((send, receive))
        self.rows = self.own.shape[1]
        self.order = [place.far, place.x, place.y, place.mate]
        half, x, y = self.rows // 2, place.of(place.x), place.of(place.y)
        own, relay, arrived = self.own, self.relay, self.arrived
        self.far_low = self.make(4, own.at[0, :half], relay.at[0], y)
        self.far_high = self.make(5, own.at[0, half:], relay.at[1], x)
        self.x_high = self.make(6, own.at[1, half:], arrived.at[0, half:], x)
        self.y_low = self.make(7, own.at[2, :half], arrived.at[1, :half], y)
        self.x_low = self.make(8, own.at[1, :half], arrived.at[0, :half], x)
        self.y_high = self.make(9, own.at[2, half:], arrived.at[1, half:], y)
        self.swaps = [
            self.make(
                slot,
                self.other.at[slot] if compute else partial.at[1, mate],
                self.swapped.at[slot],
                place.sibling,
            )
            for slot, mate in enumerate(self.order)
        ]

    def load(self, slot):
        return pltpu.make_async_copy(
            self.partial.at[0, self.order[slot]], self.own.at[slot], self.local_sems.at[slot]
        )

    def begin(self):
        for slot, mate in enumerate(self.order):
            if self.compute:
                self.compute(1, mate, self.other, slot)
            else:
                self.load(slot).start()
            self.swaps[slot].start()

    def add(self, target, target_slot, source, source_slot, first, last, shift=0):
        def body(here):
            there = pl.ds(pl.multiple_of(here.start - shift, STEP), STEP) if shift else here
            target[target_slot, here] = (
                target[target_slot, here].astype(wide) + source[source_slot, there].astype(wide)
            ).astype(low)

        row_steps(first, last, body)

    def sum_cores(self, slot):
        if self.compute:
            self.compute(0, self.order[slot], self.own, slot)
        else:
            self.load(slot).wait()
        self.swaps[slot].wait_recv()
        self.add(self.own, slot, self.swapped, slot, 0, self.rows)

    def send_far(self):
        self.sum_cores(0)
        self.far_low.start()
        self.far_high.start()

    def send_near(self):
        self.sum_cores(1)
        self.x_high.start()
        self.sum_cores(2)
        self.y_low.start()

    def send_relayed(self):
        half = self.rows // 2
        self.far_low.wait_recv()
        self.add(self.own, 1, self.relay, 0, 0, half)
        self.x_low.start()
        self.far_high.wait_recv()
        self.add(self.own, 2, self.relay, 1, half, self.rows, shift=half)
        self.y_high.start()
        self.sum_cores(3)

    def wait_half(self, upper):
        if upper:
            self.x_high.wait_recv()
            self.y_high.wait_recv()
        else:
            self.x_low.wait_recv()
            self.y_low.wait_recv()

    def total(self, here):
        return (
            self.own[3, here].astype(wide)
            + self.arrived[0, here].astype(wide)
            + self.arrived[1, here].astype(wide)
        )

    def finish(self):
        for copy in self.swaps + [
            self.far_low, self.far_high, self.x_high, self.y_low, self.x_low, self.y_high,
        ]:
            copy.wait_send()


class ShareRows:
    @staticmethod
    def scratch():
        return [
            pltpu.SemaphoreType.DMA((1,)),
            pltpu.SemaphoreType.DMA((11,)),
            pltpu.SemaphoreType.DMA((11,)),
        ]

    def __init__(self, place, source, target, scratch):
        self.place, self.source, self.target = place, source, target
        self.local_sem, send, receive = scratch
        self.make = sender((send, receive))
        self.rows = target.shape[2]

    def copy(self, index):
        place, half = self.place, self.rows // 2
        lower, upper, whole = pl.ds(0, half), pl.ds(half, half), pl.ds(0, self.rows)
        x, y, sibling = place.of(place.x), place.of(place.y), place.sibling

        def own(rows, device, side=0):
            return self.source.at[rows], self.target.at[side, place.mate, rows], device

        def passed(mate, rows, device, side=0):
            return self.target.at[0, mate, rows], self.target.at[side, mate, rows], device

        return self.make(
            index,
            *(
                lambda: own(upper, y),
                lambda: own(upper, x),
                lambda: own(lower, x),
                lambda: own(lower, y),
                lambda: passed(place.x, lower, y),
                lambda: passed(place.y, upper, x),
                lambda: own(whole, sibling, 1),
                lambda: passed(place.x, whole, sibling, 1),
                lambda: passed(place.y, whole, sibling, 1),
                lambda: passed(place.far, lower, sibling, 1),
                lambda: passed(place.far, upper, sibling, 1),
            )[index](),
        )

    def local(self):
        return pltpu.make_async_copy(
            self.source, self.target.at[0, self.place.mate], self.local_sem.at[0]
        )

    def begin_half(self, upper):
        for index in (0, 1) if upper else (2, 3):
            self.copy(index).start()

    def begin_rest(self):
        self.local().start()
        self.copy(6).start()

    def forward(self):
        for came, then in ((2, 4), (0, 5), (1, 7), (3, 8)):
            self.copy(came).wait_recv()
            self.copy(then).start()

    def forward_far(self):
        for came, then in ((4, 9), (5, 10)):
            self.copy(came).wait_recv()
            self.copy(then).start()

    def finish(self):
        self.local().wait()
        for index in range(6, 11):
            self.copy(index).wait_recv()
        for index in range(11):
            self.copy(index).wait_send()


class GatherLines:
    @staticmethod
    def scratch(lines):
        return [
            pltpu.SemaphoreType.DMA((1,)),
            pltpu.SemaphoreType.DMA((3,)),
            pltpu.SemaphoreType.DMA((3,)),
            pltpu.SemaphoreType.DMA((lines, MATES)),
            pltpu.SemaphoreType.DMA((lines, MATES)),
            pltpu.SemaphoreType.DMA((lines, MATES)),
        ]

    def __init__(self, place, blocks, target, scratch, rows=None):
        self.place, self.blocks, self.target = place, blocks, target
        self.lines = target.shape[0]
        self.part = pl.ds(*(rows or (0, target.shape[2])))
        self.local_sem, send, receive, self.up_sem, self.down_sem, self.got = scratch
        self.make = sender((send, receive))
        self.order = [place.mate, place.x, place.y, place.far]

    def plane(self, slot):
        place, mate = self.place, self.order[slot]
        here = self.target.at[place.line, place.mate]
        if slot == 0:
            return pltpu.make_async_copy(self.blocks.at[mate], here, self.local_sem.at[0])
        return self.make(slot - 1, self.blocks.at[mate], here, place.of(mate))

    def begin(self):
        for slot in range(MATES):
            self.plane(slot).start()

    def arrive(self, slot):
        copy = self.plane(slot)
        copy.wait_recv() if slot else copy.wait()

    def hop(self, step, mate, direction):
        place = self.place
        line = place.line - step * direction
        piece = self.target.at[line, mate, self.part]
        sems = self.up_sem if direction > 0 else self.down_sem
        copy = pltpu.make_async_remote_copy(
            src_ref=piece,
            dst_ref=piece,
            send_sem=sems.at[step, mate],
            recv_sem=self.got.at[line, mate],
            device_id=place.lines_away(direction),
            device_id_type=MESH,
        )
        came = (line >= 0) & (line < self.lines)
        goes = (place.line < self.lines - 1) if direction > 0 else (place.line > 0)
        return copy, came, goes

    def leave(self, arriving=True):
        for slot, mate in enumerate(self.order):
            if arriving:
                self.arrive(slot)
            for direction in (1, -1):
                copy, _, goes = self.hop(0, mate, direction)
                pl.when(goes)(copy.start)

    def onwards(self, step):
        if step >= self.lines:
            return
        for mate in self.order:
            for direction in (1, -1):
                copy, came, goes = self.hop(step, mate, direction)
                pl.when(came)(copy.wait_recv)
                if step < self.lines - 1:
                    pl.when(came & goes)(copy.start)

    def finish_plane(self):
        for slot in range(1, MATES):
            self.plane(slot).wait_send()

    def finish_lines(self):
        for step in range(self.lines - 1):
            for mate in self.order:
                for direction in (1, -1):
                    copy, came, goes = self.hop(step, mate, direction)
                    pl.when(came & goes)(copy.wait_send)


class SwapBlocks:
    @staticmethod
    def scratch():
        return [
            pltpu.SemaphoreType.DMA((1,)),
            pltpu.SemaphoreType.DMA((2 * MATES,)),
            pltpu.SemaphoreType.DMA((2 * MATES,)),
        ]

    def __init__(self, place, piece, target, scratch):
        self.place, self.piece, self.target = place, piece, target
        self.local_sem, send, receive = scratch
        self.make = sender((send, receive))
        self.order = [place.far, place.x, place.y, place.mate]

    def copy(self, slot, index):
        place, mate = self.place, self.order[index]
        source, target = self.piece(slot, mate), self.target.at[slot, place.mate]
        if slot == 0 and index == MATES - 1:
            return pltpu.make_async_copy(source, target, self.local_sem.at[0]), True
        return self.make(slot * MATES + index, source, target, place.of(mate, slot)), False

    def begin(self, slot, index=None):
        for each in range(MATES) if index is None else (index,):
            self.copy(slot, each)[0].start()

    def finish(self):
        for slot in range(2):
            for index in range(MATES):
                self.copy(slot, index)[0].wait()


class SumLines:
    @staticmethod
    def scratch(lines, shape):
        return [
            pltpu.VMEM((lines,) + shape, low),
            pltpu.VMEM((2, max(lines - 1, 1)) + shape, low),
            pltpu.SemaphoreType.DMA((lines + 1,)),
            pltpu.SemaphoreType.DMA((2, lines, MATES)),
            pltpu.SemaphoreType.DMA((2, lines, MATES)),
            pltpu.SemaphoreType.DMA((3,)),
            pltpu.SemaphoreType.DMA((3,)),
        ]

    def __init__(self, place, blocks, result, scratch, first=0):
        self.place, self.blocks, self.result, self.first = place, blocks, result, first
        self.held, self.came, self.local_sems, self.send, self.got, send, receive = scratch
        self.lines = self.held.shape[0]
        self.make = sender((send, receive))
        self.order = [place.far, place.x, place.y, place.mate]

    def load(self, line):
        return pltpu.make_async_copy(
            self.blocks.at[
                line, :, pl.ds(self.first, self.held.shape[2]), pl.ds(0, self.held.shape[3])
            ],
            self.held.at[line],
            self.local_sems.at[line],
        )

    def begin(self):
        for line in range(self.lines):
            self.load(line).start()

    def wait_loads(self):
        for line in range(self.lines):
            self.load(line).wait()

    def put_gains(self, gains):
        lines, mates, height, lanes = self.held.shape
        top = lax.broadcasted_iota(jnp.int32, (height, lanes), 0) == 0
        for line in range(lines):
            for mate in range(mates):
                first = (line * mates + mate) * lanes
                part = jnp.broadcast_to(gains[:, first : first + lanes], (height, lanes))
                self.held[line, mate] = jnp.where(
                    top, part, self.held[line, mate].astype(wide)
                ).astype(low)

    def add_top(self, other, count):
        lines, mates, height, lanes = self.held.shape
        top = lax.broadcasted_iota(jnp.int32, (height, lanes), 0) < count
        for line in range(lines):
            for mate in range(mates):
                own = self.held[line, mate].astype(wide)
                both = own + other[line, mate].astype(wide)
                self.held[line, mate] = jnp.where(top, both, own).astype(low)

    def copy(self, turn, way, mate):
        direction = 1 - 2 * way
        line = self.place.line + direction * (self.lines - turn)
        return line, pltpu.make_async_remote_copy(
            src_ref=self.held.at[line, mate],
            dst_ref=self.came.at[way, turn - 1, mate],
            send_sem=self.send.at[way, turn, mate],
            recv_sem=self.got.at[way, turn, mate],
            device_id=self.place.lines_away(direction),
            device_id_type=MESH,
        )

    def arrival(self, turn, way, mate):
        slot = self.came.at[way, turn - 1, mate]
        return pltpu.make_async_remote_copy(
            src_ref=slot,
            dst_ref=slot,
            send_sem=self.send.at[way, turn, mate],
            recv_sem=self.got.at[way, turn, mate],
            device_id=self.place.sibling,
            device_id_type=MESH,
        )

    def sends(self, turn, way):
        line = self.place.line
        return line <= turn - 1 if way == 0 else line >= self.lines - turn

    def inner(self, way):
        return self.place.line >= 1 if way == 0 else self.place.line <= self.lines - 2

    def add(self, line, way, turn, mate):
        def body(here):
            self.held[line, mate, here] = (
                self.held[line, mate, here].astype(wide)
                + self.came[way, turn - 1, mate, here].astype(wide)
            ).astype(low)

        row_steps(0, self.held.shape[2], body)

    def round(self, turn):
        if turn >= self.lines:
            return
        for mate in self.order:
            for way in (0, 1):
                line, copy = self.copy(turn, way, mate)

                @pl.when(self.sends(turn, way))
                def _(line=line, copy=copy, way=way, mate=mate):
                    if turn > 1:

                        @pl.when(self.inner(way))
                        def _():
                            self.arrival(turn - 1, way, mate).wait_recv()
                            self.add(line, way, turn - 1, mate)

                    copy.start()

    def plane(self, index):
        place, mate = self.place, self.order[index]
        return self.make(
            index, self.held.at[place.line, mate], self.result.at[place.mate], place.of(mate)
        )

    def local(self):
        place = self.place
        return pltpu.make_async_copy(
            self.held.at[place.line, place.mate],
            self.result.at[place.mate],
            self.local_sems.at[self.lines],
        )

    def exchange(self):
        for index, mate in enumerate(self.order):
            for way in (0, 1):
                if self.lines > 1:

                    @pl.when(self.inner(way))
                    def _(way=way, mate=mate):
                        self.arrival(self.lines - 1, way, mate).wait_recv()
                        self.add(self.place.line, way, self.lines - 1, mate)

            if index < 3:
                self.plane(index).start()
            else:
                self.local().start()

    def straight(self, step):
        line = (self.place.line + step) % self.lines
        return pltpu.make_async_remote_copy(
            src_ref=self.held.at[line],
            dst_ref=self.came.at[0, step - 1],
            send_sem=self.send.at[0, step, 0],
            recv_sem=self.got.at[0, step, 0],
            device_id=(line * MATES + self.place.mate, self.place.core),
            device_id_type=MESH,
        )

    def direct(self):
        for step in range(1, self.lines):
            self.straight(step).start()

    def exchange_direct(self):
        for step in range(1, self.lines):
            self.straight(step).wait_recv()
            for mate in range(MATES):
                self.add(self.place.line, 0, step, mate)
        for index in range(3):
            self.plane(index).start()
        self.local().start()

    def finish(self, direct=False):
        self.local().wait()
        for index in range(3):
            self.plane(index).wait()
        if direct:
            for step in range(1, self.lines):
                self.straight(step).wait_send()
            return
        for turn in range(1, self.lines):
            for way in (0, 1):
                for mate in self.order:
                    _, copy = self.copy(turn, way, mate)
                    pl.when(self.sends(turn, way))(copy.wait_send)


def remote_call(body, identity, ins, outs, scratch, aliases=None):
    anywhere = pl.BlockSpec(memory_space=pl.ANY)
    held = pl.BlockSpec(memory_space=pltpu.VMEM)
    return pl.pallas_call(
        body,
        in_specs=[anywhere if kind == "any" else held for _, kind in ins],
        out_specs=[anywhere if kind == "any" else held for _, _, kind in outs],
        out_shape=[jax.ShapeDtypeStruct(shape, dtype) for shape, dtype, _ in outs],
        scratch_shapes=scratch,
        input_output_aliases=aliases or {},
        compiler_params=pltpu.CompilerParams(
            vmem_limit_bytes=VMEM_BYTES, collective_id=identity, has_side_effects=True
        ),
    )(*[array for array, _ in ins])


def inverse_rms(value):
    return lax.rsqrt(jnp.mean(value * value, axis=1, keepdims=True) + epsilon)


def norm_back_rows(grad, source, scale):
    inverse = inverse_rms(source)
    scaled = grad * scale
    unit = source * inverse
    inner = jnp.mean(scaled * source, axis=1, keepdims=True)
    return inverse * (scaled - unit * (inverse * inner)), grad * unit


def load_weights(weights, held, sems):
    return [
        pltpu.make_async_copy(weights.at[slot, mate], held.at[slot, mate], sems.at[slot, mate])
        for slot in range(2)
        for mate in range(MATES)
    ]


def middle_kernel(lines, moves, gathered, weights, input_ref, scale_ref, grad_any, *rest):
    place = Place()
    count = len(moves)
    middle_ref, turned_out, grads, acts_out, hidden_out = rest[count : count + 5]
    targets, scratch = rest[count + 5 : 2 * count + 5], rest[2 * count + 5 :]
    normed, held, weight_sems, all_normed, turned, ups, acts, hidden, out_sems, load_sems = scratch[:10]
    scratch = scratch[10:]
    share = ShareRows(place, normed, all_normed, scratch[:3])
    other = ShareRows(place, grad_any.at[place.core], grads, scratch[3:6])
    gathers = [
        GatherLines(place, None, target, scratch[6 + 6 * index : 12 + 6 * index], moves[index])
        for index, target in enumerate(targets)
        if moves[index]
    ]
    meet(place, lines=lines if gathers else 0)
    loads = load_weights(weights, held, weight_sems)
    for load in loads:
        load.start()
    other.begin_half(False)
    other.begin_half(True)
    other.begin_rest()
    for gather in gathers[:1]:
        gather.leave(False)
    _, _, all_lines, _, depth, width = held.shape
    early = moves[0][0] if gathers else depth

    def load_ups(index):
        part = (pl.ds(0, early), pl.ds(early, depth - early))[index]
        return pltpu.make_async_copy(
            targets[0].at[:, :, part], ups.at[:, :, part], load_sems.at[index]
        )

    load_ups(0).start()
    for load in loads:
        load.wait()
    rows, model_width = normed.shape
    half = rows // 2
    height = MATES * depth
    some = max(1, 512 // height)

    def product(step, carry):
        columns = pl.ds(pl.multiple_of(step * some * height, 128), some * height)
        part = pl.ds(step * some, some)
        for first in (0, half):
            total = None
            for slot in range(2):
                for mate in range(MATES):
                    term = dot(
                        gathered[slot, mate, first : first + half],
                        held[slot, mate, part].reshape(some * height, width),
                        NT,
                    )
                    total = term if total is None else total + term
            here = pl.ds(first, half)
            middle_ref[here, columns] = input_ref[here, columns].astype(wide) + total
        return carry

    def body(here):
        middle = middle_ref[here]
        normed[here] = (middle * inverse_rms(middle) * scale_ref[...]).astype(low)

    lax.fori_loop(0, all_lines // some, product, 0)
    row_steps(0, half, body)
    share.begin_half(False)
    row_steps(half, rows, body)
    share.begin_half(True)
    share.begin_rest()
    for gather in gathers[:1]:
        gather.onwards(1)
    for gather in gathers[1:]:
        gather.leave(False)
    for gather in gathers[:1]:
        gather.onwards(2)
    share.forward()
    for gather in gathers[:1]:
        for number in range(3, lines):
            gather.onwards(number)
    if early < depth:
        load_ups(1).start()
    for gather in gathers[1:]:
        gather.onwards(1)
    other.forward()
    share.forward_far()
    share.finish()
    load_ups(0).wait()
    if early < depth:
        load_ups(1).wait()
    weight = ups[...].reshape(model_width, ups.shape[3])
    units = hidden.shape[2]
    outs = []
    for slot in range(2):
        for mate in range(MATES):
            index = slot * MATES + mate
            values = dot(all_normed[slot, mate], weight, NN)
            acts[index] = values.astype(low)
            gate, up = values[:, :units], values[:, units:]
            hidden[index] = (gate * jax.nn.sigmoid(gate) * up).astype(low)
            here = pl.ds(index * rows, rows)
            turned[:, here] = all_normed[slot, mate].T
            outs += [
                pltpu.make_async_copy(acts.at[index], acts_out.at[here], out_sems.at[0, index]),
                pltpu.make_async_copy(hidden.at[index], hidden_out.at[here], out_sems.at[1, index]),
                pltpu.make_async_copy(
                    turned.at[:, here], turned_out.at[:, here], out_sems.at[2, index]
                ),
            ]
            for out in outs[-3:]:
                out.start()
        if slot == 0:
            for gather in gathers[1:]:
                gather.onwards(2)
            other.forward_far()
    for number in range(3, lines):
        for gather in gathers[1:]:
            gather.onwards(number)
    for gather in gathers:
        gather.finish_lines()
    other.finish()
    for out in outs:
        out.wait()


def columns_in_steps(lines, depth, body):
    height = MATES * depth
    some = max(1, 512 // height)

    def one(step, carry):
        body(
            pl.ds(pl.multiple_of(step * some * height, 128), some * height),
            pl.ds(step * some, some),
            some * height,
        )
        return carry

    lax.fori_loop(0, lines // some, one, 0)


class Tiles:
    def __init__(self, source, target, held_in, held_out, sems, body):
        self.source, self.target, self.body = source, target, body
        self.held_in, self.held_out, self.sems = held_in, held_out, sems
        self.rows = held_in.shape[1]
        self.count = source.shape[0] // self.rows

    def load(self, tile):
        return pltpu.make_async_copy(
            self.source.at[pl.ds(tile * self.rows, self.rows)],
            self.held_in.at[tile % 2],
            self.sems.at[0, tile % 2],
        )

    def store(self, tile):
        return pltpu.make_async_copy(
            self.held_out.at[tile % 2],
            self.target.at[pl.ds(tile * self.rows, self.rows)],
            self.sems.at[1, tile % 2],
        )

    def begin(self):
        self.load(0).start()

    def run(self, first, last):
        for tile in range(first, last):
            self.load(tile).wait()
            if tile + 1 < self.count:
                self.load(tile + 1).start()
            if tile >= 2:
                self.store(tile - 2).wait()
            self.body(self.held_in.at[tile % 2], self.held_out.at[tile % 2])
            self.store(tile).start()

    def finish(self):
        for tile in range(max(self.count - 2, 0), self.count):
            self.store(tile).wait()


def turn_rows_kernel(
    lines, parts, acts_grad, ups_any, weights, turned, hidden, downs_any, middle_ref, grad_ref,
    scale_ref, *rest
):
    place = Place()
    count = len(parts)
    blocks, rest = rest[:count], rest[count:]
    middle_grad_ref, gain_ref, low_grad, gated_grads, ups_grad, mlp_part = rest[:6]
    results, scratch = rest[6 : 6 + count], rest[6 + count :]
    held, load_sems, sent, acts, ups, downs = scratch[:6]
    turned_in, grad_out, grad_sems, hidden_in, part_out, part_sems = scratch[6:12]
    scratch = scratch[12:]
    all_lines, _, depth, units = ups.shape
    tokens = low_grad.shape[0]

    def compute(side_of, mate, target, slot):
        first = pl.ds(pl.multiple_of((side_of * MATES + mate) * tokens, STEP), tokens)

        def step(columns, part, size):
            target[slot, :, columns] = dot(
                acts[first], ups[part].reshape(size, units), NT
            ).astype(low)

        columns_in_steps(all_lines, depth, step)

    def weight_grad(tile_in, tile_out):
        tile_out[...] = dot(tile_in[...], acts[...], NN).astype(low)

    def back_down(tile_in, tile_out):
        def step(columns, part, size):
            tile_out[:, columns] = dot(
                tile_in[...], downs[part].reshape(size, downs.shape[3]), NT
            ).astype(low)

        columns_in_steps(all_lines, depth, step)

    grad_tiles = Tiles(turned, ups_grad, turned_in, grad_out, grad_sems, weight_grad)
    part_tiles = Tiles(hidden, mlp_part, hidden_in, part_out, part_sems, back_down)
    rows = SumRows(place, None, scratch[:8], compute)
    swap = SwapBlocks(place, lambda slot, mate: sent.at[slot, mate], gated_grads, scratch[8:11])
    sums = [
        SumLines(place, blocks[index], results[index], scratch[11 + 7 * index : 18 + 7 * index], first)
        for index, (first, _) in enumerate(parts)
    ]
    meet(place, lines=lines if parts else 0, cores=True)
    for each in sums:
        each.begin()
    loads = [
        pltpu.make_async_copy(acts_grad, acts, load_sems.at[0]),
        pltpu.make_async_copy(ups_any, ups, load_sems.at[1]),
    ]
    for load in loads:
        load.start()

    def load_weight(slot):
        return pltpu.make_async_copy(weights.at[slot], held, load_sems.at[2])

    load_downs = pltpu.make_async_copy(downs_any, downs, load_sems.at[3])
    for each in sums:
        each.wait_loads()
        each.round(1)
    load_weight(0).start()
    load_downs.start()
    grad_tiles.begin()
    part_tiles.begin()
    gain_ref[...] = jnp.zeros_like(gain_ref)
    for load in loads:
        load.wait()
    rows.begin()
    rows.send_far()
    rows.send_near()
    some, all_tiles = grad_tiles.count // 4, grad_tiles.count
    grad_tiles.run(0, some)
    for each in sums:
        each.round(2)
    rows.send_relayed()
    grad_tiles.run(some, 3 * some)
    for each in sums:
        each.round(3)
    rows.wait_half(False)
    rows.wait_half(True)

    def body(here):
        part, gains = norm_back_rows(rows.total(here), middle_ref[here], scale_ref[...])
        total = grad_ref[here].astype(wide) + part
        middle_grad_ref[here] = total
        low_grad[here] = total.astype(low)
        gain_ref[...] += jnp.sum(gains, axis=0, keepdims=True)

    row_steps(0, tokens, body)
    width = held.shape[-1]
    for slot in range(2):
        load_weight(slot).wait()
        for index, mate in enumerate(swap.order):
            weight = held[mate].reshape(all_lines * MATES * depth, width)
            sent[slot, mate] = dot(low_grad[...], weight, NN).astype(low)
            swap.begin(slot, index)
        if slot == 0:
            load_weight(1).start()
    rows.finish()
    grad_tiles.run(3 * some, all_tiles)
    for each in sums:
        for number in range(4, lines):
            each.round(number)
        each.exchange()
    load_downs.wait()
    part_tiles.run(0, part_tiles.count)
    swap.finish()
    for tiles in (grad_tiles, part_tiles):
        tiles.finish()
    for each in sums:
        each.finish()


def last_rows_kernel(
    lines, pieces, heads, all_grads, attn_any, turned, beta_ref, input_ref, middle_grad_ref, scale_ref, *rest
):
    place = Place()
    blocks, rest = rest[:pieces], rest[pieces:]
    input_grad, gain_ref = rest[:2]
    count = pieces + 1 if pieces else 0
    results, scratch = rest[2 : 2 + count], rest[2 + count :]
    low_grad, grads, attn, load_sems = scratch[:4]
    all_lines, _, depth, width = attn.shape
    tokens = low_grad.shape[0]

    def compute(side_of, mate, target, slot):
        first = pl.ds(pl.multiple_of((side_of * MATES + mate) * tokens, STEP), tokens)

        def step(columns, part, size):
            total = dot(grads[first, :width], attn[part].reshape(size, width), NT)
            total = total + dot(grads[first, width:], beta_ref[:, columns], NN)
            target[slot, :, columns] = total.astype(low)

        columns_in_steps(all_lines, depth, step)

    meet(place, far=bool(pieces), lines=lines if pieces else 0, straight=True)
    rows = SumRows(place, None, scratch[4:12], compute)
    make = sender(scratch[12:14])
    scratch = scratch[14:]
    sums = [
        SumLines(
            place,
            blocks[index] if index < pieces else None,
            results[index],
            scratch[7 * index : 7 * index + 7],
        )
        for index in range(count)
    ]
    loads = [
        pltpu.make_async_copy(all_grads, grads, load_sems.at[0]),
        pltpu.make_async_copy(attn_any, attn, load_sems.at[1]),
    ]
    for load in loads:
        load.start()
    for each in sums[:pieces]:
        each.begin()
    gain_ref[...] = jnp.zeros_like(gain_ref)
    if sums:
        small, _, streams = sums
        mine, theirs, turned_in, turned_sems = scratch[7 * count :]
        lines_here = place.line * 2 < lines

        def line_of_turn(turn):
            return jnp.where(lines_here, lines - 1 - turn, turn)

        height = turned_in.shape[1]
        each_line = MATES * depth // height
        mates_each = height // depth

        def load_turned(index):
            line = line_of_turn(index // each_line)
            first = line * (MATES * depth) + index % each_line * height
            return pltpu.make_async_copy(
                turned.at[pl.ds(pl.multiple_of(first, 128), height)],
                turned_in.at[index % 2],
                turned_sems.at[index % 2],
            )

        kept = lax.broadcasted_iota(jnp.int32, (SMALL, CHUNK), 0)
        kept = (kept >= BETA_ROW) & (kept < BETA_ROW + heads)

        def weight_grads(first, last):
            for index in range(first * each_line, last * each_line):
                load_turned(index).wait()
                if index + 1 < lines * each_line:
                    load_turned(index + 1).start()
                line = line_of_turn(index // each_line)
                found = dot(turned_in[index % 2], grads[...], NN)
                for number in range(mates_each):
                    mate = index % each_line * mates_each + number
                    part = found[number * depth : (number + 1) * depth]
                    streams.held[line, mate] = part[:, :width].astype(low)
                    small.held[line, mate] = jnp.where(
                        kept, part[:, width:].T[:SMALL], small.held[line, mate].astype(wide)
                    ).astype(low)

        load_turned(0).start()
        loads[0].wait()
        small.wait_loads()
        weight_grads(0, 1)
        streams.round(1)
        sums[1].wait_loads()
        sums[1].round(1)
        weight_grads(1, 2)
    for load in loads[0 if not sums else 1 :]:
        load.wait()
    rows.begin()
    rows.send_far()
    rows.send_near()
    if sums:
        weight_grads(2, lines)
    for each in sums[1:]:
        each.round(2)
    rows.send_relayed()
    rows.wait_half(False)
    rows.wait_half(True)

    def body(here):
        part, gains = norm_back_rows(
            rows.total(here), input_ref[here].astype(wide), scale_ref[...]
        )
        low_grad[here] = (middle_grad_ref[here] + part).astype(low)
        gain_ref[...] += jnp.sum(gains, axis=0, keepdims=True)

    row_steps(0, tokens, body)
    first = make(0, low_grad, input_grad.at[place.core], place.sibling)
    first.start()
    first_local = pltpu.make_async_copy(low_grad, input_grad.at[place.core], load_sems.at[2])
    first_local.start()
    if sums:
        small.put_gains(gain_ref)
        mine[...] = small.held[...]
        swap = make(1, mine, theirs, place.sibling)
        swap.start()
        swap.wait_recv()
        small.add_top(theirs, CONV_ROW)
        small.direct()
    for each in sums[1:]:
        each.round(3)
    for each in sums[:1]:
        each.exchange_direct()
    for turn in range(4, lines):
        for each in sums[1:]:
            each.round(turn)
    for each in sums[1:]:
        each.exchange()
    rows.finish()
    first_local.wait()
    first.wait()
    if sums:
        swap.wait_send()
    for each in sums:
        each.finish(direct=each is sums[0])


def first_rows_kernel(input_ref, inputs, *scratch):
    place = Place()
    meet(place)
    share = ShareRows(place, input_ref.at[place.core], inputs, scratch)
    share.begin_half(False)
    share.begin_half(True)
    share.begin_rest()
    share.forward()
    share.forward_far()
    share.finish()


def first_rows(block_input):
    seqs, rows, columns = block_input.shape
    return remote_call(
        first_rows_kernel,
        0,
        [(block_input, "any")],
        [((seqs, MATES, rows, columns), low, "any")],
        ShareRows.scratch(),
    )[0]


def first_kernel(lines, pieces, input_ref, *rest):
    place = Place()
    blocks, rest = rest[:pieces], rest[pieces:]
    turned_out, raw_ref, logit_ref, small_ref, attn_out = rest[:5]
    others, scratch = rest[5 : 3 + pieces], rest[3 + pieces :]
    inputs, normed, turned, small, attn, scale, out_sems = scratch[:7]
    scratch = scratch[7:]
    targets = (small, attn) + tuple(others)
    meet(place, far=True, lines=lines)
    share = ShareRows(place, input_ref.at[place.core], inputs, scratch[:3])
    gathers = [
        GatherLines(place, blocks[index], targets[index], scratch[3 + 6 * index : 9 + 6 * index])
        for index in range(pieces)
    ]
    few, main, later = gathers[:3]
    for gather in (few, main):
        gather.begin()
    for gather in (few, main):
        gather.leave()
    share.begin_half(False)
    share.begin_half(True)
    share.begin_rest()
    later.begin()
    for gather in (few, main):
        gather.onwards(1)
    later.leave()
    share.forward()
    later.onwards(1)
    for gather in gathers[3:]:
        gather.begin()
    few.onwards(2)
    main.onwards(2)
    for step in range(3, lines):
        few.onwards(step)
    share.forward_far()
    later.onwards(2)
    share.finish()
    small_ref[...] = small[...]
    _, _, tokens, model_width = inputs.shape
    depth = small.shape[3]
    parts = [(line, mate) for line in range(lines) for mate in range(MATES)]
    for index, (line, mate) in enumerate(parts):
        scale[:, index * depth : (index + 1) * depth] = small[line, mate, :1].astype(wide)
    beta = jnp.concatenate([small[line, mate] for line, mate in parts], axis=1)
    beta = over(beta, jnp.zeros((CHUNK - beta.shape[0], model_width), low))
    outs = []
    for slot in range(2):
        for mate in range(MATES):
            first = (slot * MATES + mate) * tokens

            def body(here, slot=slot, mate=mate, first=first):
                value = inputs[slot, mate, here].astype(wide)
                there = pl.ds(pl.multiple_of(first + here.start, STEP), STEP)
                normed[there] = (value * inverse_rms(value) * scale[...]).astype(low)

            row_steps(0, tokens, body)
            block = pl.ds(first, tokens)
            logit_ref[block] = dot(normed[block], beta, NT)
            turned[:, block] = normed[block].T
            outs.append(
                pltpu.make_async_copy(
                    turned.at[:, block], turned_out.at[:, block], out_sems.at[slot * MATES + mate]
                )
            )
            outs[-1].start()
    for step in range(3, lines):
        main.onwards(step)
    outs.append(pltpu.make_async_copy(attn, attn_out, out_sems.at[2 * MATES]))
    outs[-1].start()
    weight = attn[...].reshape(model_width, attn.shape[3])

    def product(index, carry):
        here = pl.ds(pl.multiple_of(index * tokens, STEP), tokens)
        raw_ref[here] = dot(normed[here], weight, NN).astype(low)
        return carry

    lax.fori_loop(0, 2 * MATES, product, 0)
    for step in range(3, lines):
        later.onwards(step)
    for gather in gathers[3:]:
        for slot in range(MATES):
            gather.arrive(slot)
    for out in outs:
        out.wait()
    for gather in gathers:
        gather.finish_plane()
    for gather in gathers[:3]:
        gather.finish_lines()


def first_call(block_input, blocks, lines):
    seqs, tokens, model_width = block_input.shape
    rows = seqs * MATES * tokens
    small, attn = ((lines,) + block.shape for block in blocks[:2])
    shared = (seqs, MATES, tokens, model_width)
    return remote_call(
        functools.partial(first_kernel, lines, len(blocks)),
        0,
        [(array, "any") for array in (block_input, *blocks)],
        [
            ((model_width, rows), low, "any"),
            ((rows, attn[3]), low, "held"),
            ((rows, CHUNK), wide, "held"),
            (small, low, "held"),
            (attn, low, "any"),
        ]
        + [((lines,) + block.shape, low, "any") for block in blocks[2:]],
        [
            pltpu.VMEM(shared, low),
            pltpu.VMEM((rows, model_width), low),
            pltpu.VMEM((model_width, rows), low),
            pltpu.VMEM(small, low),
            pltpu.VMEM(attn, low),
            pltpu.VMEM((1, model_width), wide),
            pltpu.SemaphoreType.DMA((2 * MATES + 1,)),
        ]
        + ShareRows.scratch()
        + GatherLines.scratch(lines) * len(blocks),
    )


def middle_rows(gathered, weights, mine, scale, out_grad, moving, lines):
    rows, columns = mine.shape
    shared = (2, MATES, rows, columns)
    arrays = [array for array, _ in moving]
    ups, downs = arrays
    several = 2 * MATES
    return remote_call(
        functools.partial(middle_kernel, lines, tuple(part for _, part in moving)),
        1,
        [(gathered, "held"), (weights, "any"), (mine, "held"), (scale, "held"), (out_grad, "any")]
        + [(array, "any") for array in arrays],
        [
            ((rows, columns), wide, "held"),
            ((columns, several * rows), low, "any"),
            (shared, low, "any"),
            ((several * rows, ups.shape[3]), low, "any"),
            ((several * rows, downs.shape[3]), low, "any"),
        ]
        + [(array.shape, low, "any") for array in arrays],
        [
            pltpu.VMEM((rows, columns), low),
            pltpu.VMEM(weights.shape, low),
            pltpu.SemaphoreType.DMA((2, MATES)),
            pltpu.VMEM(shared, low),
            pltpu.VMEM((columns, several * rows), low),
            pltpu.VMEM(ups.shape, low),
            pltpu.VMEM((several, rows, ups.shape[3]), low),
            pltpu.VMEM((several, rows, downs.shape[3]), low),
            pltpu.SemaphoreType.DMA((3, several)),
            pltpu.SemaphoreType.DMA((2,)),
        ]
        + ShareRows.scratch() * 2
        + GatherLines.scratch(lines) * len(arrays),
        {5 + index: 5 + index for index in range(len(arrays))},
    )


def turn_rows(
    acts_grad, ups, weights, turned, hidden, downs, middle, grad, scale, summing, lines
):
    rows, columns = middle.shape
    width = weights.shape[-1]
    blocks = (2, MATES, rows, width)
    all_rows, units = hidden.shape
    scratch = [
        pltpu.VMEM(weights.shape[1:], low),
        pltpu.SemaphoreType.DMA((4,)),
        pltpu.VMEM(blocks, low),
        pltpu.VMEM(acts_grad.shape, low),
        pltpu.VMEM(ups.shape, low),
        pltpu.VMEM(downs.shape, low),
        pltpu.VMEM((2, rows, turned.shape[1]), low),
        pltpu.VMEM((2, rows, acts_grad.shape[1]), low),
        pltpu.SemaphoreType.DMA((2, 2)),
        pltpu.VMEM((2, rows, units), low),
        pltpu.VMEM((2, rows, columns), low),
        pltpu.SemaphoreType.DMA((2, 2)),
    ]
    scratch += SumRows.scratch(rows, columns, True) + SwapBlocks.scratch()
    outs = []
    for array, (_, height) in summing:
        shape = (MATES, height, array.shape[3])
        scratch += SumLines.scratch(lines, shape)
        outs.append((shape, low, "any"))
    return remote_call(
        functools.partial(turn_rows_kernel, lines, tuple(part for _, part in summing)),
        2,
        [(array, "any") for array in (acts_grad, ups, weights, turned, hidden, downs)]
        + [(array, "held") for array in (middle, grad, scale)]
        + [(array, "any") for array, _ in summing],
        [
            ((rows, columns), wide, "held"),
            ((1, columns), wide, "held"),
            ((rows, columns), low, "held"),
            (blocks, low, "any"),
            ((turned.shape[0], acts_grad.shape[1]), low, "any"),
            ((all_rows, columns), low, "any"),
        ]
        + outs,
        scratch,
    )


def last_rows(all_grads, attn, turned, beta, mine, middle_grad, scale, blocks, lines, heads):
    rows, columns = mine.shape
    scratch = [
        pltpu.VMEM((rows, columns), low),
        pltpu.VMEM(all_grads.shape, low),
        pltpu.VMEM(attn.shape, low),
        pltpu.SemaphoreType.DMA((3,)),
    ]
    scratch += SumRows.scratch(rows, columns, True) + [pltpu.SemaphoreType.DMA((2,))] * 2
    results = [block.shape[1:] for block in blocks] + [attn.shape[1:]] * bool(blocks)
    for shape in results:
        scratch += SumLines.scratch(lines, shape)
    if blocks:
        scratch += [pltpu.VMEM(blocks[0].shape, low)] * 2
        scratch += [pltpu.VMEM((2, 256, turned.shape[1]), low), pltpu.SemaphoreType.DMA((2,))]
    return remote_call(
        functools.partial(last_rows_kernel, lines, len(blocks), heads),
        3,
        [(array, "any") for array in (all_grads, attn, turned)]
        + [(array, "held") for array in (beta, mine, middle_grad, scale)]
        + [(block, "any") for block in blocks],
        [((2, rows, columns), low, "any"), ((1, columns), wide, "held")]
        + [(shape, low, "any") for shape in results],
        scratch,
    )


class Steps:
    def __init__(self, seqs, heads, span):
        self.seqs, self.heads, self.span = seqs, heads, span
        self.chains, self.chunks = seqs * heads, span // CHUNK

    def chain(self, step, when):
        if when == "first":
            return jnp.minimum(step, self.chains - 1)
        if when == "second":
            return jnp.maximum(step - self.chains, 0)
        return step % self.chains

    def rows(self, when, columns, place):
        def index(step):
            chain = self.chain(step, when)
            return chain // self.heads, place(chain % self.heads)

        return pl.BlockSpec((self.span, columns), index)

    def streams(self, when):
        return self.rows(when, 3 * CHUNK, lambda head: head)

    def head(self, when):
        return self.rows(when, CHUNK, lambda head: head)

    def gate(self, when):
        return self.rows(when, CHUNK, lambda head: 3 * self.heads + head)

    def logit(self, when):
        return self.rows(when, CHUNK, lambda head: 0)

    def taps(self, when):
        return pl.BlockSpec(
            (1, 3 * CONV, CHUNK), lambda step: (self.chain(step, when) % self.heads, 0, 0)
        )

    def blocks(self, when, columns=CHUNK):
        return pl.BlockSpec(
            (1, self.chunks, CHUNK, columns), lambda step: (self.chain(step, when), 0, 0, 0)
        )

    def few(self, when, columns):
        return pl.BlockSpec((1, 8, columns), lambda step: (self.chain(step, when), 0, 0))

    def whole(self, shape):
        return pl.BlockSpec(shape, lambda step: (0,) * len(shape), pipeline_mode=pl.Buffered(1))

    def call(self, body, identity, ins, outs, scratch, aliases=None):
        return pl.pallas_call(
            body,
            grid=(2 * self.chains,),
            in_specs=[spec for _, spec in ins],
            out_specs=[spec for _, _, spec in outs],
            out_shape=[jax.ShapeDtypeStruct(shape, dtype) for shape, dtype, _ in outs],
            scratch_shapes=scratch,
            input_output_aliases=aliases or {},
            compiler_params=pltpu.CompilerParams(
                vmem_limit_bytes=VMEM_BYTES,
                dimension_semantics=("arbitrary",),
                collective_id=identity,
                has_side_effects=True,
            ),
        )(*[array for array, _ in ins])


def delta_front(limit, raw, taps, logits, scale, moving, lines, seqs, heads, span):
    steps = Steps(seqs, heads, span)
    chains, chunks, size = steps.chains, steps.chunks, CHUNK
    squares, doubles = (chains, chunks, CHUNK, size), (chains, chunks, CHUNK, 2 * size)
    states, tails = (chains, size, size), (seqs, 16, 3 * heads * size)
    tokens = span // MATES
    anywhere = pl.BlockSpec(memory_space=pl.ANY)
    arrays = [array for array, _ in moving]
    ins = [
        (limit, pl.BlockSpec(memory_space=pltpu.SMEM)),
        (raw, anywhere),
        (raw, steps.streams("first")),
        (taps, steps.taps("first")),
        (logits, steps.logit("first")),
        (raw, steps.gate("second")),
        (scale, steps.whole((1, size))),
    ] + [(array, anywhere) for array in arrays]
    outs = [
        ((seqs * span, 3 * heads * size), low, steps.streams("first")),
        (squares, wide, steps.blocks("first")),
        (doubles, wide, steps.blocks("first", 2 * size)),
        (squares, wide, steps.blocks("first")),
        (states, wide, steps.whole(states)),
        (tails, low, steps.whole(tails)),
        (squares, wide, steps.blocks("second")),
        (squares, wide, steps.blocks("second")),
        ((seqs * span, heads * size), wide, steps.head("second")),
        ((seqs * span, heads * size), low, steps.head("second")),
        ((seqs, MATES, tokens, heads * size), low, anywhere),
        ((seqs, MATES) + arrays[0].shape, low, anywhere),
    ] + [(array.shape, low, anywhere) for array in arrays]
    scratch = [
        pltpu.VMEM((span + 16, 3 * size), wide),
        pltpu.VMEM(squares, wide),
        pltpu.VMEM(squares, wide),
        pltpu.VMEM(squares, wide),
        pltpu.VMEM(squares, wide),
        pltpu.VMEM(doubles, wide),
        pltpu.VMEM((chains, span, 3 * size), low),
        pltpu.VMEM(states, low),
        pltpu.VMEM(states, low),
        pltpu.VMEM(tails, low),
        pltpu.SemaphoreType.DMA((2, seqs)),
        pltpu.SemaphoreType.DMA((2,)),
        pltpu.VMEM((seqs, span, heads * size), low),
    ]
    scratch += ShareRows.scratch() + SwapBlocks.scratch()
    scratch += GatherLines.scratch(lines) * len(arrays)
    moves = tuple(part for _, part in moving)
    return steps.call(
        functools.partial(front_kernel, lines, heads, moves),
        4,
        ins,
        outs,
        scratch,
        {7 + index: 12 + index for index in range(len(arrays))},
    )


def delta_back(
    limit, raw, tails, taps, logits, scale, qkv, wu, maps, total, grad, mixed, solved, state, fresh,
    row_grad, mlp_partial, middle, summing, lines, seqs, heads, span,
):
    steps = Steps(seqs, heads, span)
    chains, chunks, size = steps.chains, steps.chunks, CHUNK
    squares, states = (chains, chunks, CHUNK, size), (chains, size, size)
    all_shape = (seqs * span, (4 * heads + 1) * size)
    anywhere = pl.BlockSpec(memory_space=pl.ANY)
    ins = [
        (limit, pl.BlockSpec(memory_space=pltpu.SMEM)),
        (raw, steps.streams("second")),
        (tails, steps.whole(tails.shape)),
        (taps, steps.taps("second")),
        (logits, steps.logit("second")),
        (raw, steps.gate("first")),
        (scale, steps.whole((1, size))),
        (qkv, steps.streams("both")),
        (wu, steps.blocks("both", 2 * size)),
        (maps, steps.blocks("first")),
        (total, steps.whole(states)),
        (grad, steps.head("first")),
        (mixed, steps.head("first")),
        (solved, steps.blocks("second")),
        (state, steps.blocks("second")),
        (fresh, steps.blocks("second")),
        (row_grad, anywhere),
        (mlp_partial, anywhere),
        (middle, steps.whole(middle.shape)),
    ] + [(array, anywhere) for array, _ in summing]
    outs = [
        (all_shape, low, steps.whole(all_shape)),
        ((chains, 8, size), wide, steps.few("first", size)),
        ((chains, 8, 3 * size), wide, steps.few("second", 3 * size)),
        ((seqs, MATES) + row_grad.shape, low, anywhere),
        ((seqs,) + row_grad.shape, low, anywhere),
    ]
    edges = (chains, 16, 3 * size)
    scratch = [
        pltpu.VMEM((span + 16, 3 * size), wide),
        pltpu.VMEM((span + 32, 3 * size), wide),
        pltpu.VMEM(squares, wide),
        pltpu.VMEM(squares, wide),
        pltpu.VMEM(squares, wide),
        pltpu.VMEM(squares, wide),
        pltpu.VMEM(squares, wide),
        pltpu.VMEM(states, low),
        pltpu.VMEM(states, low),
        pltpu.VMEM(edges, low),
        pltpu.VMEM(edges, wide),
        pltpu.VMEM(edges, low),
        pltpu.SemaphoreType.DMA((2, chains)),
        pltpu.SemaphoreType.DMA((2,)),
    ] + ShareRows.scratch()
    scratch += [pltpu.VMEM(row_grad.shape, low)] + [pltpu.SemaphoreType.DMA((1,))] * 3
    scratch += SumRows.scratch(*row_grad.shape)
    for array, (_, height) in summing:
        shape = (MATES, height, array.shape[3])
        scratch += SumLines.scratch(lines, shape)
        outs.append((shape, low, anywhere))
    return steps.call(
        functools.partial(back_kernel, lines, heads, tuple(part for _, part in summing)),
        5,
        ins,
        outs,
        scratch,
    )


def units_back_kernel(grad_ref, acts_ref, weight_ref, out_ref):
    units = weight_ref.shape[1]
    grad = dot(grad_ref[...], weight_ref[...], NN)
    acts = acts_ref[...].astype(wide)
    gate, up = acts[:, :units], acts[:, units:]
    silu, slope = silu_parts(gate)
    out_ref[:, :units] = (grad * up * slope).astype(low)
    out_ref[:, units:] = (grad * silu).astype(low)


def tiled_call(body, ins, wholes, outs):
    tile = 256

    def tall(shape):
        return pl.BlockSpec((tile, shape[1]), lambda step: (step, 0))

    def whole(array):
        return pl.BlockSpec(array.shape, lambda step: (0, 0), pipeline_mode=pl.Buffered(1))

    return pl.pallas_call(
        body,
        grid=(ins[0].shape[0] // tile,),
        in_specs=[tall(array.shape) for array in ins] + [whole(array) for array in wholes],
        out_specs=[tall(shape) for shape, _ in outs],
        out_shape=[jax.ShapeDtypeStruct(shape, dtype) for shape, dtype in outs],
        compiler_params=pltpu.CompilerParams(vmem_limit_bytes=VMEM_BYTES),
    )(*ins, *wholes)


def project(inputs, scale, weight, beta):
    rows, model_width = inputs.shape
    return tiled_call(
        project_kernel,
        (inputs,),
        (scale, weight, beta),
        [((rows, model_width), low), ((rows, weight.shape[1]), low), ((rows, beta.shape[0]), wide)],
    )


def held_call(body, ins, outs):
    held = pl.BlockSpec(memory_space=pltpu.VMEM)
    return pl.pallas_call(
        body,
        in_specs=[held] * len(ins),
        out_specs=[held] * len(outs),
        out_shape=[jax.ShapeDtypeStruct(shape, dtype) for shape, dtype in outs],
        compiler_params=pltpu.CompilerParams(vmem_limit_bytes=VMEM_BYTES),
    )(*ins)


def pack_kernel(
    heads, query, key, value, outgate, output, swish, upward, downward,
    attn_ref, output_ref, ups_ref, downs_ref,
):
    size = CHUNK
    width = heads * size
    units = downs_ref.shape[2]
    for mate in range(MATES):
        first = mate * width
        for head in range(heads):
            for stream, weight in enumerate((query, key, value)):
                lanes = (3 * head + stream) * size
                attn_ref[mate, :, lanes : lanes + size] = weight[
                    :, first + head * size : first + (head + 1) * size
                ].astype(low)
        attn_ref[mate, :, 3 * width : 4 * width] = outgate[:, first : first + width].astype(low)
        output_ref[mate] = output[first : first + width, :].T.astype(low)
        here = mate * units
        ups_ref[mate, :, :units] = swish[:, here : here + units].astype(low)
        ups_ref[mate, :, units:] = upward[:, here : here + units].astype(low)
        downs_ref[mate] = downward[here : here + units, :].T.astype(low)


def unpack_kernel(
    heads, attn, outs, ups, downs,
    query, key, value, outgate, output, swish, upward, downward,
):
    size = CHUNK
    width = heads * size
    units = downs.shape[2]
    for mate in range(MATES):
        first = mate * width
        for head in range(heads):
            for stream, grad in enumerate((query, key, value)):
                lanes = (3 * head + stream) * size
                grad[:, first + head * size : first + (head + 1) * size] = attn[
                    mate, :, lanes : lanes + size
                ].astype(wide)
        outgate[:, first : first + width] = attn[mate, :, 3 * width : 4 * width].astype(wide)
        output[first : first + width, :] = outs[mate].astype(wide).T
        here = mate * units
        swish[:, here : here + units] = ups[mate, :, :units].astype(wide)
        upward[:, here : here + units] = ups[mate, :, units:].astype(wide)
        downward[here : here + units, :] = downs[mate].astype(wide).T


def cut_columns(weight):
    depth, columns = weight.shape
    return weight.reshape(depth, MATES, columns // MATES).transpose(1, 0, 2)


def join_columns(blocks):
    return blocks.transpose(1, 0, 2).reshape(blocks.shape[1], -1)


def gather_weights(blocks):
    return gather_lines(swap_blocks(blocks))


def scatter_grads(blocks):
    return swap_blocks(scatter_lines(blocks.astype(low))).astype(wide)


def on_device(
    block_input,
    lengths,
    attn_gain,
    query_weight,
    key_weight,
    value_weight,
    outgate_weight,
    beta_weight,
    conv_kernel,
    head_gain,
    output_weight,
    mlp_gain,
    swish_weight,
    upward_weight,
    downward_weight,
    out_grad,
):
    count = lax.axis_size("seq")
    lines = count // MATES
    core = lax.axis_index("tp")
    seq_count, tokens, model_width = block_input.shape
    depth = attn_gain.shape[0]
    gain_part = head_gain.shape[0]
    head_size = gain_part * count
    heads = beta_weight.shape[1] // MATES
    width = heads * head_size
    units = swish_weight.shape[1] // MATES

    conv_rows = -(-heads * 3 * CONV * gain_part // CHUNK)
    near = 1 < lines <= 4 and depth == CHUNK and conv_rows == BETA_ROW - CONV_ROW
    rows = seq_count * MATES * tokens
    span = MATES * tokens

    def in_rows(array):
        return jnp.pad(array, ((0, 0), (0, -array.shape[1] % 128)))

    def gains_of(attn, mlp, head):
        return jnp.concatenate([attn, mlp, in_rows(head)], axis=1)

    gains_cut = gains_of(attn_gain[None], mlp_gain[None], head_gain[None]).astype(low)
    conv_cut = in_rows(conv_kernel.astype(low).reshape(MATES, -1))
    beta_cut = beta_weight.astype(low).reshape(depth, MATES, heads).transpose(1, 2, 0)
    small_cut = jnp.concatenate(
        [jnp.broadcast_to(gains_cut, (MATES, gains_cut.shape[1])), conv_cut], axis=1
    )
    conv_start, conv_size = gains_cut.shape[1], heads * 3 * CONV * gain_part
    beta_start = small_cut.shape[1]
    small_cut = jnp.concatenate([small_cut, beta_cut.reshape(MATES, -1)], axis=1)
    small_size = small_cut.shape[1]
    small_cut = jnp.pad(small_cut, ((0, 0), (0, SMALL * 128 - small_size)))
    small_cut = small_cut.reshape(MATES, SMALL, 128)
    streams_end, gates_end = 3 * width, 4 * width
    if near:
        cuts = held_call(
            functools.partial(pack_kernel, heads),
            (
                query_weight, key_weight, value_weight, outgate_weight, output_weight,
                swish_weight, upward_weight, downward_weight,
            ),
            [
                ((MATES, depth, columns), low)
                for columns in (gates_end, width, 2 * units, units)
            ],
        )
        normed_turned, raw, logits, small, attn_full, output_full, ups_full, downward_full = first_call(
            block_input, (small_cut, *cuts), lines
        )
        ups_split = depth // 128 * 96
        front_moves = ((output_full, None), (ups_full, (0, ups_split)))
    else:
        streams_cut = jnp.stack(
            [
                w.astype(low).reshape(depth, MATES, heads, head_size)
                for w in (query_weight, key_weight, value_weight)
            ],
            axis=3,
        )
        streams_cut = streams_cut.transpose(1, 0, 2, 3, 4).reshape(MATES, depth, streams_end)
        cuts = (
            small_cut,
            jnp.concatenate([streams_cut, cut_columns(outgate_weight.astype(low))], axis=2),
            cut_columns(output_weight.astype(low).T),
            jnp.concatenate([cut_columns(w.astype(low)) for w in (swish_weight, upward_weight)], axis=2),
            cut_columns(downward_weight.astype(low).T),
        )
        input_rows = first_rows(block_input).reshape(rows, model_width)
        small, attn_full, output_full, ups_full, downward_full = (gather_weights(cut) for cut in cuts)
        front_moves = ((output_full, None),)
    attn_blocks = attn_full
    attn_full = attn_full.reshape(model_width, gates_end)
    small = small.reshape(count, SMALL * 128)
    attn_scale = small[:, :depth].reshape(1, model_width).astype(wide)
    mlp_scale = small[:, depth : 2 * depth].reshape(1, model_width).astype(wide)
    head_scale = small[:, 2 * depth : 2 * depth + gain_part].reshape(1, head_size).astype(wide)
    taps = (
        small[:, conv_start : conv_start + conv_size]
        .reshape(count, heads, 3, CONV, gain_part)
        .transpose(1, 2, 3, 0, 4)
        .reshape(heads, 3 * CONV, head_size)
        .astype(wide)
    )
    beta_rows = (
        small[:, beta_start:small_size]
        .reshape(count, heads, depth)
        .transpose(1, 0, 2)
        .reshape(heads, model_width)
    )
    beta_rows = jnp.pad(beta_rows, ((BETA_ROW, CHUNK - BETA_ROW - heads), (0, 0)))

    mine_low = pick(block_input, core)
    grad_mine = pick(out_grad, core)
    blocked = (seq_count, MATES, tokens, model_width)
    lengths_here = jnp.stack([pick(lengths, core), pick(lengths, 1 - core)])
    limit = lengths_here - line_of() * span

    if not near:
        flat_normed, raw, logits = project(input_rows, attn_scale, attn_full, beta_rows)
        normed_turned = flat_normed.T
    sizes_of = (lines, seq_count, heads, span)
    (
        qkv, solved, wu, maps, total, tails, state, fresh, mixed, gated, gathered, output_all, *moved
    ) = delta_front(limit, raw, taps, logits, head_scale, front_moves, *sizes_of)
    middle_moves = ((ups_full, None), (downward_full, None))
    if near:
        middle_moves = ((moved[1], (ups_split, depth - ups_split)), (downward_full, (0, depth)))
    middle, mlp_turned, grad_rows, acts, hidden, ups_full, downward_blocks = middle_rows(
        gathered, output_all, mine_low, mlp_scale, out_grad, middle_moves, lines
    )
    grad_rows = grad_rows.reshape(rows, model_width)
    downward_full = downward_blocks.reshape(model_width, units)
    downward_grad = matmul("rd,rf->df", grad_rows, hidden).astype(low)
    (acts_grad,) = tiled_call(
        units_back_kernel, (grad_rows, acts), (downward_full,), [(acts.shape, low)]
    )

    def cut_rows(grad):
        return grad.reshape(lines, MATES, depth, grad.shape[1])

    downward_grad = cut_rows(downward_grad)
    turn_sums = ((downward_grad, (0, depth)),) if near else ()
    middle_grad, mlp_gain_grad, attn_grad_mine, gated_grad, ups_grad, mlp_part, *summed = turn_rows(
        acts_grad, ups_full, output_all, mlp_turned, hidden, downward_blocks, middle, grad_mine,
        mlp_scale, turn_sums, lines,
    )
    ups_grad = cut_rows(ups_grad)
    back_sums = ((ups_grad, (0, depth)),) if near else ()
    if near:
        downward_sum, = summed
    all_grads, head_gain_parts, taps_grad, attn_grad_rows, block_output, *summed = delta_back(
        limit, raw, tails, taps, logits, head_scale, qkv, wu, maps, total,
        gated_grad.reshape(rows, width), mixed, solved, state, fresh, attn_grad_mine, mlp_part.reshape(blocked), middle,
        back_sums, *sizes_of,
    )
    attn_grad_rows = attn_grad_rows.reshape(rows, model_width)
    output_grad = cut_rows(matmul("rd,rc->dc", attn_grad_rows, gated).astype(low))
    beta_grad = jnp.zeros((model_width, heads), low)
    if not near:
        attn_grads = matmul("dr,rc->dc", normed_turned, all_grads).astype(low)
        beta_grad = attn_grads[:, gates_end + BETA_ROW : gates_end + BETA_ROW + heads]
        attn_grads = cut_rows(attn_grads)

    conv_grad = (
        taps_grad[:, :CONV]
        .reshape(seq_count, heads, CONV, 3, count, gain_part)
        .sum(axis=0)
        .transpose(3, 0, 2, 1, 4)
        .reshape(count, -1)
    )

    def small_blocks(attn_gain_grad):
        gains = gains_of(
            attn_gain_grad.reshape(count, depth),
            mlp_gain_grad.reshape(count, depth),
            jnp.sum(head_gain_parts[:, 0], axis=0).reshape(count, gain_part),
        )
        beta = beta_grad.reshape(count, depth, heads).transpose(0, 2, 1).reshape(count, -1)
        flat = jnp.concatenate([gains.astype(low), in_rows(conv_grad.astype(low)), beta], axis=1)
        flat = jnp.pad(flat, ((0, 0), (0, SMALL * 128 - small_size)))
        return flat.reshape(lines, MATES, SMALL, 128)

    last_ins = (all_grads, attn_blocks, normed_turned, beta_rows, mine_low, middle_grad, attn_scale)
    if near:
        ups_sum, = summed
        blocks = (small_blocks(jnp.zeros((1, model_width), wide)), output_grad)
        input_grad, _, small_sum, output_sum, attn_sum = last_rows(*last_ins, blocks, lines, heads)
        grads = held_call(
            functools.partial(unpack_kernel, heads),
            (attn_sum, output_sum, ups_sum, downward_sum),
            [
                (w.shape, wide)
                for w in (
                    query_weight, key_weight, value_weight, outgate_weight, output_weight,
                    swish_weight, upward_weight, downward_weight,
                )
            ],
        )
        small_sum = small_sum.reshape(MATES, SMALL * 128).astype(wide)
        gains_sum = jnp.sum(small_sum[:, :conv_start], axis=0)
    else:
        input_grad, attn_gain_grad = last_rows(*last_ins, (), lines, heads)
        small_sum, attn_sum, output_sum, ups_sum, downward_sum = (
            scatter_grads(block)
            for block in (
                small_blocks(attn_gain_grad), attn_grads[..., :gates_end], output_grad, ups_grad, downward_grad
            )
        )
        small_sum = small_sum.reshape(MATES, SMALL * 128)
        gains_sum = jnp.sum(small_sum[:, :conv_start], axis=0)
        gains_sum = gains_sum + other_core(gains_sum)
        streams_sum = (
            attn_sum[:, :, :streams_end]
            .reshape(MATES, depth, heads, 3, head_size)
            .transpose(3, 1, 0, 2, 4)
            .reshape(3, depth, MATES * width)
        )
        grads = (
            streams_sum[0],
            streams_sum[1],
            streams_sum[2],
            join_columns(attn_sum[:, :, streams_end:gates_end]),
            join_columns(output_sum).T,
            join_columns(ups_sum[:, :, :units]),
            join_columns(ups_sum[:, :, units:]),
            join_columns(downward_sum).T,
        )
    conv_sum = small_sum[:, conv_start : conv_start + conv_size]
    beta_sum = small_sum[:, beta_start:small_size].reshape(MATES * heads, depth).T
    return (
        block_output,
        input_grad,
        gains_sum[:depth],
        *grads[:4],
        beta_sum,
        conv_sum.reshape(MATES * heads, 3, CONV, gain_part),
        gains_sum[2 * depth : 2 * depth + gain_part],
        grads[4],
        gains_sum[depth : 2 * depth],
        *grads[5:],
    )


def solution(mesh):
    return jax.shard_map(
        on_device,
        mesh=mesh,
        in_specs=(
            P(None, "seq", None),
            P(),
            P("seq"),
            P("seq", "tp"),
            P("seq", "tp"),
            P("seq", "tp"),
            P("seq", "tp"),
            P("seq", "tp"),
            P("tp", None, None, "seq"),
            P("seq"),
            P("tp", "seq"),
            P("seq"),
            P("seq", "tp"),
            P("seq", "tp"),
            P("tp", "seq"),
            P(None, "seq", None),
        ),
        out_specs=(
            P(None, "seq", None),
            P(None, "seq", None),
            P("seq"),
            P("seq", "tp"),
            P("seq", "tp"),
            P("seq", "tp"),
            P("seq", "tp"),
            P("seq", "tp"),
            P("tp", None, None, "seq"),
            P("seq"),
            P("tp", "seq"),
            P("seq"),
            P("seq", "tp"),
            P("seq", "tp"),
            P("tp", "seq"),
        ),
        check_vma=False,
    )
```

```python
import functools

import jax
import jax.numpy as jnp
from jax import lax
from jax.experimental import pallas as pl
from jax.experimental.pallas import tpu as pltpu
from jax.sharding import PartitionSpec as P

CONV = 4
MATES = 4
SMALL = 16
CONV_ROW = 3
BETA_ROW = 5


epsilon = 1e-06
low = jnp.bfloat16
wide = jnp.float32


def other_core(value):
    return lax.ppermute(value, "tp", [(0, 1), (1, 0)])


def to_mate(value, flip):
    count = lax.axis_size("seq")
    return lax.ppermute(value, "seq", [(source, source ^ flip) for source in range(count)])


def mate_of():
    return lax.axis_index("seq") % MATES


def line_of():
    return lax.axis_index("seq") // MATES


def line_groups():
    lines = lax.axis_size("seq") // MATES
    return [[mate + MATES * line for line in range(lines)] for mate in range(MATES)]


def pick(blocks, index):
    return lax.dynamic_index_in_dim(blocks, index, 0, False)


def in_order(by_flip):
    mate = mate_of()
    out = jnp.zeros((MATES,) + by_flip[0].shape, by_flip[0].dtype)
    for flip, piece in enumerate(by_flip):
        out = lax.dynamic_update_index_in_dim(out, piece, mate ^ flip, 0)
    return out


def swap_blocks(blocks):
    mate = mate_of()
    pieces = [pick(blocks, mate)]
    for flip in range(1, MATES):
        pieces.append(to_mate(pick(blocks, mate ^ flip), flip))
    return in_order(pieces)


def gather_lines(block):
    return lax.all_gather(block, "seq", axis_index_groups=line_groups())


def scatter_lines(blocks):
    return lax.psum_scatter(blocks, "seq", scatter_dimension=0, axis_index_groups=line_groups())


def matmul(form, left, right):
    return jnp.einsum(form, left, right, preferred_element_type=wide)


CHUNK = 128
TOGETHER = 4
VMEM_BYTES = 60 * 1024 * 1024
NN = (((1,), (0,)), ((), ()))
NT = (((1,), (1,)), ((), ()))


def dot(left, right, dims):
    return lax.dot_general(left, right, dims, preferred_element_type=wide)


def pair(value):
    high = value.astype(low)
    return high, (value - high.astype(wide)).astype(low)


def side(left, right):
    return jnp.concatenate([left, right], axis=1)


def over(top, bottom):
    return jnp.concatenate([top, bottom], axis=0)


def nn(left, right):
    width = right[0].shape[1]
    both = side(*right)
    out = dot(side(*left), over(both, both), NN)
    return out[:, :width] + out[:, width:]


def nt(left, right):
    width = right[0].shape[0]
    out = dot(side(*left), over(side(right[0], right[0]), side(right[1], right[1])), NT)
    return out[:, :width] + out[:, width:]


def nn_wide(left, right):
    return dot(side(*left), over(right[0], right[0]), NN) + dot(left[0], right[1], NN)


def nn_low(left, right):
    return dot(side(*left), over(right, right), NN)


def low_nn(left, right):
    return dot(side(left, left), over(*right), NN)


def grid_of_rows():
    rows = lax.broadcasted_iota(jnp.int32, (CHUNK, CHUNK), 0)
    columns = lax.broadcasted_iota(jnp.int32, (CHUNK, CHUNK), 1)
    return rows, columns


def inverse_of(strict):
    rows, columns = grid_of_rows()
    one = jnp.where(rows == columns, 1.0, 0.0).astype(wide)

    def joining(shift):
        upper = columns >> shift
        return ((rows >> shift) == upper + 1) & ((upper & 1) == 0)

    solved = [one - jnp.where(joining(0), s, 0.0) for s in strict]
    shift = 1
    while (1 << shift) < CHUNK:
        mask = joining(shift)
        pairs = [pair(d) for d in solved]
        crossed = [nn(pair(jnp.where(mask, s, 0.0)), p) for s, p in zip(strict, pairs)]
        solved = [d - nn(p, pair(c)) for d, p, c in zip(solved, pairs, crossed)]
        shift += 1
    return solved


def convolved(block, taps, stream):
    columns = block[:, stream * CHUNK : (stream + 1) * CHUNK]
    total = None
    for offset in range(CONV):
        first = 16 - (CONV - 1) + offset
        term = taps[stream * CONV + offset][None, :] * columns[first : first + CHUNK]
        total = term if total is None else total + term
    return total


def silu_parts(value):
    squash = jax.nn.sigmoid(value)
    return value * squash, squash * (1.0 + value * (1.0 - squash))


def live_rows(limit, start):
    rows = lax.broadcasted_iota(jnp.int32, (CHUNK, CHUNK), 0)
    return jnp.where(rows + start < limit, 1.0, 0.0).astype(wide)


def head_squash(logits, head):
    lanes = lax.broadcasted_iota(jnp.int32, logits.shape, 1)
    column = jnp.sum(jnp.where(lanes == BETA_ROW + head, logits, 0.0), axis=1, keepdims=True)
    return jax.nn.sigmoid(jnp.broadcast_to(column, logits.shape))


def front_kernel(
    lines, heads, moves, limit_ref, raw_any, raw_ref, taps_ref, logit_ref, gate_ref, scale_ref, *rest,
):
    count = len(moves)
    outs = rest[count:]
    qkv_ref, solved_ref, wu_ref, map_ref, total_ref, tails_ref = outs[:6]
    state_ref, fresh_ref, mixed_ref, gated_ref, gathered, weights = outs[6:12]
    targets, scratch = outs[12 : 12 + count], outs[12 + count :]
    ext, offsets, maps, prefixes, locals_, wus, qkvs, enters, leaves, tails = scratch[:10]
    tail_sems, state_sems, gateds = scratch[10:13]
    scratch = scratch[13:]
    step = pl.program_id(0)
    chains, chunks = maps.shape[0], maps.shape[1]
    span = chunks * CHUNK
    head_size = CHUNK
    streams = 3 * heads * head_size
    place = Place()
    tokens = gathered.shape[2]
    share = ShareRows(place, targets[0], weights, scratch[:3])
    swap = SwapBlocks(
        place,
        lambda slot, mate: gateds.at[slot, pl.ds(pl.multiple_of(mate * tokens, 16), tokens)],
        gathered,
        scratch[3:6],
    )
    gathers = [
        GatherLines(place, None, target, scratch[6 + 6 * index : 12 + 6 * index], moves[index])
        for index, target in enumerate(targets)
        if moves[index]
    ]
    below, above = place.line > 0, place.line < lines - 1
    rows, columns = grid_of_rows()
    identity = jnp.where(rows == columns, 1.0, 0.0).astype(wide)

    def tail(seq):
        return pltpu.make_async_remote_copy(
            src_ref=raw_any.at[pl.ds((seq + 1) * span - 16, 16), pl.ds(0, streams)],
            dst_ref=tails.at[seq],
            send_sem=tail_sems.at[0, seq],
            recv_sem=tail_sems.at[1, seq],
            device_id=place.lines_away(1),
            device_id_type=MESH,
        )

    def state_copy(chain):
        return pltpu.make_async_remote_copy(
            src_ref=leaves.at[chain],
            dst_ref=enters.at[chain],
            send_sem=state_sems.at[0, chain],
            recv_sem=state_sems.at[1, chain],
            device_id=place.lines_away(1),
            device_id_type=MESH,
        )

    seqs = chains // heads

    @pl.when(step == 0)
    def _():
        meet(place, lines=lines, cores=True)
        for seq in range(seqs):
            pl.when(above)(tail(seq).start)
        for gather in gathers:
            gather.leave(False)
        share.begin_half(False)
        share.begin_half(True)
        share.begin_rest()
        for seq in range(seqs):

            @pl.when(below)
            def _(seq=seq):
                tail(seq).wait_recv()

            @pl.when(place.line == 0)
            def _(seq=seq):
                tails[seq] = jnp.zeros(tails.shape[1:], low)

        tails_ref[...] = tails[...]

    def form(chain):
        seq, head = chain // heads, chain % heads
        ext[:16] = tails[seq, :, pl.ds(pl.multiple_of(head * 3 * head_size, 128), 3 * head_size)].astype(wide)
        ext[16:] = raw_ref[...].astype(wide)
        taps = taps_ref[0]
        limit = limit_ref[seq]

        def group(index, carry):
            first = index * TOGETHER
            parts = []
            for number in range(TOGETHER):
                start = pl.multiple_of((first + number) * CHUNK, CHUNK)
                block = ext[pl.ds(start, CHUNK + 16)]
                query = jax.nn.silu(convolved(block, taps, 0))
                key = jax.nn.silu(convolved(block, taps, 1))
                value = jax.nn.silu(convolved(block, taps, 2)).astype(low)
                query = query * lax.rsqrt(jnp.sum(query * query, axis=1, keepdims=True) + epsilon)
                query = (query * head_size ** (-0.5)).astype(low)
                key = key * lax.rsqrt(jnp.sum(key * key, axis=1, keepdims=True) + epsilon)
                key = key.astype(low)
                beta = head_squash(logit_ref[pl.ds(start, CHUNK)], head) * live_rows(limit, start)
                together = jnp.concatenate([query, key, value], axis=1)
                qkv_ref[pl.ds(start, CHUNK)] = together
                qkvs[chain, pl.ds(start, CHUNK)] = together
                parts.append((key, value, beta))
            strict = [
                jnp.where(rows > columns, beta * dot(key, key, NT), 0.0) for key, _, beta in parts
            ]
            solved = inverse_of(strict)
            for number in range(TOGETHER):
                key, value, beta = parts[number]
                solved_ref[0, first + number] = solved[number]
                weighted = pair(solved[number] * beta.T)
                both = nn_low(weighted, side(key, value))
                wu_ref[0, first + number] = both
                wus[chain, first + number] = both
                moved = low_nn(key.T, pair(both))
                step_map = identity - moved[:, :head_size]
                map_ref[0, first + number] = step_map
                maps[chain, first + number] = step_map
                offsets[chain, first + number] = moved[:, head_size:]
            return carry

        lax.fori_loop(0, chunks // TOGETHER, group, 0)

    @pl.when(step < chains)
    def _():
        form(step)

    @pl.when(step == chains - 2)
    def _():
        for gather in gathers:
            gather.onwards(1)

    @pl.when(step == chains - 1)
    def _():
        start = side(identity, jnp.zeros_like(identity))

        def advance(chunk, states):
            out = []
            for index in range(chains):
                state = states[index]
                prefixes[index, chunk] = state[:, :head_size]
                locals_[index, chunk] = state[:, head_size:]
                moved = nn_wide(pair(maps[index, chunk]), pair(state))
                out.append(
                    side(moved[:, :head_size], moved[:, head_size:] + offsets[index, chunk])
                )
            return tuple(out)

        ends = lax.fori_loop(0, chunks, advance, (start,) * chains)

        @pl.when(place.line == 0)
        def _():
            enters[...] = jnp.zeros_like(enters)

        for index in range(chains):
            pl.when(below)(state_copy(index).wait_recv)
            total_ref[index] = ends[index][:, :head_size]
            leaving = nn_low(pair(ends[index][:, :head_size]), enters[index])
            leaves[index] = (leaving + ends[index][:, head_size:]).astype(low)
            pl.when(above)(state_copy(index).start)
        share.forward()

    def outputs(chain):
        enter = enters[chain]
        scale = scale_ref[...]

        def group(index, carry):
            for number in range(TOGETHER):
                chunk = index * TOGETHER + number
                start = pl.multiple_of(chunk * CHUNK, CHUNK)
                here = pl.ds(start, CHUNK)
                state = nn_low(pair(prefixes[chain, chunk]), enter) + locals_[chain, chunk]
                state_ref[0, chunk] = state
                states = pair(state)
                both = wus[chain, chunk]
                fresh = both[:, head_size:] - nn(pair(both[:, :head_size]), states)
                fresh_ref[0, chunk] = fresh
                query = qkvs[chain, here, :head_size]
                key = qkvs[chain, here, head_size : 2 * head_size]
                scores = jnp.where(rows >= columns, dot(query, key, NT), 0.0)
                mixed = low_nn(query, states) + nn(pair(scores), pair(fresh))
                mixed_ref[here] = mixed
                inverse = lax.rsqrt(jnp.mean(mixed * mixed, axis=1, keepdims=True) + epsilon)
                normed = mixed * inverse * scale
                gated = (normed * jax.nn.silu(gate_ref[here].astype(wide))).astype(low)
                gated_ref[here] = gated
                lanes = pl.ds(pl.multiple_of(chain % heads * head_size, 128), head_size)
                gateds[chain // heads, here, lanes] = gated
            return carry

        lax.fori_loop(0, chunks // TOGETHER, group, 0)

    @pl.when(step >= chains)
    def _():
        outputs(step - chains)

    @pl.when(step == chains + heads - 1)
    def _():
        swap.begin(0)
        share.forward_far()
        for gather in gathers:
            gather.onwards(2)

    @pl.when(step == 2 * chains - 1)
    def _():
        swap.begin(1)
        for gather in gathers:
            for number in range(3, lines):
                gather.onwards(number)
        for gather in gathers:
            gather.finish_lines()
        share.finish()
        swap.finish()
        for seq in range(seqs):
            pl.when(above)(tail(seq).wait_send)
        for chain in range(chains):
            pl.when(above)(state_copy(chain).wait_send)


def back_kernel(
    lines, heads, parts, limit_ref, raw_ref, tails_ref, taps_ref, logit_ref, gate_ref, scale_ref, qkv_ref,
    wu_ref, map_ref, total_ref, grad_ref, mixed_ref, solved_ref, state_ref, fresh_in_ref, row_grad, mlp_partial,
    middle_ref, *rest,
):
    count = len(parts)
    blocks, rest = rest[:count], rest[count:]
    all_ref, gain_ref, taps_grad_ref, row_grads, block_output = rest[:5]
    results, scratch = rest[5 : 5 + count], rest[5 + count :]
    ext, pre_grads, maps, sources, out_grads, fresh_grads, leaving, leaves, enters = scratch[:9]
    halos, edges, returned, halo_sems, state_sems = scratch[9:14]
    share_scratch, scratch = scratch[14:17], scratch[17:]
    low_output, out_sems = scratch[0], scratch[1:4]
    outs_scratch, scratch = scratch[4:11], scratch[11:]
    step = pl.program_id(0)
    chains, chunks = maps.shape[0], maps.shape[1]
    span = chunks * CHUNK
    head_size = CHUNK
    streams = 3 * heads * head_size
    place = Place()
    sums = [
        SumLines(place, blocks[index], results[index], scratch[7 * index : 7 * index + 7], first)
        for index, (first, _) in enumerate(parts)
    ]
    share = ShareRows(place, row_grad, row_grads, share_scratch)
    outs = SumRows(place, mlp_partial, outs_scratch)
    to_sibling = sender(out_sems[:2])(
        0, low_output, block_output.at[place.core], place.sibling
    )
    to_self = pltpu.make_async_copy(low_output, block_output.at[place.core], out_sems[2].at[0])
    below, above = place.line > 0, place.line < lines - 1
    rows, columns = grid_of_rows()

    def halo(chain):
        return pltpu.make_async_remote_copy(
            src_ref=halos.at[chain],
            dst_ref=returned.at[chain],
            send_sem=halo_sems.at[0, chain],
            recv_sem=halo_sems.at[1, chain],
            device_id=place.lines_away(-1),
            device_id_type=MESH,
        )

    def state_copy(chain):
        return pltpu.make_async_remote_copy(
            src_ref=enters.at[chain],
            dst_ref=leaves.at[chain],
            send_sem=state_sems.at[0, chain],
            recv_sem=state_sems.at[1, chain],
            device_id=place.lines_away(-1),
            device_id_type=MESH,
        )

    @pl.when(step == 0)
    def _():
        meet(place, far=bool(parts), lines=lines)
        share.begin_half(False)
        share.begin_half(True)
        share.begin_rest()
        outs.begin()
        for each in sums:
            each.begin()
        for each in sums:
            each.wait_loads()
            each.round(1)

    def turn(chain):
        scale = scale_ref[...]

        def group(index, gain):
            for number in range(TOGETHER):
                chunk = index * TOGETHER + number
                start = pl.multiple_of(chunk * CHUNK, CHUNK)
                here = pl.ds(start, CHUNK)
                grad, mixed = grad_ref[here].astype(wide), mixed_ref[here]
                silu_gate, slope = silu_parts(gate_ref[here].astype(wide))
                inverse = lax.rsqrt(jnp.mean(mixed * mixed, axis=1, keepdims=True) + epsilon)
                unit = mixed * inverse
                gate_grad = (grad * unit * scale * slope).astype(low)
                there = pl.ds(pl.multiple_of(chain // heads * span + start, CHUNK), CHUNK)
                lanes = pl.ds(pl.multiple_of(streams + chain % heads * head_size, 128), head_size)
                all_ref[there, lanes] = gate_grad
                passed = grad * silu_gate
                gain = gain + jnp.sum(passed * unit, axis=0, keepdims=True)
                scaled = passed * scale
                mixed_grad = inverse * (
                    scaled - unit * inverse * jnp.mean(scaled * mixed, axis=1, keepdims=True)
                )
                out_grads[chain, chunk] = mixed_grad
                query, key = qkv_ref[here, :head_size], qkv_ref[here, head_size : 2 * head_size]
                scores = jnp.where(rows >= columns, dot(query, key, NT), 0.0)
                turned = jnp.where(rows <= columns, dot(key, query, NT), 0.0)
                fresh_grads[chain, chunk] = dot(turned.astype(low), mixed_grad.astype(low), NN)
                reading = query.astype(wide) - dot(
                    scores.astype(low), wu_ref[0, chunk, :, :head_size].astype(low), NN
                )
                sources[chain, chunk] = dot(mixed_grad.T.astype(low), reading.astype(low), NN)
                maps[chain, chunk] = map_ref[0, chunk]
            return gain

        gain = lax.fori_loop(0, chunks // TOGETHER, group, jnp.zeros((1, head_size), wide))
        gain_ref[0] = jnp.broadcast_to(gain, (8, head_size))

    @pl.when(step == 1)
    def _():
        outs.send_far()

    @pl.when(step == 2)
    def _():
        outs.send_near()

    @pl.when(step < chains)
    def _():
        turn(step)

    @pl.when(step == chains - 1)
    def _():
        def advance(number, states):
            chunk = chunks - 1 - number
            return tuple(
                nn(pair(states[index]), pair(maps[index, chunk])) + sources[index, chunk]
                for index in range(chains)
            )

        ends = lax.fori_loop(
            0, chunks, advance, (jnp.zeros((head_size, head_size), wide),) * chains
        )

        @pl.when(place.line == lines - 1)
        def _():
            leaves[...] = jnp.zeros_like(leaves)

        for index in range(chains):
            pl.when(above)(state_copy(index).wait_recv)
            entering = low_nn(leaves[index], pair(total_ref[index]))
            enters[index] = (entering + ends[index]).astype(low)
            pl.when(below)(state_copy(index).start)

        def again(number, states):
            chunk = chunks - 1 - number
            out = []
            for index in range(chains):
                leaving[index, chunk] = states[index]
                out.append(
                    nn(pair(states[index]), pair(maps[index, chunk])) + sources[index, chunk]
                )
            return tuple(out)

        lax.fori_loop(
            0, chunks, again, tuple(leaves[index].astype(wide) for index in range(chains))
        )
        for each in sums:
            each.round(2)

    def unwind(chain):
        seq, head = chain // heads, chain % heads
        ext[:16] = tails_ref[seq, :, pl.ds(pl.multiple_of(head * 3 * head_size, 128), 3 * head_size)].astype(wide)
        ext[16:] = raw_ref[...].astype(wide)
        taps = taps_ref[0]
        limit = limit_ref[seq]
        pre_grads[:16] = jnp.zeros((16, 3 * head_size), wide)
        pre_grads[span + 16 :] = jnp.zeros((16, 3 * head_size), wide)

        def one(chunk):
            start = pl.multiple_of(chunk * CHUNK, CHUNK)
            here = pl.ds(start, CHUNK)
            query = qkv_ref[here, :head_size]
            key = qkv_ref[here, head_size : 2 * head_size]
            value = qkv_ref[here, 2 * head_size :]
            live = live_rows(limit, start)
            squash = head_squash(logit_ref[here], head)
            beta = squash * live
            grads = out_grads[chain, chunk].astype(low)
            fresh = fresh_in_ref[0, chunk].astype(low)
            state = state_ref[0, chunk].astype(low)
            leave = leaving[chain, chunk].astype(low)
            both = wu_ref[0, chunk].astype(low)
            fresh_grad = fresh_grads[chain, chunk] + dot(key, leave, NT)
            score_grad = jnp.where(rows >= columns, dot(grads, fresh, NT), 0.0)
            turned_grad = jnp.where(rows <= columns, dot(fresh, grads, NT), 0.0)
            query_grad = dot(
                side(grads, score_grad.astype(low)), over(state.T, key), NN
            )
            key_grad = dot(side(turned_grad.astype(low), fresh), over(query, leave), NN)
            wkey_grad = -dot(fresh_grad.astype(low), state, NT)
            solved = solved_ref[0, chunk].T.astype(low)
            right_grad = dot(solved, side(wkey_grad, fresh_grad).astype(low), NN)
            system_grad = dot(right_grad.astype(low), both, NT)
            system_grad = jnp.where(rows > columns, -system_grad, 0.0)
            gram = dot(key, key, NT)
            gram_grad = beta * system_grad
            key_grad = key_grad + dot((gram_grad + gram_grad.T).astype(low), key, NN)
            key_right, value_right = right_grad[:, :head_size], right_grad[:, head_size:]
            key_grad = key_grad + beta * key_right
            value_grad = beta * value_right
            beta_grad = jnp.sum(
                key_right * key.astype(wide) + value_right * value.astype(wide) + system_grad * gram,
                axis=1,
                keepdims=True,
            )
            lanes = lax.broadcasted_iota(jnp.int32, (CHUNK, head_size), 1)
            logit_grad = jnp.where(
                lanes == BETA_ROW + head, beta_grad * (live * squash * (1.0 - squash)), 0.0
            ).astype(low)

            there = pl.ds(pl.multiple_of(seq * span + start, CHUNK), CHUNK)
            last_lanes = pl.ds(streams + heads * head_size, head_size)

            @pl.when(head == 0)
            def _():
                all_ref[there, last_lanes] = logit_grad

            @pl.when(head > 0)
            def _():
                all_ref[there, last_lanes] = all_ref[there, last_lanes] + logit_grad

            block = ext[pl.ds(start, CHUNK + 16)]
            grads_pre = []
            for stream, grad in enumerate((query_grad, key_grad, value_grad)):
                act, slope = silu_parts(convolved(block, taps, stream))
                if stream < 2:
                    inverse = lax.rsqrt(jnp.sum(act * act, axis=1, keepdims=True) + epsilon)
                    inner = jnp.sum(act * grad, axis=1, keepdims=True)
                    grad = inverse * (grad - act * (inverse * inverse * inner))
                    if stream == 0:
                        grad = grad * head_size ** (-0.5)
                grads_pre.append(grad * slope)
            pre_grads[pl.ds(start + 16, CHUNK)] = jnp.concatenate(grads_pre, axis=1)

        def group(index, carry):
            for number in range(TOGETHER):
                one(index * TOGETHER + number)
            return carry

        lax.fori_loop(0, chunks // TOGETHER, group, 0)

        def back(block):
            parts = []
            for stream in range(3):
                part = block[:, stream * head_size : (stream + 1) * head_size]
                total = None
                for offset in range(CONV):
                    first = CONV - 1 - offset
                    term = taps[stream * CONV + offset][None, :] * part[first : first + CHUNK]
                    total = term if total is None else total + term
                parts.append(total)
            return jnp.concatenate(parts, axis=1)

        lanes = pl.ds(pl.multiple_of(head * 3 * head_size, 128), 3 * head_size)

        def finish(chunk, totals):
            start = pl.multiple_of(chunk * CHUNK, CHUNK)
            block = pre_grads[pl.ds(start + 16, CHUNK + 16)]
            grad = back(block)
            there = pl.ds(pl.multiple_of(seq * span + start, CHUNK), CHUNK)
            all_ref[there, lanes] = grad.astype(low)
            edges[chain] = grad[CHUNK - 16 :]
            before = ext[pl.ds(start, CHUNK + 16)]
            pre = block[:CHUNK]
            out = []
            for offset in range(CONV):
                first = 16 - (CONV - 1) + offset
                term = jnp.sum(pre * before[first : first + CHUNK], axis=0, keepdims=True)
                out.append(totals[offset] + term)
            return tuple(out)

        zero = jnp.zeros((1, 3 * head_size), wide)
        totals = lax.fori_loop(0, chunks, finish, (zero,) * CONV)
        for offset in range(CONV):
            taps_grad_ref[0, offset : offset + 1] = totals[offset]
        halos[chain] = back(pre_grads[: CHUNK + 32])[:16].astype(low)
        pl.when(below)(halo(chain).start)

    @pl.when(step >= chains)
    def _():
        unwind(step - chains)

    @pl.when(step == chains)
    def _():
        share.forward()

    @pl.when(step == chains + 1)
    def _():
        outs.send_relayed()

    @pl.when(step == chains + 2)
    def _():
        share.forward_far()
        for each in sums:
            each.round(3)

    @pl.when(step == chains + 3)
    def _():
        outs.wait_half(False)
        outs.wait_half(True)

        def out_body(here):
            low_output[here] = (middle_ref[here] + outs.total(here)).astype(low)

        row_steps(0, low_output.shape[0], out_body)
        to_sibling.start()
        to_self.start()

    @pl.when(step == 2 * chains - 1)
    def _():
        for each in sums:
            for number in range(4, lines):
                each.round(number)
            each.exchange()
        for chain in range(chains):
            seq, head = chain // heads, chain % heads
            last = pl.ds((seq + 1) * span - 16, 16)
            lanes = pl.ds(head * 3 * head_size, 3 * head_size)

            @pl.when(above)
            def _(chain=chain, last=last, lanes=lanes):
                halo(chain).wait_recv()
                all_ref[last, lanes] = (edges[chain] + returned[chain].astype(wide)).astype(low)

        for chain in range(chains):
            pl.when(below)(halo(chain).wait_send)
        for chain in range(chains):
            pl.when(below)(state_copy(chain).wait_send)
        share.finish()
        outs.finish()
        to_self.wait()
        to_sibling.wait()
        for each in sums:
            each.finish()


def project_kernel(input_ref, scale_ref, weight_ref, beta_ref, normed_ref, raw_ref, logit_ref):
    value = input_ref[...].astype(wide)
    normed = (value * inverse_rms(value) * scale_ref[...]).astype(low)
    normed_ref[...] = normed
    raw_ref[...] = dot(normed, weight_ref[...], NN).astype(low)
    logit_ref[...] = dot(normed, beta_ref[...], NT)


MESH = pl.DeviceIdType.MESH
STEP = 16


class Place:
    def __init__(self):
        self.seq = lax.axis_index("seq")
        self.core = lax.axis_index("tp")
        self.mate = self.seq % MATES
        self.line = self.seq // MATES
        x, y = self.mate % 2, self.mate // 2
        self.x = 2 * y + (1 - x)
        self.y = 2 * (1 - y) + x
        self.far = 2 * (1 - y) + (1 - x)
        self.base = self.seq - self.mate

    def of(self, mate, other=0):
        return (self.base + mate, 1 - self.core if other else self.core)

    @property
    def sibling(self):
        return (self.seq, 1 - self.core)

    def lines_away(self, step):
        return (self.seq + step * MATES, self.core)


def meet(place, far=False, lines=0, cores=False, straight=False):
    barrier = pltpu.get_barrier_semaphore()
    partners = [place.of(place.x), place.of(place.y), place.sibling]
    if far or cores:
        partners.append(place.of(place.far))
    if cores:
        partners += [place.of(mate, 1) for mate in (place.x, place.y, place.far)]
    for partner in partners:
        pl.semaphore_signal(barrier, inc=1, device_id=partner, device_id_type=MESH)
    count = len(partners)
    if straight:
        for step in range(1, lines):
            line = (place.line + step) % lines
            pl.semaphore_signal(
                barrier,
                inc=1,
                device_id=(line * MATES + place.mate, place.core),
                device_id_type=MESH,
            )
        count = count + max(lines - 1, 0)
    elif lines > 1:
        below, above = place.line > 0, place.line < lines - 1

        @pl.when(below)
        def _():
            pl.semaphore_signal(
                barrier, inc=1, device_id=place.lines_away(-1), device_id_type=MESH
            )

        @pl.when(above)
        def _():
            pl.semaphore_signal(barrier, inc=1, device_id=place.lines_away(1), device_id_type=MESH)

        count = count + jnp.where(below, 1, 0) + jnp.where(above, 1, 0)
    pl.semaphore_wait(barrier, count)


def sender(sems):
    send, receive = sems

    def make(index, source, target, device):
        return pltpu.make_async_remote_copy(
            src_ref=source,
            dst_ref=target,
            send_sem=send.at[index],
            recv_sem=receive.at[index],
            device_id=device,
            device_id_type=MESH,
        )

    return make


def row_steps(first, last, body):
    def one(step, carry):
        body(pl.ds(pl.multiple_of(first + step * STEP, STEP), STEP))
        return carry

    lax.fori_loop(0, (last - first) // STEP, one, 0)


class SumRows:
    @staticmethod
    def scratch(rows, columns, computed=False):
        return [
            pltpu.VMEM((MATES, rows, columns), low),
            pltpu.VMEM((MATES, rows, columns), low),
            pltpu.VMEM((2, rows // 2, columns), low),
            pltpu.VMEM((2, rows, columns), low),
            pltpu.SemaphoreType.DMA((MATES,)),
            pltpu.SemaphoreType.DMA((10,)),
            pltpu.SemaphoreType.DMA((10,)),
        ] + [pltpu.VMEM((MATES, rows, columns), low)] * computed

    def __init__(self, place, partial, scratch, compute=None):
        self.place, self.partial, self.compute = place, partial, compute
        self.own, self.swapped, self.relay, self.arrived, self.local_sems, send, receive = scratch[:7]
        if compute:
            self.other = scratch[7]
        self.make = sender((send, receive))
        self.rows = self.own.shape[1]
        self.order = [place.far, place.x, place.y, place.mate]
        half, x, y = self.rows // 2, place.of(place.x), place.of(place.y)
        own, relay, arrived = self.own, self.relay, self.arrived
        self.far_low = self.make(4, own.at[0, :half], relay.at[0], y)
        self.far_high = self.make(5, own.at[0, half:], relay.at[1], x)
        self.x_high = self.make(6, own.at[1, half:], arrived.at[0, half:], x)
        self.y_low = self.make(7, own.at[2, :half], arrived.at[1, :half], y)
        self.x_low = self.make(8, own.at[1, :half], arrived.at[0, :half], x)
        self.y_high = self.make(9, own.at[2, half:], arrived.at[1, half:], y)
        self.swaps = [
            self.make(
                slot,
                self.other.at[slot] if compute else partial.at[1, mate],
                self.swapped.at[slot],
                place.sibling,
            )
            for slot, mate in enumerate(self.order)
        ]

    def load(self, slot):
        return pltpu.make_async_copy(
            self.partial.at[0, self.order[slot]], self.own.at[slot], self.local_sems.at[slot]
        )

    def begin(self):
        for slot, mate in enumerate(self.order):
            if self.compute:
                self.compute(1, mate, self.other, slot)
            else:
                self.load(slot).start()
            self.swaps[slot].start()

    def add(self, target, target_slot, source, source_slot, first, last, shift=0):
        def body(here):
            there = pl.ds(pl.multiple_of(here.start - shift, STEP), STEP) if shift else here
            target[target_slot, here] = (
                target[target_slot, here].astype(wide) + source[source_slot, there].astype(wide)
            ).astype(low)

        row_steps(first, last, body)

    def sum_cores(self, slot):
        if self.compute:
            self.compute(0, self.order[slot], self.own, slot)
        else:
            self.load(slot).wait()
        self.swaps[slot].wait_recv()
        self.add(self.own, slot, self.swapped, slot, 0, self.rows)

    def send_far(self):
        self.sum_cores(0)
        self.far_low.start()
        self.far_high.start()

    def send_near(self):
        self.sum_cores(1)
        self.x_high.start()
        self.sum_cores(2)
        self.y_low.start()

    def send_relayed(self):
        half = self.rows // 2
        self.far_low.wait_recv()
        self.add(self.own, 1, self.relay, 0, 0, half)
        self.x_low.start()
        self.far_high.wait_recv()
        self.add(self.own, 2, self.relay, 1, half, self.rows, shift=half)
        self.y_high.start()
        self.sum_cores(3)

    def wait_half(self, upper):
        if upper:
            self.x_high.wait_recv()
            self.y_high.wait_recv()
        else:
            self.x_low.wait_recv()
            self.y_low.wait_recv()

    def total(self, here):
        return (
            self.own[3, here].astype(wide)
            + self.arrived[0, here].astype(wide)
            + self.arrived[1, here].astype(wide)
        )

    def finish(self):
        for copy in self.swaps + [
            self.far_low, self.far_high, self.x_high, self.y_low, self.x_low, self.y_high,
        ]:
            copy.wait_send()


class ShareRows:
    @staticmethod
    def scratch():
        return [
            pltpu.SemaphoreType.DMA((1,)),
            pltpu.SemaphoreType.DMA((11,)),
            pltpu.SemaphoreType.DMA((11,)),
        ]

    def __init__(self, place, source, target, scratch):
        self.place, self.source, self.target = place, source, target
        self.local_sem, send, receive = scratch
        self.make = sender((send, receive))
        self.rows = target.shape[2]

    def copy(self, index):
        place, half = self.place, self.rows // 2
        lower, upper, whole = pl.ds(0, half), pl.ds(half, half), pl.ds(0, self.rows)
        x, y, sibling = place.of(place.x), place.of(place.y), place.sibling

        def own(rows, device, side=0):
            return self.source.at[rows], self.target.at[side, place.mate, rows], device

        def passed(mate, rows, device, side=0):
            return self.target.at[0, mate, rows], self.target.at[side, mate, rows], device

        return self.make(
            index,
            *(
                lambda: own(upper, y),
                lambda: own(upper, x),
                lambda: own(lower, x),
                lambda: own(lower, y),
                lambda: passed(place.x, lower, y),
                lambda: passed(place.y, upper, x),
                lambda: own(whole, sibling, 1),
                lambda: passed(place.x, whole, sibling, 1),
                lambda: passed(place.y, whole, sibling, 1),
                lambda: passed(place.far, lower, sibling, 1),
                lambda: passed(place.far, upper, sibling, 1),
            )[index](),
        )

    def local(self):
        return pltpu.make_async_copy(
            self.source, self.target.at[0, self.place.mate], self.local_sem.at[0]
        )

    def begin_half(self, upper):
        for index in (0, 1) if upper else (2, 3):
            self.copy(index).start()

    def begin_rest(self):
        self.local().start()
        self.copy(6).start()

    def forward(self):
        for came, then in ((2, 4), (0, 5), (1, 7), (3, 8)):
            self.copy(came).wait_recv()
            self.copy(then).start()

    def forward_far(self):
        for came, then in ((4, 9), (5, 10)):
            self.copy(came).wait_recv()
            self.copy(then).start()

    def finish(self, arrived=False):
        if not arrived:
            self.local().wait()
            for index in range(6, 11):
                self.copy(index).wait_recv()
        for index in range(11):
            self.copy(index).wait_send()


class GatherLines:
    @staticmethod
    def scratch(lines):
        return [
            pltpu.SemaphoreType.DMA((1,)),
            pltpu.SemaphoreType.DMA((3,)),
            pltpu.SemaphoreType.DMA((3,)),
            pltpu.SemaphoreType.DMA((lines, MATES)),
            pltpu.SemaphoreType.DMA((lines, MATES)),
            pltpu.SemaphoreType.DMA((lines, MATES)),
        ]

    def __init__(self, place, blocks, target, scratch, rows=None):
        self.place, self.blocks, self.target = place, blocks, target
        self.lines = target.shape[0]
        self.part = pl.ds(*(rows or (0, target.shape[2])))
        self.local_sem, send, receive, self.up_sem, self.down_sem, self.got = scratch
        self.make = sender((send, receive))
        self.order = [place.mate, place.x, place.y, place.far]

    def plane(self, slot):
        place, mate = self.place, self.order[slot]
        here = self.target.at[place.line, place.mate]
        if slot == 0:
            return pltpu.make_async_copy(self.blocks.at[mate], here, self.local_sem.at[0])
        return self.make(slot - 1, self.blocks.at[mate], here, place.of(mate))

    def begin(self):
        for slot in range(MATES):
            self.plane(slot).start()

    def arrive(self, slot):
        copy = self.plane(slot)
        copy.wait_recv() if slot else copy.wait()

    def hop(self, step, mate, direction):
        place = self.place
        line = place.line - step * direction
        piece = self.target.at[line, mate, self.part]
        sems = self.up_sem if direction > 0 else self.down_sem
        copy = pltpu.make_async_remote_copy(
            src_ref=piece,
            dst_ref=piece,
            send_sem=sems.at[step, mate],
            recv_sem=self.got.at[line, mate],
            device_id=place.lines_away(direction),
            device_id_type=MESH,
        )
        came = (line >= 0) & (line < self.lines)
        goes = (place.line < self.lines - 1) if direction > 0 else (place.line > 0)
        return copy, came, goes

    def leave(self, arriving=True):
        for slot, mate in enumerate(self.order):
            if arriving:
                self.arrive(slot)
            for direction in (1, -1):
                copy, _, goes = self.hop(0, mate, direction)
                pl.when(goes)(copy.start)

    def onwards(self, step):
        if step >= self.lines:
            return
        for mate in self.order:
            for direction in (1, -1):
                copy, came, goes = self.hop(step, mate, direction)
                pl.when(came)(copy.wait_recv)
                if step < self.lines - 1:
                    pl.when(came & goes)(copy.start)

    def finish_plane(self):
        for slot in range(1, MATES):
            self.plane(slot).wait_send()

    def finish_lines(self):
        for step in range(self.lines - 1):
            for mate in self.order:
                for direction in (1, -1):
                    copy, came, goes = self.hop(step, mate, direction)
                    pl.when(came & goes)(copy.wait_send)


class SwapBlocks:
    @staticmethod
    def scratch():
        return [
            pltpu.SemaphoreType.DMA((1,)),
            pltpu.SemaphoreType.DMA((2 * MATES,)),
            pltpu.SemaphoreType.DMA((2 * MATES,)),
        ]

    def __init__(self, place, piece, target, scratch):
        self.place, self.piece, self.target = place, piece, target
        self.local_sem, send, receive = scratch
        self.make = sender((send, receive))
        self.order = [place.far, place.x, place.y, place.mate]

    def copy(self, slot, index):
        place, mate = self.place, self.order[index]
        source, target = self.piece(slot, mate), self.target.at[slot, place.mate]
        if slot == 0 and index == MATES - 1:
            return pltpu.make_async_copy(source, target, self.local_sem.at[0]), True
        return self.make(slot * MATES + index, source, target, place.of(mate, slot)), False

    def begin(self, slot, index=None):
        for each in range(MATES) if index is None else (index,):
            self.copy(slot, each)[0].start()

    def finish(self):
        for slot in range(2):
            for index in range(MATES):
                self.copy(slot, index)[0].wait()


class SumLines:
    @staticmethod
    def scratch(lines, shape):
        return [
            pltpu.VMEM((lines,) + shape, low),
            pltpu.VMEM((2, max(lines - 1, 1)) + shape, low),
            pltpu.SemaphoreType.DMA((lines + 1,)),
            pltpu.SemaphoreType.DMA((2, lines, MATES)),
            pltpu.SemaphoreType.DMA((2, lines, MATES)),
            pltpu.SemaphoreType.DMA((3,)),
            pltpu.SemaphoreType.DMA((3,)),
        ]

    def __init__(self, place, blocks, result, scratch, first=0):
        self.place, self.blocks, self.result, self.first = place, blocks, result, first
        self.held, self.came, self.local_sems, self.send, self.got, send, receive = scratch
        self.lines = self.held.shape[0]
        self.make = sender((send, receive))
        self.order = [place.far, place.x, place.y, place.mate]

    def load(self, line):
        return pltpu.make_async_copy(
            self.blocks.at[
                line, :, pl.ds(self.first, self.held.shape[2]), pl.ds(0, self.held.shape[3])
            ],
            self.held.at[line],
            self.local_sems.at[line],
        )

    def begin(self):
        for line in range(self.lines):
            self.load(line).start()

    def wait_loads(self):
        for line in range(self.lines):
            self.load(line).wait()

    def put_gains(self, gains):
        lines, mates, height, lanes = self.held.shape
        top = lax.broadcasted_iota(jnp.int32, (height, lanes), 0) == 0
        for line in range(lines):
            for mate in range(mates):
                first = (line * mates + mate) * lanes
                part = jnp.broadcast_to(gains[:, first : first + lanes], (height, lanes))
                self.held[line, mate] = jnp.where(
                    top, part, self.held[line, mate].astype(wide)
                ).astype(low)

    def add_top(self, other, count):
        lines, mates, height, lanes = self.held.shape
        top = lax.broadcasted_iota(jnp.int32, (height, lanes), 0) < count
        for line in range(lines):
            for mate in range(mates):
                own = self.held[line, mate].astype(wide)
                both = own + other[line, mate].astype(wide)
                self.held[line, mate] = jnp.where(top, both, own).astype(low)

    def copy(self, turn, way, mate):
        direction = 1 - 2 * way
        line = self.place.line + direction * (self.lines - turn)
        return line, pltpu.make_async_remote_copy(
            src_ref=self.held.at[line, mate],
            dst_ref=self.came.at[way, turn - 1, mate],
            send_sem=self.send.at[way, turn, mate],
            recv_sem=self.got.at[way, turn, mate],
            device_id=self.place.lines_away(direction),
            device_id_type=MESH,
        )

    def arrival(self, turn, way, mate):
        slot = self.came.at[way, turn - 1, mate]
        return pltpu.make_async_remote_copy(
            src_ref=slot,
            dst_ref=slot,
            send_sem=self.send.at[way, turn, mate],
            recv_sem=self.got.at[way, turn, mate],
            device_id=self.place.sibling,
            device_id_type=MESH,
        )

    def sends(self, turn, way):
        line = self.place.line
        return line <= turn - 1 if way == 0 else line >= self.lines - turn

    def inner(self, way):
        return self.place.line >= 1 if way == 0 else self.place.line <= self.lines - 2

    def add(self, line, way, turn, mate):
        def body(here):
            self.held[line, mate, here] = (
                self.held[line, mate, here].astype(wide)
                + self.came[way, turn - 1, mate, here].astype(wide)
            ).astype(low)

        row_steps(0, self.held.shape[2], body)

    def round(self, turn):
        if turn >= self.lines:
            return
        for mate in self.order:
            for way in (0, 1):
                line, copy = self.copy(turn, way, mate)

                @pl.when(self.sends(turn, way))
                def _(line=line, copy=copy, way=way, mate=mate):
                    if turn > 1:

                        @pl.when(self.inner(way))
                        def _():
                            self.arrival(turn - 1, way, mate).wait_recv()
                            self.add(line, way, turn - 1, mate)

                    copy.start()

    def plane(self, index):
        place, mate = self.place, self.order[index]
        return self.make(
            index, self.held.at[place.line, mate], self.result.at[place.mate], place.of(mate)
        )

    def local(self):
        place = self.place
        return pltpu.make_async_copy(
            self.held.at[place.line, place.mate],
            self.result.at[place.mate],
            self.local_sems.at[self.lines],
        )

    def exchange(self):
        for index, mate in enumerate(self.order):
            for way in (0, 1):
                if self.lines > 1:

                    @pl.when(self.inner(way))
                    def _(way=way, mate=mate):
                        self.arrival(self.lines - 1, way, mate).wait_recv()
                        self.add(self.place.line, way, self.lines - 1, mate)

            if index < 3:
                self.plane(index).start()
            else:
                self.local().start()

    def straight(self, step):
        line = (self.place.line + step) % self.lines
        return pltpu.make_async_remote_copy(
            src_ref=self.held.at[line],
            dst_ref=self.came.at[0, step - 1],
            send_sem=self.send.at[0, step, 0],
            recv_sem=self.got.at[0, step, 0],
            device_id=(line * MATES + self.place.mate, self.place.core),
            device_id_type=MESH,
        )

    def direct(self):
        for step in range(1, self.lines):
            self.straight(step).start()

    def exchange_direct(self):
        for step in range(1, self.lines):
            self.straight(step).wait_recv()
            for mate in range(MATES):
                self.add(self.place.line, 0, step, mate)
        for index in range(3):
            self.plane(index).start()
        self.local().start()

    def finish(self, direct=False):
        self.local().wait()
        for index in range(3):
            self.plane(index).wait()
        if direct:
            for step in range(1, self.lines):
                self.straight(step).wait_send()
            return
        for turn in range(1, self.lines):
            for way in (0, 1):
                for mate in self.order:
                    _, copy = self.copy(turn, way, mate)
                    pl.when(self.sends(turn, way))(copy.wait_send)


def remote_call(body, identity, ins, outs, scratch, aliases=None):
    anywhere = pl.BlockSpec(memory_space=pl.ANY)
    held = pl.BlockSpec(memory_space=pltpu.VMEM)
    return pl.pallas_call(
        body,
        in_specs=[anywhere if kind == "any" else held for _, kind in ins],
        out_specs=[anywhere if kind == "any" else held for _, _, kind in outs],
        out_shape=[jax.ShapeDtypeStruct(shape, dtype) for shape, dtype, _ in outs],
        scratch_shapes=scratch,
        input_output_aliases=aliases or {},
        compiler_params=pltpu.CompilerParams(
            vmem_limit_bytes=VMEM_BYTES, collective_id=identity, has_side_effects=True
        ),
    )(*[array for array, _ in ins])


def inverse_rms(value):
    return lax.rsqrt(jnp.mean(value * value, axis=1, keepdims=True) + epsilon)


def norm_back_rows(grad, source, scale):
    inverse = inverse_rms(source)
    scaled = grad * scale
    unit = source * inverse
    inner = jnp.mean(scaled * source, axis=1, keepdims=True)
    return inverse * (scaled - unit * (inverse * inner)), grad * unit


def load_weights(weights, held, sems):
    return [
        pltpu.make_async_copy(weights.at[slot, mate], held.at[slot, mate], sems.at[slot, mate])
        for slot in range(2)
        for mate in range(MATES)
    ]


def middle_kernel(lines, moves, gathered, weights, input_ref, scale_ref, grad_any, *rest):
    place = Place()
    count = len(moves)
    middle_ref, turned_out, grads, acts_out, hidden_out = rest[count : count + 5]
    targets, scratch = rest[count + 5 : 2 * count + 5], rest[2 * count + 5 :]
    normed, held, weight_sems, all_normed, turned, ups, acts, hidden, out_sems, load_sems = scratch[:10]
    scratch = scratch[10:]
    share = ShareRows(place, normed, all_normed, scratch[:3])
    other = ShareRows(place, grad_any.at[place.core], grads, scratch[3:6])
    gathers = [
        GatherLines(place, None, target, scratch[6 + 6 * index : 12 + 6 * index], moves[index])
        for index, target in enumerate(targets)
        if moves[index]
    ]
    meet(place, lines=lines if gathers else 0)
    loads = load_weights(weights, held, weight_sems)
    for load in loads:
        load.start()
    other.begin_half(False)
    other.begin_half(True)
    other.begin_rest()
    for gather in gathers[:1]:
        gather.leave(False)
    _, _, all_lines, _, depth, width = held.shape
    early = moves[0][0] if gathers else depth

    def load_ups(index):
        part = (pl.ds(0, early), pl.ds(early, depth - early))[index]
        return pltpu.make_async_copy(
            targets[0].at[:, :, part], ups.at[:, :, part], load_sems.at[index]
        )

    load_ups(0).start()
    for load in loads:
        load.wait()
    rows, model_width = normed.shape
    half = rows // 2
    height = MATES * depth
    some = max(1, 512 // height)

    def product(step, carry):
        columns = pl.ds(pl.multiple_of(step * some * height, 128), some * height)
        part = pl.ds(step * some, some)
        for first in (0, half):
            total = None
            for slot in range(2):
                for mate in range(MATES):
                    term = dot(
                        gathered[slot, mate, first : first + half],
                        held[slot, mate, part].reshape(some * height, width),
                        NT,
                    )
                    total = term if total is None else total + term
            here = pl.ds(first, half)
            middle_ref[here, columns] = input_ref[here, columns].astype(wide) + total
        return carry

    def body(here):
        middle = middle_ref[here]
        normed[here] = (middle * inverse_rms(middle) * scale_ref[...]).astype(low)

    lax.fori_loop(0, all_lines // some, product, 0)
    row_steps(0, half, body)
    share.begin_half(False)
    row_steps(half, rows, body)
    share.begin_half(True)
    share.begin_rest()
    for gather in gathers[:1]:
        gather.onwards(1)
    for gather in gathers[1:]:
        gather.leave(False)
    for gather in gathers[:1]:
        gather.onwards(2)
    share.forward()
    for gather in gathers[:1]:
        for number in range(3, lines):
            gather.onwards(number)
    if early < depth:
        load_ups(1).start()
    for gather in gathers[1:]:
        gather.onwards(1)
    other.forward()
    share.forward_far()
    share.finish()
    load_ups(0).wait()
    if early < depth:
        load_ups(1).wait()
    weight = ups[...].reshape(model_width, ups.shape[3])
    units = hidden.shape[2]
    outs = []
    for slot in range(2):
        for mate in range(MATES):
            index = slot * MATES + mate
            values = dot(all_normed[slot, mate], weight, NN)
            acts[index] = values.astype(low)
            gate, up = values[:, :units], values[:, units:]
            hidden[index] = (gate * jax.nn.sigmoid(gate) * up).astype(low)
            here = pl.ds(index * rows, rows)
            turned[:, here] = all_normed[slot, mate].T
            outs += [
                pltpu.make_async_copy(acts.at[index], acts_out.at[here], out_sems.at[0, index]),
                pltpu.make_async_copy(hidden.at[index], hidden_out.at[here], out_sems.at[1, index]),
                pltpu.make_async_copy(
                    turned.at[:, here], turned_out.at[:, here], out_sems.at[2, index]
                ),
            ]
            for out in outs[-3:]:
                out.start()
        if slot == 0:
            for gather in gathers[1:]:
                gather.onwards(2)
            other.forward_far()
    for number in range(3, lines):
        for gather in gathers[1:]:
            gather.onwards(number)
    for gather in gathers:
        gather.finish_lines()
    other.finish()
    for out in outs:
        out.wait()


def columns_in_steps(lines, depth, body):
    height = MATES * depth
    some = max(1, 512 // height)

    def one(step, carry):
        body(
            pl.ds(pl.multiple_of(step * some * height, 128), some * height),
            pl.ds(step * some, some),
            some * height,
        )
        return carry

    lax.fori_loop(0, lines // some, one, 0)


class Tiles:
    def __init__(self, source, target, held_in, held_out, sems, body):
        self.source, self.target, self.body = source, target, body
        self.held_in, self.held_out, self.sems = held_in, held_out, sems
        self.rows = held_in.shape[1]
        self.count = source.shape[0] // self.rows

    def load(self, tile):
        return pltpu.make_async_copy(
            self.source.at[pl.ds(tile * self.rows, self.rows)],
            self.held_in.at[tile % 2],
            self.sems.at[0, tile % 2],
        )

    def store(self, tile):
        return pltpu.make_async_copy(
            self.held_out.at[tile % 2],
            self.target.at[pl.ds(tile * self.rows, self.rows)],
            self.sems.at[1, tile % 2],
        )

    def begin(self):
        self.load(0).start()

    def run(self, first, last):
        for tile in range(first, last):
            self.load(tile).wait()
            if tile + 1 < self.count:
                self.load(tile + 1).start()
            if tile >= 2:
                self.store(tile - 2).wait()
            self.body(tile, self.held_in.at[tile % 2], self.held_out.at[tile % 2])
            self.store(tile).start()

    def finish(self):
        for tile in range(max(self.count - 2, 0), self.count):
            self.store(tile).wait()


def turn_rows_kernel(
    lines, parts, acts_any, grads_any, ups_any, weights, turned, hidden, downs_any, middle_ref,
    grad_ref, scale_ref, *rest
):
    place = Place()
    blocks, rest = rest[: 1 if parts else 0], rest[1 if parts else 0 :]
    count = len(parts)
    middle_grad_ref, gain_ref, low_grad, gated_grads, ups_grad, mlp_part = rest[:6]
    results, scratch = rest[6 : 6 + count], rest[6 + count :]
    held, load_sems, sent, acts, ups, downs = scratch[:6]
    turned_in, grad_out, grad_sems, hidden_in, part_out, part_sems, unit_sems = scratch[6:13]
    scratch = scratch[13:]
    all_lines, _, depth, units = ups.shape
    tokens = low_grad.shape[0]

    def compute(side_of, mate, target, slot):
        first = pl.ds(pl.multiple_of((side_of * MATES + mate) * tokens, STEP), tokens)

        def step(columns, part, size):
            target[slot, :, columns] = dot(
                acts[first], ups[part].reshape(size, units), NT
            ).astype(low)

        columns_in_steps(all_lines, depth, step)

    def weight_grad(tile, tile_in, tile_out):
        found = dot(tile_in[...], acts[...], NN).astype(low)
        tile_out[...] = found
        if sums:
            each_line = MATES * depth // tokens
            for number in range(tokens // depth):
                mate = tile % each_line * (tokens // depth) + number
                sums[1].held[tile // each_line, mate] = found[
                    number * depth : number * depth + parts[1][1]
                ]

    def load_units(tile):
        here = pl.ds(tile * tokens, tokens)
        half = tile % 2
        return (
            pltpu.make_async_copy(
                grads_any.at[tile // MATES, tile % MATES], turned_in.at[half], unit_sems.at[0, half]
            ),
            pltpu.make_async_copy(acts_any.at[here], grad_out.at[half], unit_sems.at[1, half]),
        )

    def units_back():
        inner = downs.shape[3]
        for tile in range(2 * MATES):
            for load in load_units(tile):
                load.wait()
            if tile + 1 < 2 * MATES:
                for load in load_units(tile + 1):
                    load.start()
            grad = dot(turned_in[tile % 2], downs[...].reshape(-1, inner), NN)
            values = grad_out[tile % 2].astype(wide)
            gate, up = values[:, :inner], values[:, inner:]
            silu, slope = silu_parts(gate)
            here = pl.ds(tile * tokens, tokens)
            acts[here, :inner] = (grad * up * slope).astype(low)
            acts[here, inner:] = (grad * silu).astype(low)

    def back_down(tile, tile_in, tile_out):
        def step(columns, part, size):
            tile_out[:, columns] = dot(
                tile_in[...], downs[part].reshape(size, downs.shape[3]), NT
            ).astype(low)

        columns_in_steps(all_lines, depth, step)

    grad_tiles = Tiles(turned, ups_grad, turned_in, grad_out, grad_sems, weight_grad)
    part_tiles = Tiles(hidden, mlp_part, hidden_in, part_out, part_sems, back_down)
    rows = SumRows(place, None, scratch[:8], compute)
    swap = SwapBlocks(place, lambda slot, mate: sent.at[slot, mate], gated_grads, scratch[8:11])
    sums = [
        SumLines(
            place,
            None if index else blocks[0],
            results[index],
            scratch[11 + 7 * index : 18 + 7 * index],
        )
        for index in range(count)
    ]
    meet(place, lines=lines if parts else 0, cores=True)
    load_downs = pltpu.make_async_copy(downs_any, downs, load_sems.at[3])
    load_downs.start()
    for load in load_units(0):
        load.start()
    for each in sums[:1]:
        each.begin()
    load_ups = pltpu.make_async_copy(ups_any, ups, load_sems.at[1])
    load_ups.start()

    def load_weight(slot):
        return pltpu.make_async_copy(weights.at[slot], held, load_sems.at[2])

    for each in sums[:1]:
        each.wait_loads()
        each.round(1)
    load_weight(0).start()
    part_tiles.begin()
    gain_ref[...] = jnp.zeros_like(gain_ref)
    load_downs.wait()
    units_back()
    grad_tiles.begin()
    load_ups.wait()
    for each in sums[:1]:
        each.round(2)
    rows.begin()
    rows.send_far()
    rows.send_near()
    all_tiles = grad_tiles.count
    grad_tiles.run(0, all_tiles)
    for each in sums[1:]:
        each.round(1)
    rows.send_relayed()
    for each in sums[:1]:
        each.round(3)
    part_tiles.run(0, part_tiles.count // 2)
    for each in sums[1:]:
        each.round(2)
    rows.wait_half(False)
    rows.wait_half(True)

    def body(here):
        part, gains = norm_back_rows(rows.total(here), middle_ref[here], scale_ref[...])
        total = grad_ref[here].astype(wide) + part
        middle_grad_ref[here] = total
        low_grad[here] = total.astype(low)
        gain_ref[...] += jnp.sum(gains, axis=0, keepdims=True)

    row_steps(0, tokens, body)
    width = held.shape[-1]
    for slot in range(2):
        load_weight(slot).wait()
        for index, mate in enumerate(swap.order):
            weight = held[mate].reshape(all_lines * MATES * depth, width)
            sent[slot, mate] = dot(low_grad[...], weight, NN).astype(low)
            swap.begin(slot, index)
        if slot == 0:
            load_weight(1).start()
    rows.finish()
    for each in sums[1:]:
        each.round(3)
    for each in sums[:1]:
        each.exchange()
    part_tiles.run(part_tiles.count // 2, part_tiles.count)
    for each in sums[1:]:
        each.exchange()
    swap.finish()
    for tiles in (grad_tiles, part_tiles):
        tiles.finish()
    for each in sums:
        each.finish()


def last_rows_kernel(
    lines, pieces, heads, all_grads, attn_any, turned, beta_ref, input_ref, middle_grad_ref, scale_ref, *rest
):
    place = Place()
    blocks, rest = rest[:pieces], rest[pieces:]
    input_grad, gain_ref = rest[:2]
    count = pieces + 1 if pieces else 0
    results, scratch = rest[2 : 2 + count], rest[2 + count :]
    low_grad, grads, attn, load_sems = scratch[:4]
    all_lines, _, depth, width = attn.shape
    tokens = low_grad.shape[0]

    def compute(side_of, mate, target, slot):
        first = pl.ds(pl.multiple_of((side_of * MATES + mate) * tokens, STEP), tokens)

        def step(columns, part, size):
            total = dot(grads[first, :width], attn[part].reshape(size, width), NT)
            total = total + dot(grads[first, width:], beta_ref[:, columns], NN)
            target[slot, :, columns] = total.astype(low)

        columns_in_steps(all_lines, depth, step)

    meet(place, far=bool(pieces), lines=lines if pieces else 0, straight=True)
    rows = SumRows(place, None, scratch[4:12], compute)
    make = sender(scratch[12:14])
    scratch = scratch[14:]
    sums = [
        SumLines(
            place,
            blocks[index] if index < pieces else None,
            results[index],
            scratch[7 * index : 7 * index + 7],
        )
        for index in range(count)
    ]
    loads = [
        pltpu.make_async_copy(all_grads, grads, load_sems.at[0]),
        pltpu.make_async_copy(attn_any, attn, load_sems.at[1]),
    ]
    for each in sums[:pieces]:
        each.begin()
    for load in loads:
        load.start()
    gain_ref[...] = jnp.zeros_like(gain_ref)
    if sums:
        small, _, streams = sums
        mine, theirs, turned_in, turned_sems = scratch[7 * count :]
        lines_here = place.line * 2 < lines

        def line_of_turn(turn):
            return jnp.where(lines_here, lines - 1 - turn, turn)

        height = turned_in.shape[1]
        each_line = MATES * depth // height
        mates_each = height // depth

        def load_turned(index):
            line = line_of_turn(index // each_line)
            first = line * (MATES * depth) + index % each_line * height
            return pltpu.make_async_copy(
                turned.at[pl.ds(pl.multiple_of(first, 128), height)],
                turned_in.at[index % 2],
                turned_sems.at[index % 2],
            )

        kept = lax.broadcasted_iota(jnp.int32, (SMALL, CHUNK), 0)
        kept = (kept >= BETA_ROW) & (kept < BETA_ROW + heads)

        def weight_grads(first, last):
            for index in range(first * each_line, last * each_line):
                load_turned(index).wait()
                if index + 1 < lines * each_line:
                    load_turned(index + 1).start()
                line = line_of_turn(index // each_line)
                found = dot(turned_in[index % 2], grads[...], NN)
                for number in range(mates_each):
                    mate = index % each_line * mates_each + number
                    part = found[number * depth : (number + 1) * depth]
                    streams.held[line, mate] = part[:, :width].astype(low)
                    small.held[line, mate] = jnp.where(
                        kept, part[:, width:].T[:SMALL], small.held[line, mate].astype(wide)
                    ).astype(low)

        load_turned(0).start()
        sums[1].wait_loads()
        sums[1].round(1)
        loads[0].wait()
        small.wait_loads()
        weight_grads(0, 1)
        streams.round(1)
        weight_grads(1, 2)
    for load in loads[0 if not sums else 1 :]:
        load.wait()
    rows.begin()
    rows.send_far()
    rows.send_near()
    if sums:
        weight_grads(2, lines)
    for each in sums[1:]:
        each.round(2)
    rows.send_relayed()
    rows.wait_half(False)
    rows.wait_half(True)

    def body(here):
        part, gains = norm_back_rows(
            rows.total(here), input_ref[here].astype(wide), scale_ref[...]
        )
        low_grad[here] = (middle_grad_ref[here] + part).astype(low)
        gain_ref[...] += jnp.sum(gains, axis=0, keepdims=True)

    row_steps(0, tokens, body)
    first = make(0, low_grad, input_grad.at[place.core], place.sibling)
    first.start()
    first_local = pltpu.make_async_copy(low_grad, input_grad.at[place.core], load_sems.at[2])
    first_local.start()
    if sums:
        small.put_gains(gain_ref)
        mine[...] = small.held[...]
        swap = make(1, mine, theirs, place.sibling)
        swap.start()
        swap.wait_recv()
        small.add_top(theirs, CONV_ROW)
        small.direct()
    for each in sums[1:]:
        each.round(3)
    for each in sums[:1]:
        each.exchange_direct()
    for turn in range(4, lines):
        for each in sums[1:]:
            each.round(turn)
    for each in sums[1:]:
        each.exchange()
    rows.finish()
    first_local.wait()
    first.wait()
    if sums:
        swap.wait_send()
    for each in sums:
        each.finish(direct=each is sums[0])


def first_rows_kernel(input_ref, inputs, *scratch):
    place = Place()
    meet(place)
    share = ShareRows(place, input_ref.at[place.core], inputs, scratch)
    share.begin_half(False)
    share.begin_half(True)
    share.begin_rest()
    share.forward()
    share.forward_far()
    share.finish()


def first_rows(block_input):
    seqs, rows, columns = block_input.shape
    return remote_call(
        first_rows_kernel,
        0,
        [(block_input, "any")],
        [((seqs, MATES, rows, columns), low, "any")],
        ShareRows.scratch(),
    )[0]


def first_kernel(lines, pieces, input_ref, *rest):
    place = Place()
    blocks, rest = rest[:pieces], rest[pieces:]
    turned_out, raw_ref, logit_ref, small_ref, attn_out = rest[:5]
    others, scratch = rest[5 : 3 + pieces], rest[3 + pieces :]
    inputs, normed, turned, small, attn, scale, totals, out_sems = scratch[:8]
    scratch = scratch[8:]
    targets = (small, attn) + tuple(others)
    meet(place, far=True, lines=lines)
    share = ShareRows(place, input_ref.at[place.core], inputs, scratch[:3])
    gathers = [
        GatherLines(place, blocks[index], targets[index], scratch[3 + 6 * index : 9 + 6 * index])
        for index in range(pieces)
    ]
    few, main, later = gathers[:3]
    for gather in (few, main):
        gather.begin()
    for gather in (few, main):
        gather.leave()
    share.begin_half(False)
    share.begin_half(True)
    share.begin_rest()
    later.begin()
    for gather in (few, main):
        gather.onwards(1)
    later.leave()
    for step in range(2, lines):
        few.onwards(step)
    share.forward()
    later.onwards(1)
    small_ref[...] = small[...]
    _, _, tokens, model_width = inputs.shape
    depth = small.shape[3]
    parts = [(line, mate) for line in range(lines) for mate in range(MATES)]
    for index, (line, mate) in enumerate(parts):
        scale[:, index * depth : (index + 1) * depth] = small[line, mate, :1].astype(wide)
    beta = jnp.concatenate([small[line, mate] for line, mate in parts], axis=1)
    beta = over(beta, jnp.zeros((CHUNK - beta.shape[0], model_width), low))
    outs = []

    def norm(slot, mate):
        first = pl.multiple_of((slot * MATES + mate) * tokens, CHUNK)

        def body(here):
            value = inputs[slot, mate, here].astype(wide)
            there = pl.ds(pl.multiple_of(first + here.start, STEP), STEP)
            normed[there] = (value * inverse_rms(value) * scale[...]).astype(low)

        row_steps(0, tokens, body)
        block = pl.ds(first, tokens)
        logit_ref[block] = dot(normed[block], beta, NT)
        turned[:, block] = normed[block].T
        outs.append(
            pltpu.make_async_copy(
                turned.at[:, block], turned_out.at[:, block], out_sems.at[len(outs)]
            )
        )
        outs[-1].start()

    share.local().wait()
    for mate in (place.mate, place.x, place.y):
        norm(0, mate)
    main.onwards(2)
    share.forward_far()
    for gather in gathers[3:]:
        gather.begin()
    norm(0, place.far)
    later.onwards(2)
    for index, mate in ((6, place.mate), (7, place.x), (8, place.y)):
        share.copy(index).wait_recv()
        norm(1, mate)
    for index in (9, 10):
        share.copy(index).wait_recv()
    norm(1, place.far)
    height = MATES * depth
    lower = place.line * 2 < lines
    first_line = jnp.where(lower, 0, 1)
    last_line = jnp.where(lower, lines - 1, 0)
    width = attn.shape[3]

    def tile(index):
        return pl.ds(pl.multiple_of(index * tokens, STEP), tokens)

    def most(index, carry):
        here = tile(index)
        columns = pl.ds(pl.multiple_of(first_line * height, CHUNK), (lines - 1) * height)
        weight = attn[pl.ds(first_line, lines - 1)].reshape((lines - 1) * height, width)
        totals[here] = dot(normed[here, columns], weight, NN)
        return carry

    def rest_of(index, carry):
        here = tile(index)
        columns = pl.ds(pl.multiple_of(last_line * height, CHUNK), height)
        weight = attn[last_line].reshape(height, width)
        raw_ref[here] = (totals[here] + dot(normed[here, columns], weight, NN)).astype(low)
        return carry

    lax.fori_loop(0, 2 * MATES, most, 0)
    for step in range(3, lines):
        main.onwards(step)
    outs.append(pltpu.make_async_copy(attn, attn_out, out_sems.at[2 * MATES]))
    outs[-1].start()
    lax.fori_loop(0, 2 * MATES, rest_of, 0)
    for step in range(3, lines):
        later.onwards(step)
    share.finish(arrived=True)
    for gather in gathers[3:]:
        for slot in range(MATES):
            gather.arrive(slot)
    for out in outs:
        out.wait()
    for gather in gathers:
        gather.finish_plane()
    for gather in gathers[:3]:
        gather.finish_lines()


def first_call(block_input, blocks, lines):
    seqs, tokens, model_width = block_input.shape
    rows = seqs * MATES * tokens
    small, attn = ((lines,) + block.shape for block in blocks[:2])
    shared = (seqs, MATES, tokens, model_width)
    return remote_call(
        functools.partial(first_kernel, lines, len(blocks)),
        0,
        [(array, "any") for array in (block_input, *blocks)],
        [
            ((model_width, rows), low, "any"),
            ((rows, attn[3]), low, "held"),
            ((rows, CHUNK), wide, "held"),
            (small, low, "held"),
            (attn, low, "any"),
        ]
        + [((lines,) + block.shape, low, "any") for block in blocks[2:]],
        [
            pltpu.VMEM(shared, low),
            pltpu.VMEM((rows, model_width), low),
            pltpu.VMEM((model_width, rows), low),
            pltpu.VMEM(small, low),
            pltpu.VMEM(attn, low),
            pltpu.VMEM((1, model_width), wide),
            pltpu.VMEM((rows, attn[3]), wide),
            pltpu.SemaphoreType.DMA((2 * MATES + 1,)),
        ]
        + ShareRows.scratch()
        + GatherLines.scratch(lines) * len(blocks),
    )


def middle_rows(gathered, weights, mine, scale, out_grad, moving, lines):
    rows, columns = mine.shape
    shared = (2, MATES, rows, columns)
    arrays = [array for array, _ in moving]
    ups, downs = arrays
    several = 2 * MATES
    return remote_call(
        functools.partial(middle_kernel, lines, tuple(part for _, part in moving)),
        1,
        [(gathered, "held"), (weights, "any"), (mine, "held"), (scale, "held"), (out_grad, "any")]
        + [(array, "any") for array in arrays],
        [
            ((rows, columns), wide, "held"),
            ((columns, several * rows), low, "any"),
            (shared, low, "any"),
            ((several * rows, ups.shape[3]), low, "any"),
            ((several * rows, downs.shape[3]), low, "any"),
        ]
        + [(array.shape, low, "any") for array in arrays],
        [
            pltpu.VMEM((rows, columns), low),
            pltpu.VMEM(weights.shape, low),
            pltpu.SemaphoreType.DMA((2, MATES)),
            pltpu.VMEM(shared, low),
            pltpu.VMEM((columns, several * rows), low),
            pltpu.VMEM(ups.shape, low),
            pltpu.VMEM((several, rows, ups.shape[3]), low),
            pltpu.VMEM((several, rows, downs.shape[3]), low),
            pltpu.SemaphoreType.DMA((3, several)),
            pltpu.SemaphoreType.DMA((2,)),
        ]
        + ShareRows.scratch() * 2
        + GatherLines.scratch(lines) * len(arrays),
        {5 + index: 5 + index for index in range(len(arrays))},
    )


def turn_rows(
    acts, grads, ups, weights, turned, hidden, downs, middle, grad, scale, downward_grad, ups_rows, lines
):
    rows, columns = middle.shape
    width = weights.shape[-1]
    blocks = (2, MATES, rows, width)
    all_rows, units = hidden.shape
    scratch = [
        pltpu.VMEM(weights.shape[1:], low),
        pltpu.SemaphoreType.DMA((4,)),
        pltpu.VMEM(blocks, low),
        pltpu.VMEM(acts.shape, low),
        pltpu.VMEM(ups.shape, low),
        pltpu.VMEM(downs.shape, low),
        pltpu.VMEM((2, rows, columns), low),
        pltpu.VMEM((2, rows, acts.shape[1]), low),
        pltpu.SemaphoreType.DMA((2, 2)),
        pltpu.VMEM((2, rows, units), low),
        pltpu.VMEM((2, rows, columns), low),
        pltpu.SemaphoreType.DMA((2, 2)),
        pltpu.SemaphoreType.DMA((2, 2)),
    ]
    scratch += SumRows.scratch(rows, columns, True) + SwapBlocks.scratch()
    outs, parts = [], ()
    if downward_grad is not None:
        _, _, depth, _ = downward_grad.shape
        parts = ((0, depth), (0, ups_rows))
        for shape in ((MATES, depth, units), (MATES, ups_rows, acts.shape[1])):
            scratch += SumLines.scratch(lines, shape)
            outs.append((shape, low, "any"))
    return remote_call(
        functools.partial(turn_rows_kernel, lines, parts),
        2,
        [(array, "any") for array in (acts, grads, ups, weights, turned, hidden, downs)]
        + [(array, "held") for array in (middle, grad, scale)]
        + [(downward_grad, "any")] * bool(parts),
        [
            ((rows, columns), wide, "held"),
            ((1, columns), wide, "held"),
            ((rows, columns), low, "held"),
            (blocks, low, "any"),
            ((turned.shape[0], acts.shape[1]), low, "any"),
            ((all_rows, columns), low, "any"),
        ]
        + outs,
        scratch,
    )


def last_rows(all_grads, attn, turned, beta, mine, middle_grad, scale, blocks, lines, heads):
    rows, columns = mine.shape
    scratch = [
        pltpu.VMEM((rows, columns), low),
        pltpu.VMEM(all_grads.shape, low),
        pltpu.VMEM(attn.shape, low),
        pltpu.SemaphoreType.DMA((3,)),
    ]
    scratch += SumRows.scratch(rows, columns, True) + [pltpu.SemaphoreType.DMA((2,))] * 2
    results = [block.shape[1:] for block in blocks] + [attn.shape[1:]] * bool(blocks)
    for shape in results:
        scratch += SumLines.scratch(lines, shape)
    if blocks:
        scratch += [pltpu.VMEM(blocks[0].shape, low)] * 2
        scratch += [pltpu.VMEM((2, 256, turned.shape[1]), low), pltpu.SemaphoreType.DMA((2,))]
    return remote_call(
        functools.partial(last_rows_kernel, lines, len(blocks), heads),
        3,
        [(array, "any") for array in (all_grads, attn, turned)]
        + [(array, "held") for array in (beta, mine, middle_grad, scale)]
        + [(block, "any") for block in blocks],
        [((2, rows, columns), low, "any"), ((1, columns), wide, "held")]
        + [(shape, low, "any") for shape in results],
        scratch,
    )


class Steps:
    def __init__(self, seqs, heads, span):
        self.seqs, self.heads, self.span = seqs, heads, span
        self.chains, self.chunks = seqs * heads, span // CHUNK

    def chain(self, step, when):
        if when == "first":
            return jnp.minimum(step, self.chains - 1)
        if when == "second":
            return jnp.maximum(step - self.chains, 0)
        return step % self.chains

    def rows(self, when, columns, place):
        def index(step):
            chain = self.chain(step, when)
            return chain // self.heads, place(chain % self.heads)

        return pl.BlockSpec((self.span, columns), index)

    def streams(self, when):
        return self.rows(when, 3 * CHUNK, lambda head: head)

    def head(self, when):
        return self.rows(when, CHUNK, lambda head: head)

    def gate(self, when):
        return self.rows(when, CHUNK, lambda head: 3 * self.heads + head)

    def logit(self, when):
        return self.rows(when, CHUNK, lambda head: 0)

    def taps(self, when):
        return pl.BlockSpec(
            (1, 3 * CONV, CHUNK), lambda step: (self.chain(step, when) % self.heads, 0, 0)
        )

    def blocks(self, when, columns=CHUNK):
        return pl.BlockSpec(
            (1, self.chunks, CHUNK, columns), lambda step: (self.chain(step, when), 0, 0, 0)
        )

    def few(self, when, columns):
        return pl.BlockSpec((1, 8, columns), lambda step: (self.chain(step, when), 0, 0))

    def whole(self, shape):
        return pl.BlockSpec(shape, lambda step: (0,) * len(shape), pipeline_mode=pl.Buffered(1))

    def call(self, body, identity, ins, outs, scratch, aliases=None):
        return pl.pallas_call(
            body,
            grid=(2 * self.chains,),
            in_specs=[spec for _, spec in ins],
            out_specs=[spec for _, _, spec in outs],
            out_shape=[jax.ShapeDtypeStruct(shape, dtype) for shape, dtype, _ in outs],
            scratch_shapes=scratch,
            input_output_aliases=aliases or {},
            compiler_params=pltpu.CompilerParams(
                vmem_limit_bytes=VMEM_BYTES,
                dimension_semantics=("arbitrary",),
                collective_id=identity,
                has_side_effects=True,
            ),
        )(*[array for array, _ in ins])


def delta_front(limit, raw, taps, logits, scale, moving, lines, seqs, heads, span):
    steps = Steps(seqs, heads, span)
    chains, chunks, size = steps.chains, steps.chunks, CHUNK
    squares, doubles = (chains, chunks, CHUNK, size), (chains, chunks, CHUNK, 2 * size)
    states, tails = (chains, size, size), (seqs, 16, 3 * heads * size)
    tokens = span // MATES
    anywhere = pl.BlockSpec(memory_space=pl.ANY)
    arrays = [array for array, _ in moving]
    ins = [
        (limit, pl.BlockSpec(memory_space=pltpu.SMEM)),
        (raw, anywhere),
        (raw, steps.streams("first")),
        (taps, steps.taps("first")),
        (logits, steps.logit("first")),
        (raw, steps.gate("second")),
        (scale, steps.whole((1, size))),
    ] + [(array, anywhere) for array in arrays]
    outs = [
        ((seqs * span, 3 * heads * size), low, steps.streams("first")),
        (squares, wide, steps.blocks("first")),
        (doubles, wide, steps.blocks("first", 2 * size)),
        (squares, wide, steps.blocks("first")),
        (states, wide, steps.whole(states)),
        (tails, low, steps.whole(tails)),
        (squares, wide, steps.blocks("second")),
        (squares, wide, steps.blocks("second")),
        ((seqs * span, heads * size), wide, steps.head("second")),
        ((seqs * span, heads * size), low, steps.head("second")),
        ((seqs, MATES, tokens, heads * size), low, anywhere),
        ((seqs, MATES) + arrays[0].shape, low, anywhere),
    ] + [(array.shape, low, anywhere) for array in arrays]
    scratch = [
        pltpu.VMEM((span + 16, 3 * size), wide),
        pltpu.VMEM(squares, wide),
        pltpu.VMEM(squares, wide),
        pltpu.VMEM(squares, wide),
        pltpu.VMEM(squares, wide),
        pltpu.VMEM(doubles, wide),
        pltpu.VMEM((chains, span, 3 * size), low),
        pltpu.VMEM(states, low),
        pltpu.VMEM(states, low),
        pltpu.VMEM(tails, low),
        pltpu.SemaphoreType.DMA((2, seqs)),
        pltpu.SemaphoreType.DMA((2, chains)),
        pltpu.VMEM((seqs, span, heads * size), low),
    ]
    scratch += ShareRows.scratch() + SwapBlocks.scratch()
    scratch += GatherLines.scratch(lines) * len(arrays)
    moves = tuple(part for _, part in moving)
    return steps.call(
        functools.partial(front_kernel, lines, heads, moves),
        4,
        ins,
        outs,
        scratch,
        {7 + index: 12 + index for index in range(len(arrays))},
    )


def delta_back(
    limit, raw, tails, taps, logits, scale, qkv, wu, maps, total, grad, mixed, solved, state, fresh,
    row_grad, mlp_partial, middle, summing, lines, seqs, heads, span,
):
    steps = Steps(seqs, heads, span)
    chains, chunks, size = steps.chains, steps.chunks, CHUNK
    squares, states = (chains, chunks, CHUNK, size), (chains, size, size)
    all_shape = (seqs * span, (4 * heads + 1) * size)
    anywhere = pl.BlockSpec(memory_space=pl.ANY)
    ins = [
        (limit, pl.BlockSpec(memory_space=pltpu.SMEM)),
        (raw, steps.streams("second")),
        (tails, steps.whole(tails.shape)),
        (taps, steps.taps("second")),
        (logits, steps.logit("second")),
        (raw, steps.gate("first")),
        (scale, steps.whole((1, size))),
        (qkv, steps.streams("both")),
        (wu, steps.blocks("both", 2 * size)),
        (maps, steps.blocks("first")),
        (total, steps.whole(states)),
        (grad, steps.head("first")),
        (mixed, steps.head("first")),
        (solved, steps.blocks("second")),
        (state, steps.blocks("second")),
        (fresh, steps.blocks("second")),
        (row_grad, anywhere),
        (mlp_partial, anywhere),
        (middle, steps.whole(middle.shape)),
    ] + [(array, anywhere) for array, _ in summing]
    outs = [
        (all_shape, low, steps.whole(all_shape)),
        ((chains, 8, size), wide, steps.few("first", size)),
        ((chains, 8, 3 * size), wide, steps.few("second", 3 * size)),
        ((seqs, MATES) + row_grad.shape, low, anywhere),
        ((seqs,) + row_grad.shape, low, anywhere),
    ]
    edges = (chains, 16, 3 * size)
    scratch = [
        pltpu.VMEM((span + 16, 3 * size), wide),
        pltpu.VMEM((span + 32, 3 * size), wide),
        pltpu.VMEM(squares, wide),
        pltpu.VMEM(squares, wide),
        pltpu.VMEM(squares, wide),
        pltpu.VMEM(squares, wide),
        pltpu.VMEM(squares, wide),
        pltpu.VMEM(states, low),
        pltpu.VMEM(states, low),
        pltpu.VMEM(edges, low),
        pltpu.VMEM(edges, wide),
        pltpu.VMEM(edges, low),
        pltpu.SemaphoreType.DMA((2, chains)),
        pltpu.SemaphoreType.DMA((2, chains)),
    ] + ShareRows.scratch()
    scratch += [pltpu.VMEM(row_grad.shape, low)] + [pltpu.SemaphoreType.DMA((1,))] * 3
    scratch += SumRows.scratch(*row_grad.shape)
    for array, (_, height) in summing:
        shape = (MATES, height, array.shape[3])
        scratch += SumLines.scratch(lines, shape)
        outs.append((shape, low, anywhere))
    return steps.call(
        functools.partial(back_kernel, lines, heads, tuple(part for _, part in summing)),
        5,
        ins,
        outs,
        scratch,
    )


def tiled_call(body, ins, wholes, outs):
    tile = 256

    def tall(shape):
        return pl.BlockSpec((tile, shape[1]), lambda step: (step, 0))

    def whole(array):
        return pl.BlockSpec(array.shape, lambda step: (0, 0), pipeline_mode=pl.Buffered(1))

    return pl.pallas_call(
        body,
        grid=(ins[0].shape[0] // tile,),
        in_specs=[tall(array.shape) for array in ins] + [whole(array) for array in wholes],
        out_specs=[tall(shape) for shape, _ in outs],
        out_shape=[jax.ShapeDtypeStruct(shape, dtype) for shape, dtype in outs],
        compiler_params=pltpu.CompilerParams(vmem_limit_bytes=VMEM_BYTES),
    )(*ins, *wholes)


def project(inputs, scale, weight, beta):
    rows, model_width = inputs.shape
    return tiled_call(
        project_kernel,
        (inputs,),
        (scale, weight, beta),
        [((rows, model_width), low), ((rows, weight.shape[1]), low), ((rows, beta.shape[0]), wide)],
    )


def held_call(body, ins, outs):
    held = pl.BlockSpec(memory_space=pltpu.VMEM)
    return pl.pallas_call(
        body,
        in_specs=[held] * len(ins),
        out_specs=[held] * len(outs),
        out_shape=[jax.ShapeDtypeStruct(shape, dtype) for shape, dtype in outs],
        compiler_params=pltpu.CompilerParams(vmem_limit_bytes=VMEM_BYTES),
    )(*ins)


def pack_kernel(
    heads, query, key, value, outgate, output, swish, upward, downward,
    attn_ref, output_ref, ups_ref, downs_ref,
):
    size = CHUNK
    width = heads * size
    units = downs_ref.shape[2]
    for mate in range(MATES):
        first = mate * width
        for head in range(heads):
            for stream, weight in enumerate((query, key, value)):
                lanes = (3 * head + stream) * size
                attn_ref[mate, :, lanes : lanes + size] = weight[
                    :, first + head * size : first + (head + 1) * size
                ].astype(low)
        attn_ref[mate, :, 3 * width : 4 * width] = outgate[:, first : first + width].astype(low)
        output_ref[mate] = output[first : first + width, :].T.astype(low)
        here = mate * units
        ups_ref[mate, :, :units] = swish[:, here : here + units].astype(low)
        ups_ref[mate, :, units:] = upward[:, here : here + units].astype(low)
        downs_ref[mate] = downward[here : here + units, :].T.astype(low)


def unpack_kernel(
    heads, attn, outs, ups_low, ups_high, downs,
    query, key, value, outgate, output, swish, upward, downward,
):
    size = CHUNK
    width = heads * size
    units = downs.shape[2]
    for mate in range(MATES):
        first = mate * width
        for head in range(heads):
            for stream, grad in enumerate((query, key, value)):
                lanes = (3 * head + stream) * size
                grad[:, first + head * size : first + (head + 1) * size] = attn[
                    mate, :, lanes : lanes + size
                ].astype(wide)
        outgate[:, first : first + width] = attn[mate, :, 3 * width : 4 * width].astype(wide)
        output[first : first + width, :] = outs[mate].astype(wide).T
        here = mate * units
        ups = over(ups_low[mate], ups_high[mate]).astype(wide)
        swish[:, here : here + units] = ups[:, :units]
        upward[:, here : here + units] = ups[:, units:]
        downward[here : here + units, :] = downs[mate].astype(wide).T


def cut_columns(weight):
    depth, columns = weight.shape
    return weight.reshape(depth, MATES, columns // MATES).transpose(1, 0, 2)


def join_columns(blocks):
    return blocks.transpose(1, 0, 2).reshape(blocks.shape[1], -1)


def gather_weights(blocks):
    return gather_lines(swap_blocks(blocks))


def scatter_grads(blocks):
    return swap_blocks(scatter_lines(blocks.astype(low))).astype(wide)


def on_device(
    block_input,
    lengths,
    attn_gain,
    query_weight,
    key_weight,
    value_weight,
    outgate_weight,
    beta_weight,
    conv_kernel,
    head_gain,
    output_weight,
    mlp_gain,
    swish_weight,
    upward_weight,
    downward_weight,
    out_grad,
):
    count = lax.axis_size("seq")
    lines = count // MATES
    core = lax.axis_index("tp")
    seq_count, tokens, model_width = block_input.shape
    depth = attn_gain.shape[0]
    gain_part = head_gain.shape[0]
    head_size = gain_part * count
    heads = beta_weight.shape[1] // MATES
    width = heads * head_size
    units = swish_weight.shape[1] // MATES

    conv_rows = -(-heads * 3 * CONV * gain_part // CHUNK)
    near = 1 < lines <= 4 and depth == CHUNK and conv_rows == BETA_ROW - CONV_ROW
    rows = seq_count * MATES * tokens
    span = MATES * tokens

    def in_rows(array):
        return jnp.pad(array, ((0, 0), (0, -array.shape[1] % 128)))

    def gains_of(attn, mlp, head):
        return jnp.concatenate([attn, mlp, in_rows(head)], axis=1)

    gains_cut = gains_of(attn_gain[None], mlp_gain[None], head_gain[None]).astype(low)
    conv_cut = in_rows(conv_kernel.astype(low).reshape(MATES, -1))
    beta_cut = beta_weight.astype(low).reshape(depth, MATES, heads).transpose(1, 2, 0)
    small_cut = jnp.concatenate(
        [jnp.broadcast_to(gains_cut, (MATES, gains_cut.shape[1])), conv_cut], axis=1
    )
    conv_start, conv_size = gains_cut.shape[1], heads * 3 * CONV * gain_part
    beta_start = small_cut.shape[1]
    small_cut = jnp.concatenate([small_cut, beta_cut.reshape(MATES, -1)], axis=1)
    small_size = small_cut.shape[1]
    small_cut = jnp.pad(small_cut, ((0, 0), (0, SMALL * 128 - small_size)))
    small_cut = small_cut.reshape(MATES, SMALL, 128)
    streams_end, gates_end = 3 * width, 4 * width
    if near:
        cuts = held_call(
            functools.partial(pack_kernel, heads),
            (
                query_weight, key_weight, value_weight, outgate_weight, output_weight,
                swish_weight, upward_weight, downward_weight,
            ),
            [
                ((MATES, depth, columns), low)
                for columns in (gates_end, width, 2 * units, units)
            ],
        )
        normed_turned, raw, logits, small, attn_full, output_full, ups_full, downward_full = first_call(
            block_input, (small_cut, *cuts), lines
        )
        ups_split = depth // 128 * 96
        front_moves = ((output_full, None), (ups_full, (0, ups_split)))
    else:
        streams_cut = jnp.stack(
            [
                w.astype(low).reshape(depth, MATES, heads, head_size)
                for w in (query_weight, key_weight, value_weight)
            ],
            axis=3,
        )
        streams_cut = streams_cut.transpose(1, 0, 2, 3, 4).reshape(MATES, depth, streams_end)
        cuts = (
            small_cut,
            jnp.concatenate([streams_cut, cut_columns(outgate_weight.astype(low))], axis=2),
            cut_columns(output_weight.astype(low).T),
            jnp.concatenate([cut_columns(w.astype(low)) for w in (swish_weight, upward_weight)], axis=2),
            cut_columns(downward_weight.astype(low).T),
        )
        input_rows = first_rows(block_input).reshape(rows, model_width)
        small, attn_full, output_full, ups_full, downward_full = (gather_weights(cut) for cut in cuts)
        front_moves = ((output_full, None),)
    attn_blocks = attn_full
    attn_full = attn_full.reshape(model_width, gates_end)
    small = small.reshape(count, SMALL * 128)
    attn_scale = small[:, :depth].reshape(1, model_width).astype(wide)
    mlp_scale = small[:, depth : 2 * depth].reshape(1, model_width).astype(wide)
    head_scale = small[:, 2 * depth : 2 * depth + gain_part].reshape(1, head_size).astype(wide)
    taps = (
        small[:, conv_start : conv_start + conv_size]
        .reshape(count, heads, 3, CONV, gain_part)
        .transpose(1, 2, 3, 0, 4)
        .reshape(heads, 3 * CONV, head_size)
        .astype(wide)
    )
    beta_rows = (
        small[:, beta_start:small_size]
        .reshape(count, heads, depth)
        .transpose(1, 0, 2)
        .reshape(heads, model_width)
    )
    beta_rows = jnp.pad(beta_rows, ((BETA_ROW, CHUNK - BETA_ROW - heads), (0, 0)))

    mine_low = pick(block_input, core)
    grad_mine = pick(out_grad, core)
    blocked = (seq_count, MATES, tokens, model_width)
    lengths_here = jnp.stack([pick(lengths, core), pick(lengths, 1 - core)])
    limit = lengths_here - line_of() * span

    if not near:
        flat_normed, raw, logits = project(input_rows, attn_scale, attn_full, beta_rows)
        normed_turned = flat_normed.T
    sizes_of = (lines, seq_count, heads, span)
    (
        qkv, solved, wu, maps, total, tails, state, fresh, mixed, gated, gathered, output_all, *moved
    ) = delta_front(limit, raw, taps, logits, head_scale, front_moves, *sizes_of)
    middle_moves = ((ups_full, None), (downward_full, None))
    if near:
        middle_moves = ((moved[1], (ups_split, depth - ups_split)), (downward_full, (0, depth)))
    middle, mlp_turned, grad_rows, acts, hidden, ups_full, downward_blocks = middle_rows(
        gathered, output_all, mine_low, mlp_scale, out_grad, middle_moves, lines
    )
    downward_grad = matmul(
        "rd,rf->df", grad_rows.reshape(rows, model_width), hidden
    ).astype(low)

    def cut_rows(grad):
        return grad.reshape(lines, MATES, depth, grad.shape[1])

    downward_grad = cut_rows(downward_grad)
    ups_rows = depth // 4
    middle_grad, mlp_gain_grad, attn_grad_mine, gated_grad, ups_grad, mlp_part, *summed = turn_rows(
        acts, grad_rows, ups_full, output_all, mlp_turned, hidden, downward_blocks, middle, grad_mine,
        mlp_scale, downward_grad if near else None, ups_rows, lines,
    )
    ups_grad = cut_rows(ups_grad)
    back_sums = ((ups_grad, (ups_rows, depth - ups_rows)),) if near else ()
    if near:
        downward_sum, ups_low = summed
    all_grads, head_gain_parts, taps_grad, attn_grad_rows, block_output, *summed = delta_back(
        limit, raw, tails, taps, logits, head_scale, qkv, wu, maps, total,
        gated_grad.reshape(rows, width), mixed, solved, state, fresh, attn_grad_mine, mlp_part.reshape(blocked), middle,
        back_sums, *sizes_of,
    )
    attn_grad_rows = attn_grad_rows.reshape(rows, model_width)
    output_grad = cut_rows(matmul("rd,rc->dc", attn_grad_rows, gated).astype(low))
    beta_grad = jnp.zeros((model_width, heads), low)
    if not near:
        attn_grads = matmul("dr,rc->dc", normed_turned, all_grads).astype(low)
        beta_grad = attn_grads[:, gates_end + BETA_ROW : gates_end + BETA_ROW + heads]
        attn_grads = cut_rows(attn_grads)

    conv_grad = (
        taps_grad[:, :CONV]
        .reshape(seq_count, heads, CONV, 3, count, gain_part)
        .sum(axis=0)
        .transpose(3, 0, 2, 1, 4)
        .reshape(count, -1)
    )

    def small_blocks(attn_gain_grad):
        gains = gains_of(
            attn_gain_grad.reshape(count, depth),
            mlp_gain_grad.reshape(count, depth),
            jnp.sum(head_gain_parts[:, 0], axis=0).reshape(count, gain_part),
        )
        beta = beta_grad.reshape(count, depth, heads).transpose(0, 2, 1).reshape(count, -1)
        flat = jnp.concatenate([gains.astype(low), in_rows(conv_grad.astype(low)), beta], axis=1)
        flat = jnp.pad(flat, ((0, 0), (0, SMALL * 128 - small_size)))
        return flat.reshape(lines, MATES, SMALL, 128)

    last_ins = (all_grads, attn_blocks, normed_turned, beta_rows, mine_low, middle_grad, attn_scale)
    if near:
        ups_high, = summed
        blocks = (small_blocks(jnp.zeros((1, model_width), wide)), output_grad)
        input_grad, _, small_sum, output_sum, attn_sum = last_rows(*last_ins, blocks, lines, heads)
        grads = held_call(
            functools.partial(unpack_kernel, heads),
            (attn_sum, output_sum, ups_low, ups_high, downward_sum),
            [
                (w.shape, wide)
                for w in (
                    query_weight, key_weight, value_weight, outgate_weight, output_weight,
                    swish_weight, upward_weight, downward_weight,
                )
            ],
        )
        small_sum = small_sum.reshape(MATES, SMALL * 128).astype(wide)
        gains_sum = jnp.sum(small_sum[:, :conv_start], axis=0)
    else:
        input_grad, attn_gain_grad = last_rows(*last_ins, (), lines, heads)
        small_sum, attn_sum, output_sum, ups_sum, downward_sum = (
            scatter_grads(block)
            for block in (
                small_blocks(attn_gain_grad), attn_grads[..., :gates_end], output_grad, ups_grad, downward_grad
            )
        )
        small_sum = small_sum.reshape(MATES, SMALL * 128)
        gains_sum = jnp.sum(small_sum[:, :conv_start], axis=0)
        gains_sum = gains_sum + other_core(gains_sum)
        streams_sum = (
            attn_sum[:, :, :streams_end]
            .reshape(MATES, depth, heads, 3, head_size)
            .transpose(3, 1, 0, 2, 4)
            .reshape(3, depth, MATES * width)
        )
        grads = (
            streams_sum[0],
            streams_sum[1],
            streams_sum[2],
            join_columns(attn_sum[:, :, streams_end:gates_end]),
            join_columns(output_sum).T,
            join_columns(ups_sum[:, :, :units]),
            join_columns(ups_sum[:, :, units:]),
            join_columns(downward_sum).T,
        )
    conv_sum = small_sum[:, conv_start : conv_start + conv_size]
    beta_sum = small_sum[:, beta_start:small_size].reshape(MATES * heads, depth).T
    return (
        block_output,
        input_grad,
        gains_sum[:depth],
        *grads[:4],
        beta_sum,
        conv_sum.reshape(MATES * heads, 3, CONV, gain_part),
        gains_sum[2 * depth : 2 * depth + gain_part],
        grads[4],
        gains_sum[depth : 2 * depth],
        *grads[5:],
    )


def solution(mesh):
    return jax.shard_map(
        on_device,
        mesh=mesh,
        in_specs=(
            P(None, "seq", None),
            P(),
            P("seq"),
            P("seq", "tp"),
            P("seq", "tp"),
            P("seq", "tp"),
            P("seq", "tp"),
            P("seq", "tp"),
            P("tp", None, None, "seq"),
            P("seq"),
            P("tp", "seq"),
            P("seq"),
            P("seq", "tp"),
            P("seq", "tp"),
            P("tp", "seq"),
            P(None, "seq", None),
        ),
        out_specs=(
            P(None, "seq", None),
            P(None, "seq", None),
            P("seq"),
            P("seq", "tp"),
            P("seq", "tp"),
            P("seq", "tp"),
            P("seq", "tp"),
            P("seq", "tp"),
            P("tp", None, None, "seq"),
            P("seq"),
            P("tp", "seq"),
            P("seq"),
            P("seq", "tp"),
            P("seq", "tp"),
            P("tp", "seq"),
        ),
        check_vma=False,
    )
```

```python
import functools

import jax
import jax.numpy as jnp
from jax import lax
from jax.experimental import pallas as pl
from jax.experimental.pallas import tpu as pltpu
from jax.sharding import PartitionSpec as P

CONV = 4
MATES = 4
SMALL = 16
CONV_ROW = 3
BETA_ROW = 5


epsilon = 1e-06
low = jnp.bfloat16
wide = jnp.float32


def other_core(value):
    return lax.ppermute(value, "tp", [(0, 1), (1, 0)])


def to_mate(value, flip):
    count = lax.axis_size("seq")
    return lax.ppermute(value, "seq", [(source, source ^ flip) for source in range(count)])


def mate_of():
    return lax.axis_index("seq") % MATES


def line_of():
    return lax.axis_index("seq") // MATES


def line_groups():
    lines = lax.axis_size("seq") // MATES
    return [[mate + MATES * line for line in range(lines)] for mate in range(MATES)]


def pick(blocks, index):
    return lax.dynamic_index_in_dim(blocks, index, 0, False)


def in_order(by_flip):
    mate = mate_of()
    out = jnp.zeros((MATES,) + by_flip[0].shape, by_flip[0].dtype)
    for flip, piece in enumerate(by_flip):
        out = lax.dynamic_update_index_in_dim(out, piece, mate ^ flip, 0)
    return out


def swap_blocks(blocks):
    mate = mate_of()
    pieces = [pick(blocks, mate)]
    for flip in range(1, MATES):
        pieces.append(to_mate(pick(blocks, mate ^ flip), flip))
    return in_order(pieces)


def gather_lines(block):
    return lax.all_gather(block, "seq", axis_index_groups=line_groups())


def scatter_lines(blocks):
    return lax.psum_scatter(blocks, "seq", scatter_dimension=0, axis_index_groups=line_groups())


def matmul(form, left, right):
    return jnp.einsum(form, left, right, preferred_element_type=wide)


CHUNK = 128
TOGETHER = 4
VMEM_BYTES = 60 * 1024 * 1024
NN = (((1,), (0,)), ((), ()))
NT = (((1,), (1,)), ((), ()))


def dot(left, right, dims):
    return lax.dot_general(left, right, dims, preferred_element_type=wide)


def pair(value):
    high = value.astype(low)
    return high, (value - high.astype(wide)).astype(low)


def side(left, right):
    return jnp.concatenate([left, right], axis=1)


def over(top, bottom):
    return jnp.concatenate([top, bottom], axis=0)


def nn(left, right):
    width = right[0].shape[1]
    both = side(*right)
    out = dot(side(*left), over(both, both), NN)
    return out[:, :width] + out[:, width:]


def nt(left, right):
    width = right[0].shape[0]
    out = dot(side(*left), over(side(right[0], right[0]), side(right[1], right[1])), NT)
    return out[:, :width] + out[:, width:]


def nn_wide(left, right):
    return dot(side(*left), over(right[0], right[0]), NN) + dot(left[0], right[1], NN)


def nn_low(left, right):
    return dot(side(*left), over(right, right), NN)


def low_nn(left, right):
    return dot(side(left, left), over(*right), NN)


def grid_of_rows():
    rows = lax.broadcasted_iota(jnp.int32, (CHUNK, CHUNK), 0)
    columns = lax.broadcasted_iota(jnp.int32, (CHUNK, CHUNK), 1)
    return rows, columns


def inverse_of(strict):
    rows, columns = grid_of_rows()
    one = jnp.where(rows == columns, 1.0, 0.0).astype(wide)

    def joining(shift):
        upper = columns >> shift
        return ((rows >> shift) == upper + 1) & ((upper & 1) == 0)

    solved = [one - jnp.where(joining(0), s, 0.0) for s in strict]
    shift = 1
    while (1 << shift) < CHUNK:
        mask = joining(shift)
        pairs = [pair(d) for d in solved]
        crossed = [nn(pair(jnp.where(mask, s, 0.0)), p) for s, p in zip(strict, pairs)]
        solved = [d - nn(p, pair(c)) for d, p, c in zip(solved, pairs, crossed)]
        shift += 1
    return solved


def convolved(block, taps, stream):
    columns = block[:, stream * CHUNK : (stream + 1) * CHUNK]
    total = None
    for offset in range(CONV):
        first = 16 - (CONV - 1) + offset
        term = taps[stream * CONV + offset][None, :] * columns[first : first + CHUNK]
        total = term if total is None else total + term
    return total


def silu_parts(value):
    squash = jax.nn.sigmoid(value)
    return value * squash, squash * (1.0 + value * (1.0 - squash))


def live_here(lengths, place, seq, span):
    return lengths[(place.core + seq) % 2] - place.line * span


def live_rows(limit, start):
    rows = lax.broadcasted_iota(jnp.int32, (CHUNK, CHUNK), 0)
    return jnp.where(rows + start < limit, 1.0, 0.0).astype(wide)


def head_squash(logits, head):
    lanes = lax.broadcasted_iota(jnp.int32, logits.shape, 1)
    column = jnp.sum(jnp.where(lanes == BETA_ROW + head, logits, 0.0), axis=1, keepdims=True)
    return jax.nn.sigmoid(jnp.broadcast_to(column, logits.shape))


def front_kernel(
    lines, heads, moves, lengths_ref, raw_any, raw_ref, taps_ref, logit_ref, gate_ref, scale_ref, *rest,
):
    count = len(moves)
    outs = rest[count:]
    qkv_ref, solved_ref, wu_ref, map_ref, total_ref, tails_ref = outs[:6]
    state_ref, fresh_ref, mixed_ref, gated_ref, gathered, weights = outs[6:12]
    targets, scratch = outs[12 : 12 + count], outs[12 + count :]
    ext, offsets, maps, prefixes, locals_, wus, qkvs, enters, leaves, tails = scratch[:10]
    tail_sems, state_sems, gateds = scratch[10:13]
    scratch = scratch[13:]
    step = pl.program_id(0)
    chains, chunks = maps.shape[0], maps.shape[1]
    span = chunks * CHUNK
    head_size = CHUNK
    streams = 3 * heads * head_size
    place = Place()
    tokens = gathered.shape[2]
    share = ShareRows(place, targets[0], weights, scratch[:3])
    swap = SwapBlocks(
        place,
        lambda slot, mate: gateds.at[slot, pl.ds(pl.multiple_of(mate * tokens, 16), tokens)],
        gathered,
        scratch[3:6],
    )
    gathers = [
        GatherLines(place, None, target, scratch[6 + 6 * index : 12 + 6 * index], moves[index])
        for index, target in enumerate(targets)
        if moves[index]
    ]
    below, above = place.line > 0, place.line < lines - 1
    rows, columns = grid_of_rows()
    identity = jnp.where(rows == columns, 1.0, 0.0).astype(wide)

    def tail(seq):
        return pltpu.make_async_remote_copy(
            src_ref=raw_any.at[pl.ds((seq + 1) * span - 16, 16), pl.ds(0, streams)],
            dst_ref=tails.at[seq],
            send_sem=tail_sems.at[0, seq],
            recv_sem=tail_sems.at[1, seq],
            device_id=place.lines_away(1),
            device_id_type=MESH,
        )

    def state_copy(chain):
        return pltpu.make_async_remote_copy(
            src_ref=leaves.at[chain],
            dst_ref=enters.at[chain],
            send_sem=state_sems.at[0, chain],
            recv_sem=state_sems.at[1, chain],
            device_id=place.lines_away(1),
            device_id_type=MESH,
        )

    seqs = chains // heads

    @pl.when(step == 0)
    def _():
        meet(place, lines=lines, cores=True)
        for seq in range(seqs):
            pl.when(above)(tail(seq).start)
        for gather in gathers:
            gather.leave(False)
        share.begin_half(False)
        share.begin_half(True)
        share.begin_rest()
        for seq in range(seqs):

            @pl.when(below)
            def _(seq=seq):
                tail(seq).wait_recv()

            @pl.when(place.line == 0)
            def _(seq=seq):
                tails[seq] = jnp.zeros(tails.shape[1:], low)

        tails_ref[...] = tails[...]

    def form(chain):
        seq, head = chain // heads, chain % heads
        ext[:16] = tails[seq, :, pl.ds(pl.multiple_of(head * 3 * head_size, 128), 3 * head_size)].astype(wide)
        ext[16:] = raw_ref[...].astype(wide)
        taps = taps_ref[0]
        limit = live_here(lengths_ref, place, seq, span)

        def group(index, carry):
            first = index * TOGETHER
            parts = []
            for number in range(TOGETHER):
                start = pl.multiple_of((first + number) * CHUNK, CHUNK)
                block = ext[pl.ds(start, CHUNK + 16)]
                query = jax.nn.silu(convolved(block, taps, 0))
                key = jax.nn.silu(convolved(block, taps, 1))
                value = jax.nn.silu(convolved(block, taps, 2)).astype(low)
                query = query * lax.rsqrt(jnp.sum(query * query, axis=1, keepdims=True) + epsilon)
                query = (query * head_size ** (-0.5)).astype(low)
                key = key * lax.rsqrt(jnp.sum(key * key, axis=1, keepdims=True) + epsilon)
                key = key.astype(low)
                beta = head_squash(logit_ref[pl.ds(start, CHUNK)], head) * live_rows(limit, start)
                together = jnp.concatenate([query, key, value], axis=1)
                qkv_ref[pl.ds(start, CHUNK)] = together
                qkvs[chain, pl.ds(start, CHUNK)] = together
                parts.append((key, value, beta))
            strict = [
                jnp.where(rows > columns, beta * dot(key, key, NT), 0.0) for key, _, beta in parts
            ]
            solved = inverse_of(strict)
            for number in range(TOGETHER):
                key, value, beta = parts[number]
                solved_ref[0, first + number] = solved[number]
                weighted = pair(solved[number] * beta.T)
                both = nn_low(weighted, side(key, value))
                wu_ref[0, first + number] = both
                wus[chain, first + number] = both
                moved = low_nn(key.T, pair(both))
                step_map = identity - moved[:, :head_size]
                map_ref[0, first + number] = step_map
                maps[chain, first + number] = step_map
                offsets[chain, first + number] = moved[:, head_size:]
            return carry

        lax.fori_loop(0, chunks // TOGETHER, group, 0)

    @pl.when(step < chains)
    def _():
        form(step)

    @pl.when(step == chains - 2)
    def _():
        for gather in gathers:
            gather.onwards(1)

    @pl.when(step == chains - 1)
    def _():
        start = side(identity, jnp.zeros_like(identity))

        def advance(chunk, states):
            out = []
            for index in range(chains):
                state = states[index]
                prefixes[index, chunk] = state[:, :head_size]
                locals_[index, chunk] = state[:, head_size:]
                moved = nn_wide(pair(maps[index, chunk]), pair(state))
                out.append(
                    side(moved[:, :head_size], moved[:, head_size:] + offsets[index, chunk])
                )
            return tuple(out)

        ends = lax.fori_loop(0, chunks, advance, (start,) * chains)

        @pl.when(place.line == 0)
        def _():
            enters[...] = jnp.zeros_like(enters)

        for index in range(chains):
            pl.when(below)(state_copy(index).wait_recv)
            total_ref[index] = ends[index][:, :head_size]
            leaving = nn_low(pair(ends[index][:, :head_size]), enters[index])
            leaves[index] = (leaving + ends[index][:, head_size:]).astype(low)
            pl.when(above)(state_copy(index).start)
        share.forward()

    def outputs(chain):
        enter = enters[chain]
        scale = scale_ref[...]

        def group(index, carry):
            for number in range(TOGETHER):
                chunk = index * TOGETHER + number
                start = pl.multiple_of(chunk * CHUNK, CHUNK)
                here = pl.ds(start, CHUNK)
                state = nn_low(pair(prefixes[chain, chunk]), enter) + locals_[chain, chunk]
                state_ref[0, chunk] = state
                states = pair(state)
                both = wus[chain, chunk]
                fresh = both[:, head_size:] - nn(pair(both[:, :head_size]), states)
                fresh_ref[0, chunk] = fresh
                query = qkvs[chain, here, :head_size]
                key = qkvs[chain, here, head_size : 2 * head_size]
                scores = jnp.where(rows >= columns, dot(query, key, NT), 0.0)
                mixed = low_nn(query, states) + nn(pair(scores), pair(fresh))
                mixed_ref[here] = mixed
                inverse = lax.rsqrt(jnp.mean(mixed * mixed, axis=1, keepdims=True) + epsilon)
                normed = mixed * inverse * scale
                gated = (normed * jax.nn.silu(gate_ref[here].astype(wide))).astype(low)
                gated_ref[here] = gated
                lanes = pl.ds(pl.multiple_of(chain % heads * head_size, 128), head_size)
                gateds[chain // heads, here, lanes] = gated
            return carry

        lax.fori_loop(0, chunks // TOGETHER, group, 0)

    @pl.when(step >= chains)
    def _():
        outputs(step - chains)

    @pl.when(step == chains + heads - 1)
    def _():
        swap.begin(0)
        share.forward_far()
        for gather in gathers:
            gather.onwards(2)

    @pl.when(step == 2 * chains - 1)
    def _():
        swap.begin(1)
        for gather in gathers:
            for number in range(3, lines):
                gather.onwards(number)
        for gather in gathers:
            gather.finish_lines()
        share.finish()
        swap.finish()
        for seq in range(seqs):
            pl.when(above)(tail(seq).wait_send)
        for chain in range(chains):
            pl.when(above)(state_copy(chain).wait_send)


def back_kernel(
    lines, heads, parts, lengths_ref, raw_ref, tails_ref, taps_ref, logit_ref, gate_ref, scale_ref, qkv_ref,
    wu_ref, map_ref, total_ref, grad_ref, mixed_ref, solved_ref, state_ref, fresh_in_ref, row_grad, mlp_partial,
    middle_ref, *rest,
):
    count = len(parts)
    blocks, rest = rest[:count], rest[count:]
    all_ref, gain_ref, taps_grad_ref, row_grads, block_output = rest[:5]
    results, scratch = rest[5 : 5 + count], rest[5 + count :]
    ext, pre_grads, maps, sources, out_grads, fresh_grads, leaving, leaves, enters = scratch[:9]
    halos, edges, returned, halo_sems, state_sems = scratch[9:14]
    share_scratch, scratch = scratch[14:17], scratch[17:]
    low_output, out_sems = scratch[0], scratch[1:4]
    outs_scratch, scratch = scratch[4:11], scratch[11:]
    step = pl.program_id(0)
    chains, chunks = maps.shape[0], maps.shape[1]
    span = chunks * CHUNK
    head_size = CHUNK
    streams = 3 * heads * head_size
    place = Place()
    sums = [
        SumLines(place, blocks[index], results[index], scratch[7 * index : 7 * index + 7], first)
        for index, (first, _) in enumerate(parts)
    ]
    share = ShareRows(place, row_grad, row_grads, share_scratch)
    outs = SumRows(place, mlp_partial, outs_scratch)
    to_sibling = sender(out_sems[:2])(
        0, low_output, block_output.at[place.core], place.sibling
    )
    to_self = pltpu.make_async_copy(low_output, block_output.at[place.core], out_sems[2].at[0])
    below, above = place.line > 0, place.line < lines - 1
    rows, columns = grid_of_rows()

    def halo(chain):
        return pltpu.make_async_remote_copy(
            src_ref=halos.at[chain],
            dst_ref=returned.at[chain],
            send_sem=halo_sems.at[0, chain],
            recv_sem=halo_sems.at[1, chain],
            device_id=place.lines_away(-1),
            device_id_type=MESH,
        )

    def state_copy(chain):
        return pltpu.make_async_remote_copy(
            src_ref=enters.at[chain],
            dst_ref=leaves.at[chain],
            send_sem=state_sems.at[0, chain],
            recv_sem=state_sems.at[1, chain],
            device_id=place.lines_away(-1),
            device_id_type=MESH,
        )

    @pl.when(step == 0)
    def _():
        meet(place, far=bool(parts), lines=lines)
        share.begin_half(False)
        share.begin_half(True)
        share.begin_rest()
        outs.begin()
        for each in sums:
            each.begin()
        for each in sums:
            each.wait_loads()
            each.round(1)

    def turn(chain):
        scale = scale_ref[...]

        def group(index, gain):
            for number in range(TOGETHER):
                chunk = index * TOGETHER + number
                start = pl.multiple_of(chunk * CHUNK, CHUNK)
                here = pl.ds(start, CHUNK)
                grad, mixed = grad_ref[here].astype(wide), mixed_ref[here]
                silu_gate, slope = silu_parts(gate_ref[here].astype(wide))
                inverse = lax.rsqrt(jnp.mean(mixed * mixed, axis=1, keepdims=True) + epsilon)
                unit = mixed * inverse
                gate_grad = (grad * unit * scale * slope).astype(low)
                there = pl.ds(pl.multiple_of(chain // heads * span + start, CHUNK), CHUNK)
                lanes = pl.ds(pl.multiple_of(streams + chain % heads * head_size, 128), head_size)
                all_ref[there, lanes] = gate_grad
                passed = grad * silu_gate
                gain = gain + jnp.sum(passed * unit, axis=0, keepdims=True)
                scaled = passed * scale
                mixed_grad = inverse * (
                    scaled - unit * inverse * jnp.mean(scaled * mixed, axis=1, keepdims=True)
                )
                out_grads[chain, chunk] = mixed_grad
                query, key = qkv_ref[here, :head_size], qkv_ref[here, head_size : 2 * head_size]
                scores = jnp.where(rows >= columns, dot(query, key, NT), 0.0)
                turned = jnp.where(rows <= columns, dot(key, query, NT), 0.0)
                fresh_grads[chain, chunk] = dot(turned.astype(low), mixed_grad.astype(low), NN)
                reading = query.astype(wide) - dot(
                    scores.astype(low), wu_ref[0, chunk, :, :head_size].astype(low), NN
                )
                sources[chain, chunk] = dot(mixed_grad.T.astype(low), reading.astype(low), NN)
                maps[chain, chunk] = map_ref[0, chunk]
            return gain

        gain = lax.fori_loop(0, chunks // TOGETHER, group, jnp.zeros((1, head_size), wide))
        gain_ref[0] = jnp.broadcast_to(gain, (8, head_size))

    @pl.when(step == 1)
    def _():
        outs.send_far()

    @pl.when(step == 2)
    def _():
        outs.send_near()

    @pl.when(step < chains)
    def _():
        turn(step)

    @pl.when(step == chains - 1)
    def _():
        def advance(number, states):
            chunk = chunks - 1 - number
            return tuple(
                nn(pair(states[index]), pair(maps[index, chunk])) + sources[index, chunk]
                for index in range(chains)
            )

        ends = lax.fori_loop(
            0, chunks, advance, (jnp.zeros((head_size, head_size), wide),) * chains
        )

        @pl.when(place.line == lines - 1)
        def _():
            leaves[...] = jnp.zeros_like(leaves)

        for index in range(chains):
            pl.when(above)(state_copy(index).wait_recv)
            entering = low_nn(leaves[index], pair(total_ref[index]))
            enters[index] = (entering + ends[index]).astype(low)
            pl.when(below)(state_copy(index).start)

        def again(number, states):
            chunk = chunks - 1 - number
            out = []
            for index in range(chains):
                leaving[index, chunk] = states[index]
                out.append(
                    nn(pair(states[index]), pair(maps[index, chunk])) + sources[index, chunk]
                )
            return tuple(out)

        lax.fori_loop(
            0, chunks, again, tuple(leaves[index].astype(wide) for index in range(chains))
        )
        for each in sums:
            each.round(2)

    def unwind(chain):
        seq, head = chain // heads, chain % heads
        ext[:16] = tails_ref[seq, :, pl.ds(pl.multiple_of(head * 3 * head_size, 128), 3 * head_size)].astype(wide)
        ext[16:] = raw_ref[...].astype(wide)
        taps = taps_ref[0]
        limit = live_here(lengths_ref, place, seq, span)
        pre_grads[:16] = jnp.zeros((16, 3 * head_size), wide)
        pre_grads[span + 16 :] = jnp.zeros((16, 3 * head_size), wide)

        def one(chunk):
            start = pl.multiple_of(chunk * CHUNK, CHUNK)
            here = pl.ds(start, CHUNK)
            query = qkv_ref[here, :head_size]
            key = qkv_ref[here, head_size : 2 * head_size]
            value = qkv_ref[here, 2 * head_size :]
            live = live_rows(limit, start)
            squash = head_squash(logit_ref[here], head)
            beta = squash * live
            grads = out_grads[chain, chunk].astype(low)
            fresh = fresh_in_ref[0, chunk].astype(low)
            state = state_ref[0, chunk].astype(low)
            leave = leaving[chain, chunk].astype(low)
            both = wu_ref[0, chunk].astype(low)
            fresh_grad = fresh_grads[chain, chunk] + dot(key, leave, NT)
            score_grad = jnp.where(rows >= columns, dot(grads, fresh, NT), 0.0)
            turned_grad = jnp.where(rows <= columns, dot(fresh, grads, NT), 0.0)
            query_grad = dot(
                side(grads, score_grad.astype(low)), over(state.T, key), NN
            )
            key_grad = dot(side(turned_grad.astype(low), fresh), over(query, leave), NN)
            wkey_grad = -dot(fresh_grad.astype(low), state, NT)
            solved = solved_ref[0, chunk].T.astype(low)
            right_grad = dot(solved, side(wkey_grad, fresh_grad).astype(low), NN)
            system_grad = dot(right_grad.astype(low), both, NT)
            system_grad = jnp.where(rows > columns, -system_grad, 0.0)
            gram = dot(key, key, NT)
            gram_grad = beta * system_grad
            key_grad = key_grad + dot((gram_grad + gram_grad.T).astype(low), key, NN)
            key_right, value_right = right_grad[:, :head_size], right_grad[:, head_size:]
            key_grad = key_grad + beta * key_right
            value_grad = beta * value_right
            beta_grad = jnp.sum(
                key_right * key.astype(wide) + value_right * value.astype(wide) + system_grad * gram,
                axis=1,
                keepdims=True,
            )
            lanes = lax.broadcasted_iota(jnp.int32, (CHUNK, head_size), 1)
            logit_grad = jnp.where(
                lanes == BETA_ROW + head, beta_grad * (live * squash * (1.0 - squash)), 0.0
            ).astype(low)

            there = pl.ds(pl.multiple_of(seq * span + start, CHUNK), CHUNK)
            last_lanes = pl.ds(streams + heads * head_size, head_size)

            @pl.when(head == 0)
            def _():
                all_ref[there, last_lanes] = logit_grad

            @pl.when(head > 0)
            def _():
                all_ref[there, last_lanes] = all_ref[there, last_lanes] + logit_grad

            block = ext[pl.ds(start, CHUNK + 16)]
            grads_pre = []
            for stream, grad in enumerate((query_grad, key_grad, value_grad)):
                act, slope = silu_parts(convolved(block, taps, stream))
                if stream < 2:
                    inverse = lax.rsqrt(jnp.sum(act * act, axis=1, keepdims=True) + epsilon)
                    inner = jnp.sum(act * grad, axis=1, keepdims=True)
                    grad = inverse * (grad - act * (inverse * inverse * inner))
                    if stream == 0:
                        grad = grad * head_size ** (-0.5)
                grads_pre.append(grad * slope)
            pre_grads[pl.ds(start + 16, CHUNK)] = jnp.concatenate(grads_pre, axis=1)

        def group(index, carry):
            for number in range(TOGETHER):
                one(index * TOGETHER + number)
            return carry

        lax.fori_loop(0, chunks // TOGETHER, group, 0)

        def back(block):
            parts = []
            for stream in range(3):
                part = block[:, stream * head_size : (stream + 1) * head_size]
                total = None
                for offset in range(CONV):
                    first = CONV - 1 - offset
                    term = taps[stream * CONV + offset][None, :] * part[first : first + CHUNK]
                    total = term if total is None else total + term
                parts.append(total)
            return jnp.concatenate(parts, axis=1)

        lanes = pl.ds(pl.multiple_of(head * 3 * head_size, 128), 3 * head_size)

        def finish(chunk, totals):
            start = pl.multiple_of(chunk * CHUNK, CHUNK)
            block = pre_grads[pl.ds(start + 16, CHUNK + 16)]
            grad = back(block)
            there = pl.ds(pl.multiple_of(seq * span + start, CHUNK), CHUNK)
            all_ref[there, lanes] = grad.astype(low)
            edges[chain] = grad[CHUNK - 16 :]
            before = ext[pl.ds(start, CHUNK + 16)]
            pre = block[:CHUNK]
            out = []
            for offset in range(CONV):
                first = 16 - (CONV - 1) + offset
                term = jnp.sum(pre * before[first : first + CHUNK], axis=0, keepdims=True)
                out.append(totals[offset] + term)
            return tuple(out)

        zero = jnp.zeros((1, 3 * head_size), wide)
        totals = lax.fori_loop(0, chunks, finish, (zero,) * CONV)
        for offset in range(CONV):
            taps_grad_ref[0, offset : offset + 1] = totals[offset]
        halos[chain] = back(pre_grads[: CHUNK + 32])[:16].astype(low)
        pl.when(below)(halo(chain).start)

    @pl.when(step >= chains)
    def _():
        unwind(step - chains)

    @pl.when(step == chains)
    def _():
        share.forward()

    @pl.when(step == chains + 1)
    def _():
        outs.send_relayed()

    @pl.when(step == chains + 2)
    def _():
        share.forward_far()
        for each in sums:
            each.round(3)

    @pl.when(step == chains + 3)
    def _():
        outs.wait_half(False)
        outs.wait_half(True)

        def out_body(here):
            low_output[here] = (middle_ref[here] + outs.total(here)).astype(low)

        row_steps(0, low_output.shape[0], out_body)
        to_sibling.start()
        to_self.start()

    @pl.when(step == 2 * chains - 1)
    def _():
        for each in sums:
            for number in range(4, lines):
                each.round(number)
            each.exchange()
        for chain in range(chains):
            seq, head = chain // heads, chain % heads
            last = pl.ds((seq + 1) * span - 16, 16)
            lanes = pl.ds(head * 3 * head_size, 3 * head_size)

            @pl.when(above)
            def _(chain=chain, last=last, lanes=lanes):
                halo(chain).wait_recv()
                all_ref[last, lanes] = (edges[chain] + returned[chain].astype(wide)).astype(low)

        for chain in range(chains):
            pl.when(below)(halo(chain).wait_send)
        for chain in range(chains):
            pl.when(below)(state_copy(chain).wait_send)
        share.finish()
        outs.finish()
        to_self.wait()
        to_sibling.wait()
        for each in sums:
            each.finish()


def project_kernel(input_ref, scale_ref, weight_ref, beta_ref, normed_ref, raw_ref, logit_ref):
    value = input_ref[...].astype(wide)
    normed = (value * inverse_rms(value) * scale_ref[...]).astype(low)
    normed_ref[...] = normed
    raw_ref[...] = dot(normed, weight_ref[...], NN).astype(low)
    logit_ref[...] = dot(normed, beta_ref[...], NT)


MESH = pl.DeviceIdType.MESH
STEP = 16


class Place:
    def __init__(self):
        self.seq = lax.axis_index("seq")
        self.core = lax.axis_index("tp")
        self.mate = self.seq % MATES
        self.line = self.seq // MATES
        x, y = self.mate % 2, self.mate // 2
        self.x = 2 * y + (1 - x)
        self.y = 2 * (1 - y) + x
        self.far = 2 * (1 - y) + (1 - x)
        self.base = self.seq - self.mate

    def of(self, mate, other=0):
        return (self.base + mate, 1 - self.core if other else self.core)

    @property
    def sibling(self):
        return (self.seq, 1 - self.core)

    def lines_away(self, step):
        return (self.seq + step * MATES, self.core)


def meet(place, far=False, lines=0, cores=False, straight=False):
    barrier = pltpu.get_barrier_semaphore()
    partners = [place.of(place.x), place.of(place.y), place.sibling]
    if far or cores:
        partners.append(place.of(place.far))
    if cores:
        partners += [place.of(mate, 1) for mate in (place.x, place.y, place.far)]
    for partner in partners:
        pl.semaphore_signal(barrier, inc=1, device_id=partner, device_id_type=MESH)
    count = len(partners)
    if straight:
        for step in range(1, lines):
            line = (place.line + step) % lines
            pl.semaphore_signal(
                barrier,
                inc=1,
                device_id=(line * MATES + place.mate, place.core),
                device_id_type=MESH,
            )
        count = count + max(lines - 1, 0)
    elif lines > 1:
        below, above = place.line > 0, place.line < lines - 1

        @pl.when(below)
        def _():
            pl.semaphore_signal(
                barrier, inc=1, device_id=place.lines_away(-1), device_id_type=MESH
            )

        @pl.when(above)
        def _():
            pl.semaphore_signal(barrier, inc=1, device_id=place.lines_away(1), device_id_type=MESH)

        count = count + jnp.where(below, 1, 0) + jnp.where(above, 1, 0)
    pl.semaphore_wait(barrier, count)


def sender(sems):
    send, receive = sems

    def make(index, source, target, device):
        return pltpu.make_async_remote_copy(
            src_ref=source,
            dst_ref=target,
            send_sem=send.at[index],
            recv_sem=receive.at[index],
            device_id=device,
            device_id_type=MESH,
        )

    return make


def row_steps(first, last, body):
    def one(step, carry):
        body(pl.ds(pl.multiple_of(first + step * STEP, STEP), STEP))
        return carry

    lax.fori_loop(0, (last - first) // STEP, one, 0)


class SumRows:
    @staticmethod
    def scratch(rows, columns, computed=False):
        return [
            pltpu.VMEM((MATES, rows, columns), low),
            pltpu.VMEM((MATES, rows, columns), low),
            pltpu.VMEM((2, rows // 2, columns), low),
            pltpu.VMEM((2, rows, columns), low),
            pltpu.SemaphoreType.DMA((MATES,)),
            pltpu.SemaphoreType.DMA((10,)),
            pltpu.SemaphoreType.DMA((10,)),
        ] + [pltpu.VMEM((MATES, rows, columns), low)] * computed

    def __init__(self, place, partial, scratch, compute=None):
        self.place, self.partial, self.compute = place, partial, compute
        self.own, self.swapped, self.relay, self.arrived, self.local_sems, send, receive = scratch[:7]
        if compute:
            self.other = scratch[7]
        self.make = sender((send, receive))
        self.rows = self.own.shape[1]
        self.order = [place.far, place.x, place.y, place.mate]
        half, x, y = self.rows // 2, place.of(place.x), place.of(place.y)
        own, relay, arrived = self.own, self.relay, self.arrived
        self.far_low = self.make(4, own.at[0, :half], relay.at[0], y)
        self.far_high = self.make(5, own.at[0, half:], relay.at[1], x)
        self.x_high = self.make(6, own.at[1, half:], arrived.at[0, half:], x)
        self.y_low = self.make(7, own.at[2, :half], arrived.at[1, :half], y)
        self.x_low = self.make(8, own.at[1, :half], arrived.at[0, :half], x)
        self.y_high = self.make(9, own.at[2, half:], arrived.at[1, half:], y)
        self.swaps = [
            self.make(
                slot,
                self.other.at[slot] if compute else partial.at[1, mate],
                self.swapped.at[slot],
                place.sibling,
            )
            for slot, mate in enumerate(self.order)
        ]

    def load(self, slot):
        return pltpu.make_async_copy(
            self.partial.at[0, self.order[slot]], self.own.at[slot], self.local_sems.at[slot]
        )

    def begin(self):
        for slot, mate in enumerate(self.order):
            if self.compute:
                self.compute(1, mate, self.other, slot)
            else:
                self.load(slot).start()
            self.swaps[slot].start()

    def add(self, target, target_slot, source, source_slot, first, last, shift=0):
        def body(here):
            there = pl.ds(pl.multiple_of(here.start - shift, STEP), STEP) if shift else here
            target[target_slot, here] = (
                target[target_slot, here].astype(wide) + source[source_slot, there].astype(wide)
            ).astype(low)

        row_steps(first, last, body)

    def sum_cores(self, slot):
        if self.compute:
            self.compute(0, self.order[slot], self.own, slot)
        else:
            self.load(slot).wait()
        self.swaps[slot].wait_recv()
        self.add(self.own, slot, self.swapped, slot, 0, self.rows)

    def send_far(self):
        self.sum_cores(0)
        self.far_low.start()
        self.far_high.start()

    def send_near(self):
        self.sum_cores(1)
        self.x_high.start()
        self.sum_cores(2)
        self.y_low.start()

    def send_relayed(self):
        half = self.rows // 2
        self.far_low.wait_recv()
        self.add(self.own, 1, self.relay, 0, 0, half)
        self.x_low.start()
        self.far_high.wait_recv()
        self.add(self.own, 2, self.relay, 1, half, self.rows, shift=half)
        self.y_high.start()
        self.sum_cores(3)

    def wait_half(self, upper):
        if upper:
            self.x_high.wait_recv()
            self.y_high.wait_recv()
        else:
            self.x_low.wait_recv()
            self.y_low.wait_recv()

    def total(self, here):
        return (
            self.own[3, here].astype(wide)
            + self.arrived[0, here].astype(wide)
            + self.arrived[1, here].astype(wide)
        )

    def finish(self):
        for copy in self.swaps + [
            self.far_low, self.far_high, self.x_high, self.y_low, self.x_low, self.y_high,
        ]:
            copy.wait_send()


class ShareRows:
    @staticmethod
    def scratch():
        return [
            pltpu.SemaphoreType.DMA((1,)),
            pltpu.SemaphoreType.DMA((11,)),
            pltpu.SemaphoreType.DMA((11,)),
        ]

    def __init__(self, place, source, target, scratch):
        self.place, self.source, self.target = place, source, target
        self.local_sem, send, receive = scratch
        self.make = sender((send, receive))
        self.rows = target.shape[2]

    def copy(self, index):
        place, half = self.place, self.rows // 2
        lower, upper, whole = pl.ds(0, half), pl.ds(half, half), pl.ds(0, self.rows)
        x, y, sibling = place.of(place.x), place.of(place.y), place.sibling

        def own(rows, device, side=0):
            return self.source.at[rows], self.target.at[side, place.mate, rows], device

        def passed(mate, rows, device, side=0):
            return self.target.at[0, mate, rows], self.target.at[side, mate, rows], device

        return self.make(
            index,
            *(
                lambda: own(upper, y),
                lambda: own(upper, x),
                lambda: own(lower, x),
                lambda: own(lower, y),
                lambda: passed(place.x, lower, y),
                lambda: passed(place.y, upper, x),
                lambda: own(whole, sibling, 1),
                lambda: passed(place.x, whole, sibling, 1),
                lambda: passed(place.y, whole, sibling, 1),
                lambda: passed(place.far, lower, sibling, 1),
                lambda: passed(place.far, upper, sibling, 1),
            )[index](),
        )

    def local(self):
        return pltpu.make_async_copy(
            self.source, self.target.at[0, self.place.mate], self.local_sem.at[0]
        )

    def begin_half(self, upper):
        for index in (0, 1) if upper else (2, 3):
            self.copy(index).start()

    def begin_rest(self):
        self.local().start()
        self.copy(6).start()

    def forward(self):
        for came, then in ((2, 4), (0, 5), (1, 7), (3, 8)):
            self.copy(came).wait_recv()
            self.copy(then).start()

    def forward_far(self):
        for came, then in ((4, 9), (5, 10)):
            self.copy(came).wait_recv()
            self.copy(then).start()

    def finish(self, arrived=False):
        if not arrived:
            self.local().wait()
            for index in range(6, 11):
                self.copy(index).wait_recv()
        for index in range(11):
            self.copy(index).wait_send()


class GatherLines:
    @staticmethod
    def scratch(lines):
        return [
            pltpu.SemaphoreType.DMA((1,)),
            pltpu.SemaphoreType.DMA((3,)),
            pltpu.SemaphoreType.DMA((3,)),
            pltpu.SemaphoreType.DMA((lines, MATES)),
            pltpu.SemaphoreType.DMA((lines, MATES)),
            pltpu.SemaphoreType.DMA((lines, MATES)),
        ]

    def __init__(self, place, blocks, target, scratch, rows=None):
        self.place, self.blocks, self.target = place, blocks, target
        self.lines = target.shape[0]
        self.part = pl.ds(*(rows or (0, target.shape[2])))
        self.local_sem, send, receive, self.up_sem, self.down_sem, self.got = scratch
        self.make = sender((send, receive))
        self.order = [place.mate, place.x, place.y, place.far]

    def plane(self, slot):
        place, mate = self.place, self.order[slot]
        here = self.target.at[place.line, place.mate]
        if slot == 0:
            return pltpu.make_async_copy(self.blocks.at[mate], here, self.local_sem.at[0])
        return self.make(slot - 1, self.blocks.at[mate], here, place.of(mate))

    def begin(self):
        for slot in range(MATES):
            self.plane(slot).start()

    def arrive(self, slot):
        copy = self.plane(slot)
        copy.wait_recv() if slot else copy.wait()

    def hop(self, step, mate, direction):
        place = self.place
        line = place.line - step * direction
        piece = self.target.at[line, mate, self.part]
        sems = self.up_sem if direction > 0 else self.down_sem
        copy = pltpu.make_async_remote_copy(
            src_ref=piece,
            dst_ref=piece,
            send_sem=sems.at[step, mate],
            recv_sem=self.got.at[line, mate],
            device_id=place.lines_away(direction),
            device_id_type=MESH,
        )
        came = (line >= 0) & (line < self.lines)
        goes = (place.line < self.lines - 1) if direction > 0 else (place.line > 0)
        return copy, came, goes

    def leave(self, arriving=True):
        for slot, mate in enumerate(self.order):
            if arriving:
                self.arrive(slot)
            for direction in (1, -1):
                copy, _, goes = self.hop(0, mate, direction)
                pl.when(goes)(copy.start)

    def onwards(self, step):
        if step >= self.lines:
            return
        for mate in self.order:
            for direction in (1, -1):
                copy, came, goes = self.hop(step, mate, direction)
                pl.when(came)(copy.wait_recv)
                if step < self.lines - 1:
                    pl.when(came & goes)(copy.start)

    def finish_plane(self):
        for slot in range(1, MATES):
            self.plane(slot).wait_send()

    def finish_lines(self):
        for step in range(self.lines - 1):
            for mate in self.order:
                for direction in (1, -1):
                    copy, came, goes = self.hop(step, mate, direction)
                    pl.when(came & goes)(copy.wait_send)


class SwapBlocks:
    @staticmethod
    def scratch():
        return [
            pltpu.SemaphoreType.DMA((1,)),
            pltpu.SemaphoreType.DMA((2 * MATES,)),
            pltpu.SemaphoreType.DMA((2 * MATES,)),
        ]

    def __init__(self, place, piece, target, scratch):
        self.place, self.piece, self.target = place, piece, target
        self.local_sem, send, receive = scratch
        self.make = sender((send, receive))
        self.order = [place.far, place.x, place.y, place.mate]

    def copy(self, slot, index):
        place, mate = self.place, self.order[index]
        source, target = self.piece(slot, mate), self.target.at[slot, place.mate]
        if slot == 0 and index == MATES - 1:
            return pltpu.make_async_copy(source, target, self.local_sem.at[0]), True
        return self.make(slot * MATES + index, source, target, place.of(mate, slot)), False

    def begin(self, slot, index=None):
        for each in range(MATES) if index is None else (index,):
            self.copy(slot, each)[0].start()

    def finish(self):
        for slot in range(2):
            for index in range(MATES):
                self.copy(slot, index)[0].wait()


class SumLines:
    @staticmethod
    def scratch(lines, shape):
        return [
            pltpu.VMEM((lines,) + shape, low),
            pltpu.VMEM((2, max(lines - 1, 1)) + shape, low),
            pltpu.SemaphoreType.DMA((lines * MATES + 1,)),
            pltpu.SemaphoreType.DMA((2, lines, MATES)),
            pltpu.SemaphoreType.DMA((2, lines, MATES)),
            pltpu.SemaphoreType.DMA((3,)),
            pltpu.SemaphoreType.DMA((3,)),
        ]

    def __init__(self, place, blocks, result, scratch, first=0):
        self.place, self.blocks, self.result, self.first = place, blocks, result, first
        self.held, self.came, self.local_sems, self.send, self.got, send, receive = scratch
        self.lines = self.held.shape[0]
        self.make = sender((send, receive))
        self.order = [place.far, place.x, place.y, place.mate]

    def loads(self):
        lines, mates, height, width = self.held.shape
        if len(self.blocks.shape) == 4:
            return [
                pltpu.make_async_copy(
                    self.blocks.at[line, :, pl.ds(self.first, height)],
                    self.held.at[line],
                    self.local_sems.at[line],
                )
                for line in range(lines)
            ]
        return [
            pltpu.make_async_copy(
                self.blocks.at[:, pl.ds((line * mates + mate) * width, width)],
                self.held.at[line, mate],
                self.local_sems.at[line * mates + mate],
            )
            for line in range(lines)
            for mate in range(mates)
        ]

    def begin(self):
        for load in self.loads():
            load.start()

    def wait_loads(self):
        for load in self.loads():
            load.wait()

    def put_gains(self, gains):
        lines, mates, height, lanes = self.held.shape
        top = lax.broadcasted_iota(jnp.int32, (height, lanes), 0) == 0
        for line in range(lines):
            for mate in range(mates):
                first = (line * mates + mate) * lanes
                part = jnp.broadcast_to(gains[:, first : first + lanes], (height, lanes))
                self.held[line, mate] = jnp.where(
                    top, part, self.held[line, mate].astype(wide)
                ).astype(low)

    def add_top(self, other, count):
        lines, mates, height, lanes = self.held.shape
        top = lax.broadcasted_iota(jnp.int32, (height, lanes), 0) < count
        for line in range(lines):
            for mate in range(mates):
                own = self.held[line, mate].astype(wide)
                both = own + other[line, mate].astype(wide)
                self.held[line, mate] = jnp.where(top, both, own).astype(low)

    def copy(self, turn, way, mate):
        direction = 1 - 2 * way
        line = self.place.line + direction * (self.lines - turn)
        return line, pltpu.make_async_remote_copy(
            src_ref=self.held.at[line, mate],
            dst_ref=self.came.at[way, turn - 1, mate],
            send_sem=self.send.at[way, turn, mate],
            recv_sem=self.got.at[way, turn, mate],
            device_id=self.place.lines_away(direction),
            device_id_type=MESH,
        )

    def arrival(self, turn, way, mate):
        slot = self.came.at[way, turn - 1, mate]
        return pltpu.make_async_remote_copy(
            src_ref=slot,
            dst_ref=slot,
            send_sem=self.send.at[way, turn, mate],
            recv_sem=self.got.at[way, turn, mate],
            device_id=self.place.sibling,
            device_id_type=MESH,
        )

    def sends(self, turn, way):
        line = self.place.line
        return line <= turn - 1 if way == 0 else line >= self.lines - turn

    def inner(self, way):
        return self.place.line >= 1 if way == 0 else self.place.line <= self.lines - 2

    def add(self, line, way, turn, mate):
        def body(here):
            self.held[line, mate, here] = (
                self.held[line, mate, here].astype(wide)
                + self.came[way, turn - 1, mate, here].astype(wide)
            ).astype(low)

        row_steps(0, self.held.shape[2], body)

    def round(self, turn):
        if turn >= self.lines:
            return
        for mate in self.order:
            for way in (0, 1):
                line, copy = self.copy(turn, way, mate)

                @pl.when(self.sends(turn, way))
                def _(line=line, copy=copy, way=way, mate=mate):
                    if turn > 1:

                        @pl.when(self.inner(way))
                        def _():
                            self.arrival(turn - 1, way, mate).wait_recv()
                            self.add(line, way, turn - 1, mate)

                    copy.start()

    def plane(self, index):
        place, mate = self.place, self.order[index]
        return self.make(
            index, self.held.at[place.line, mate], self.result.at[place.mate], place.of(mate)
        )

    def local(self):
        place = self.place
        return pltpu.make_async_copy(
            self.held.at[place.line, place.mate],
            self.result.at[place.mate],
            self.local_sems.at[self.lines * MATES],
        )

    def exchange(self):
        for index, mate in enumerate(self.order):
            for way in (0, 1):
                if self.lines > 1:

                    @pl.when(self.inner(way))
                    def _(way=way, mate=mate):
                        self.arrival(self.lines - 1, way, mate).wait_recv()
                        self.add(self.place.line, way, self.lines - 1, mate)

            if index < 3:
                self.plane(index).start()
            else:
                self.local().start()

    def straight(self, step):
        line = (self.place.line + step) % self.lines
        return pltpu.make_async_remote_copy(
            src_ref=self.held.at[line],
            dst_ref=self.came.at[0, step - 1],
            send_sem=self.send.at[0, step, 0],
            recv_sem=self.got.at[0, step, 0],
            device_id=(line * MATES + self.place.mate, self.place.core),
            device_id_type=MESH,
        )

    def direct(self):
        for step in range(1, self.lines):
            self.straight(step).start()

    def exchange_direct(self):
        for step in range(1, self.lines):
            self.straight(step).wait_recv()
            for mate in range(MATES):
                self.add(self.place.line, 0, step, mate)
        for index in range(3):
            self.plane(index).start()
        self.local().start()

    def finish(self, direct=False):
        self.local().wait()
        for index in range(3):
            self.plane(index).wait()
        if direct:
            for step in range(1, self.lines):
                self.straight(step).wait_send()
            return
        for turn in range(1, self.lines):
            for way in (0, 1):
                for mate in self.order:
                    _, copy = self.copy(turn, way, mate)
                    pl.when(self.sends(turn, way))(copy.wait_send)


def remote_call(body, identity, ins, outs, scratch, aliases=None):
    anywhere = pl.BlockSpec(memory_space=pl.ANY)
    held = pl.BlockSpec(memory_space=pltpu.VMEM)
    return pl.pallas_call(
        body,
        in_specs=[anywhere if kind == "any" else held for _, kind in ins],
        out_specs=[anywhere if kind == "any" else held for _, _, kind in outs],
        out_shape=[jax.ShapeDtypeStruct(shape, dtype) for shape, dtype, _ in outs],
        scratch_shapes=scratch,
        input_output_aliases=aliases or {},
        compiler_params=pltpu.CompilerParams(
            vmem_limit_bytes=VMEM_BYTES, collective_id=identity, has_side_effects=True
        ),
    )(*[array for array, _ in ins])


def inverse_rms(value):
    return lax.rsqrt(jnp.mean(value * value, axis=1, keepdims=True) + epsilon)


def norm_back_rows(grad, source, scale):
    inverse = inverse_rms(source)
    scaled = grad * scale
    unit = source * inverse
    inner = jnp.mean(scaled * source, axis=1, keepdims=True)
    return inverse * (scaled - unit * (inverse * inner)), grad * unit


def load_weights(weights, held, sems):
    return [
        pltpu.make_async_copy(weights.at[slot, mate], held.at[slot, mate], sems.at[slot, mate])
        for slot in range(2)
        for mate in range(MATES)
    ]


def middle_kernel(lines, moves, gathered, weights, input_any, scale_ref, grad_any, *rest):
    place = Place()
    count = len(moves)
    middle_ref, turned_out, grads, acts_out, hidden_out = rest[count : count + 5]
    targets, scratch = rest[count + 5 : 2 * count + 5], rest[2 * count + 5 :]
    normed, held, weight_sems, all_normed, turned, ups, acts, hidden, out_sems, load_sems = scratch[:10]
    input_ref, scratch = scratch[10], scratch[11:]
    share = ShareRows(place, normed, all_normed, scratch[:3])
    other = ShareRows(place, grad_any.at[place.core], grads, scratch[3:6])
    gathers = [
        GatherLines(place, None, target, scratch[6 + 6 * index : 12 + 6 * index], moves[index])
        for index, target in enumerate(targets)
        if moves[index]
    ]
    meet(place, lines=lines if gathers else 0)
    loads = load_weights(weights, held, weight_sems)
    loads.append(pltpu.make_async_copy(input_any.at[place.core], input_ref, load_sems.at[2]))
    for load in loads:
        load.start()
    other.begin_half(False)
    other.begin_half(True)
    other.begin_rest()
    for gather in gathers[:1]:
        gather.leave(False)
    _, _, all_lines, _, depth, width = held.shape
    early = moves[0][0] if gathers else depth

    def load_ups(index):
        part = (pl.ds(0, early), pl.ds(early, depth - early))[index]
        return pltpu.make_async_copy(
            targets[0].at[:, :, part], ups.at[:, :, part], load_sems.at[index]
        )

    load_ups(0).start()
    for load in loads:
        load.wait()
    rows, model_width = normed.shape
    half = rows // 2
    height = MATES * depth
    some = max(1, 512 // height)

    def product(step, carry):
        columns = pl.ds(pl.multiple_of(step * some * height, 128), some * height)
        part = pl.ds(step * some, some)
        for first in (0, half):
            total = None
            for slot in range(2):
                for mate in range(MATES):
                    term = dot(
                        gathered[slot, mate, first : first + half],
                        held[slot, mate, part].reshape(some * height, width),
                        NT,
                    )
                    total = term if total is None else total + term
            here = pl.ds(first, half)
            middle_ref[here, columns] = input_ref[here, columns].astype(wide) + total
        return carry

    def body(here):
        middle = middle_ref[here]
        normed[here] = (middle * inverse_rms(middle) * scale_ref[...]).astype(low)

    lax.fori_loop(0, all_lines // some, product, 0)
    row_steps(0, half, body)
    share.begin_half(False)
    row_steps(half, rows, body)
    share.begin_half(True)
    share.begin_rest()
    for gather in gathers[:1]:
        gather.onwards(1)
    for gather in gathers[1:]:
        gather.leave(False)
    for gather in gathers[:1]:
        gather.onwards(2)
    share.forward()
    for gather in gathers[:1]:
        for number in range(3, lines):
            gather.onwards(number)
    if early < depth:
        load_ups(1).start()
    for gather in gathers[1:]:
        gather.onwards(1)
    other.forward()
    share.forward_far()
    share.finish()
    load_ups(0).wait()
    if early < depth:
        load_ups(1).wait()
    weight = ups[...].reshape(model_width, ups.shape[3])
    units = hidden.shape[2]
    outs = []
    for slot in range(2):
        for mate in range(MATES):
            index = slot * MATES + mate
            values = dot(all_normed[slot, mate], weight, NN)
            acts[index] = values.astype(low)
            gate, up = values[:, :units], values[:, units:]
            hidden[index] = (gate * jax.nn.sigmoid(gate) * up).astype(low)
            here = pl.ds(index * rows, rows)
            turned[:, here] = all_normed[slot, mate].T
            outs += [
                pltpu.make_async_copy(acts.at[index], acts_out.at[here], out_sems.at[0, index]),
                pltpu.make_async_copy(hidden.at[index], hidden_out.at[here], out_sems.at[1, index]),
                pltpu.make_async_copy(
                    turned.at[:, here], turned_out.at[:, here], out_sems.at[2, index]
                ),
            ]
            for out in outs[-3:]:
                out.start()
        if slot == 0:
            for gather in gathers[1:]:
                gather.onwards(2)
            other.forward_far()
    for number in range(3, lines):
        for gather in gathers[1:]:
            gather.onwards(number)
    for gather in gathers:
        gather.finish_lines()
    other.finish()
    for out in outs:
        out.wait()


def columns_in_steps(lines, depth, body):
    height = MATES * depth
    some = max(1, 512 // height)

    def one(step, carry):
        body(
            pl.ds(pl.multiple_of(step * some * height, 128), some * height),
            pl.ds(step * some, some),
            some * height,
        )
        return carry

    lax.fori_loop(0, lines // some, one, 0)


class Tiles:
    def __init__(self, source, target, held_in, held_out, sems, body):
        self.source, self.target, self.body = source, target, body
        self.held_in, self.held_out, self.sems = held_in, held_out, sems
        self.rows = held_in.shape[1]
        self.count = source.shape[0] // self.rows

    def load(self, tile):
        return pltpu.make_async_copy(
            self.source.at[pl.ds(tile * self.rows, self.rows)],
            self.held_in.at[tile % 2],
            self.sems.at[0, tile % 2],
        )

    def store(self, tile):
        return pltpu.make_async_copy(
            self.held_out.at[tile % 2],
            self.target.at[pl.ds(tile * self.rows, self.rows)],
            self.sems.at[1, tile % 2],
        )

    def begin(self):
        self.load(0).start()

    def run(self, first, last):
        for tile in range(first, last):
            self.load(tile).wait()
            if tile + 1 < self.count:
                self.load(tile + 1).start()
            if tile >= 2:
                self.store(tile - 2).wait()
            self.body(tile, self.held_in.at[tile % 2], self.held_out.at[tile % 2])
            self.store(tile).start()

    def finish(self):
        for tile in range(max(self.count - 2, 0), self.count):
            self.store(tile).wait()


def turn_rows_kernel(
    lines, parts, acts_any, grads_any, ups_any, weights, turned, hidden, downs_any, out_grad_any,
    middle_ref, scale_ref, *rest
):
    place = Place()
    blocks, rest = rest[: 1 if parts else 0], rest[1 if parts else 0 :]
    count = len(parts)
    middle_grad_ref, gain_ref, low_grad, gated_grads, ups_grad, mlp_part = rest[:6]
    results, scratch = rest[6 : 6 + count], rest[6 + count :]
    held, load_sems, sent, acts, ups, downs = scratch[:6]
    turned_in, grad_out, grad_sems, hidden_in, part_out, part_sems, unit_sems = scratch[6:13]
    grad_ref, scratch = scratch[13], scratch[14:]
    all_lines, _, depth, units = ups.shape
    tokens = low_grad.shape[0]

    def compute(side_of, mate, target, slot):
        first = pl.ds(pl.multiple_of((side_of * MATES + mate) * tokens, STEP), tokens)

        def step(columns, part, size):
            target[slot, :, columns] = dot(
                acts[first], ups[part].reshape(size, units), NT
            ).astype(low)

        columns_in_steps(all_lines, depth, step)

    def weight_grad(tile, tile_in, tile_out):
        found = dot(tile_in[...], acts[...], NN).astype(low)
        tile_out[...] = found
        if sums:
            each_line = MATES * depth // tokens
            for number in range(tokens // depth):
                mate = tile % each_line * (tokens // depth) + number
                sums[1].held[tile // each_line, mate] = found[
                    number * depth : number * depth + parts[1][1]
                ]

    def load_units(tile):
        here = pl.ds(tile * tokens, tokens)
        half = tile % 2
        return (
            pltpu.make_async_copy(
                grads_any.at[tile // MATES, tile % MATES], turned_in.at[half], unit_sems.at[0, half]
            ),
            pltpu.make_async_copy(acts_any.at[here], grad_out.at[half], unit_sems.at[1, half]),
        )

    def units_back():
        inner = downs.shape[0]
        for tile in range(2 * MATES):
            for load in load_units(tile):
                load.wait()
            if tile + 1 < 2 * MATES:
                for load in load_units(tile + 1):
                    load.start()
            grad = dot(turned_in[tile % 2], downs[...], NT)
            values = grad_out[tile % 2].astype(wide)
            gate, up = values[:, :inner], values[:, inner:]
            silu, slope = silu_parts(gate)
            here = pl.ds(tile * tokens, tokens)
            acts[here, :inner] = (grad * up * slope).astype(low)
            acts[here, inner:] = (grad * silu).astype(low)

    def back_down(tile, tile_in, tile_out):
        def step(columns, part, size):
            tile_out[:, columns] = dot(tile_in[...], downs[:, columns], NN).astype(low)

        columns_in_steps(all_lines, depth, step)

    grad_tiles = Tiles(turned, ups_grad, turned_in, grad_out, grad_sems, weight_grad)
    part_tiles = Tiles(hidden, mlp_part, hidden_in, part_out, part_sems, back_down)
    rows = SumRows(place, None, scratch[:8], compute)
    swap = SwapBlocks(place, lambda slot, mate: sent.at[slot, mate], gated_grads, scratch[8:11])
    sums = [
        SumLines(
            place,
            None if index else blocks[0],
            results[index],
            scratch[11 + 7 * index : 18 + 7 * index],
        )
        for index in range(count)
    ]
    meet(place, lines=lines if parts else 0, cores=True)
    if len(downs_any.shape) == 2:
        load_downs = [pltpu.make_async_copy(downs_any, downs, load_sems.at[3])]
    else:
        load_downs = [
            pltpu.make_async_copy(
                downs_any.at[line, mate],
                downs.at[:, pl.ds((line * MATES + mate) * depth, depth)],
                load_sems.at[3 + line * MATES + mate],
            )
            for line in range(lines)
            for mate in range(MATES)
        ]
    for load in load_downs:
        load.start()
    for load in load_units(0):
        load.start()
    for each in sums[:1]:
        each.begin()
    load_ups = pltpu.make_async_copy(ups_any, ups, load_sems.at[1])
    load_ups.start()
    load_grad = pltpu.make_async_copy(out_grad_any.at[place.core], grad_ref, load_sems.at[0])
    load_grad.start()

    def load_weight(slot):
        return pltpu.make_async_copy(weights.at[slot], held, load_sems.at[2])

    for each in sums[:1]:
        each.wait_loads()
        each.round(1)
    load_weight(0).start()
    part_tiles.begin()
    gain_ref[...] = jnp.zeros_like(gain_ref)
    for load in load_downs:
        load.wait()
    units_back()
    grad_tiles.begin()
    load_ups.wait()
    load_grad.wait()
    for each in sums[:1]:
        each.round(2)
    rows.begin()
    rows.send_far()
    rows.send_near()
    all_tiles = grad_tiles.count
    grad_tiles.run(0, all_tiles)
    for each in sums[1:]:
        each.round(1)
    rows.send_relayed()
    for each in sums[:1]:
        each.round(3)
    part_tiles.run(0, part_tiles.count // 2)
    for each in sums[1:]:
        each.round(2)
    rows.wait_half(False)
    rows.wait_half(True)

    def body(here):
        part, gains = norm_back_rows(rows.total(here), middle_ref[here], scale_ref[...])
        total = grad_ref[here].astype(wide) + part
        middle_grad_ref[here] = total
        low_grad[here] = total.astype(low)
        gain_ref[...] += jnp.sum(gains, axis=0, keepdims=True)

    row_steps(0, tokens, body)
    width = held.shape[-1]
    for slot in range(2):
        load_weight(slot).wait()
        for index, mate in enumerate(swap.order):
            weight = held[mate].reshape(all_lines * MATES * depth, width)
            sent[slot, mate] = dot(low_grad[...], weight, NN).astype(low)
            swap.begin(slot, index)
        if slot == 0:
            load_weight(1).start()
    rows.finish()
    for each in sums[1:]:
        each.round(3)
    for each in sums[:1]:
        each.exchange()
    part_tiles.run(part_tiles.count // 2, part_tiles.count)
    for each in sums[1:]:
        each.exchange()
    swap.finish()
    for tiles in (grad_tiles, part_tiles):
        tiles.finish()
    for each in sums:
        each.finish()


def last_rows_kernel(
    lines, pieces, heads, all_grads, attn_any, turned, input_any, beta_ref, middle_grad_ref, scale_ref, *rest
):
    place = Place()
    blocks, rest = rest[:pieces], rest[pieces:]
    input_grad, gain_ref = rest[:2]
    count = pieces + 1 if pieces else 0
    results, scratch = rest[2 : 2 + count], rest[2 + count :]
    low_grad, grads, attn, load_sems, input_ref = scratch[:5]
    scratch = scratch[1:]
    all_lines, _, depth, width = attn.shape
    tokens = low_grad.shape[0]

    def compute(side_of, mate, target, slot):
        first = pl.ds(pl.multiple_of((side_of * MATES + mate) * tokens, STEP), tokens)

        def step(columns, part, size):
            total = dot(grads[first, :width], attn[part].reshape(size, width), NT)
            total = total + dot(grads[first, width:], beta_ref[:, columns], NN)
            target[slot, :, columns] = total.astype(low)

        columns_in_steps(all_lines, depth, step)

    meet(place, far=bool(pieces), lines=lines if pieces else 0, straight=True)
    rows = SumRows(place, None, scratch[4:12], compute)
    make = sender(scratch[12:14])
    scratch = scratch[14:]
    sums = [
        SumLines(
            place,
            blocks[index] if index < pieces else None,
            results[index],
            scratch[7 * index : 7 * index + 7],
        )
        for index in range(count)
    ]
    loads = [
        pltpu.make_async_copy(all_grads, grads, load_sems.at[0]),
        pltpu.make_async_copy(attn_any, attn, load_sems.at[1]),
        pltpu.make_async_copy(input_any.at[place.core], input_ref, load_sems.at[3]),
    ]
    for each in sums[:pieces]:
        each.begin()
    for load in loads:
        load.start()
    gain_ref[...] = jnp.zeros_like(gain_ref)
    if sums:
        small, _, streams = sums
        mine, theirs, turned_in, turned_sems = scratch[7 * count :]
        lines_here = place.line * 2 < lines

        def line_of_turn(turn):
            return jnp.where(lines_here, lines - 1 - turn, turn)

        height = turned_in.shape[1]
        each_line = MATES * depth // height
        mates_each = height // depth

        def load_turned(index):
            line = line_of_turn(index // each_line)
            first = line * (MATES * depth) + index % each_line * height
            return pltpu.make_async_copy(
                turned.at[pl.ds(pl.multiple_of(first, 128), height)],
                turned_in.at[index % 2],
                turned_sems.at[index % 2],
            )

        kept = lax.broadcasted_iota(jnp.int32, (SMALL, CHUNK), 0)
        kept = (kept >= BETA_ROW) & (kept < BETA_ROW + heads)

        def weight_grads(first, last):
            for index in range(first * each_line, last * each_line):
                load_turned(index).wait()
                if index + 1 < lines * each_line:
                    load_turned(index + 1).start()
                line = line_of_turn(index // each_line)
                found = dot(turned_in[index % 2], grads[...], NN)
                for number in range(mates_each):
                    mate = index % each_line * mates_each + number
                    part = found[number * depth : (number + 1) * depth]
                    streams.held[line, mate] = part[:, :width].astype(low)
                    small.held[line, mate] = jnp.where(
                        kept, part[:, width:].T[:SMALL], small.held[line, mate].astype(wide)
                    ).astype(low)

        load_turned(0).start()
        sums[1].wait_loads()
        sums[1].round(1)
        loads[0].wait()
        small.wait_loads()
        weight_grads(0, 1)
        streams.round(1)
        weight_grads(1, 2)
    for load in loads[0 if not sums else 1 :]:
        load.wait()
    rows.begin()
    rows.send_far()
    rows.send_near()
    if sums:
        weight_grads(2, lines)
    for each in sums[1:]:
        each.round(2)
    rows.send_relayed()
    rows.wait_half(False)
    rows.wait_half(True)

    def body(here):
        part, gains = norm_back_rows(
            rows.total(here), input_ref[here].astype(wide), scale_ref[...]
        )
        low_grad[here] = (middle_grad_ref[here] + part).astype(low)
        gain_ref[...] += jnp.sum(gains, axis=0, keepdims=True)

    row_steps(0, tokens, body)
    first = make(0, low_grad, input_grad.at[place.core], place.sibling)
    first.start()
    first_local = pltpu.make_async_copy(low_grad, input_grad.at[place.core], load_sems.at[2])
    first_local.start()
    if sums:
        small.put_gains(gain_ref)
        mine[...] = small.held[...]
        swap = make(1, mine, theirs, place.sibling)
        swap.start()
        swap.wait_recv()
        small.add_top(theirs, CONV_ROW)
        small.direct()
    for each in sums[1:]:
        each.round(3)
    for each in sums[:1]:
        each.exchange_direct()
    for turn in range(4, lines):
        for each in sums[1:]:
            each.round(turn)
    for each in sums[1:]:
        each.exchange()
    rows.finish()
    first_local.wait()
    first.wait()
    if sums:
        swap.wait_send()
    for each in sums:
        each.finish(direct=each is sums[0])


def first_rows_kernel(input_ref, inputs, *scratch):
    place = Place()
    meet(place)
    share = ShareRows(place, input_ref.at[place.core], inputs, scratch)
    share.begin_half(False)
    share.begin_half(True)
    share.begin_rest()
    share.forward()
    share.forward_far()
    share.finish()


def first_rows(block_input):
    seqs, rows, columns = block_input.shape
    return remote_call(
        first_rows_kernel,
        0,
        [(block_input, "any")],
        [((seqs, MATES, rows, columns), low, "any")],
        ShareRows.scratch(),
    )[0]


def first_kernel(lines, pieces, input_ref, *rest):
    place = Place()
    blocks, rest = rest[:pieces], rest[pieces:]
    turned_out, raw_ref, logit_ref, small_ref, attn_out = rest[:5]
    others, scratch = rest[5 : 3 + pieces], rest[3 + pieces :]
    inputs, normed, turned, small, attn, scale, totals, out_sems = scratch[:8]
    scratch = scratch[8:]
    targets = (small, attn) + tuple(others)
    meet(place, far=True, lines=lines)
    share = ShareRows(place, input_ref.at[place.core], inputs, scratch[:3])
    gathers = [
        GatherLines(place, blocks[index], targets[index], scratch[3 + 6 * index : 9 + 6 * index])
        for index in range(pieces)
    ]
    few, main, later = gathers[:3]
    for gather in (few, main):
        gather.begin()
    for gather in (few, main):
        gather.leave()
    share.begin_half(False)
    share.begin_half(True)
    share.begin_rest()
    later.begin()
    for gather in (few, main):
        gather.onwards(1)
    later.leave()
    for step in range(2, lines):
        few.onwards(step)
    share.forward()
    later.onwards(1)
    small_ref[...] = small[...]
    _, _, tokens, model_width = inputs.shape
    depth = small.shape[3]
    parts = [(line, mate) for line in range(lines) for mate in range(MATES)]
    for index, (line, mate) in enumerate(parts):
        scale[:, index * depth : (index + 1) * depth] = small[line, mate, :1].astype(wide)
    beta = jnp.concatenate([small[line, mate] for line, mate in parts], axis=1)
    beta = over(beta, jnp.zeros((CHUNK - beta.shape[0], model_width), low))
    outs = []

    def norm(slot, mate):
        first = pl.multiple_of((slot * MATES + mate) * tokens, CHUNK)

        def body(here):
            value = inputs[slot, mate, here].astype(wide)
            there = pl.ds(pl.multiple_of(first + here.start, STEP), STEP)
            normed[there] = (value * inverse_rms(value) * scale[...]).astype(low)

        row_steps(0, tokens, body)
        block = pl.ds(first, tokens)
        logit_ref[block] = dot(normed[block], beta, NT)
        turned[:, block] = normed[block].T
        outs.append(
            pltpu.make_async_copy(
                turned.at[:, block], turned_out.at[:, block], out_sems.at[len(outs)]
            )
        )
        outs[-1].start()

    share.local().wait()
    for mate in (place.mate, place.x, place.y):
        norm(0, mate)
    main.onwards(2)
    share.forward_far()
    for gather in gathers[3:]:
        gather.begin()
    norm(0, place.far)
    later.onwards(2)
    for index, mate in ((6, place.mate), (7, place.x), (8, place.y)):
        share.copy(index).wait_recv()
        norm(1, mate)
    for index in (9, 10):
        share.copy(index).wait_recv()
    norm(1, place.far)
    height = MATES * depth
    lower = place.line * 2 < lines
    first_line = jnp.where(lower, 0, 1)
    last_line = jnp.where(lower, lines - 1, 0)
    width = attn.shape[3]

    def tile(index):
        return pl.ds(pl.multiple_of(index * tokens, STEP), tokens)

    def most(index, carry):
        here = tile(index)
        columns = pl.ds(pl.multiple_of(first_line * height, CHUNK), (lines - 1) * height)
        weight = attn[pl.ds(first_line, lines - 1)].reshape((lines - 1) * height, width)
        totals[here] = dot(normed[here, columns], weight, NN)
        return carry

    def rest_of(index, carry):
        here = tile(index)
        columns = pl.ds(pl.multiple_of(last_line * height, CHUNK), height)
        weight = attn[last_line].reshape(height, width)
        raw_ref[here] = (totals[here] + dot(normed[here, columns], weight, NN)).astype(low)
        return carry

    lax.fori_loop(0, 2 * MATES, most, 0)
    for step in range(3, lines):
        main.onwards(step)
    outs.append(pltpu.make_async_copy(attn, attn_out, out_sems.at[2 * MATES]))
    outs[-1].start()
    lax.fori_loop(0, 2 * MATES, rest_of, 0)
    for step in range(3, lines):
        later.onwards(step)
    share.finish(arrived=True)
    for gather in gathers[3:]:
        for slot in range(MATES):
            gather.arrive(slot)
    for out in outs:
        out.wait()
    for gather in gathers:
        gather.finish_plane()
    for gather in gathers[:3]:
        gather.finish_lines()


def first_call(block_input, blocks, lines):
    seqs, tokens, model_width = block_input.shape
    rows = seqs * MATES * tokens
    small, attn = ((lines,) + block.shape for block in blocks[:2])
    shared = (seqs, MATES, tokens, model_width)
    return remote_call(
        functools.partial(first_kernel, lines, len(blocks)),
        0,
        [(array, "any") for array in (block_input, *blocks)],
        [
            ((model_width, rows), low, "any"),
            ((rows, attn[3]), low, "held"),
            ((rows, CHUNK), wide, "held"),
            (small, low, "held"),
            (attn, low, "any"),
        ]
        + [((lines,) + block.shape, low, "any") for block in blocks[2:]],
        [
            pltpu.VMEM(shared, low),
            pltpu.VMEM((rows, model_width), low),
            pltpu.VMEM((model_width, rows), low),
            pltpu.VMEM(small, low),
            pltpu.VMEM(attn, low),
            pltpu.VMEM((1, model_width), wide),
            pltpu.VMEM((rows, attn[3]), wide),
            pltpu.SemaphoreType.DMA((2 * MATES + 1,)),
        ]
        + ShareRows.scratch()
        + GatherLines.scratch(lines) * len(blocks),
    )


def middle_rows(gathered, weights, block_input, scale, out_grad, moving, lines):
    _, rows, columns = block_input.shape
    shared = (2, MATES, rows, columns)
    arrays = [array for array, _ in moving]
    ups, downs = arrays
    several = 2 * MATES
    return remote_call(
        functools.partial(middle_kernel, lines, tuple(part for _, part in moving)),
        1,
        [(gathered, "held"), (weights, "any"), (block_input, "any"), (scale, "held"), (out_grad, "any")]
        + [(array, "any") for array in arrays],
        [
            ((rows, columns), wide, "held"),
            ((columns, several * rows), low, "any"),
            (shared, low, "any"),
            ((several * rows, ups.shape[3]), low, "any"),
            ((several * rows, downs.shape[2]), low, "any"),
        ]
        + [(array.shape, low, "any") for array in arrays],
        [
            pltpu.VMEM((rows, columns), low),
            pltpu.VMEM(weights.shape, low),
            pltpu.SemaphoreType.DMA((2, MATES)),
            pltpu.VMEM(shared, low),
            pltpu.VMEM((columns, several * rows), low),
            pltpu.VMEM(ups.shape, low),
            pltpu.VMEM((several, rows, ups.shape[3]), low),
            pltpu.VMEM((several, rows, downs.shape[2]), low),
            pltpu.SemaphoreType.DMA((3, several)),
            pltpu.SemaphoreType.DMA((3,)),
            pltpu.VMEM((rows, columns), low),
        ]
        + ShareRows.scratch() * 2
        + GatherLines.scratch(lines) * len(arrays),
        {5 + index: 5 + index for index in range(len(arrays))},
    )


def turn_rows(
    acts, grads, ups, weights, turned, hidden, downs, out_grad, middle, scale, downward_grad, ups_rows,
    lines,
):
    rows, columns = middle.shape
    width = weights.shape[-1]
    blocks = (2, MATES, rows, width)
    all_rows, units = hidden.shape
    scratch = [
        pltpu.VMEM(weights.shape[1:], low),
        pltpu.SemaphoreType.DMA((3 + lines * MATES,)),
        pltpu.VMEM(blocks, low),
        pltpu.VMEM(acts.shape, low),
        pltpu.VMEM(ups.shape, low),
        pltpu.VMEM((units, columns), low),
        pltpu.VMEM((2, rows, columns), low),
        pltpu.VMEM((2, rows, acts.shape[1]), low),
        pltpu.SemaphoreType.DMA((2, 2)),
        pltpu.VMEM((2, rows, units), low),
        pltpu.VMEM((2, rows, columns), low),
        pltpu.SemaphoreType.DMA((2, 2)),
        pltpu.SemaphoreType.DMA((2, 2)),
        pltpu.VMEM((rows, columns), low),
    ]
    scratch += SumRows.scratch(rows, columns, True) + SwapBlocks.scratch()
    outs, parts = [], ()
    if downward_grad is not None:
        depth = ups.shape[2]
        parts = ((0, units), (0, ups_rows))
        for shape in ((MATES, units, depth), (MATES, ups_rows, acts.shape[1])):
            scratch += SumLines.scratch(lines, shape)
            outs.append((shape, low, "any"))
    return remote_call(
        functools.partial(turn_rows_kernel, lines, parts),
        2,
        [(array, "any") for array in (acts, grads, ups, weights, turned, hidden, downs, out_grad)]
        + [(array, "held") for array in (middle, scale)]
        + [(downward_grad, "any")] * bool(parts),
        [
            ((rows, columns), wide, "held"),
            ((1, columns), wide, "held"),
            ((rows, columns), low, "held"),
            (blocks, low, "any"),
            ((turned.shape[0], acts.shape[1]), low, "any"),
            ((all_rows, columns), low, "any"),
        ]
        + outs,
        scratch,
    )


def last_rows(
    all_grads, attn, turned, block_input, beta, middle_grad, scale, blocks, lines, heads
):
    _, rows, columns = block_input.shape
    scratch = [
        pltpu.VMEM((rows, columns), low),
        pltpu.VMEM(all_grads.shape, low),
        pltpu.VMEM(attn.shape, low),
        pltpu.SemaphoreType.DMA((4,)),
        pltpu.VMEM((rows, columns), low),
    ]
    scratch += SumRows.scratch(rows, columns, True) + [pltpu.SemaphoreType.DMA((2,))] * 2
    results = [block.shape[1:] for block in blocks] + [attn.shape[1:]] * bool(blocks)
    for shape in results:
        scratch += SumLines.scratch(lines, shape)
    if blocks:
        scratch += [pltpu.VMEM(blocks[0].shape, low)] * 2
        scratch += [pltpu.VMEM((2, 256, turned.shape[1]), low), pltpu.SemaphoreType.DMA((2,))]
    return remote_call(
        functools.partial(last_rows_kernel, lines, len(blocks), heads),
        3,
        [(array, "any") for array in (all_grads, attn, turned, block_input)]
        + [(array, "held") for array in (beta, middle_grad, scale)]
        + [(block, "any") for block in blocks],
        [((2, rows, columns), low, "any"), ((1, columns), wide, "held")]
        + [(shape, low, "any") for shape in results],
        scratch,
    )


class Steps:
    def __init__(self, seqs, heads, span):
        self.seqs, self.heads, self.span = seqs, heads, span
        self.chains, self.chunks = seqs * heads, span // CHUNK

    def chain(self, step, when):
        if when == "first":
            return jnp.minimum(step, self.chains - 1)
        if when == "second":
            return jnp.maximum(step - self.chains, 0)
        return step % self.chains

    def rows(self, when, columns, place):
        def index(step):
            chain = self.chain(step, when)
            return chain // self.heads, place(chain % self.heads)

        return pl.BlockSpec((self.span, columns), index)

    def streams(self, when):
        return self.rows(when, 3 * CHUNK, lambda head: head)

    def head(self, when):
        return self.rows(when, CHUNK, lambda head: head)

    def gate(self, when):
        return self.rows(when, CHUNK, lambda head: 3 * self.heads + head)

    def logit(self, when):
        return self.rows(when, CHUNK, lambda head: 0)

    def taps(self, when):
        return pl.BlockSpec(
            (1, 3 * CONV, CHUNK), lambda step: (self.chain(step, when) % self.heads, 0, 0)
        )

    def blocks(self, when, columns=CHUNK):
        return pl.BlockSpec(
            (1, self.chunks, CHUNK, columns), lambda step: (self.chain(step, when), 0, 0, 0)
        )

    def few(self, when, columns):
        return pl.BlockSpec((1, 8, columns), lambda step: (self.chain(step, when), 0, 0))

    def whole(self, shape):
        return pl.BlockSpec(shape, lambda step: (0,) * len(shape), pipeline_mode=pl.Buffered(1))

    def call(self, body, identity, ins, outs, scratch, aliases=None):
        return pl.pallas_call(
            body,
            grid=(2 * self.chains,),
            in_specs=[spec for _, spec in ins],
            out_specs=[spec for _, _, spec in outs],
            out_shape=[jax.ShapeDtypeStruct(shape, dtype) for shape, dtype, _ in outs],
            scratch_shapes=scratch,
            input_output_aliases=aliases or {},
            compiler_params=pltpu.CompilerParams(
                vmem_limit_bytes=VMEM_BYTES,
                dimension_semantics=("arbitrary",),
                collective_id=identity,
                has_side_effects=True,
            ),
        )(*[array for array, _ in ins])


def delta_front(lengths, raw, taps, logits, scale, moving, lines, seqs, heads, span):
    steps = Steps(seqs, heads, span)
    chains, chunks, size = steps.chains, steps.chunks, CHUNK
    squares, doubles = (chains, chunks, CHUNK, size), (chains, chunks, CHUNK, 2 * size)
    states, tails = (chains, size, size), (seqs, 16, 3 * heads * size)
    tokens = span // MATES
    anywhere = pl.BlockSpec(memory_space=pl.ANY)
    arrays = [array for array, _ in moving]
    ins = [
        (lengths, pl.BlockSpec(memory_space=pltpu.SMEM)),
        (raw, anywhere),
        (raw, steps.streams("first")),
        (taps, steps.taps("first")),
        (logits, steps.logit("first")),
        (raw, steps.gate("second")),
        (scale, steps.whole((1, size))),
    ] + [(array, anywhere) for array in arrays]
    outs = [
        ((seqs * span, 3 * heads * size), low, steps.streams("first")),
        (squares, wide, steps.blocks("first")),
        (doubles, wide, steps.blocks("first", 2 * size)),
        (squares, wide, steps.blocks("first")),
        (states, wide, steps.whole(states)),
        (tails, low, steps.whole(tails)),
        (squares, wide, steps.blocks("second")),
        (squares, wide, steps.blocks("second")),
        ((seqs * span, heads * size), wide, steps.head("second")),
        ((seqs * span, heads * size), low, steps.head("second")),
        ((seqs, MATES, tokens, heads * size), low, anywhere),
        ((seqs, MATES) + arrays[0].shape, low, anywhere),
    ] + [(array.shape, low, anywhere) for array in arrays]
    scratch = [
        pltpu.VMEM((span + 16, 3 * size), wide),
        pltpu.VMEM(squares, wide),
        pltpu.VMEM(squares, wide),
        pltpu.VMEM(squares, wide),
        pltpu.VMEM(squares, wide),
        pltpu.VMEM(doubles, wide),
        pltpu.VMEM((chains, span, 3 * size), low),
        pltpu.VMEM(states, low),
        pltpu.VMEM(states, low),
        pltpu.VMEM(tails, low),
        pltpu.SemaphoreType.DMA((2, seqs)),
        pltpu.SemaphoreType.DMA((2, chains)),
        pltpu.VMEM((seqs, span, heads * size), low),
    ]
    scratch += ShareRows.scratch() + SwapBlocks.scratch()
    scratch += GatherLines.scratch(lines) * len(arrays)
    moves = tuple(part for _, part in moving)
    return steps.call(
        functools.partial(front_kernel, lines, heads, moves),
        4,
        ins,
        outs,
        scratch,
        {7 + index: 12 + index for index in range(len(arrays))},
    )


def delta_back(
    lengths, raw, tails, taps, logits, scale, qkv, wu, maps, total, grad, mixed, solved, state, fresh,
    row_grad, mlp_partial, middle, summing, lines, seqs, heads, span,
):
    steps = Steps(seqs, heads, span)
    chains, chunks, size = steps.chains, steps.chunks, CHUNK
    squares, states = (chains, chunks, CHUNK, size), (chains, size, size)
    all_shape = (seqs * span, (4 * heads + 1) * size)
    anywhere = pl.BlockSpec(memory_space=pl.ANY)
    ins = [
        (lengths, pl.BlockSpec(memory_space=pltpu.SMEM)),
        (raw, steps.streams("second")),
        (tails, steps.whole(tails.shape)),
        (taps, steps.taps("second")),
        (logits, steps.logit("second")),
        (raw, steps.gate("first")),
        (scale, steps.whole((1, size))),
        (qkv, steps.streams("both")),
        (wu, steps.blocks("both", 2 * size)),
        (maps, steps.blocks("first")),
        (total, steps.whole(states)),
        (grad, steps.head("first")),
        (mixed, steps.head("first")),
        (solved, steps.blocks("second")),
        (state, steps.blocks("second")),
        (fresh, steps.blocks("second")),
        (row_grad, anywhere),
        (mlp_partial, anywhere),
        (middle, steps.whole(middle.shape)),
    ] + [(array, anywhere) for array, _ in summing]
    outs = [
        (all_shape, low, steps.whole(all_shape)),
        ((chains, 8, size), wide, steps.few("first", size)),
        ((chains, 8, 3 * size), wide, steps.few("second", 3 * size)),
        ((seqs, MATES) + row_grad.shape, low, anywhere),
        ((seqs,) + row_grad.shape, low, anywhere),
    ]
    edges = (chains, 16, 3 * size)
    scratch = [
        pltpu.VMEM((span + 16, 3 * size), wide),
        pltpu.VMEM((span + 32, 3 * size), wide),
        pltpu.VMEM(squares, wide),
        pltpu.VMEM(squares, wide),
        pltpu.VMEM(squares, wide),
        pltpu.VMEM(squares, wide),
        pltpu.VMEM(squares, wide),
        pltpu.VMEM(states, low),
        pltpu.VMEM(states, low),
        pltpu.VMEM(edges, low),
        pltpu.VMEM(edges, wide),
        pltpu.VMEM(edges, low),
        pltpu.SemaphoreType.DMA((2, chains)),
        pltpu.SemaphoreType.DMA((2, chains)),
    ] + ShareRows.scratch()
    scratch += [pltpu.VMEM(row_grad.shape, low)] + [pltpu.SemaphoreType.DMA((1,))] * 3
    scratch += SumRows.scratch(*row_grad.shape)
    for array, (_, height) in summing:
        shape = (MATES, height, array.shape[3])
        scratch += SumLines.scratch(lines, shape)
        outs.append((shape, low, anywhere))
    return steps.call(
        functools.partial(back_kernel, lines, heads, tuple(part for _, part in summing)),
        5,
        ins,
        outs,
        scratch,
    )


def tiled_call(body, ins, wholes, outs):
    tile = 256

    def tall(shape):
        return pl.BlockSpec((tile, shape[1]), lambda step: (step, 0))

    def whole(array):
        return pl.BlockSpec(array.shape, lambda step: (0, 0), pipeline_mode=pl.Buffered(1))

    return pl.pallas_call(
        body,
        grid=(ins[0].shape[0] // tile,),
        in_specs=[tall(array.shape) for array in ins] + [whole(array) for array in wholes],
        out_specs=[tall(shape) for shape, _ in outs],
        out_shape=[jax.ShapeDtypeStruct(shape, dtype) for shape, dtype in outs],
        compiler_params=pltpu.CompilerParams(vmem_limit_bytes=VMEM_BYTES),
    )(*ins, *wholes)


def project(inputs, scale, weight, beta):
    rows, model_width = inputs.shape
    return tiled_call(
        project_kernel,
        (inputs,),
        (scale, weight, beta),
        [((rows, model_width), low), ((rows, weight.shape[1]), low), ((rows, beta.shape[0]), wide)],
    )


def held_call(body, ins, outs):
    held = pl.BlockSpec(memory_space=pltpu.VMEM)
    return pl.pallas_call(
        body,
        in_specs=[held] * len(ins),
        out_specs=[held] * len(outs),
        out_shape=[jax.ShapeDtypeStruct(shape, dtype) for shape, dtype in outs],
        compiler_params=pltpu.CompilerParams(vmem_limit_bytes=VMEM_BYTES),
    )(*ins)


def pack_kernel(
    heads, query, key, value, outgate, output, swish, upward, downward,
    attn_ref, output_ref, ups_ref, downs_ref,
):
    size = CHUNK
    width = heads * size
    units = downs_ref.shape[1]
    for mate in range(MATES):
        first = mate * width
        for head in range(heads):
            for stream, weight in enumerate((query, key, value)):
                lanes = (3 * head + stream) * size
                attn_ref[mate, :, lanes : lanes + size] = weight[
                    :, first + head * size : first + (head + 1) * size
                ].astype(low)
        attn_ref[mate, :, 3 * width : 4 * width] = outgate[:, first : first + width].astype(low)
        output_ref[mate] = output[first : first + width, :].T.astype(low)
        here = mate * units
        ups_ref[mate, :, :units] = swish[:, here : here + units].astype(low)
        ups_ref[mate, :, units:] = upward[:, here : here + units].astype(low)
        downs_ref[mate] = downward[here : here + units, :].astype(low)


def unpack_kernel(
    heads, attn, outs, ups_low, ups_high, downs,
    query, key, value, outgate, output, swish, upward, downward,
):
    size = CHUNK
    width = heads * size
    units = downs.shape[1]
    for mate in range(MATES):
        first = mate * width
        for head in range(heads):
            for stream, grad in enumerate((query, key, value)):
                lanes = (3 * head + stream) * size
                grad[:, first + head * size : first + (head + 1) * size] = attn[
                    mate, :, lanes : lanes + size
                ].astype(wide)
        outgate[:, first : first + width] = attn[mate, :, 3 * width : 4 * width].astype(wide)
        output[first : first + width, :] = outs[mate].astype(wide).T
        here = mate * units
        ups = over(ups_low[mate], ups_high[mate]).astype(wide)
        swish[:, here : here + units] = ups[:, :units]
        upward[:, here : here + units] = ups[:, units:]
        downward[here : here + units, :] = downs[mate].astype(wide)


def cut_columns(weight):
    depth, columns = weight.shape
    return weight.reshape(depth, MATES, columns // MATES).transpose(1, 0, 2)


def join_columns(blocks):
    return blocks.transpose(1, 0, 2).reshape(blocks.shape[1], -1)


def gather_weights(blocks):
    return gather_lines(swap_blocks(blocks))


def scatter_grads(blocks):
    return swap_blocks(scatter_lines(blocks.astype(low))).astype(wide)


def on_device(
    block_input,
    lengths,
    attn_gain,
    query_weight,
    key_weight,
    value_weight,
    outgate_weight,
    beta_weight,
    conv_kernel,
    head_gain,
    output_weight,
    mlp_gain,
    swish_weight,
    upward_weight,
    downward_weight,
    out_grad,
):
    count = lax.axis_size("seq")
    lines = count // MATES
    core = lax.axis_index("tp")
    seq_count, tokens, model_width = block_input.shape
    depth = attn_gain.shape[0]
    gain_part = head_gain.shape[0]
    head_size = gain_part * count
    heads = beta_weight.shape[1] // MATES
    width = heads * head_size
    units = swish_weight.shape[1] // MATES

    conv_rows = -(-heads * 3 * CONV * gain_part // CHUNK)
    near = 1 < lines <= 4 and depth == CHUNK and conv_rows == BETA_ROW - CONV_ROW
    rows = seq_count * MATES * tokens
    span = MATES * tokens

    def in_rows(array):
        return jnp.pad(array, ((0, 0), (0, -array.shape[1] % 128)))

    def gains_of(attn, mlp, head):
        return jnp.concatenate([attn, mlp, in_rows(head)], axis=1)

    gains_cut = gains_of(attn_gain[None], mlp_gain[None], head_gain[None]).astype(low)
    conv_cut = in_rows(conv_kernel.astype(low).reshape(MATES, -1))
    beta_cut = beta_weight.astype(low).reshape(depth, MATES, heads).transpose(1, 2, 0)
    small_cut = jnp.concatenate(
        [jnp.broadcast_to(gains_cut, (MATES, gains_cut.shape[1])), conv_cut], axis=1
    )
    conv_start, conv_size = gains_cut.shape[1], heads * 3 * CONV * gain_part
    beta_start = small_cut.shape[1]
    small_cut = jnp.concatenate([small_cut, beta_cut.reshape(MATES, -1)], axis=1)
    small_size = small_cut.shape[1]
    small_cut = jnp.pad(small_cut, ((0, 0), (0, SMALL * 128 - small_size)))
    small_cut = small_cut.reshape(MATES, SMALL, 128)
    streams_end, gates_end = 3 * width, 4 * width
    if near:
        cuts = held_call(
            functools.partial(pack_kernel, heads),
            (
                query_weight, key_weight, value_weight, outgate_weight, output_weight,
                swish_weight, upward_weight, downward_weight,
            ),
            [
                ((MATES, depth, columns), low)
                for columns in (gates_end, width, 2 * units)
            ]
            + [((MATES, units, depth), low)],
        )
        normed_turned, raw, logits, small, attn_full, output_full, ups_full, downward_full = first_call(
            block_input, (small_cut, *cuts), lines
        )
        ups_split = depth // 128 * 96
        front_moves = ((output_full, None), (ups_full, (0, ups_split)))
    else:
        streams_cut = jnp.stack(
            [
                w.astype(low).reshape(depth, MATES, heads, head_size)
                for w in (query_weight, key_weight, value_weight)
            ],
            axis=3,
        )
        streams_cut = streams_cut.transpose(1, 0, 2, 3, 4).reshape(MATES, depth, streams_end)
        cuts = (
            small_cut,
            jnp.concatenate([streams_cut, cut_columns(outgate_weight.astype(low))], axis=2),
            cut_columns(output_weight.astype(low).T),
            jnp.concatenate([cut_columns(w.astype(low)) for w in (swish_weight, upward_weight)], axis=2),
            downward_weight.astype(low).reshape(MATES, units, depth),
        )
        input_rows = first_rows(block_input).reshape(rows, model_width)
        small, attn_full, output_full, ups_full, downward_full = (gather_weights(cut) for cut in cuts)
        front_moves = ((output_full, None),)
    attn_blocks = attn_full
    attn_full = attn_full.reshape(model_width, gates_end)
    small = small.reshape(count, SMALL * 128)
    attn_scale = small[:, :depth].reshape(1, model_width).astype(wide)
    mlp_scale = small[:, depth : 2 * depth].reshape(1, model_width).astype(wide)
    head_scale = small[:, 2 * depth : 2 * depth + gain_part].reshape(1, head_size).astype(wide)
    taps = (
        small[:, conv_start : conv_start + conv_size]
        .reshape(count, heads, 3, CONV, gain_part)
        .transpose(1, 2, 3, 0, 4)
        .reshape(heads, 3 * CONV, head_size)
        .astype(wide)
    )
    beta_rows = (
        small[:, beta_start:small_size]
        .reshape(count, heads, depth)
        .transpose(1, 0, 2)
        .reshape(heads, model_width)
    )
    beta_rows = jnp.pad(beta_rows, ((BETA_ROW, CHUNK - BETA_ROW - heads), (0, 0)))

    blocked = (seq_count, MATES, tokens, model_width)

    if not near:
        flat_normed, raw, logits = project(input_rows, attn_scale, attn_full, beta_rows)
        normed_turned = flat_normed.T
    sizes_of = (lines, seq_count, heads, span)
    (
        qkv, solved, wu, maps, total, tails, state, fresh, mixed, gated, gathered, output_all, *moved
    ) = delta_front(lengths, raw, taps, logits, head_scale, front_moves, *sizes_of)
    middle_moves = ((ups_full, None), (downward_full, None))
    if near:
        middle_moves = ((moved[1], (ups_split, depth - ups_split)), (downward_full, (0, units)))
    middle, mlp_turned, grad_rows, acts, hidden, ups_full, downward_blocks = middle_rows(
        gathered, output_all, block_input, mlp_scale, out_grad, middle_moves, lines
    )
    downward_grad = matmul(
        "rf,rd->fd", hidden, grad_rows.reshape(rows, model_width)
    ).astype(low)

    def cut_rows(grad):
        return grad.reshape(lines, MATES, depth, grad.shape[1])

    ups_rows = depth // 4
    if not near:
        downward_blocks = downward_blocks.transpose(2, 0, 1, 3).reshape(units, model_width)
    middle_grad, mlp_gain_grad, attn_grad_mine, gated_grad, ups_grad, mlp_part, *summed = turn_rows(
        acts, grad_rows, ups_full, output_all, mlp_turned, hidden, downward_blocks, out_grad, middle,
        mlp_scale, downward_grad if near else None, ups_rows, lines,
    )
    ups_grad = cut_rows(ups_grad)
    back_sums = ((ups_grad, (ups_rows, depth - ups_rows)),) if near else ()
    if near:
        downward_sum, ups_low = summed
    all_grads, head_gain_parts, taps_grad, attn_grad_rows, block_output, *summed = delta_back(
        lengths, raw, tails, taps, logits, head_scale, qkv, wu, maps, total,
        gated_grad.reshape(rows, width), mixed, solved, state, fresh, attn_grad_mine, mlp_part.reshape(blocked), middle,
        back_sums, *sizes_of,
    )
    attn_grad_rows = attn_grad_rows.reshape(rows, model_width)
    output_grad = cut_rows(matmul("rd,rc->dc", attn_grad_rows, gated).astype(low))
    beta_grad = jnp.zeros((model_width, heads), low)
    if not near:
        attn_grads = matmul("dr,rc->dc", normed_turned, all_grads).astype(low)
        beta_grad = attn_grads[:, gates_end + BETA_ROW : gates_end + BETA_ROW + heads]
        attn_grads = cut_rows(attn_grads)

    conv_grad = (
        taps_grad[:, :CONV]
        .reshape(seq_count, heads, CONV, 3, count, gain_part)
        .sum(axis=0)
        .transpose(3, 0, 2, 1, 4)
        .reshape(count, -1)
    )

    def small_blocks(attn_gain_grad):
        gains = gains_of(
            attn_gain_grad.reshape(count, depth),
            mlp_gain_grad.reshape(count, depth),
            jnp.sum(head_gain_parts[:, 0], axis=0).reshape(count, gain_part),
        )
        beta = beta_grad.reshape(count, depth, heads).transpose(0, 2, 1).reshape(count, -1)
        flat = jnp.concatenate([gains.astype(low), in_rows(conv_grad.astype(low)), beta], axis=1)
        flat = jnp.pad(flat, ((0, 0), (0, SMALL * 128 - small_size)))
        return flat.reshape(lines, MATES, SMALL, 128)

    last_ins = (all_grads, attn_blocks, normed_turned, block_input, beta_rows, middle_grad, attn_scale)
    if near:
        ups_high, = summed
        blocks = (small_blocks(jnp.zeros((1, model_width), wide)), output_grad)
        input_grad, _, small_sum, output_sum, attn_sum = last_rows(*last_ins, blocks, lines, heads)
        grads = held_call(
            functools.partial(unpack_kernel, heads),
            (attn_sum, output_sum, ups_low, ups_high, downward_sum),
            [
                (w.shape, wide)
                for w in (
                    query_weight, key_weight, value_weight, outgate_weight, output_weight,
                    swish_weight, upward_weight, downward_weight,
                )
            ],
        )
        small_sum = small_sum.reshape(MATES, SMALL * 128).astype(wide)
        gains_sum = jnp.sum(small_sum[:, :conv_start], axis=0)
    else:
        input_grad, attn_gain_grad = last_rows(*last_ins, (), lines, heads)
        downward_cut = downward_grad.reshape(units, lines, MATES, depth).transpose(1, 2, 0, 3)
        small_sum, attn_sum, output_sum, ups_sum, downward_sum = (
            scatter_grads(block)
            for block in (
                small_blocks(attn_gain_grad), attn_grads[..., :gates_end], output_grad, ups_grad, downward_cut
            )
        )
        small_sum = small_sum.reshape(MATES, SMALL * 128)
        gains_sum = jnp.sum(small_sum[:, :conv_start], axis=0)
        gains_sum = gains_sum + other_core(gains_sum)
        streams_sum = (
            attn_sum[:, :, :streams_end]
            .reshape(MATES, depth, heads, 3, head_size)
            .transpose(3, 1, 0, 2, 4)
            .reshape(3, depth, MATES * width)
        )
        grads = (
            streams_sum[0],
            streams_sum[1],
            streams_sum[2],
            join_columns(attn_sum[:, :, streams_end:gates_end]),
            join_columns(output_sum).T,
            join_columns(ups_sum[:, :, :units]),
            join_columns(ups_sum[:, :, units:]),
            downward_sum.reshape(MATES * units, depth),
        )
    conv_sum = small_sum[:, conv_start : conv_start + conv_size]
    beta_sum = small_sum[:, beta_start:small_size].reshape(MATES * heads, depth).T
    return (
        block_output,
        input_grad,
        gains_sum[:depth],
        *grads[:4],
        beta_sum,
        conv_sum.reshape(MATES * heads, 3, CONV, gain_part),
        gains_sum[2 * depth : 2 * depth + gain_part],
        grads[4],
        gains_sum[depth : 2 * depth],
        *grads[5:],
    )


def solution(mesh):
    return jax.shard_map(
        on_device,
        mesh=mesh,
        in_specs=(
            P(None, "seq", None),
            P(),
            P("seq"),
            P("seq", "tp"),
            P("seq", "tp"),
            P("seq", "tp"),
            P("seq", "tp"),
            P("seq", "tp"),
            P("tp", None, None, "seq"),
            P("seq"),
            P("tp", "seq"),
            P("seq"),
            P("seq", "tp"),
            P("seq", "tp"),
            P("tp", "seq"),
            P(None, "seq", None),
        ),
        out_specs=(
            P(None, "seq", None),
            P(None, "seq", None),
            P("seq"),
            P("seq", "tp"),
            P("seq", "tp"),
            P("seq", "tp"),
            P("seq", "tp"),
            P("seq", "tp"),
            P("tp", None, None, "seq"),
            P("seq"),
            P("tp", "seq"),
            P("seq"),
            P("seq", "tp"),
            P("seq", "tp"),
            P("tp", "seq"),
        ),
        check_vma=False,
    )
```
